32 devices in a mesh: dp: 8 (over z, y), chan: 4 (over x, core).
Axes of the slice: x: 2, y: 2, z: 4, core: 2. Of those that a mesh axis runs over, the one named last changes fastest.
Arguments:
- frames_in: bfloat16 [24, 512, 512], P('dp', None, 'chan'), may hold values from -6 to 6
- segments: int32 [24, 512], P('dp'), may hold values from 0 to 7, never falling along the last dimension, each value on 1 to 128 neighbouring positions
- cotangent: bfloat16 [24, 512, 512], P('dp', None, 'chan'), may hold values from -6 to 6
- channel_params: float32 [2, 12, 512], P(None, None, 'chan'), may hold values from -4 to 4, as said below
- weight_up: float32 [2, 512, 1536], P(None, None, 'chan'), may hold values from -0.25 to 0.25
- bias_up: float32 [2, 1536], P(None, 'chan'), may hold values from -3 to 3
- weight_down: float32 [2, 1536, 512], P(None, 'chan'), may hold values from -0.15625 to 0.15625
- momentum_channel: float32 [2, 12, 512], P(None, None, 'chan'), may hold values from -60 to 60
- variance_channel: float32 [2, 12, 512], P(None, None, 'chan'), may hold values from 100 to 10000
- momentum_up: float32 [2, 512, 1536], P(None, 'dp', 'chan'), may hold values from -60 to 60
- variance_up: float32 [2, 512, 1536], P(None, 'dp', 'chan'), may hold values from 100 to 10000
- momentum_bias: float32 [2, 1536], P(None, 'chan'), may hold values from -60 to 60
- variance_bias: float32 [2, 1536], P(None, 'chan'), may hold values from 100 to 10000
- momentum_down: float32 [2, 1536, 512], P(None, 'chan', 'dp'), may hold values from -60 to 60
- variance_down: float32 [2, 1536, 512], P(None, 'chan', 'dp'), may hold values from 100 to 10000
Outputs:
- layer_output: bfloat16 [24, 512, 512], P('dp', None, 'chan')
- input_grad: bfloat16 [24, 512, 512], P('dp', None, 'chan')
- params_channel: float32 [2, 12, 512], P(None, None, 'chan')
- params_up: float32 [2, 512, 1536], P(None, None, 'chan')
- params_bias: float32 [2, 1536], P(None, 'chan')
- params_down: float32 [2, 1536, 512], P(None, 'chan')
- first_channel: float32 [2, 12, 512], P(None, None, 'chan')
- second_channel: float32 [2, 12, 512], P(None, None, 'chan')
- first_up: float32 [2, 512, 1536], P(None, 'dp', 'chan')
- second_up: float32 [2, 512, 1536], P(None, 'dp', 'chan')
- first_bias: float32 [2, 1536], P(None, 'chan')
- second_bias: float32 [2, 1536], P(None, 'chan')
- first_down: float32 [2, 1536, 512], P(None, 'chan', 'dp')
- second_down: float32 [2, 1536, 512], P(None, 'chan', 'dp')
The draws below stay inside these ranges and needn't reach their ends.
Inputs may be any that keep to these rules, and one draw needn't show every extreme that they name: `segments`: along each row the ids never fall; a run of equal ids is one utterance of 1 to 128 frames, and some run in the row has exactly 128. `channel_params`: rows 0 to 6 hold the taps, 7 the conv bias, 8 and 9 the norm gain and bias, 10 the down bias, 11 the layer scale; the norm gains and layer scales lie in 0.5 to 1.5.
All inputs are finite; a program needn't handle non-finite values.
Results may differ from the reference program's by a relative error of at most 0.0085.
Values may be sent and summed in bfloat16 or wider, within the bound.
No kernel may reach another device: no remote copies, remote signals or barrier semaphores. Data moves between devices by JAX's collectives and lax.ppermute only.
A program may use at most 128 MiB of HBM per device.

```python
import math
import jax
import jax.numpy as jnp
import numpy as np
from jax import lax

C = 512
H = 1536
LAYERS = 2
FRAMES = 512
ROWS = 24


def draw_channel_params(key, part):
    key = jax.random.fold_in(key, 11)
    keys = jax.random.split(key, 4)
    position = jnp.arange(C, dtype=jnp.float32) / C
    spread = jnp.exp(jax.random.uniform(keys[0], (LAYERS, 1, C), minval=-0.7, maxval=0.7))
    channel_scale = 0.4 * jnp.exp(jnp.log(3.0) * position) * spread
    base = jnp.clip(jax.random.normal(keys[1], (LAYERS, 7, C)), -3.0, 3.0)
    taps = base * 0.38 * channel_scale
    shifts = 0.3 * jnp.clip(jax.random.normal(keys[2], (LAYERS, 3, C)), -3.0, 3.0)
    gains = jax.random.uniform(keys[3], (LAYERS, 2, C), minval=0.5, maxval=1.5)
    return jnp.concatenate([taps, shifts[:, 0:1], gains[:, 0:1], shifts[:, 1:2], shifts[:, 2:3], gains[:, 1:2]], axis=1).astype(jnp.float32)


def block_scale(stream_key, extent, pieces, smallest, largest):
    factor_of = 1.0
    for axis_at, parts in pieces:
        steps = jax.random.uniform(jax.random.fold_in(jax.random.fold_in(stream_key, 6), axis_at), (parts,), jnp.float32, smallest / len(pieces), largest / len(pieces))
        factor_of = factor_of * jnp.repeat(jnp.exp(steps), extent[axis_at] // parts).reshape((-1,) + (1,) * (len(extent) - 1 - axis_at))
    return factor_of


def split_up(count, total, reach, skew):
    loads = [(1 << 20) // math.isqrt(grade ** skew) + 1 for grade in range(2, count + 1)]
    rest, given = total - reach - (count - 1), [1] * (count - 1)
    while rest > 0:
        movable = [i for i in range(count - 1) if given[i] < reach]
        mass, left = sum([loads[i] for i in movable]), rest
        for i in movable:
            addition = min(reach - given[i], max(1, left * loads[i] // mass), rest)
            given[i] = given[i] + addition
            rest = rest - addition
    return np.array([reach] + given)


def uneven_parts(key, count, total, reach, skew):
    if count == 2:
        one = jax.random.randint(key, (), max(1, total - reach), min(reach, total - 1) + 1)
        return jnp.stack([one, total - one])
    lengths = jnp.asarray(split_up(count, total, reach, skew), jnp.int32)
    pairs = (count - 1) // 2
    source_of, taker = lengths[1:1 + 2 * pairs:2], lengths[2:2 + 2 * pairs:2]
    margin = jnp.minimum(source_of - 1, reach - taker)
    passed = jax.random.randint(jax.random.fold_in(key, 1), (pairs,), 0, 1 << 20) % (margin + 1)
    lengths = lengths.at[1:1 + 2 * pairs:2].set(source_of - passed).at[2:2 + 2 * pairs:2].set(taker + passed)
    return lengths[jax.random.permutation(jax.random.fold_in(key, 2), count)]


def gaussian(key, dims, width, most, cuts=(), held_as=jnp.bfloat16):
    array = jax.random.normal(key, dims, jnp.float32) * width
    if len(cuts) > 0:
        array = block_scale(key, dims, cuts, -0.22, 0.18) * array
    return jnp.clip(array, min=-most, max=most).astype(held_as)


def setup_inputs(seed: int = 0) -> dict:
    key_of = jax.random.split(jax.random.key(seed), 16)
    return {
        "frames_in": gaussian(key_of[0], (ROWS, FRAMES, C), 1.0, 6.0, ((0, 8), (2, 4))),
        "segments": jax.vmap(lambda own: jnp.searchsorted(jnp.cumsum(uneven_parts(own, 8, FRAMES, FRAMES // 4, 0)), jnp.arange(FRAMES), side="right"))(jax.random.split(key_of[1], ROWS)).reshape((ROWS, FRAMES)).astype(jnp.int32),
        "cotangent": gaussian(key_of[2], (ROWS, FRAMES, C), 1.0, 6.0, ((0, 8), (2, 4))),
        "channel_params": draw_channel_params(jax.random.fold_in(key_of[15], 71), 0),
        "weight_up": gaussian(key_of[4], (LAYERS, C, H), C ** -0.5, 0.25, ((2, 4),), jnp.float32),
        "bias_up": gaussian(key_of[5], (LAYERS, H), 0.3, 3.0, ((1, 4),), jnp.float32),
        "weight_down": gaussian(key_of[6], (LAYERS, H, C), H ** -0.5, 0.15625, ((1, 4),), jnp.float32),
        "momentum_channel": gaussian(key_of[7], (LAYERS, 12, C), 10.0, 60.0, ((2, 4),), jnp.float32),
        "variance_channel": jnp.clip(jnp.exp(math.log(10000.0) - 4.6051702 * jax.random.uniform(key_of[8], (LAYERS, 12, C), jnp.float32) ** block_scale(key_of[8], (LAYERS, 12, C), ((2, 4),), -0.2, 0.2)), 100.0, 10000.0),
        "momentum_up": gaussian(key_of[9], (LAYERS, C, H), 10.0, 60.0, ((1, 8), (2, 4)), jnp.float32),
        "variance_up": jnp.clip(jnp.exp(math.log(10000.0) - 4.6051702 * jax.random.uniform(key_of[10], (LAYERS, C, H), jnp.float32) ** block_scale(key_of[10], (LAYERS, C, H), ((1, 8), (2, 4)), -0.2, 0.2)), 100.0, 10000.0),
        "momentum_bias": gaussian(key_of[11], (LAYERS, H), 10.0, 60.0, ((1, 4),), jnp.float32),
        "variance_bias": jnp.clip(jnp.exp(math.log(10000.0) - 4.6051702 * jax.random.uniform(key_of[12], (LAYERS, H), jnp.float32) ** block_scale(key_of[12], (LAYERS, H), ((1, 4),), -0.2, 0.2)), 100.0, 10000.0),
        "momentum_down": gaussian(key_of[13], (LAYERS, H, C), 10.0, 60.0, ((1, 4), (2, 8)), jnp.float32),
        "variance_down": jnp.clip(jnp.exp(math.log(10000.0) - 4.6051702 * jax.random.uniform(key_of[14], (LAYERS, H, C), jnp.float32) ** block_scale(key_of[14], (LAYERS, H, C), ((1, 4), (2, 8)), -0.2, 0.2)), 100.0, 10000.0),
    }


kernel_taps = 7
norm_eps = 1e-06
beta_first = 0.8
beta_second = 0.9
adam_eps = 1e-08
decay_rate = 0.01
adam_step = 10.0

@jax.custom_vjp
def low(v):
    return lax.optimization_barrier(v.astype(jnp.bfloat16)).astype(jnp.float32)

@jax.custom_vjp
def low_back(v):
    return v

def low_keep(v):
    return (low(v), None)

def low_pass(kept, grad):
    return (grad,)

def back_keep(v):
    return (v, None)

def back_low(kept, grad):
    return (low(grad),)
low.defvjp(low_keep, low_pass)
low_back.defvjp(back_keep, back_low)

def tap_masks(segments):
    frame_count = segments.shape[1]
    padded = jnp.pad(segments, ((0, 0), (3, 3)), constant_values=-1)
    masks = []
    for tap_index in range(kernel_taps):
        masks.append((padded[:, tap_index:tap_index + frame_count] == segments).astype(jnp.float32))
    return masks

def conv_forward(source, masks, params):
    frame_count = source.shape[1]
    padded = jnp.pad(source, ((0, 0), (3, 3), (0, 0)))
    total = params[7]
    for tap_index in range(kernel_taps):
        total = total + params[tap_index] * padded[:, tap_index:tap_index + frame_count] * masks[tap_index][:, :, None]
    return total

def layer_apply(source, masks, params, up_matrix, up_bias, down_matrix):
    conv = conv_forward(source, masks, params)
    mean = lax.optimization_barrier(jnp.mean(conv, axis=2, keepdims=True))
    spread = lax.optimization_barrier(jnp.mean(conv * conv, axis=2, keepdims=True)) - mean * mean
    scale = lax.rsqrt(spread + norm_eps)
    normed = (conv - mean) * scale * params[8] + params[9]
    hidden = low_back(jnp.einsum('rfc,ch->rfh', low(normed), low(up_matrix), precision=lax.Precision.HIGHEST)) + up_bias
    active = low(jax.nn.gelu(hidden, approximate=False))
    branch = low_back(jnp.einsum('rfh,hc->rfc', active, low(down_matrix), precision=lax.Precision.HIGHEST)) + params[10]
    return source + params[11] * branch

def adamw(param, first, second, grad):
    first = beta_first * first + (1.0 - beta_first) * grad
    second = beta_second * second + (1.0 - beta_second) * grad * grad
    first_hat = first / (1.0 - beta_first ** adam_step)
    second_hat = second / (1.0 - beta_second ** adam_step)
    update = first_hat / (jnp.sqrt(second_hat) + adam_eps) + decay_rate * param
    return (update, first, second)

def reference(frames_in, segments, cotangent, channel_params, weight_up, bias_up, weight_down, momentum_channel, variance_channel, momentum_up, variance_up, momentum_bias, variance_bias, momentum_down, variance_down):
    row_total = frames_in.shape[0]
    group = 8
    count = row_total // group
    x_groups = frames_in.reshape(count, group, FRAMES, C)
    c_groups = cotangent.reshape(count, group, FRAMES, C)
    s_groups = segments.reshape(count, group, FRAMES)

    def step(carry, items):
        x_group, c_group, s_group = items
        masks = tap_masks(s_group)

        def model(source, chan, up_matrix, up_bias, down_matrix):
            for layer in range(LAYERS):
                source = layer_apply(source, masks, chan[layer], up_matrix[layer], up_bias[layer], down_matrix[layer])
            return source
        output, back = jax.vjp(model, x_group.astype(jnp.float32), channel_params, weight_up, bias_up, weight_down)
        grads = back(c_group.astype(jnp.float32))
        carry = tuple((carry[i] + grads[i + 1] for i in range(4)))
        return (carry, (output.astype(jnp.bfloat16), grads[0].astype(jnp.bfloat16)))
    init = (jnp.zeros(channel_params.shape, jnp.float32), jnp.zeros(weight_up.shape, jnp.float32), jnp.zeros(bias_up.shape, jnp.float32), jnp.zeros(weight_down.shape, jnp.float32))
    totals, (outputs, in_grads) = lax.scan(step, init, (x_groups, c_groups, s_groups))
    layer_output = outputs.reshape(row_total, FRAMES, C)
    input_grad = in_grads.reshape(row_total, FRAMES, C)
    params_channel, first_channel, second_channel = adamw(channel_params, momentum_channel, variance_channel, totals[0])
    params_up, first_up, second_up = adamw(weight_up, momentum_up, variance_up, totals[1])
    params_bias, first_bias, second_bias = adamw(bias_up, momentum_bias, variance_bias, totals[2])
    params_down, first_down, second_down = adamw(weight_down, momentum_down, variance_down, totals[3])
    return (layer_output, input_grad, params_channel, params_up, params_bias, params_down, first_channel, second_channel, first_up, second_up, first_bias, second_bias, first_down, second_down)
```

```python
import functools

import jax
import jax.numpy as jnp
from jax import lax
from jax.experimental import pallas as pl
from jax.experimental.pallas import tpu as pltpu
from jax.sharding import PartitionSpec as P

kernel_taps = 7
reach = kernel_taps // 2
norm_eps = 1e-06
beta_first = 0.8
beta_second = 0.9
adam_eps = 1e-08
decay_rate = 0.01
adam_step = 10.0

HALO = 16
PAD = 8
LANES = 128
PARAM_ROWS = 32
f32 = jnp.float32
bf16 = jnp.bfloat16


def xor_perm(size, bit):
    return [(i, i ^ bit) for i in range(size)]


def hi_lo(value):
    hi = lax.reduce_precision(value, 8, 7)
    return hi.astype(bf16), (value - hi).astype(bf16)


def row_tiles(ext):
    own = ext - 2 * HALO
    tiles = [(0, HALO, False)]
    tiles += [(HALO + at, 32, True) for at in range(0, own, 32)]
    return tiles + [(HALO + own, HALO, False)]


def lane(j):
    return slice(j * LANES, (j + 1) * LANES)


def fold(value):
    return value.reshape(value.shape[0] // 8, 8, value.shape[1]).sum(axis=0)


def gelu_parts(h):
    tail = jnp.exp(-0.5 * h * h)
    d = 1.0 + (0.3275911 * 0.7071067811865476) * jnp.abs(h)
    t = pl.reciprocal(d, approx=True)
    t = t * (2.0 - d * t)
    poly = t * (
        0.127414796
        + t * (-0.142248368 + t * (0.7107068705 + t * (-0.7265760135 + t * 0.5307027145)))
    )
    low = poly * tail
    phi = jnp.where(h < 0.0, low, 1.0 - low)
    return h * phi, phi + h * tail * 0.3989422804014327


def load_frames(x, c, mine, other, ext, source, params):
    for side, ref in ((0, mine), (1, other)):
        for far in range(2):
            at = pl.multiple_of(((x ^ far) * 2 + (c ^ side)) * LANES, LANES)
            source[PAD : PAD + ext, pl.ds(at, LANES)] = ref[far, 0:ext, :].astype(f32)
            hi = ref[far, ext : ext + PARAM_ROWS, :].astype(f32)
            lo = ref[far, ext + PARAM_ROWS : ext + 2 * PARAM_ROWS, :].astype(f32)
            params[:, pl.ds(at, LANES)] = hi + lo
    clear_pads(source, ext)


def load_params(x, c, mine, other, ext, params):
    for side, ref in ((0, mine), (1, other)):
        for far in range(2):
            at = pl.multiple_of(((x ^ far) * 2 + (c ^ side)) * LANES, LANES)
            hi = ref[far, ext : ext + PARAM_ROWS, :].astype(f32)
            lo = ref[far, ext + PARAM_ROWS : ext + 2 * PARAM_ROWS, :].astype(f32)
            params[:, pl.ds(at, LANES)] = hi + lo


def clear_pads(ref, ext):
    zeros = jnp.zeros((PAD, ref.shape[1]), ref.dtype)
    ref[0:PAD, :] = zeros
    ref[PAD + ext : PAD + ext + PAD, :] = zeros


def load_bias(x, c, layer, params, bias):
    width = bias.shape[1] // 4
    for r in range(4):
        at = pl.multiple_of(((x ^ (r // 2)) * 2 + (c ^ (r % 2))) * LANES, LANES)
        rows = params[:, pl.ds(at, LANES)]
        for j in range(width // LANES):
            k = 24 + layer * (width // LANES) + j
            bias[0:1, r * width + j * LANES : r * width + (j + 1) * LANES] = rows[k : k + 1]


def start_weights(layer, y, own, core, near, near_core, far, far_core, held, sems):
    width = own.shape[-1]

    def columns(r):
        return slice(r * width, (r + 1) * width)

    copies = []
    for r, ref in ((0, own), (1, core)):
        for m in range(2):
            copies.append((ref.at[layer, m], held.at[m, :, columns(r)]))
    for r, first, second in ((2, near, far), (3, near_core, far_core)):
        copies.append((first, held.at[y, :, columns(r)]))
        copies.append((second, held.at[1 - y, :, columns(r)]))
    started = []
    for i, (src, dst) in enumerate(copies):
        copy = pltpu.make_async_copy(src, dst, sems.at[i])
        copy.start()
        started.append(copy)
    return started


def masks_at(ids, start, rows):
    here = ids[PAD + start : PAD + start + rows, :]
    masks = []
    for k in range(kernel_taps):
        at = PAD + start + k - reach
        masks.append(ids[at : at + rows, :] == here)
    return masks


def forward_norm(layer, source, ids, params, centred, rstd, normed, ext):
    width = source.shape[1]
    tiles = width // LANES
    base = layer * 12
    for start, rows, _ in row_tiles(ext):
        masks = masks_at(ids, start, rows)
        convs = []
        total = square = None
        for j in range(tiles):
            acc = params[base + 7 : base + 8, lane(j)]
            for k in range(kernel_taps):
                at = PAD + start + k - reach
                piece = source[at : at + rows, lane(j)]
                tap = params[base + k : base + k + 1, lane(j)]
                acc = acc + tap * (piece if k == reach else jnp.where(masks[k], piece, 0.0))
            convs.append(acc)
            total = acc if total is None else total + acc
            square = acc * acc if square is None else square + acc * acc
        mean = jnp.sum(total, axis=1, keepdims=True) * (1.0 / width)
        var = jnp.sum(square, axis=1, keepdims=True) * (1.0 / width) - mean * mean
        scale = lax.rsqrt(var + norm_eps)
        rstd[start : start + rows, :] = jnp.broadcast_to(scale, (rows, LANES))
        for j in range(tiles):
            value = (convs[j] - mean) * scale
            centred[start : start + rows, lane(j)] = value
            gain = params[base + 8 : base + 9, lane(j)]
            shift = params[base + 9 : base + 10, lane(j)]
            normed[start : start + rows, lane(j)] = (value * gain + shift).astype(bf16)


def forward_mlp(layer, source, params, bias, held, normed, active, slope, branch, ext, put):
    hidden = held.shape[2]
    quarter = hidden // 4
    half = ext // 2
    base = layer * 12
    for r in range(4):
        cols = slice(r * quarter, (r + 1) * quarter)
        for at in (0, half):
            rows = slice(at, at + half)
            h = (
                jnp.dot(normed[rows, :], held[0, :, cols], preferred_element_type=f32)
                + bias[0:1, cols]
            )
            value, grad = gelu_parts(h)
            active[rows, cols] = value.astype(bf16)
            slope[rows, cols] = grad
    for at in (0, half):
        rows = slice(at, at + half)
        value = (
            lax.dot_general(
                active[rows, :], held[1], (((1,), (1,)), ((), ())), preferred_element_type=f32
            )
            + params[base + 10 : base + 11, :]
        )
        branch[rows, :] = value
        put(at, half, source[PAD + at : PAD + at + half, :] + params[base + 11 : base + 12, :] * value)


def backward(
    layer, x, c, dp, dy, source, ids, params, held, centred, rstd, normed, active, slope, branch,
    low, low_t, normed_t, hidden_low, dnormed, dconv, small_c, give, keep, small, put, ext,
):
    width = source.shape[1]
    tiles = width // LANES
    hidden = held.shape[2]
    quarter = hidden // 4
    half = ext // 2
    own = ext - 2 * HALO
    base = layer * 12
    small_c[...] = jnp.zeros_like(small_c)

    def column_sum(value):
        return jnp.sum(value, axis=0, keepdims=True)

    for j in range(tiles):
        scale = params[base + 11 : base + 12, lane(j)]
        sum_gamma = sum_bias = None
        for start, rows, inner in row_tiles(ext):
            grad = dy[start : start + rows, lane(j)]
            grad_branch = scale * grad
            low[start : start + rows, lane(j)] = grad_branch.astype(bf16)
            if inner:
                gamma = fold(grad * branch[start : start + rows, lane(j)])
                bias = fold(grad_branch)
                sum_gamma = gamma if sum_gamma is None else sum_gamma + gamma
                sum_bias = bias if sum_bias is None else sum_bias + bias
        small_c[10:11, lane(j)] = column_sum(sum_bias)
        small_c[11:12, lane(j)] = column_sum(sum_gamma)

    low_t[...] = low[HALO : HALO + own, :].T
    normed_t[...] = normed[HALO : HALO + own, :].T

    def put_grad(r, m, value):
        out, i = (keep, r // 2) if r % 2 == 0 else (give, r // 2)
        blocks, parts, rows = out.shape[2], out.shape[3], out.shape[4]
        value = value.astype(out.dtype)
        for d in range(blocks):
            for j in range(parts):
                out[i, m, d ^ dp, j] = value[d * rows : (d + 1) * rows, lane(j)]

    for r in range(4):
        cols = slice(r * quarter, (r + 1) * quarter)
        sums = None
        for at in (0, half):
            rows = slice(at, at + half)
            grad = (
                jnp.dot(low[rows, :], held[1, :, cols], preferred_element_type=f32)
                * slope[rows, cols]
            )
            hidden_low[rows, cols] = grad.astype(bf16)
            inner = grad[HALO:] if at == 0 else grad[: half - HALO]
            part = fold(inner)
            sums = part if sums is None else sums + part
        sums = column_sum(sums)
        for j in range(quarter // LANES):
            small[r, 12 + j : 13 + j, :] = sums[:, lane(j)]
        small[r, 15:16, :] = jnp.zeros((1, LANES), f32)
        inner = slice(HALO, HALO + own)
        put_grad(r, 1, jnp.dot(low_t[...], active[inner, cols], preferred_element_type=f32))
        put_grad(r, 0, jnp.dot(normed_t[...], hidden_low[inner, cols], preferred_element_type=f32))

    for at in (0, half):
        rows = slice(at, at + half)
        dnormed[rows, :] = lax.dot_general(
            hidden_low[rows, :], held[0], (((1,), (1,)), ((), ())), preferred_element_type=f32
        )

    clear_pads(dconv, ext)
    sums = [[None] * 3 for _ in range(tiles)]
    for start, rows, inner in row_tiles(ext):
        scale = rstd[start : start + rows, :]
        weighted, norms = [], []
        first = second = None
        for j in range(tiles):
            grad = dnormed[start : start + rows, lane(j)]
            norm = centred[start : start + rows, lane(j)]
            w = grad * params[base + 8 : base + 9, lane(j)]
            wn = w * norm
            first = w if first is None else first + w
            second = wn if second is None else second + wn
            weighted.append(w)
            norms.append(norm)
            if inner:
                for i, value in ((0, fold(grad * norm)), (1, fold(grad))):
                    sums[j][i] = value if sums[j][i] is None else sums[j][i] + value
        first = jnp.sum(first, axis=1, keepdims=True) * (1.0 / width)
        second = jnp.sum(second, axis=1, keepdims=True) * (1.0 / width)
        for j in range(tiles):
            value = scale * (weighted[j] - first - norms[j] * second)
            dconv[PAD + start : PAD + start + rows, lane(j)] = value
            if inner:
                value = fold(value)
                sums[j][2] = value if sums[j][2] is None else sums[j][2] + value
    for j in range(tiles):
        small_c[8:9, lane(j)] = column_sum(sums[j][0])
        small_c[9:10, lane(j)] = column_sum(sums[j][1])
        small_c[7:8, lane(j)] = column_sum(sums[j][2])

    for j in range(tiles):
        taps = [params[base + k : base + k + 1, lane(j)] for k in range(kernel_taps)]
        sums = [None] * kernel_taps
        for start, rows, inner in row_tiles(ext):
            masks = masks_at(ids, start, rows)
            here = dconv[PAD + start : PAD + start + rows, lane(j)]
            total = dy[start : start + rows, lane(j)]
            for k in range(kernel_taps):
                mirror = kernel_taps - 1 - k
                at = PAD + start + mirror - reach
                piece = dconv[at : at + rows, lane(j)]
                total = total + taps[k] * (
                    piece if k == reach else jnp.where(masks[mirror], piece, 0.0)
                )
                if inner:
                    at = PAD + start + k - reach
                    piece = source[at : at + rows, lane(j)]
                    if k != reach:
                        piece = jnp.where(masks[k], piece, 0.0)
                    part = fold(piece * here)
                    sums[k] = part if sums[k] is None else sums[k] + part
            put(start, rows, inner, j, total)
        for k in range(kernel_taps):
            small_c[k : k + 1, lane(j)] = column_sum(sums[k])
    for r in range(4):
        at = pl.multiple_of(((x ^ (r // 2)) * 2 + (c ^ (r % 2))) * LANES, LANES)
        small[r, 0:12, :] = small_c[0:12, pl.ds(at, LANES)]


def first_kernel(
    where, ids, mine, other, own, core, near, near_core, far, far_core,
    next_source, centred, rstd, normed, active, slope, branch,
    source, params, bias, held, sems,
):
    ext = next_source.shape[0]
    x, c, y = where[0], where[1], where[2]
    copies = start_weights(0, y, own, core, near, near_core, far, far_core, held, sems)
    load_frames(x, c, mine, other, ext, source, params)
    load_bias(x, c, 0, params, bias)
    forward_norm(0, source, ids, params, centred, rstd, normed, ext)
    for copy in copies:
        copy.wait()

    def put(at, rows, value):
        next_source[at : at + rows, :] = value

    forward_mlp(0, source, params, bias, held, normed, active, slope, branch, ext, put)


def second_kernel(
    where, ids, mine, other, cot_mine, cot_other, source_in, own, core, near, near_core, far, far_core,
    grad_source, give, keep, small, out_give, out_keep,
    source, params, bias, held, sems, centred, rstd, normed, active, slope, branch,
    dy, low, low_t, normed_t, hidden_low, dnormed, dconv, small_c, out,
):
    ext = source_in.shape[0]
    own_rows = ext - 2 * HALO
    x, c, y, dp = where[0], where[1], where[2], where[3]
    copies = start_weights(1, y, own, core, near, near_core, far, far_core, held, sems)
    load_params(x, c, mine, other, ext, params)
    load_bias(x, c, 1, params, bias)
    source[PAD : PAD + ext, :] = source_in[...]
    clear_pads(source, ext)
    for side, ref in ((0, cot_mine), (1, cot_other)):
        for far_side in range(2):
            at = pl.multiple_of(((x ^ far_side) * 2 + (c ^ side)) * LANES, LANES)
            dy[:, pl.ds(at, LANES)] = ref[far_side].astype(f32)
    forward_norm(1, source, ids, params, centred, rstd, normed, ext)
    for copy in copies:
        copy.wait()

    def put(at, rows, value):
        out[at : at + rows, :] = value.astype(bf16)

    forward_mlp(1, source, params, bias, held, normed, active, slope, branch, ext, put)
    for i in range(2):
        at = pl.multiple_of(((x ^ i) * 2 + c) * LANES, LANES)
        out_keep[i] = out[HALO : HALO + own_rows, pl.ds(at, LANES)]
        at = pl.multiple_of(((x ^ i) * 2 + (c ^ 1)) * LANES, LANES)
        out_give[i] = out[HALO : HALO + own_rows, pl.ds(at, LANES)]

    def put_grad(start, rows, inner, j, value):
        grad_source[start : start + rows, lane(j)] = value

    backward(
        1, x, c, dp, dy, source, ids, params, held, centred, rstd, normed, active, slope, branch,
        low, low_t, normed_t, hidden_low, dnormed, dconv, small_c, give, keep, small, put_grad, ext,
    )


def third_kernel(
    where, ids, mine, other, dy, centred, rstd, normed, active, slope, branch,
    own, core, near, near_core, far, far_core,
    give, keep, small, out_give, out_keep,
    source, params, held, sems, low, low_t, normed_t, hidden_low, dnormed, dconv, small_c, out,
):
    ext = dy.shape[0]
    own_rows = ext - 2 * HALO
    x, c, y, dp = where[0], where[1], where[2], where[3]
    copies = start_weights(0, y, own, core, near, near_core, far, far_core, held, sems)
    load_frames(x, c, mine, other, ext, source, params)
    for copy in copies:
        copy.wait()

    def put_grad(start, rows, inner, j, value):
        if inner:
            out[start - HALO : start - HALO + rows, lane(j)] = value.astype(bf16)

    backward(
        0, x, c, dp, dy, source, ids, params, held, centred, rstd, normed, active, slope, branch,
        low, low_t, normed_t, hidden_low, dnormed, dconv, small_c, give, keep, small, put_grad, ext,
    )
    for i in range(2):
        at = pl.multiple_of(((x ^ i) * 2 + c) * LANES, LANES)
        out_keep[i] = out[:, pl.ds(at, LANES)]
        at = pl.multiple_of(((x ^ i) * 2 + (c ^ 1)) * LANES, LANES)
        out_give[i] = out[:, pl.ds(at, LANES)]
    del own_rows


def adamw(param, first, second, grad):
    first = beta_first * first + (1.0 - beta_first) * grad
    second = beta_second * second + (1.0 - beta_second) * grad * grad
    first_hat = first * (1.0 / (1.0 - beta_first**adam_step))
    second_hat = second * (1.0 / (1.0 - beta_second**adam_step))
    update = first_hat / (jnp.sqrt(second_hat) + adam_eps) + decay_rate * param
    return update, first, second


def adam_kernel(
    grads, smalls, up, down, chan, bias,
    m_chan, v_chan, m_up, v_up, m_bias, v_bias, m_down, v_down,
    sent, u_chan, u_bias, f_chan, s_chan, f_up, s_up, f_bias, s_bias, f_down, s_down,
):
    layers, parts = grads.shape[0], grads.shape[2]
    for l in range(layers):
        g = smalls[l]
        u_chan[l], f_chan[l], s_chan[l] = adamw(chan[l], m_chan[l], v_chan[l], g[0:12])
        for j in range(parts):
            cols = lane(j)
            u, m, v = adamw(
                bias[l : l + 1, cols],
                m_bias[l : l + 1, cols],
                v_bias[l : l + 1, cols],
                g[12 + j : 13 + j],
            )
            u_bias[l : l + 1, cols] = u
            f_bias[l : l + 1, cols] = m
            s_bias[l : l + 1, cols] = v
            u, m, v = adamw(up[l, :, cols], m_up[l, :, cols], v_up[l, :, cols], grads[l, 0, j])
            sent[l, 0, j] = u.astype(bf16)
            f_up[l, :, cols] = m
            s_up[l, :, cols] = v
            u, m, v = adamw(
                down[l, cols, :], m_down[l, cols, :], v_down[l, cols, :], grads[l, 1, j].T
            )
            sent[l, 1, j] = u.T.astype(bf16)
            f_down[l, cols, :] = m
            s_down[l, cols, :] = v


def spread_kernel(held, up, down):
    blocks, layers, _, parts, rows, _ = held.shape
    for l in range(layers):
        for j in range(parts):
            for d in range(blocks):
                up[l, d * rows : (d + 1) * rows, lane(j)] = held[d, l, 0, j].astype(f32)
            whole = jnp.concatenate([held[d, l, 1, j].astype(f32) for d in range(blocks)], axis=0)
            down[l, lane(j), :] = whole.T


VMEM = pl.BlockSpec(memory_space=pltpu.VMEM)
SMEM = pl.BlockSpec(memory_space=pltpu.SMEM)
ANY = pl.BlockSpec(memory_space=pl.ANY)


def call(kernel, outs, in_specs, scratch, flops, size, name):
    return pl.pallas_call(
        kernel,
        out_shape=[jax.ShapeDtypeStruct(s, t) for s, t in outs],
        in_specs=in_specs,
        out_specs=[VMEM] * len(outs),
        scratch_shapes=scratch,
        compiler_params=pltpu.CompilerParams(vmem_limit_bytes=48 * 1024 * 1024),
        cost_estimate=pl.CostEstimate(flops=flops, bytes_accessed=size, transcendentals=0),
        name=name,
    )


def on_device(
    n_dp, frames_in, segments, cotangent, channel_params, weight_up, bias_up, weight_down,
    momentum_channel, variance_channel, momentum_up, variance_up, momentum_bias, variance_bias,
    momentum_down, variance_down,
):
    rows, frames, part = frames_in.shape
    layers, width, quarter = weight_up.shape
    hidden = 4 * quarter
    tokens = rows * frames
    own = tokens // 4
    ext = own + 2 * HALO
    shard = width // n_dp
    parts = quarter // LANES
    me = lax.axis_index("chan")
    x, c = me // 2, me % 2
    dp = lax.axis_index("dp")
    y = dp % 2
    where = jnp.stack([x, c, y, dp]).astype(jnp.int32)

    def core_swap(v):
        return lax.ppermute(v, "chan", xor_perm(4, 1))

    def x_swap(v):
        return lax.ppermute(v, "chan", xor_perm(4, 2))

    def dp_swap(v, bit):
        return lax.ppermute(v, "dp", xor_perm(n_dp, bit))

    flat = (segments + 8 * jnp.arange(rows, dtype=jnp.int32)[:, None]).reshape(tokens)
    flat = jnp.pad(flat, HALO + PAD, constant_values=-1)
    ids = lax.dynamic_slice(flat, (me * own,), (ext + 2 * PAD,))
    ids = jnp.broadcast_to(ids[:, None], (ext + 2 * PAD, LANES))

    packed = jnp.concatenate(
        [channel_params.reshape(layers * 12, LANES), bias_up.reshape(layers * parts, LANES)]
    )
    packed = jnp.pad(packed, ((0, PARAM_ROWS - packed.shape[0]), (0, 0)))
    packed = jnp.concatenate(hi_lo(packed))

    def spread_tokens(array, extra):
        padded = jnp.pad(array.reshape(tokens, part), ((HALO, HALO), (0, 0)))
        chip = 2 * own + 2 * HALO
        mine = lax.dynamic_slice(padded, (x * 2 * own, 0), (chip, part))
        sent = lax.dynamic_slice(padded, ((1 - x) * 2 * own, 0), (chip, part))
        if extra is not None:
            mine = jnp.concatenate([mine, extra])
            sent = jnp.concatenate([sent, extra])
        both = jnp.stack([mine, x_swap(sent)])

        def chunk(core):
            piece = lax.dynamic_slice(both, (0, core * own, 0), (2, ext, part))
            if extra is not None:
                piece = jnp.concatenate([piece, both[:, chip:]], axis=1)
            return piece

        return chunk(c), core_swap(chunk(1 - c))

    mine, other = spread_tokens(frames_in, packed)
    weights = jnp.stack(
        [weight_up.astype(bf16), jnp.swapaxes(weight_down, 1, 2).astype(bf16)], axis=1
    )
    core = core_swap(weights)
    quarters = []
    for l in range(layers):
        near = x_swap(lax.dynamic_index_in_dim(weights[l], y, 0, keepdims=False))
        far = dp_swap(near, 1)
        quarters.append((near, core_swap(near), far, core_swap(far)))
    cot_mine, cot_other = spread_tokens(cotangent, None)

    wide = (ext, width)
    deep = (ext, hidden)
    half_flops = 2 * ext * width * hidden
    held = pltpu.VMEM((2, width, hidden), bf16)
    sems = pltpu.SemaphoreType.DMA((8,))
    padded_rows = pltpu.VMEM((ext + 2 * PAD, width), f32)
    params = pltpu.VMEM((PARAM_ROWS, width), f32)
    bias = pltpu.VMEM((1, hidden), f32)
    kept_shapes = [(wide, f32), ((ext, LANES), f32), (wide, bf16), (deep, bf16), (deep, f32), (wide, f32)]
    back_scratch = [
        pltpu.VMEM(wide, bf16),
        pltpu.VMEM((width, own), bf16),
        pltpu.VMEM((width, own), bf16),
        pltpu.VMEM(deep, bf16),
        pltpu.VMEM(wide, f32),
        padded_rows,
        pltpu.VMEM((16, width), f32),
    ]
    grad_shapes = [
        ((2, 2, n_dp, parts, shard, LANES), bf16),
        ((2, 2, n_dp, parts, shard, LANES), f32),
        ((4, 16, LANES), f32),
    ]
    out_shapes = [((2, own, LANES), bf16), ((2, own, LANES), bf16)]

    first = call(
        first_kernel,
        [(wide, f32)] + kept_shapes,
        [SMEM] + [VMEM] * 3 + [ANY] * 6,
        [padded_rows, params, bias, held, sems],
        2 * half_flops,
        12 << 20,
        "layer0_forward",
    )
    source1, *kept = first(where, ids, mine, other, weights, core, *quarters[0])

    second = call(
        second_kernel,
        [(wide, f32)] + grad_shapes + out_shapes,
        [SMEM] + [VMEM] * 6 + [ANY] * 6,
        [padded_rows, params, bias, held, sems]
        + [pltpu.VMEM(s, t) for s, t in kept_shapes]
        + [pltpu.VMEM(wide, f32)]
        + back_scratch
        + [pltpu.VMEM(wide, bf16)],
        6 * half_flops,
        12 << 20,
        "layer1_both",
    )
    grad1, give1, keep1, small1, out_give, out_keep = second(
        where, ids, mine, other, cot_mine, cot_other, source1, weights, core, *quarters[1]
    )

    third = call(
        third_kernel,
        grad_shapes + out_shapes,
        [SMEM] + [VMEM] * 10 + [ANY] * 6,
        [padded_rows, params, held, sems] + back_scratch + [pltpu.VMEM((own, width), bf16)],
        4 * half_flops,
        16 << 20,
        "layer0_backward",
    )
    give0, keep0, small0, in_give, in_keep = third(
        where, ids, mine, other, grad1, *kept, weights, core, *quarters[0]
    )

    def reduce_grads(give, keep, small):
        def packet(main, side):
            return jnp.concatenate([main.reshape(-1, LANES)] + [s.reshape(-1, LANES) for s in side])

        def unpack(got, shape, side_shape):
            count = 1
            for s in shape[:-1]:
                count *= s
            main = got[:count].reshape(shape).astype(f32)
            rest = got[count:].astype(f32)
            half = rest.shape[0] // 2
            return main, (rest[:half] + rest[half:]).reshape(side_shape)

        give_small, keep_small = small[1::2], small[0::2]
        got = core_swap(packet(give, hi_lo(give_small)))
        main, side = unpack(got, give.shape, give_small.shape)
        main, side = main + keep, side + keep_small
        got = x_swap(packet(main[1].astype(bf16), hi_lo(side[1])))
        more, more_side = unpack(got, main.shape[1:], side.shape[1:])
        main, side = main[0] + more, side[0] + more_side
        bit = 1
        while bit < n_dp:
            main = main.reshape((2, -1, 2) + main.shape[-3:])
            hi, lo = hi_lo(side)
            got = dp_swap(packet(main[:, :, 1].astype(bf16), (hi, lo)), bit)
            more, more_side = unpack(got, main[:, :, 1].shape, side.shape)
            main = main[:, :, 0] + more
            side = (hi.astype(f32) + lo.astype(f32)) + more_side
            bit *= 2
        return main.reshape(2, parts, shard, LANES), side

    main1, side1 = reduce_grads(give1, keep1, small1)
    main0, side0 = reduce_grads(give0, keep0, small0)

    offset = dp * shard
    up_slice = lax.dynamic_slice_in_dim(weight_up, offset, shard, 1)
    down_slice = lax.dynamic_slice_in_dim(weight_down, offset, shard, 2)
    adam_outs = [
        ((layers, 2, parts, shard, LANES), bf16),
        (channel_params.shape, f32),
        (bias_up.shape, f32),
        (channel_params.shape, f32),
        (channel_params.shape, f32),
        (momentum_up.shape, f32),
        (momentum_up.shape, f32),
        (bias_up.shape, f32),
        (bias_up.shape, f32),
        (momentum_down.shape, f32),
        (momentum_down.shape, f32),
    ]
    adam = call(adam_kernel, adam_outs, [VMEM] * 14, [], 1 << 20, 4 << 20, "adam")
    (
        sent, params_channel, params_bias, first_channel, second_channel,
        first_up, second_up, first_bias, second_bias, first_down, second_down,
    ) = adam(
        jnp.stack([main0, main1]), jnp.stack([side0, side1]), up_slice, down_slice,
        channel_params, bias_up, momentum_channel, variance_channel, momentum_up, variance_up,
        momentum_bias, variance_bias, momentum_down, variance_down,
    )

    order = list(range(0, n_dp, 2)) + list(range(n_dp - 1, 0, -2))
    ahead = [(order[i], order[(i + 1) % n_dp]) for i in range(n_dp)]
    back = [(b, a) for a, b in ahead]
    place = [0] * n_dp
    for i, d in enumerate(order):
        place[d] = i
    spot = jnp.asarray(place, jnp.int32)[dp]
    ring = jnp.asarray(order, jnp.int32)
    shape = sent.shape
    sent = sent.reshape(-1, LANES)
    gathered = jnp.zeros((n_dp,) + sent.shape, bf16)
    gathered = lax.dynamic_update_index_in_dim(gathered, sent, dp, 0)
    right = left = sent
    cut = sent.shape[0] // 2
    for step in range(1, n_dp // 2):
        right = lax.ppermute(right, "dp", ahead)
        left = lax.ppermute(left, "dp", back)
        gathered = lax.dynamic_update_index_in_dim(
            gathered, right, ring[(spot - step) % n_dp], 0
        )
        gathered = lax.dynamic_update_index_in_dim(gathered, left, ring[(spot + step) % n_dp], 0)
    top = lax.ppermute(right[:cut], "dp", ahead)
    bottom = lax.ppermute(left[cut:], "dp", back)
    across = ring[(spot + n_dp // 2) % n_dp]
    gathered = lax.dynamic_update_slice(gathered, top[None], (across, 0, 0))
    gathered = lax.dynamic_update_slice(gathered, bottom[None], (across, cut, 0))

    spread = call(
        spread_kernel,
        [(weight_up.shape, f32), (weight_down.shape, f32)],
        [VMEM],
        [],
        1 << 20,
        5 << 20,
        "spread",
    )
    params_up, params_down = spread(gathered.reshape((n_dp,) + shape))

    def collect_tokens(give, keep):
        got = core_swap(give)
        other = x_swap(jnp.stack([keep[1], got[1]]))
        here = jnp.stack([keep[0], got[0]])
        here = jnp.where(c == 0, here, here[::-1])
        other = jnp.where(c == 0, other, other[::-1])
        whole = jnp.where(x == 0, jnp.stack([here, other]), jnp.stack([other, here]))
        return whole.reshape(rows, frames, part)

    layer_output = collect_tokens(out_give, out_keep)
    input_grad = collect_tokens(in_give, in_keep)
    return (
        layer_output,
        input_grad,
        params_channel,
        params_up,
        params_bias,
        params_down,
        first_channel,
        second_channel,
        first_up,
        second_up,
        first_bias,
        second_bias,
        first_down,
        second_down,
    )


def solution(mesh):
    return jax.shard_map(
        functools.partial(on_device, mesh.shape["dp"]),
        mesh=mesh,
        in_specs=(
            P("dp", None, "chan"),
            P("dp", None),
            P("dp", None, "chan"),
            P(None, None, "chan"),
            P(None, None, "chan"),
            P(None, "chan"),
            P(None, "chan", None),
            P(None, None, "chan"),
            P(None, None, "chan"),
            P(None, "dp", "chan"),
            P(None, "dp", "chan"),
            P(None, "chan"),
            P(None, "chan"),
            P(None, "chan", "dp"),
            P(None, "chan", "dp"),
        ),
        out_specs=(
            P("dp", None, "chan"),
            P("dp", None, "chan"),
            P(None, None, "chan"),
            P(None, None, "chan"),
            P(None, "chan"),
            P(None, "chan", None),
            P(None, None, "chan"),
            P(None, None, "chan"),
            P(None, "dp", "chan"),
            P(None, "dp", "chan"),
            P(None, "chan"),
            P(None, "chan"),
            P(None, "chan", "dp"),
            P(None, "chan", "dp"),
        ),
        check_vma=False,
    )
```

```python
import functools

import jax
import jax.numpy as jnp
from jax import lax
from jax.experimental import pallas as pl
from jax.experimental.pallas import tpu as pltpu
from jax.sharding import PartitionSpec as P

kernel_taps = 7
reach = kernel_taps // 2
norm_eps = 1e-06
beta_first = 0.8
beta_second = 0.9
adam_eps = 1e-08
decay_rate = 0.01
adam_step = 10.0

HALO = 16
PAD = 8
LANES = 128
PARAM_ROWS = 32
f32 = jnp.float32
bf16 = jnp.bfloat16


def xor_perm(size, bit):
    return [(i, i ^ bit) for i in range(size)]


def hi_lo(value):
    hi = lax.reduce_precision(value, 8, 7)
    return hi.astype(bf16), (value - hi).astype(bf16)


def place():
    me = lax.axis_index("chan")
    return me // 2, me % 2, lax.axis_index("dp")


def lanes_of(x, c, r):
    return pl.ds(pl.multiple_of(((x ^ (r // 2)) * 2 + (c ^ (r % 2))) * LANES, LANES), LANES)


def row_tiles(ext):
    own = ext - 2 * HALO
    tiles = [(0, HALO, False)]
    tiles += [(HALO + at, 32, True) for at in range(0, own, 32)]
    return tiles + [(HALO + own, HALO, False)]


def lane(j):
    return slice(j * LANES, (j + 1) * LANES)


def fold(value):
    return value.reshape(value.shape[0] // 8, 8, value.shape[1]).sum(axis=0)


def plus(total, value):
    return value if total is None else total + value


def column_sum(value):
    return jnp.sum(value, axis=0, keepdims=True)


def gelu_parts(h):
    tail = jnp.exp(-0.5 * h * h)
    d = 1.0 + (0.3275911 * 0.7071067811865476) * jnp.abs(h)
    t = pl.reciprocal(d, approx=True)
    t = t * (2.0 - d * t)
    poly = t * (
        0.127414796
        + t * (-0.142248368 + t * (0.7107068705 + t * (-0.7265760135 + t * 0.5307027145)))
    )
    low = poly * tail
    phi = jnp.where(h < 0.0, low, 1.0 - low)
    return h * phi, phi + h * tail * 0.3989422804014327


def load_frames(x, c, packets, ext, source):
    for r, ref in enumerate(packets):
        source[PAD : PAD + ext, lanes_of(x, c, r)] = ref[0:ext, :].astype(f32)
    clear_pads(source, ext)


def load_params(x, c, packets, ext, params):
    for r, ref in enumerate(packets):
        hi = ref[ext : ext + PARAM_ROWS, :].astype(f32)
        lo = ref[ext + PARAM_ROWS : ext + 2 * PARAM_ROWS, :].astype(f32)
        params[:, lanes_of(x, c, r)] = hi + lo


def clear_pads(ref, ext):
    zeros = jnp.zeros((PAD, ref.shape[1]), ref.dtype)
    ref[0:PAD, :] = zeros
    ref[PAD + ext : PAD + ext + PAD, :] = zeros


def load_bias(x, c, layer, chip, params, bias):
    width = bias.shape[1] // 2
    for r in range(2):
        rows = params[:, lanes_of(x, c, 2 * chip + r)]
        for j in range(width // LANES):
            k = 24 + layer * (width // LANES) + j
            bias[0:1, r * width + j * LANES : r * width + (j + 1) * LANES] = rows[k : k + 1]


def start_copies(pairs, sems):
    started = []
    for i, (src, dst) in enumerate(pairs):
        copy = pltpu.make_async_copy(src, dst, sems.at[i])
        copy.start()
        started.append(copy)
    return started


def local_weights(own, core, held):
    width = own.shape[-1]
    return [
        (ref.at[m], held.at[m, :, r * width : (r + 1) * width])
        for r, ref in ((0, own), (1, core))
        for m in range(2)
    ]


def far_weights(y, near, near_core, far, far_core, held):
    width = near.shape[-1]
    pairs = []
    for r, first, second in ((0, near, far), (1, near_core, far_core)):
        columns = slice(r * width, (r + 1) * width)
        pairs.append((first, held.at[y, :, columns]))
        pairs.append((second, held.at[1 - y, :, columns]))
    return pairs


def masks_at(ids, start, rows):
    here = ids[PAD + start : PAD + start + rows, :]
    masks = []
    for k in range(kernel_taps):
        at = PAD + start + k - reach
        masks.append(ids[at : at + rows, :] == here)
    return masks


def forward_norm(layer, source, ids, params, centred, rstd, normed, ext):
    width = source.shape[1]
    tiles = width // LANES
    base = layer * 12
    for start, rows, _ in row_tiles(ext):
        masks = masks_at(ids, start, rows)
        convs = []
        total = square = None
        for j in range(tiles):
            acc = params[base + 7 : base + 8, lane(j)]
            for k in range(kernel_taps):
                at = PAD + start + k - reach
                piece = source[at : at + rows, lane(j)]
                tap = params[base + k : base + k + 1, lane(j)]
                acc = acc + tap * (piece if k == reach else jnp.where(masks[k], piece, 0.0))
            convs.append(acc)
            total = plus(total, acc)
            square = plus(square, acc * acc)
        mean = jnp.sum(total, axis=1, keepdims=True) * (1.0 / width)
        var = jnp.sum(square, axis=1, keepdims=True) * (1.0 / width) - mean * mean
        scale = lax.rsqrt(var + norm_eps)
        rstd[start : start + rows, :] = jnp.broadcast_to(scale, (rows, LANES))
        for j in range(tiles):
            value = (convs[j] - mean) * scale
            centred[start : start + rows, lane(j)] = value
            gain = params[base + 8 : base + 9, lane(j)]
            shift = params[base + 9 : base + 10, lane(j)]
            normed[start : start + rows, lane(j)] = (value * gain + shift).astype(bf16)


def forward_half(bias, held, normed, active, slope, ext):
    quarter = held.shape[2] // 2
    half = ext // 2
    for r in range(2):
        cols = slice(r * quarter, (r + 1) * quarter)
        for at in (0, half):
            rows = slice(at, at + half)
            h = (
                jnp.dot(normed[rows, :], held[0, :, cols], preferred_element_type=f32)
                + bias[0:1, cols]
            )
            value, grad = gelu_parts(h)
            active[rows, cols] = value.astype(bf16)
            slope[rows, cols] = grad


def down_half(held, active, rows):
    return lax.dot_general(
        active[rows, :], held[1], (((1,), (1,)), ((), ())), preferred_element_type=f32
    )


def finish_branch(layer, source, params, held, active, partial, branch, ext, put):
    half = ext // 2
    base = layer * 12
    for at in (0, half):
        rows = slice(at, at + half)
        value = partial[rows, :] + down_half(held, active, rows) + params[base + 10 : base + 11, :]
        branch[rows, :] = value
        put(at, half, source[PAD + at : PAD + at + half, :] + params[base + 11 : base + 12, :] * value)


def backward(
    layer, x, c, dp, dy, source, ids, params, helds, centred, rstd, normed, actives, slopes, branch,
    low, low_t, normed_t, hidden_lows, dnormed, dconv, small_c, gives, keeps, small_give, small_keep,
    put, ext,
):
    width = source.shape[1]
    tiles = width // LANES
    quarter = helds[0].shape[2] // 2
    half = ext // 2
    own = ext - 2 * HALO
    base = layer * 12
    small_c[...] = jnp.zeros_like(small_c)

    for j in range(tiles):
        scale = params[base + 11 : base + 12, lane(j)]
        sum_gamma = sum_bias = None
        for start, rows, inner in row_tiles(ext):
            grad = dy[start : start + rows, lane(j)]
            grad_branch = scale * grad
            low[start : start + rows, lane(j)] = grad_branch.astype(bf16)
            if inner:
                sum_gamma = plus(sum_gamma, fold(grad * branch[start : start + rows, lane(j)]))
                sum_bias = plus(sum_bias, fold(grad_branch))
        small_c[10:11, lane(j)] = column_sum(sum_bias)
        small_c[11:12, lane(j)] = column_sum(sum_gamma)

    low_t[...] = low[HALO : HALO + own, :].T
    normed_t[...] = normed[HALO : HALO + own, :].T

    def put_grad(r, m, value):
        out = (gives if r % 2 else keeps)[m]
        _, blocks, parts, rows, _ = out.shape
        value = value.astype(out.dtype)
        for d in range(blocks):
            for j in range(parts):
                out[r // 2, d ^ dp, j] = value[d * rows : (d + 1) * rows, lane(j)]

    bias_sums = []
    for r in range(4):
        chip, side = r // 2, r % 2
        cols = slice(side * quarter, (side + 1) * quarter)
        sums = None
        for at in (0, half):
            rows = slice(at, at + half)
            grad = (
                jnp.dot(low[rows, :], helds[chip][1, :, cols], preferred_element_type=f32)
                * slopes[chip][rows, cols]
            )
            hidden_lows[chip][rows, cols] = grad.astype(bf16)
            sums = plus(sums, fold(grad[HALO:] if at == 0 else grad[: half - HALO]))
        bias_sums.append(column_sum(sums))
        inner = slice(HALO, HALO + own)
        put_grad(r, 1, jnp.dot(low_t[...], actives[chip][inner, cols], preferred_element_type=f32))
        put_grad(
            r, 0, jnp.dot(normed_t[...], hidden_lows[chip][inner, cols], preferred_element_type=f32)
        )

    def back_half(chip, rows):
        return lax.dot_general(
            hidden_lows[chip][rows, :], helds[chip][0], (((1,), (1,)), ((), ())),
            preferred_element_type=f32,
        )

    for at in (0, half):
        rows = slice(at, at + half)
        dnormed[rows, :] = back_half(0, rows) + back_half(1, rows)

    clear_pads(dconv, ext)
    sums = [[None] * 3 for _ in range(tiles)]
    for start, rows, inner in row_tiles(ext):
        scale = rstd[start : start + rows, :]
        weighted, norms = [], []
        first = second = None
        for j in range(tiles):
            grad = dnormed[start : start + rows, lane(j)]
            norm = centred[start : start + rows, lane(j)]
            w = grad * params[base + 8 : base + 9, lane(j)]
            first = plus(first, w)
            second = plus(second, w * norm)
            weighted.append(w)
            norms.append(norm)
            if inner:
                sums[j][0] = plus(sums[j][0], fold(grad * norm))
                sums[j][1] = plus(sums[j][1], fold(grad))
        first = jnp.sum(first, axis=1, keepdims=True) * (1.0 / width)
        second = jnp.sum(second, axis=1, keepdims=True) * (1.0 / width)
        for j in range(tiles):
            value = scale * (weighted[j] - first - norms[j] * second)
            dconv[PAD + start : PAD + start + rows, lane(j)] = value
            if inner:
                sums[j][2] = plus(sums[j][2], fold(value))
    for j in range(tiles):
        small_c[8:9, lane(j)] = column_sum(sums[j][0])
        small_c[9:10, lane(j)] = column_sum(sums[j][1])
        small_c[7:8, lane(j)] = column_sum(sums[j][2])

    for j in range(tiles):
        taps = [params[base + k : base + k + 1, lane(j)] for k in range(kernel_taps)]
        sums = [None] * kernel_taps
        for start, rows, inner in row_tiles(ext):
            masks = masks_at(ids, start, rows)
            here = dconv[PAD + start : PAD + start + rows, lane(j)]
            total = dy[start : start + rows, lane(j)]
            for k in range(kernel_taps):
                mirror = kernel_taps - 1 - k
                at = PAD + start + mirror - reach
                piece = dconv[at : at + rows, lane(j)]
                total = total + taps[k] * (
                    piece if k == reach else jnp.where(masks[mirror], piece, 0.0)
                )
                if inner:
                    at = PAD + start + k - reach
                    piece = source[at : at + rows, lane(j)]
                    if k != reach:
                        piece = jnp.where(masks[k], piece, 0.0)
                    sums[k] = plus(sums[k], fold(piece * here))
            put(start, rows, inner, j, total)
        for k in range(kernel_taps):
            small_c[k : k + 1, lane(j)] = column_sum(sums[k])

    for r in range(4):
        sums = bias_sums[r]
        rows = [small_c[0:12, lanes_of(x, c, r)]]
        rows += [sums[:, lane(j)] for j in range(quarter // LANES)]
        rows += [jnp.zeros((16 - 12 - quarter // LANES, LANES), f32)]
        value = jnp.concatenate(rows, axis=0)
        if r % 2 == 0:
            small_keep[r // 2] = value
        else:
            hi = value.astype(bf16)
            small_give[r // 2, 0] = hi
            small_give[r // 2, 1] = (value - hi.astype(f32)).astype(bf16)


def frames_kernel(frames, chan, bias, give0, give1, here, beside, flat):
    tokens = frames.shape[0] * frames.shape[1]
    own = tokens // 4
    ext = own + 2 * HALO
    x, c, _ = place()
    zeros = jnp.zeros((HALO, LANES), bf16)
    flat[0:HALO, :] = zeros
    flat[HALO + tokens :, :] = zeros
    for r in range(frames.shape[0]):
        at = HALO + r * frames.shape[1]
        flat[at : at + frames.shape[1], :] = frames[r]
    rows = [chan[l] for l in range(chan.shape[0])]
    rows += [bias[l : l + 1, lane(j)] for l in range(bias.shape[0]) for j in range(bias.shape[1] // LANES)]
    rows += [jnp.zeros((PARAM_ROWS - 24 - bias.shape[0] * (bias.shape[1] // LANES), LANES), f32)]
    value = jnp.concatenate(rows, axis=0)
    hi = value.astype(bf16)
    lo = (value - hi.astype(f32)).astype(bf16)
    for out, dx, dc in ((give0, 1, 0), (give1, 1, 1), (here, 0, 0), (beside, 0, 1)):
        at = pl.multiple_of(((x ^ dx) * 2 + (c ^ dc)) * own, HALO)
        out[0:ext, :] = flat[pl.ds(at, ext), :]
        out[ext : ext + PARAM_ROWS, :] = hi
        out[ext + PARAM_ROWS :, :] = lo


def cotangent_kernel(frames, segments, give0, give1, here, beside, ids, flat, columns):
    rows, count, _ = frames.shape
    tokens = rows * count
    own = tokens // 4
    ext = own + 2 * HALO
    x, c, _ = place()
    zeros = jnp.zeros((HALO, LANES), bf16)
    flat[0:HALO, :] = zeros
    flat[HALO + tokens :, :] = zeros
    edge = HALO + PAD
    none = jnp.full((edge, LANES), -1, jnp.int32)
    columns[0:edge, :] = none
    columns[edge + tokens :, :] = none
    for r in range(rows):
        at = HALO + r * count
        flat[at : at + count, :] = frames[r]
        row = jnp.broadcast_to(segments[r : r + 1, :] + 8 * r, (LANES, count))
        at = edge + r * count
        columns[at : at + count, :] = row.T
    for out, dx, dc in ((give0, 1, 0), (give1, 1, 1), (here, 0, 0), (beside, 0, 1)):
        at = pl.multiple_of(((x ^ dx) * 2 + (c ^ dc)) * own, HALO)
        out[...] = flat[pl.ds(at, ext), :]
    at = pl.multiple_of((x * 2 + c) * own, HALO)
    ids[...] = columns[pl.ds(at, ext + 2 * PAD), :]


def weights_kernel(up, down, both, chosen):
    _, _, dp = place()
    both[0] = up[0].astype(bf16)
    both[1] = down[0].T.astype(bf16)
    chosen[...] = both[dp % 2]


def first_kernel(
    ids, here, beside, near, far, own, core,
    centred, rstd, normed, active, slope, partial, source, params, bias, held, sems,
):
    ext = ids.shape[0] - 2 * PAD
    x, c, _ = place()
    packets = (here, beside, near, far)
    copies = start_copies(local_weights(own, core, held), sems)
    load_frames(x, c, packets, ext, source)
    load_params(x, c, packets, ext, params)
    load_bias(x, c, 0, 0, params, bias)
    forward_norm(0, source, ids, params, centred, rstd, normed, ext)
    for copy in copies:
        copy.wait()
    forward_half(bias, held, normed, active, slope, ext)
    for at in (0, ext // 2):
        rows = slice(at, at + ext // 2)
        partial[rows, :] = down_half(held, active, rows)


def second_kernel(
    here, beside, near, far, normed, partial, w_near, w_near_core, w_far, w_far_core,
    next_source, active, slope, branch, source, params, bias, held, sems,
):
    ext = normed.shape[0]
    x, c, dp = place()
    packets = (here, beside, near, far)
    copies = start_copies(far_weights(dp % 2, w_near, w_near_core, w_far, w_far_core, held), sems)
    load_frames(x, c, packets, ext, source)
    load_params(x, c, packets, ext, params)
    load_bias(x, c, 0, 1, params, bias)
    for copy in copies:
        copy.wait()
    forward_half(bias, held, normed, active, slope, ext)

    def put(at, rows, value):
        next_source[at : at + rows, :] = value

    finish_branch(0, source, params, held, active, partial, branch, ext, put)


def third_kernel(
    ids, here, beside, near, far, source_in, own, core,
    centred, rstd, normed, active, slope, partial, source, params, bias, held, sems,
):
    ext = source_in.shape[0]
    x, c, _ = place()
    copies = start_copies(local_weights(own, core, held), sems)
    load_params(x, c, (here, beside, near, far), ext, params)
    load_bias(x, c, 1, 0, params, bias)
    source[PAD : PAD + ext, :] = source_in[...]
    clear_pads(source, ext)
    forward_norm(1, source, ids, params, centred, rstd, normed, ext)
    for copy in copies:
        copy.wait()
    forward_half(bias, held, normed, active, slope, ext)
    for at in (0, ext // 2):
        rows = slice(at, at + ext // 2)
        partial[rows, :] = down_half(held, active, rows)


def fourth_kernel(
    ids, here, beside, near, far, cot_here, cot_beside, cot_near, cot_far, source_in,
    centred, rstd, normed, active0, slope0, partial,
    own, core, w_near, w_near_core, w_far, w_far_core,
    grad_source, give0, give1, keep0, keep1, small_give, small_keep, out_give, out_keep,
    source, params, bias, held0, held1, sems, active1, slope1, branch,
    dy, low, low_t, normed_t, hidden0, hidden1, dnormed, dconv, small_c, out,
):
    ext = source_in.shape[0]
    own_rows = ext - 2 * HALO
    x, c, dp = place()
    pairs = far_weights(dp % 2, w_near, w_near_core, w_far, w_far_core, held1)
    copies = start_copies(pairs + local_weights(own, core, held0), sems)
    load_params(x, c, (here, beside, near, far), ext, params)
    load_bias(x, c, 1, 1, params, bias)
    source[PAD : PAD + ext, :] = source_in[...]
    clear_pads(source, ext)
    for r, ref in enumerate((cot_here, cot_beside, cot_near, cot_far)):
        dy[:, lanes_of(x, c, r)] = ref[...].astype(f32)
    for copy in copies:
        copy.wait()
    forward_half(bias, held1, normed, active1, slope1, ext)

    def put(at, rows, value):
        out[at : at + rows, :] = value.astype(bf16)

    finish_branch(1, source, params, held1, active1, partial, branch, ext, put)
    for i in range(2):
        out_keep[i] = out[HALO : HALO + own_rows, lanes_of(x, c, 2 * i)]
        out_give[i] = out[HALO : HALO + own_rows, lanes_of(x, c, 2 * i + 1)]

    def put_grad(start, rows, inner, j, value):
        grad_source[start : start + rows, lane(j)] = value

    backward(
        1, x, c, dp, dy, source, ids, params, (held0, held1), centred, rstd, normed,
        (active0, active1), (slope0, slope1), branch, low, low_t, normed_t, (hidden0, hidden1),
        dnormed, dconv, small_c, (give0, give1), (keep0, keep1), small_give, small_keep, put_grad, ext,
    )


def fifth_kernel(
    ids, here, beside, near, far, dy, centred, rstd, normed, active0, slope0, active1, slope1, branch,
    own, core, w_near, w_near_core, w_far, w_far_core,
    give0, give1, keep0, keep1, small_give, small_keep, out_give, out_keep,
    source, params, held0, held1, sems, low, low_t, normed_t, hidden0, hidden1, dnormed, dconv, small_c, out,
):
    ext = dy.shape[0]
    x, c, dp = place()
    packets = (here, beside, near, far)
    pairs = far_weights(dp % 2, w_near, w_near_core, w_far, w_far_core, held1)
    copies = start_copies(pairs + local_weights(own, core, held0), sems)
    load_frames(x, c, packets, ext, source)
    load_params(x, c, packets, ext, params)
    for copy in copies:
        copy.wait()

    def put_grad(start, rows, inner, j, value):
        if inner:
            out[start - HALO : start - HALO + rows, lane(j)] = value.astype(bf16)

    backward(
        0, x, c, dp, dy, source, ids, params, (held0, held1), centred, rstd, normed,
        (active0, active1), (slope0, slope1), branch, low, low_t, normed_t, (hidden0, hidden1),
        dnormed, dconv, small_c, (give0, give1), (keep0, keep1), small_give, small_keep, put_grad, ext,
    )
    for i in range(2):
        out_keep[i] = out[:, lanes_of(x, c, 2 * i)]
        out_give[i] = out[:, lanes_of(x, c, 2 * i + 1)]


def adamw(param, first, second, grad):
    first = beta_first * first + (1.0 - beta_first) * grad
    second = beta_second * second + (1.0 - beta_second) * grad * grad
    first_hat = first * (1.0 / (1.0 - beta_first**adam_step))
    second_hat = second * (1.0 / (1.0 - beta_second**adam_step))
    update = first_hat / (jnp.sqrt(second_hat) + adam_eps) + decay_rate * param
    return update, first, second


def update_kernel(grads, up, down, m_up, v_up, m_down, v_down, sent):
    for j in range(grads.shape[1]):
        cols = lane(j)
        u, _, _ = adamw(up[0, :, cols], m_up[0, :, cols], v_up[0, :, cols], grads[0, j])
        sent[0, j] = u.astype(bf16)
        u, _, _ = adamw(down[0, cols, :], m_down[0, cols, :], v_down[0, cols, :], grads[1, j].T)
        sent[1, j] = u.T.astype(bf16)


def adam_kernel(
    grads0, grads1, small0, small1, chan, bias,
    m_chan, v_chan, m_up, v_up, m_bias, v_bias, m_down, v_down,
    u_chan, u_bias, f_chan, s_chan, f_up, s_up, f_bias, s_bias, f_down, s_down,
):
    for l, (grads, small) in enumerate(((grads0, small0), (grads1, small1))):
        g = small[...]
        u_chan[l], f_chan[l], s_chan[l] = adamw(chan[l], m_chan[l], v_chan[l], g[0:12])
        for j in range(grads.shape[1]):
            cols = lane(j)
            row = slice(l, l + 1)
            u_bias[row, cols], f_bias[row, cols], s_bias[row, cols] = adamw(
                bias[row, cols], m_bias[row, cols], v_bias[row, cols], g[12 + j : 13 + j]
            )
            _, f_up[l, :, cols], s_up[l, :, cols] = adamw(
                0.0, m_up[l, :, cols], v_up[l, :, cols], grads[0, j]
            )
            _, f_down[l, cols, :], s_down[l, cols, :] = adamw(
                0.0, m_down[l, cols, :], v_down[l, cols, :], grads[1, j].T
            )


def ring_order(n_dp):
    return list(range(0, n_dp, 2)) + list(range(n_dp - 1, 0, -2))


def spread_kernel(n_dp, layers, parts, *refs):
    blocks, (up, down, held) = refs[: n_dp * layers], refs[n_dp * layers :]
    dp = lax.axis_index("dp")
    half = n_dp // 2
    spot = jnp.where(dp % 2 == 0, dp // 2, n_dp - 1 - dp // 2)

    def owner(distance):
        at = lax.rem(spot + distance + n_dp, n_dp)
        return jnp.where(at < half, 2 * at, 2 * (n_dp - 1 - at) + 1)

    distances = [0]
    for step in range(1, half):
        distances += [-step, step]
    distances += [half]
    rows = up.shape[1] // n_dp
    size = parts * rows
    for l in range(layers):
        for i, distance in enumerate(distances):
            block = blocks[l * n_dp + i]
            at = pl.multiple_of(owner(distance) * rows, rows)
            for j in range(parts):
                start = j * rows
                up[l, pl.ds(at, rows), lane(j)] = block[start : start + rows, :].astype(f32)
                start = size + j * rows
                held[pl.ds(at, rows), lane(j)] = block[start : start + rows, :].astype(f32)
        for j in range(parts):
            down[l, lane(j), :] = held[:, lane(j)].T


def collect_kernel(own, core, near, far, out):
    x, c, _ = place()
    rows = own.shape[0]
    for r, ref in enumerate((own, core, near, far)):
        at = pl.multiple_of(((x ^ (r // 2)) * 2 + (c ^ (r % 2))) * rows, HALO)
        out[pl.ds(at, rows), :] = ref[...]


VMEM = pl.BlockSpec(memory_space=pltpu.VMEM)
ANY = pl.BlockSpec(memory_space=pl.ANY)


def call(kernel, outs, in_specs, scratch, flops, size, name, limit=24):
    return pl.pallas_call(
        kernel,
        out_shape=[jax.ShapeDtypeStruct(s, t) for s, t in outs],
        in_specs=in_specs,
        out_specs=[VMEM] * len(outs),
        scratch_shapes=scratch,
        compiler_params=pltpu.CompilerParams(vmem_limit_bytes=limit * 1024 * 1024),
        cost_estimate=pl.CostEstimate(flops=flops, bytes_accessed=size, transcendentals=0),
        name=name,
    )


def on_device(
    n_dp, frames_in, segments, cotangent, channel_params, weight_up, bias_up, weight_down,
    momentum_channel, variance_channel, momentum_up, variance_up, momentum_bias, variance_bias,
    momentum_down, variance_down,
):
    rows, frames, part = frames_in.shape
    layers, width, quarter = weight_up.shape
    chip_hidden = 2 * quarter
    tokens = rows * frames
    own = tokens // 4
    ext = own + 2 * HALO
    shard = width // n_dp
    parts = quarter // LANES

    def core_swap(v):
        return lax.ppermute(v, "chan", xor_perm(4, 1))

    def x_swap(v):
        return lax.ppermute(v, "chan", xor_perm(4, 2))

    def dp_swap(v, bit):
        return lax.ppermute(v, "dp", xor_perm(n_dp, bit))

    packet = ((ext + 2 * PARAM_ROWS, LANES), bf16)
    flat = pltpu.VMEM((tokens + 2 * HALO, LANES), bf16)
    frames_call = call(frames_kernel, [packet] * 4, [VMEM] * 3, [flat], 0, 1 << 20, "frames", 8)
    give0, give1, here, beside = frames_call(frames_in, channel_params, bias_up)
    packets = [here, core_swap(beside), x_swap(give0), core_swap(x_swap(give1))]

    def one_layer(shape, l):
        return pl.BlockSpec((1,) + shape[1:], lambda i: (l, 0, 0))

    def layer_weights(l):
        both, chosen = pl.pallas_call(
            weights_kernel,
            grid=(1,),
            out_shape=[
                jax.ShapeDtypeStruct((2, width, quarter), bf16),
                jax.ShapeDtypeStruct((width, quarter), bf16),
            ],
            in_specs=[one_layer(weight_up.shape, l), one_layer(weight_down.shape, l)],
            out_specs=[
                pl.BlockSpec((2, width, quarter), lambda i: (0, 0, 0)),
                pl.BlockSpec((width, quarter), lambda i: (0, 0)),
            ],
            compiler_params=pltpu.CompilerParams(vmem_limit_bytes=16 * 1024 * 1024),
            cost_estimate=pl.CostEstimate(flops=0, bytes_accessed=3 << 20, transcendentals=0),
            name="weights",
        )(weight_up, weight_down)
        near = x_swap(chosen)
        far = dp_swap(near, 1)
        return [both, core_swap(both)], [near, core_swap(near), far, core_swap(far)]

    local0, away0 = layer_weights(0)
    local1, away1 = layer_weights(1)

    cot_packet = ((ext, LANES), bf16)
    cot_call = call(
        cotangent_kernel,
        [cot_packet] * 4 + [((ext + 2 * PAD, LANES), jnp.int32)],
        [VMEM] * 2,
        [flat, pltpu.VMEM((tokens + 2 * HALO + 2 * PAD, LANES), jnp.int32)],
        0,
        2 << 20,
        "cotangent",
        8,
    )
    give0, give1, here, beside, ids = cot_call(cotangent, segments)
    cots = [here, core_swap(beside), x_swap(give0), core_swap(x_swap(give1))]

    wide = (ext, width)
    deep = (ext, chip_hidden)
    flops = 2 * ext * width * chip_hidden
    held = pltpu.VMEM((2, width, chip_hidden), bf16)
    sems = pltpu.SemaphoreType.DMA((8,))
    padded_rows = pltpu.VMEM((ext + 2 * PAD, width), f32)
    params = pltpu.VMEM((PARAM_ROWS, width), f32)
    bias = pltpu.VMEM((1, chip_hidden), f32)
    norm_shapes = [(wide, f32), ((ext, LANES), f32), (wide, bf16)]
    half_shapes = [(deep, bf16), (deep, f32), (wide, f32)]
    back_scratch = [
        pltpu.VMEM(wide, bf16),
        pltpu.VMEM((width, own), bf16),
        pltpu.VMEM((width, own), bf16),
        pltpu.VMEM(deep, bf16),
        pltpu.VMEM(deep, bf16),
        pltpu.VMEM(wide, f32),
        padded_rows,
        pltpu.VMEM((16, width), f32),
    ]
    grad_shape = (2, n_dp, parts, shard, LANES)
    grad_shapes = [
        (grad_shape, bf16),
        (grad_shape, bf16),
        (grad_shape, f32),
        (grad_shape, f32),
        ((2, 2, 16, LANES), bf16),
        ((2, 16, LANES), f32),
    ]
    out_shapes = [((2, own, LANES), bf16), ((2, own, LANES), bf16)]

    first = call(
        first_kernel, norm_shapes + half_shapes, [VMEM] * 5 + [ANY] * 2,
        [padded_rows, params, bias, held, sems], 2 * flops, 6 << 20, "layer0_near",
    )
    centred0, rstd0, normed0, active00, slope00, partial0 = first(ids, *packets, *local0)
    second = call(
        second_kernel, [(wide, f32)] + half_shapes, [VMEM] * 6 + [ANY] * 4,
        [padded_rows, params, bias, held, sems], 2 * flops, 6 << 20, "layer0_far",
    )
    source1, active01, slope01, branch0 = second(*packets, normed0, partial0, *away0)
    third = call(
        third_kernel, norm_shapes + half_shapes, [VMEM] * 6 + [ANY] * 2,
        [padded_rows, params, bias, held, sems], 2 * flops, 6 << 20, "layer1_near",
    )
    kept1 = third(ids, *packets, source1, *local1)
    fourth = call(
        fourth_kernel,
        [(wide, f32)] + grad_shapes + out_shapes,
        [VMEM] * 16 + [ANY] * 6,
        [padded_rows, params, bias, held, held, sems]
        + [pltpu.VMEM(s, t) for s, t in half_shapes]
        + [pltpu.VMEM(wide, f32)]
        + back_scratch
        + [pltpu.VMEM(wide, bf16)],
        10 * flops,
        16 << 20,
        "layer1_both",
        40,
    )
    grad1, give10, give11, keep10, keep11, small_give1, small_keep1, out_give, out_keep = fourth(
        ids, *packets, *cots, source1, *kept1, *local1, *away1
    )

    def first_exchange(gives, keeps, small_give, small_keep):
        mains = [core_swap(gives[m]).astype(f32) + keeps[m] for m in range(2)]
        got = core_swap(small_give).astype(f32)
        side = got[:, 0] + got[:, 1] + small_keep
        to_x = jnp.concatenate(
            [mains[0][1].astype(bf16).reshape(-1, LANES), *hi_lo(side[1])]
        )
        down = mains[1].reshape((2, n_dp // 2, 2) + grad_shape[2:])
        to_y = down[:, :, 1].astype(bf16).reshape(-1, LANES)
        return to_x, to_y, mains[0][0], down[:, :, 0], side[0]

    def other_exchanges(to_x, to_y, up, down, side):
        small = side.shape[0]

        def unpack(got, like):
            count = like.size // LANES
            return got[:count].reshape(like.shape).astype(f32)

        def unpack_side(got):
            rest = got[-2 * small :].astype(f32)
            return rest[:small] + rest[small:]

        from_x, from_y = x_swap(to_x), dp_swap(to_y, 1)
        up = (up + unpack(from_x, up)).reshape((n_dp // 2, 2) + grad_shape[2:])
        side = side + unpack_side(from_x)
        down = down + unpack(from_y, down)
        hi, lo = hi_lo(side)
        to_y = jnp.concatenate([up[:, 1].astype(bf16).reshape(-1, LANES), hi, lo])
        to_x = down[1].astype(bf16).reshape(-1, LANES)
        from_y, from_x = dp_swap(to_y, 1), x_swap(to_x)
        up = up[:, 0] + unpack(from_y, up[:, 0])
        side = (hi.astype(f32) + lo.astype(f32)) + unpack_side(from_y)
        down = down[0] + unpack(from_x, down[0])
        main = jnp.stack([up, down])
        bit = 2
        while bit < n_dp:
            main = main.reshape((2, -1, 2) + grad_shape[2:])
            hi, lo = hi_lo(side)
            packed = main[:, :, 1].astype(bf16).reshape(-1, LANES)
            got = dp_swap(jnp.concatenate([packed, hi, lo]), bit)
            main = main[:, :, 0] + unpack(got, main[:, :, 1])
            side = (hi.astype(f32) + lo.astype(f32)) + unpack_side(got)
            bit *= 2
        return main.reshape(2, parts, shard, LANES), side

    packed1 = first_exchange((give10, give11), (keep10, keep11), small_give1, small_keep1)
    grad1, *packed1 = lax.optimization_barrier((grad1, *packed1))

    fifth = call(
        fifth_kernel,
        grad_shapes + out_shapes,
        [VMEM] * 14 + [ANY] * 6,
        [padded_rows, params, held, held, sems] + back_scratch + [pltpu.VMEM((own, width), bf16)],
        8 * flops,
        20 << 20,
        "layer0_backward",
        36,
    )
    give00, give01, keep00, keep01, small_give0, small_keep0, in_give, in_keep = fifth(
        ids, *packets, grad1, centred0, rstd0, normed0, active00, slope00, active01, slope01, branch0,
        *local0, *away0,
    )
    packed0 = first_exchange((give00, give01), (keep00, keep01), small_give0, small_keep0)

    dp = lax.axis_index("dp")
    up_slice = lax.dynamic_slice_in_dim(weight_up, dp * shard, shard, 1)
    down_slice = lax.dynamic_slice_in_dim(weight_down, dp * shard, shard, 2)

    order = ring_order(n_dp)
    ahead = [(order[i], order[(i + 1) % n_dp]) for i in range(n_dp)]
    back = [(b, a) for a, b in ahead]

    def updates(l, grads):
        def one(array):
            return pl.BlockSpec((1,) + array.shape[1:], lambda i: (l, 0, 0))

        arrays = (up_slice, down_slice, momentum_up, variance_up, momentum_down, variance_down)
        shape = (2, parts, shard, LANES)
        sent = pl.pallas_call(
            update_kernel,
            grid=(1,),
            out_shape=jax.ShapeDtypeStruct(shape, bf16),
            in_specs=[pl.BlockSpec(shape, lambda i: (0, 0, 0, 0))] + [one(a) for a in arrays],
            out_specs=pl.BlockSpec(shape, lambda i: (0, 0, 0, 0)),
            cost_estimate=pl.CostEstimate(flops=1 << 20, bytes_accessed=1 << 20, transcendentals=0),
            name="update",
        )(grads, *arrays)
        sent = sent.reshape(-1, LANES)
        blocks = [sent]
        right = left = sent
        cut = sent.shape[0] // 2
        for _ in range(1, n_dp // 2):
            right = lax.ppermute(right, "dp", ahead)
            left = lax.ppermute(left, "dp", back)
            blocks += [right, left]
        top = lax.ppermute(right[:cut], "dp", ahead)
        bottom = lax.ppermute(left[cut:], "dp", back)
        return blocks + [jnp.concatenate([top, bottom])]

    main1, side1 = other_exchanges(*packed1)
    blocks1 = updates(1, main1)
    main0, side0 = other_exchanges(*packed0)
    blocks0 = updates(0, main0)

    adam_outs = [
        (channel_params.shape, f32),
        (bias_up.shape, f32),
        (channel_params.shape, f32),
        (channel_params.shape, f32),
        (momentum_up.shape, f32),
        (momentum_up.shape, f32),
        (bias_up.shape, f32),
        (bias_up.shape, f32),
        (momentum_down.shape, f32),
        (momentum_down.shape, f32),
    ]
    adam = call(adam_kernel, adam_outs, [VMEM] * 14, [], 1 << 20, 4 << 20, "adam", 16)
    (
        params_channel, params_bias, first_channel, second_channel,
        first_up, second_up, first_bias, second_bias, first_down, second_down,
    ) = adam(
        main0, main1, side0, side1,
        channel_params, bias_up, momentum_channel, variance_channel, momentum_up, variance_up,
        momentum_bias, variance_bias, momentum_down, variance_down,
    )

    spread = call(
        functools.partial(spread_kernel, n_dp, layers, parts),
        [(weight_up.shape, f32), (weight_down.shape, f32)],
        [VMEM] * (n_dp * layers),
        [pltpu.VMEM((width, quarter), f32)],
        1 << 20,
        5 << 20,
        "spread",
    )
    params_up, params_down = spread(*blocks0, *blocks1)

    def collect_tokens(give, keep):
        got = core_swap(give)
        near, far = x_swap(keep[1]), x_swap(got[1])
        whole = call(
            collect_kernel, [((tokens, part), bf16)], [VMEM] * 4, [], 0, 1 << 20, "collect", 8
        )(keep[0], got[0], near, far)[0]
        return whole.reshape(rows, frames, part)

    layer_output = collect_tokens(out_give, out_keep)
    input_grad = collect_tokens(in_give, in_keep)
    return (
        layer_output,
        input_grad,
        params_channel,
        params_up,
        params_bias,
        params_down,
        first_channel,
        second_channel,
        first_up,
        second_up,
        first_bias,
        second_bias,
        first_down,
        second_down,
    )


def solution(mesh):
    return jax.shard_map(
        functools.partial(on_device, mesh.shape["dp"]),
        mesh=mesh,
        in_specs=(
            P("dp", None, "chan"),
            P("dp", None),
            P("dp", None, "chan"),
            P(None, None, "chan"),
            P(None, None, "chan"),
            P(None, "chan"),
            P(None, "chan", None),
            P(None, None, "chan"),
            P(None, None, "chan"),
            P(None, "dp", "chan"),
            P(None, "dp", "chan"),
            P(None, "chan"),
            P(None, "chan"),
            P(None, "chan", "dp"),
            P(None, "chan", "dp"),
        ),
        out_specs=(
            P("dp", None, "chan"),
            P("dp", None, "chan"),
            P(None, None, "chan"),
            P(None, None, "chan"),
            P(None, "chan"),
            P(None, "chan", None),
            P(None, None, "chan"),
            P(None, None, "chan"),
            P(None, "dp", "chan"),
            P(None, "dp", "chan"),
            P(None, "chan"),
            P(None, "chan"),
            P(None, "chan", "dp"),
            P(None, "chan", "dp"),
        ),
        check_vma=False,
    )
```

```python
import functools

import jax
import jax.numpy as jnp
from jax import lax
from jax.experimental import pallas as pl
from jax.experimental.pallas import tpu as pltpu
from jax.sharding import PartitionSpec as P

kernel_taps = 7
reach = kernel_taps // 2
norm_eps = 1e-06
beta_first = 0.8
beta_second = 0.9
adam_eps = 1e-08
decay_rate = 0.01
adam_step = 10.0

HALO = 16
PAD = 8
LANES = 128
PARAM_ROWS = 32
f32 = jnp.float32
bf16 = jnp.bfloat16


def xor_perm(size, bit):
    return [(i, i ^ bit) for i in range(size)]


def hi_lo(value):
    hi = lax.reduce_precision(value, 8, 7)
    return hi.astype(bf16), (value - hi).astype(bf16)


def place():
    me = lax.axis_index("chan")
    return me // 2, me % 2, lax.axis_index("dp")


def lanes_of(x, c, r):
    return pl.ds(pl.multiple_of(((x ^ (r // 2)) * 2 + (c ^ (r % 2))) * LANES, LANES), LANES)


def row_tiles(ext):
    own = ext - 2 * HALO
    tiles = [(0, HALO, False)]
    tiles += [(HALO + at, 32, True) for at in range(0, own, 32)]
    return tiles + [(HALO + own, HALO, False)]


def lane(j):
    return slice(j * LANES, (j + 1) * LANES)


def fold(value):
    return value.reshape(value.shape[0] // 8, 8, value.shape[1]).sum(axis=0)


def plus(total, value):
    return value if total is None else total + value


def column_sum(value):
    return jnp.sum(value, axis=0, keepdims=True)


def gelu_parts(h):
    tail = jnp.exp(-0.5 * h * h)
    d = 1.0 + (0.3275911 * 0.7071067811865476) * jnp.abs(h)
    t = pl.reciprocal(d, approx=True)
    t = t * (2.0 - d * t)
    poly = t * (
        0.127414796
        + t * (-0.142248368 + t * (0.7107068705 + t * (-0.7265760135 + t * 0.5307027145)))
    )
    low = poly * tail
    phi = jnp.where(h < 0.0, low, 1.0 - low)
    return h * phi, phi + h * tail * 0.3989422804014327


def load_frames(x, c, packets, ext, source):
    for r, ref in enumerate(packets):
        source[PAD : PAD + ext, lanes_of(x, c, r)] = ref[0:ext, :].astype(f32)
    clear_pads(source, ext)


def load_params(x, c, packets, ext, params):
    for r, ref in enumerate(packets):
        hi = ref[ext : ext + PARAM_ROWS, :].astype(f32)
        lo = ref[ext + PARAM_ROWS : ext + 2 * PARAM_ROWS, :].astype(f32)
        params[:, lanes_of(x, c, r)] = hi + lo


def clear_pads(ref, ext):
    zeros = jnp.zeros((PAD, ref.shape[1]), ref.dtype)
    ref[0:PAD, :] = zeros
    ref[PAD + ext : PAD + ext + PAD, :] = zeros


def load_bias(x, c, layer, chip, params, bias):
    width = bias.shape[1] // 2
    for r in range(2):
        rows = params[:, lanes_of(x, c, 2 * chip + r)]
        for j in range(width // LANES):
            k = 24 + layer * (width // LANES) + j
            bias[0:1, r * width + j * LANES : r * width + (j + 1) * LANES] = rows[k : k + 1]


def start_copies(pairs, sems):
    started = []
    for i, (src, dst) in enumerate(pairs):
        copy = pltpu.make_async_copy(src, dst, sems.at[i])
        copy.start()
        started.append(copy)
    return started


def local_weights(own, core, held):
    width = own.shape[-1]
    return [
        (ref.at[m], held.at[m, :, r * width : (r + 1) * width])
        for r, ref in ((0, own), (1, core))
        for m in range(2)
    ]


def far_weights(y, near, near_core, far, far_core, held):
    width = near.shape[-1]
    pairs = []
    for r, first, second in ((0, near, far), (1, near_core, far_core)):
        columns = slice(r * width, (r + 1) * width)
        pairs.append((first, held.at[y, :, columns]))
        pairs.append((second, held.at[1 - y, :, columns]))
    return pairs


def masks_at(ids, start, rows):
    here = ids[PAD + start : PAD + start + rows, :]
    masks = []
    for k in range(kernel_taps):
        at = PAD + start + k - reach
        masks.append(ids[at : at + rows, :] == here)
    return masks


def forward_norm(layer, source, ids, params, centred, rstd, normed, ext):
    width = source.shape[1]
    tiles = width // LANES
    base = layer * 12
    for start, rows, _ in row_tiles(ext):
        masks = masks_at(ids, start, rows)
        convs = []
        total = square = None
        for j in range(tiles):
            acc = params[base + 7 : base + 8, lane(j)]
            for k in range(kernel_taps):
                at = PAD + start + k - reach
                piece = source[at : at + rows, lane(j)]
                tap = params[base + k : base + k + 1, lane(j)]
                acc = acc + tap * (piece if k == reach else jnp.where(masks[k], piece, 0.0))
            convs.append(acc)
            total = plus(total, acc)
            square = plus(square, acc * acc)
        mean = jnp.sum(total, axis=1, keepdims=True) * (1.0 / width)
        var = jnp.sum(square, axis=1, keepdims=True) * (1.0 / width) - mean * mean
        scale = lax.rsqrt(var + norm_eps)
        rstd[start : start + rows, :] = jnp.broadcast_to(scale, (rows, LANES))
        for j in range(tiles):
            value = (convs[j] - mean) * scale
            centred[start : start + rows, lane(j)] = value
            gain = params[base + 8 : base + 9, lane(j)]
            shift = params[base + 9 : base + 10, lane(j)]
            normed[start : start + rows, lane(j)] = (value * gain + shift).astype(bf16)


def forward_half(bias, held, normed, active, slope, ext):
    quarter = held.shape[2] // 2
    half = ext // 2
    for r in range(2):
        cols = slice(r * quarter, (r + 1) * quarter)
        for at in (0, half):
            rows = slice(at, at + half)
            h = (
                jnp.dot(normed[rows, :], held[0, :, cols], preferred_element_type=f32)
                + bias[0:1, cols]
            )
            value, grad = gelu_parts(h)
            active[rows, cols] = value.astype(bf16)
            slope[rows, cols] = grad


def down_half(held, active, rows):
    return lax.dot_general(
        active[rows, :], held[1], (((1,), (1,)), ((), ())), preferred_element_type=f32
    )


def finish_branch(layer, source, params, held, active, partial, branch, ext, put):
    half = ext // 2
    base = layer * 12
    for at in (0, half):
        rows = slice(at, at + half)
        value = partial[rows, :] + down_half(held, active, rows) + params[base + 10 : base + 11, :]
        branch[rows, :] = value
        put(at, half, source[PAD + at : PAD + at + half, :] + params[base + 11 : base + 12, :] * value)


def backward(
    layer, x, c, dp, dy, source, ids, params, helds, centred, rstd, normed, actives, slopes, branch,
    low, low_t, normed_t, hidden_lows, dnormed, dconv, small_c, gives, keeps, small_give, small_keep,
    put, ext,
):
    width = source.shape[1]
    tiles = width // LANES
    quarter = helds[0].shape[2] // 2
    half = ext // 2
    own = ext - 2 * HALO
    base = layer * 12
    small_c[...] = jnp.zeros_like(small_c)

    for j in range(tiles):
        scale = params[base + 11 : base + 12, lane(j)]
        sum_gamma = sum_bias = None
        for start, rows, inner in row_tiles(ext):
            grad = dy[start : start + rows, lane(j)]
            grad_branch = scale * grad
            low[start : start + rows, lane(j)] = grad_branch.astype(bf16)
            if inner:
                sum_gamma = plus(sum_gamma, fold(grad * branch[start : start + rows, lane(j)]))
                sum_bias = plus(sum_bias, fold(grad_branch))
        small_c[10:11, lane(j)] = column_sum(sum_bias)
        small_c[11:12, lane(j)] = column_sum(sum_gamma)

    low_t[...] = low[HALO : HALO + own, :].T
    normed_t[...] = normed[HALO : HALO + own, :].T

    def put_grad(r, m, value):
        out = (gives if r % 2 else keeps)[m]
        _, blocks, size, _ = out.shape
        parts = quarter // LANES
        rows = size // parts
        value = value.astype(out.dtype)
        for d in range(blocks):
            for j in range(parts):
                out[r // 2, d ^ dp, j * rows : (j + 1) * rows] = value[d * rows : (d + 1) * rows, lane(j)]

    bias_sums = []
    for r in range(4):
        chip, side = r // 2, r % 2
        cols = slice(side * quarter, (side + 1) * quarter)
        sums = None
        for at in (0, half):
            rows = slice(at, at + half)
            grad = (
                jnp.dot(low[rows, :], helds[chip][1, :, cols], preferred_element_type=f32)
                * slopes[chip][rows, cols]
            )
            hidden_lows[chip][rows, cols] = grad.astype(bf16)
            sums = plus(sums, fold(grad[HALO:] if at == 0 else grad[: half - HALO]))
        bias_sums.append(column_sum(sums))
        inner = slice(HALO, HALO + own)
        put_grad(r, 1, jnp.dot(low_t[...], actives[chip][inner, cols], preferred_element_type=f32))
        put_grad(
            r, 0, jnp.dot(normed_t[...], hidden_lows[chip][inner, cols], preferred_element_type=f32)
        )

    def back_half(chip, rows):
        return lax.dot_general(
            hidden_lows[chip][rows, :], helds[chip][0], (((1,), (1,)), ((), ())),
            preferred_element_type=f32,
        )

    for at in (0, half):
        rows = slice(at, at + half)
        dnormed[rows, :] = back_half(0, rows) + back_half(1, rows)

    clear_pads(dconv, ext)
    sums = [[None] * 3 for _ in range(tiles)]
    for start, rows, inner in row_tiles(ext):
        scale = rstd[start : start + rows, :]
        weighted, norms = [], []
        first = second = None
        for j in range(tiles):
            grad = dnormed[start : start + rows, lane(j)]
            norm = centred[start : start + rows, lane(j)]
            w = grad * params[base + 8 : base + 9, lane(j)]
            first = plus(first, w)
            second = plus(second, w * norm)
            weighted.append(w)
            norms.append(norm)
            if inner:
                sums[j][0] = plus(sums[j][0], fold(grad * norm))
                sums[j][1] = plus(sums[j][1], fold(grad))
        first = jnp.sum(first, axis=1, keepdims=True) * (1.0 / width)
        second = jnp.sum(second, axis=1, keepdims=True) * (1.0 / width)
        for j in range(tiles):
            value = scale * (weighted[j] - first - norms[j] * second)
            dconv[PAD + start : PAD + start + rows, lane(j)] = value
            if inner:
                sums[j][2] = plus(sums[j][2], fold(value))
    for j in range(tiles):
        small_c[8:9, lane(j)] = column_sum(sums[j][0])
        small_c[9:10, lane(j)] = column_sum(sums[j][1])
        small_c[7:8, lane(j)] = column_sum(sums[j][2])

    for j in range(tiles):
        taps = [params[base + k : base + k + 1, lane(j)] for k in range(kernel_taps)]
        sums = [None] * kernel_taps
        for start, rows, inner in row_tiles(ext):
            masks = masks_at(ids, start, rows)
            here = dconv[PAD + start : PAD + start + rows, lane(j)]
            total = dy[start : start + rows, lane(j)]
            for k in range(kernel_taps):
                mirror = kernel_taps - 1 - k
                at = PAD + start + mirror - reach
                piece = dconv[at : at + rows, lane(j)]
                total = total + taps[k] * (
                    piece if k == reach else jnp.where(masks[mirror], piece, 0.0)
                )
                if inner:
                    at = PAD + start + k - reach
                    piece = source[at : at + rows, lane(j)]
                    if k != reach:
                        piece = jnp.where(masks[k], piece, 0.0)
                    sums[k] = plus(sums[k], fold(piece * here))
            put(start, rows, inner, j, total)
        for k in range(kernel_taps):
            small_c[k : k + 1, lane(j)] = column_sum(sums[k])

    for r in range(4):
        sums = bias_sums[r]
        rows = [small_c[0:12, lanes_of(x, c, r)]]
        rows += [sums[:, lane(j)] for j in range(quarter // LANES)]
        rows += [jnp.zeros((16 - 12 - quarter // LANES, LANES), f32)]
        value = jnp.concatenate(rows, axis=0)
        if r % 2 == 0:
            small_keep[r // 2] = value
        else:
            hi = value.astype(bf16)
            small_give[r // 2, 0] = hi
            small_give[r // 2, 1] = (value - hi.astype(f32)).astype(bf16)


def frames_kernel(frames, chan, bias, give0, give1, here, beside, flat):
    tokens = frames.shape[0] * frames.shape[1]
    own = tokens // 4
    ext = own + 2 * HALO
    x, c, _ = place()
    zeros = jnp.zeros((HALO, LANES), bf16)
    flat[0:HALO, :] = zeros
    flat[HALO + tokens :, :] = zeros
    for r in range(frames.shape[0]):
        at = HALO + r * frames.shape[1]
        flat[at : at + frames.shape[1], :] = frames[r]
    rows = [chan[l] for l in range(chan.shape[0])]
    rows += [bias[l : l + 1, lane(j)] for l in range(bias.shape[0]) for j in range(bias.shape[1] // LANES)]
    rows += [jnp.zeros((PARAM_ROWS - 24 - bias.shape[0] * (bias.shape[1] // LANES), LANES), f32)]
    value = jnp.concatenate(rows, axis=0)
    hi = value.astype(bf16)
    lo = (value - hi.astype(f32)).astype(bf16)
    for out, dx, dc in ((give0, 1, 0), (give1, 1, 1), (here, 0, 0), (beside, 0, 1)):
        at = pl.multiple_of(((x ^ dx) * 2 + (c ^ dc)) * own, HALO)
        out[0:ext, :] = flat[pl.ds(at, ext), :]
        out[ext : ext + PARAM_ROWS, :] = hi
        out[ext + PARAM_ROWS :, :] = lo


def cotangent_kernel(frames, _, give0, give1, here, beside, flat):
    rows, count, _ = frames.shape
    tokens = rows * count
    own = tokens // 4
    ext = own + 2 * HALO
    x, c, _ = place()
    zeros = jnp.zeros((HALO, LANES), bf16)
    flat[0:HALO, :] = zeros
    flat[HALO + tokens :, :] = zeros
    for r in range(rows):
        at = HALO + r * count
        flat[at : at + count, :] = frames[r]
    for out, dx, dc in ((give0, 1, 0), (give1, 1, 1), (here, 0, 0), (beside, 0, 1)):
        at = pl.multiple_of(((x ^ dx) * 2 + (c ^ dc)) * own, HALO)
        out[...] = flat[pl.ds(at, ext), :]


def ids_kernel(segments, _, ids, columns):
    rows, count = segments.shape
    tokens = rows * count
    x, c, _ = place()
    edge = HALO + PAD
    none = jnp.full((edge, LANES), -1, jnp.int32)
    columns[0:edge, :] = none
    columns[edge + tokens :, :] = none
    for r in range(rows):
        row = jnp.broadcast_to(segments[r : r + 1, :] + 8 * r, (LANES, count))
        at = edge + r * count
        columns[at : at + count, :] = row.T
    at = pl.multiple_of((x * 2 + c) * (tokens // 4), HALO)
    ids[...] = columns[pl.ds(at, ids.shape[0]), :]


def weights_kernel(up, down, _, both, chosen, up_slice, down_slice, turned):
    _, _, dp = place()
    both[0] = up[0].astype(bf16)
    turned[...] = down[0].T
    both[1] = turned[...].astype(bf16)
    chosen[...] = both[dp % 2]
    rows = up_slice.shape[0]
    at = pl.ds(pl.multiple_of(dp * rows, rows), rows)
    up_slice[...] = up[0, at, :]
    down_slice[...] = turned[at, :]


def first_kernel(
    ids, here, beside, near, far, own, core, _,
    centred, rstd, normed, active, slope, partial, source, params, bias, held, sems,
):
    ext = ids.shape[0] - 2 * PAD
    x, c, _ = place()
    packets = (here, beside, near, far)
    copies = start_copies(local_weights(own, core, held), sems)
    load_frames(x, c, packets, ext, source)
    load_params(x, c, packets, ext, params)
    load_bias(x, c, 0, 0, params, bias)
    forward_norm(0, source, ids, params, centred, rstd, normed, ext)
    for copy in copies:
        copy.wait()
    forward_half(bias, held, normed, active, slope, ext)
    for at in (0, ext // 2):
        rows = slice(at, at + ext // 2)
        partial[rows, :] = down_half(held, active, rows)


def second_kernel(
    here, beside, near, far, normed, partial, w_near, w_near_core, w_far, w_far_core,
    next_source, active, slope, branch, source, params, bias, held, sems,
):
    ext = normed.shape[0]
    x, c, dp = place()
    packets = (here, beside, near, far)
    copies = start_copies(far_weights(dp % 2, w_near, w_near_core, w_far, w_far_core, held), sems)
    load_frames(x, c, packets, ext, source)
    load_params(x, c, packets, ext, params)
    load_bias(x, c, 0, 1, params, bias)
    for copy in copies:
        copy.wait()
    forward_half(bias, held, normed, active, slope, ext)

    def put(at, rows, value):
        next_source[at : at + rows, :] = value

    finish_branch(0, source, params, held, active, partial, branch, ext, put)


def third_kernel(
    ids, here, beside, near, far, source_in, own, core,
    centred, rstd, normed, active, slope, partial, source, params, bias, held, sems,
):
    ext = source_in.shape[0]
    x, c, _ = place()
    copies = start_copies(local_weights(own, core, held), sems)
    load_params(x, c, (here, beside, near, far), ext, params)
    load_bias(x, c, 1, 0, params, bias)
    source[PAD : PAD + ext, :] = source_in[...]
    clear_pads(source, ext)
    forward_norm(1, source, ids, params, centred, rstd, normed, ext)
    for copy in copies:
        copy.wait()
    forward_half(bias, held, normed, active, slope, ext)
    for at in (0, ext // 2):
        rows = slice(at, at + ext // 2)
        partial[rows, :] = down_half(held, active, rows)


def fourth_kernel(
    ids, here, beside, near, far, cot_here, cot_beside, cot_near, cot_far, source_in,
    centred, rstd, normed, active0, slope0, partial,
    own, core, w_near, w_near_core, w_far, w_far_core,
    grad_source, give0, give1, keep0, keep1, small_give, small_keep, out,
    source, params, bias, held0, held1, sems, active1, slope1, branch,
    dy, low, low_t, normed_t, hidden0, hidden1, dnormed, dconv, small_c,
):
    ext = source_in.shape[0]
    x, c, dp = place()
    pairs = far_weights(dp % 2, w_near, w_near_core, w_far, w_far_core, held1)
    copies = start_copies(pairs + local_weights(own, core, held0), sems)
    load_params(x, c, (here, beside, near, far), ext, params)
    load_bias(x, c, 1, 1, params, bias)
    source[PAD : PAD + ext, :] = source_in[...]
    clear_pads(source, ext)
    for r, ref in enumerate((cot_here, cot_beside, cot_near, cot_far)):
        dy[:, lanes_of(x, c, r)] = ref[...].astype(f32)
    for copy in copies:
        copy.wait()
    forward_half(bias, held1, normed, active1, slope1, ext)

    def put(at, rows, value):
        if at == 0:
            out[0 : rows - HALO, :] = value[HALO:].astype(bf16)
        else:
            out[at - HALO :, :] = value[: rows - HALO].astype(bf16)

    finish_branch(1, source, params, held1, active1, partial, branch, ext, put)

    def put_grad(start, rows, inner, j, value):
        grad_source[start : start + rows, lane(j)] = value

    backward(
        1, x, c, dp, dy, source, ids, params, (held0, held1), centred, rstd, normed,
        (active0, active1), (slope0, slope1), branch, low, low_t, normed_t, (hidden0, hidden1),
        dnormed, dconv, small_c, (give0, give1), (keep0, keep1), small_give, small_keep, put_grad, ext,
    )


def fifth_kernel(
    ids, here, beside, near, far, dy, centred, rstd, normed, active0, slope0, active1, slope1, branch,
    own, core, w_near, w_near_core, w_far, w_far_core, first_out, _x, _y,
    give0, give1, keep0, keep1, small_give, small_keep, out_give0, out_give1, out_keep0, out_keep1,
    source, params, held0, held1, sems, low, low_t, normed_t, hidden0, hidden1, dnormed, dconv, small_c, out,
):
    ext = dy.shape[0]
    x, c, dp = place()
    packets = (here, beside, near, far)
    pairs = far_weights(dp % 2, w_near, w_near_core, w_far, w_far_core, held1)
    copies = start_copies(pairs + local_weights(own, core, held0), sems)
    load_frames(x, c, packets, ext, source)
    load_params(x, c, packets, ext, params)
    for copy in copies:
        copy.wait()

    def put_grad(start, rows, inner, j, value):
        if inner:
            out[start - HALO : start - HALO + rows, lane(j)] = value.astype(bf16)

    backward(
        0, x, c, dp, dy, source, ids, params, (held0, held1), centred, rstd, normed,
        (active0, active1), (slope0, slope1), branch, low, low_t, normed_t, (hidden0, hidden1),
        dnormed, dconv, small_c, (give0, give1), (keep0, keep1), small_give, small_keep, put_grad, ext,
    )
    for i, ref in enumerate((first_out, out)):
        for r, piece in enumerate((out_keep0, out_give0, out_keep1, out_give1)):
            piece[i] = ref[:, lanes_of(x, c, r)]


def adamw(param, first, second, grad):
    first = beta_first * first + (1.0 - beta_first) * grad
    second = beta_second * second + (1.0 - beta_second) * grad * grad
    first_hat = first * (1.0 / (1.0 - beta_first**adam_step))
    second_hat = second * (1.0 / (1.0 - beta_second**adam_step))
    update = first_hat / (jnp.sqrt(second_hat) + adam_eps) + decay_rate * param
    return update, first, second


def to_packet(packet, at, value):
    packet[at : at + value.shape[0], :] = value.astype(bf16)


def side_to_packet(packet, value):
    rows = value.shape[0]
    at = packet.shape[0] - 2 * rows
    hi = value.astype(bf16)
    lo = (value - hi.astype(f32)).astype(bf16)
    packet[at : at + rows, :] = hi
    packet[at + rows :, :] = lo
    return hi.astype(f32) + lo.astype(f32)


def side_of(packet):
    at = packet.shape[0] - 32
    return packet[at : at + 16, :].astype(f32) + packet[at + 16 :, :].astype(f32)


def core_sum_kernel(got_up, got_down, got_side, keep_up, keep_down, keep_side, *refs):
    to_x, to_y, up, down, side = refs[-5:]
    _, blocks, size, _ = got_up.shape
    for d in range(blocks):
        up[d] = keep_up[0, d] + got_up[0, d].astype(f32)
        to_packet(to_x, d * size, keep_up[1, d] + got_up[1, d].astype(f32))
        for i in range(2):
            value = keep_down[i, d] + got_down[i, d].astype(f32)
            if d % 2:
                to_packet(to_y, (i * (blocks // 2) + d // 2) * size, value)
            else:
                down[i, d // 2] = value
    got = got_side[:, 0].astype(f32) + got_side[:, 1].astype(f32) + keep_side[...]
    side[...] = got[0]
    side_to_packet(to_x, got[1])


def cross_sum_kernel(from_x, from_y, up, down, side, *refs):
    to_y, to_x, up_out, down_out, side_out = refs[-5:]
    blocks, size, _ = up.shape
    for d in range(blocks):
        value = up[d] + from_x[d * size : (d + 1) * size, :].astype(f32)
        if d % 2:
            to_packet(to_y, (d // 2) * size, value)
        else:
            up_out[d // 2] = value
    for d in range(blocks // 2):
        for i in range(2):
            at = (i * (blocks // 2) + d) * size
            value = down[i, d] + from_y[at : at + size, :].astype(f32)
            if i:
                to_packet(to_x, d * size, value)
            else:
                down_out[d] = value
    side_out[...] = side_to_packet(to_y, side[...] + side_of(from_x))


def plane_sum_kernel(from_y, from_x, up, down, side, *refs):
    packet, main, side_out = refs[-3:]
    blocks, size, _ = up.shape
    for m, (got, held) in enumerate(((from_y, up), (from_x, down))):
        for d in range(blocks):
            value = held[d] + got[d * size : (d + 1) * size, :].astype(f32)
            if d % 2:
                to_packet(packet, (m * (blocks // 2) + d // 2) * size, value)
            else:
                main[m, d // 2] = value
    side_out[...] = side_to_packet(packet, side[...] + side_of(from_y))


def line_sum_kernel(got, held, side, *refs):
    packet, main, side_out = refs[-3:]
    _, blocks, size, _ = held.shape
    for m in range(2):
        for d in range(blocks):
            at = (m * blocks + d) * size
            value = held[m, d] + got[at : at + size, :].astype(f32)
            if d % 2:
                to_packet(packet, (m * (blocks // 2) + d // 2) * size, value)
            else:
                main[m, d // 2] = value
    side_out[...] = side_to_packet(packet, side[...] + side_of(got))


def update_kernel(layer, got, held, side, up, down, m_up, v_up, m_down, v_down, *refs):
    sent, main, side_out = refs[-3:]
    size = held.shape[2]
    rows = up.shape[0]
    for m in range(2):
        main[m] = held[m, 0] + got[m * size : (m + 1) * size, :].astype(f32)
    side_out[...] = side[...] + side_of(got)
    for m, (p, first, second) in enumerate(((up, m_up, v_up), (down, m_down, v_down))):
        for j in range(size // rows):
            cols, at = lane(j), j * rows
            u, _, _ = adamw(
                p[:, cols], first[layer, :, cols], second[layer, :, cols], main[m, at : at + rows]
            )
            sent[m * size + at : m * size + at + rows, :] = u.astype(bf16)


def adam_kernel(
    main0, main1, side0, side1, chan, bias,
    m_chan, v_chan, m_up, v_up, m_bias, v_bias, m_down, v_down,
    u_chan, u_bias, f_chan, s_chan, f_up, s_up, f_bias, s_bias, f_down, s_down,
):
    rows = m_up.shape[1]
    for l, (main, side) in enumerate(((main0, side0), (main1, side1))):
        g = side[...]
        u_chan[l], f_chan[l], s_chan[l] = adamw(chan[l], m_chan[l], v_chan[l], g[0:12])
        for j in range(main.shape[1] // rows):
            cols, at = lane(j), j * rows
            row = slice(l, l + 1)
            u_bias[row, cols], f_bias[row, cols], s_bias[row, cols] = adamw(
                bias[row, cols], m_bias[row, cols], v_bias[row, cols], g[12 + j : 13 + j]
            )
            _, f_up[l, :, cols], s_up[l, :, cols] = adamw(
                0.0, m_up[l, :, cols], v_up[l, :, cols], main[0, at : at + rows]
            )
            _, f_down[l, :, cols], s_down[l, :, cols] = adamw(
                0.0, m_down[l, :, cols], v_down[l, :, cols], main[1, at : at + rows]
            )


def ring_order(n_dp):
    return list(range(0, n_dp, 2)) + list(range(n_dp - 1, 0, -2))


def spread_kernel(n_dp, layers, parts, *refs):
    count = n_dp + 1
    blocks, (up, down, held) = refs[: count * layers], refs[count * layers :]
    dp = lax.axis_index("dp")
    half = n_dp // 2
    spot = jnp.where(dp % 2 == 0, dp // 2, n_dp - 1 - dp // 2)

    def owner(distance):
        at = lax.rem(spot + distance + n_dp, n_dp)
        return jnp.where(at < half, 2 * at, 2 * (n_dp - 1 - at) + 1)

    distances = [0]
    for step in range(1, half):
        distances += [-step, step]
    rows = up.shape[1] // n_dp
    size = parts * rows
    for l in range(layers):
        mine = blocks[l * count : (l + 1) * count]
        halves = [(d, ref, 0, ref, size) for d, ref in zip(distances, mine)]
        halves.append((half, mine[-2], 0, mine[-1], 0))
        for distance, first, first_at, second, second_at in halves:
            at = pl.ds(pl.multiple_of(owner(distance) * rows, rows), rows)
            for j in range(parts):
                start = first_at + j * rows
                up[l, at, lane(j)] = first[start : start + rows, :].astype(f32)
                start = second_at + j * rows
                held[at, lane(j)] = second[start : start + rows, :].astype(f32)
        for j in range(parts):
            down[l, lane(j), :] = held[:, lane(j)].T


def collect_kernel(own, core, near, far, out, grad):
    x, c, _ = place()
    rows = own.shape[1]
    for r, ref in enumerate((own, core, near, far)):
        at = pl.multiple_of(((x ^ (r // 2)) * 2 + (c ^ (r % 2))) * rows, HALO)
        out[pl.ds(at, rows), :] = ref[0]
        grad[pl.ds(at, rows), :] = ref[1]


VMEM = pl.BlockSpec(memory_space=pltpu.VMEM)
ANY = pl.BlockSpec(memory_space=pl.ANY)


def call(kernel, outs, in_specs, scratch, flops, size, name, limit=24):
    return pl.pallas_call(
        kernel,
        out_shape=[jax.ShapeDtypeStruct(s, t) for s, t in outs],
        in_specs=in_specs,
        out_specs=[VMEM] * len(outs),
        scratch_shapes=scratch,
        compiler_params=pltpu.CompilerParams(vmem_limit_bytes=limit * 1024 * 1024),
        cost_estimate=pl.CostEstimate(flops=flops, bytes_accessed=size, transcendentals=0),
        name=name,
    )


def on_device(
    n_dp, frames_in, segments, cotangent, channel_params, weight_up, bias_up, weight_down,
    momentum_channel, variance_channel, momentum_up, variance_up, momentum_bias, variance_bias,
    momentum_down, variance_down,
):
    rows, frames, part = frames_in.shape
    layers, width, quarter = weight_up.shape
    chip_hidden = 2 * quarter
    tokens = rows * frames
    own = tokens // 4
    ext = own + 2 * HALO
    shard = width // n_dp
    parts = quarter // LANES

    def core_swap(v):
        return lax.ppermute(v, "chan", xor_perm(4, 1))

    def x_swap(v):
        return lax.ppermute(v, "chan", xor_perm(4, 2))

    def dp_swap(v, bit):
        return lax.ppermute(v, "dp", xor_perm(n_dp, bit))

    def after(value, *others):
        return lax.optimization_barrier((value, *others))[0]

    packet = ((ext + 2 * PARAM_ROWS, LANES), bf16)
    flat = pltpu.VMEM((tokens + 2 * HALO, LANES), bf16)
    frames_call = call(frames_kernel, [packet] * 4, [VMEM] * 3, [flat], 0, 1 << 20, "frames", 8)
    give0, give1, here, beside = frames_call(frames_in, channel_params, bias_up)
    packets = [here, core_swap(beside), x_swap(give0), core_swap(x_swap(give1))]

    ids_call = call(
        ids_kernel, [((ext + 2 * PAD, LANES), jnp.int32)], [VMEM, ANY],
        [pltpu.VMEM((tokens + 2 * HALO + 2 * PAD, LANES), jnp.int32)], 0, 1 << 20, "ids", 8,
    )
    ids = ids_call(segments, give0)[0]

    def layer_weights(l, before):
        def one(array):
            return pl.BlockSpec((1,) + array.shape[1:], lambda i: (l, 0, 0))

        def whole(shape):
            return pl.BlockSpec(shape, lambda i: (0,) * len(shape))

        outs = [((2, width, quarter), bf16), ((width, quarter), bf16)]
        outs += [((shard, quarter), f32)] * 2
        return pl.pallas_call(
            weights_kernel,
            grid=(1,),
            out_shape=[jax.ShapeDtypeStruct(s, t) for s, t in outs],
            in_specs=[one(weight_up), one(weight_down), ANY],
            out_specs=[whole(s) for s, _ in outs],
            scratch_shapes=[pltpu.VMEM((width, quarter), f32)],
            compiler_params=pltpu.CompilerParams(vmem_limit_bytes=16 * 1024 * 1024),
            cost_estimate=pl.CostEstimate(flops=0, bytes_accessed=3 << 20, transcendentals=0),
            name="weights",
        )(weight_up, weight_down, before)

    both0, chosen0, *slices0 = layer_weights(0, give0)
    both1, chosen1, *slices1 = layer_weights(1, packets[2])
    near0, near1 = x_swap(chosen0), x_swap(chosen1)
    local0, local1 = [both0, core_swap(both0)], [both1, core_swap(both1)]

    cot_packet = ((ext, LANES), bf16)
    cot_call = call(
        cotangent_kernel, [cot_packet] * 4, [VMEM, ANY], [flat], 0, 2 << 20, "cotangent", 8
    )
    give0, give1, here, beside = cot_call(cotangent, near0)
    cots = [here, core_swap(beside), x_swap(give0), core_swap(x_swap(give1))]

    wide = (ext, width)
    deep = (ext, chip_hidden)
    flops = 2 * ext * width * chip_hidden
    held = pltpu.VMEM((2, width, chip_hidden), bf16)
    sems = pltpu.SemaphoreType.DMA((8,))
    padded_rows = pltpu.VMEM((ext + 2 * PAD, width), f32)
    params = pltpu.VMEM((PARAM_ROWS, width), f32)
    bias = pltpu.VMEM((1, chip_hidden), f32)
    norm_shapes = [(wide, f32), ((ext, LANES), f32), (wide, bf16)]
    half_shapes = [(deep, bf16), (deep, f32), (wide, f32)]
    back_scratch = [
        pltpu.VMEM(wide, bf16),
        pltpu.VMEM((width, own), bf16),
        pltpu.VMEM((width, own), bf16),
        pltpu.VMEM(deep, bf16),
        pltpu.VMEM(deep, bf16),
        pltpu.VMEM(wide, f32),
        padded_rows,
        pltpu.VMEM((16, width), f32),
    ]
    size = parts * shard
    grad_shape = (2, n_dp, size, LANES)
    grad_shapes = [
        (grad_shape, bf16),
        (grad_shape, bf16),
        (grad_shape, f32),
        (grad_shape, f32),
        ((2, 2, 16, LANES), bf16),
        ((2, 16, LANES), f32),
    ]
    out_shapes = [((2, own, LANES), bf16)] * 4

    first = call(
        first_kernel, norm_shapes + half_shapes, [VMEM] * 5 + [ANY] * 3,
        [padded_rows, params, bias, held, sems], 2 * flops, 6 << 20, "layer0_near",
    )
    centred0, rstd0, normed0, active00, slope00, partial0 = first(
        ids, *packets, *local0, chosen1
    )
    far0 = dp_swap(after(near0, partial0), 1)
    far1 = dp_swap(after(near1, far0), 1)
    away0 = [near0, core_swap(near0), far0, core_swap(far0)]
    away1 = [near1, core_swap(near1), far1, core_swap(far1)]
    second = call(
        second_kernel, [(wide, f32)] + half_shapes, [VMEM] * 6 + [ANY] * 4,
        [padded_rows, params, bias, held, sems], 2 * flops, 6 << 20, "layer0_far",
    )
    source1, active01, slope01, branch0 = second(*packets, normed0, partial0, *away0)
    third = call(
        third_kernel, norm_shapes + half_shapes, [VMEM] * 6 + [ANY] * 2,
        [padded_rows, params, bias, held, sems], 2 * flops, 6 << 20, "layer1_near",
    )
    kept1 = third(ids, *packets, source1, *local1)
    fourth = call(
        fourth_kernel,
        [(wide, f32)] + grad_shapes + [((own, width), bf16)],
        [VMEM] * 16 + [ANY] * 6,
        [padded_rows, params, bias, held, held, sems]
        + [pltpu.VMEM(s, t) for s, t in half_shapes]
        + [pltpu.VMEM(wide, f32)]
        + back_scratch,
        10 * flops,
        16 << 20,
        "layer1_both",
        40,
    )
    grad1, *parts1, first_out = fourth(ids, *packets, *cots, source1, *kept1, *local1, *away1)

    half = n_dp // 2
    piece = (size, LANES)
    side_shape = ((16, LANES), f32)

    def packet_of(blocks, side):
        return ((blocks * size + (32 if side else 0), LANES), bf16)

    def combine(kernel, outs, args, before, name):
        specs = [VMEM] * len(args) + [ANY] * len(before)
        return call(kernel, outs, specs, [], 0, 1 << 20, name, 16)(*args, *before)

    def core_step(give_up, give_down, keep_up, keep_down, give_side, keep_side, before):
        outs = [packet_of(n_dp, True), packet_of(n_dp, False), ((n_dp,) + piece, f32)]
        outs += [((2, half) + piece, f32), side_shape]
        args = [core_swap(v) for v in (give_up, give_down, give_side)]
        args += [keep_up, keep_down, keep_side]
        return combine(core_sum_kernel, outs, args, before, "core_sum")

    def cross_step(to_x, to_y, up, down, side, before):
        outs = [packet_of(half, True), packet_of(half, False)]
        outs += [((half,) + piece, f32), ((half,) + piece, f32), side_shape]
        args = [x_swap(to_x), dp_swap(to_y, 1), up, down, side]
        return combine(cross_sum_kernel, outs, args, before, "cross_sum")

    def plane_step(to_y, to_x, up, down, side, before):
        outs = [packet_of(half, True), ((2, half // 2) + piece, f32), side_shape]
        args = [dp_swap(to_y, 1), x_swap(to_x), up, down, side]
        return combine(plane_sum_kernel, outs, args, before, "plane_sum")

    def line_step(packet, main, side, bit, before):
        left = main.shape[1] // 2
        outs = [packet_of(2 * left, True), ((2, left) + piece, f32), side_shape]
        return combine(line_sum_kernel, outs, [dp_swap(packet, bit), main, side], before, "line_sum")

    turned = [jnp.swapaxes(v, 1, 2) for v in (momentum_down, variance_down)]
    matrix_moments = [momentum_up, variance_up] + turned

    def update_step(layer, packet, main, side, slices, before):
        outs = [packet_of(2, False), ((2,) + piece, f32), side_shape]
        args = [dp_swap(packet, half), main, side, *slices, *matrix_moments]
        return combine(functools.partial(update_kernel, layer), outs, args, before, "update")

    def line_steps(state, before):
        bit = 2
        while bit < half:
            state = line_step(*state, bit, before)
            bit *= 2
        return state

    crossing1 = core_step(*parts1, [])
    fifth = call(
        fifth_kernel,
        grad_shapes + out_shapes,
        [VMEM] * 14 + [ANY] * 6 + [VMEM] + [ANY] * 2,
        [padded_rows, params, held, held, sems] + back_scratch + [pltpu.VMEM((own, width), bf16)],
        8 * flops,
        20 << 20,
        "layer0_backward",
        36,
    )
    *parts0, give_near, give_far, keep_near, keep_far = fifth(
        ids, *packets, grad1, centred0, rstd0, normed0, active00, slope00, active01, slope01, branch0,
        *local0, *away0, first_out, crossing1[0], crossing1[1],
    )
    plane1 = cross_step(*crossing1, [])
    crossing0 = core_step(*parts0, [plane1[0]])
    line1 = line_steps(plane_step(*plane1, []), [])
    plane0 = cross_step(*crossing0, [line1[0]])
    sent1, main1, side1 = update_step(1, *line1, slices1, [])

    order = ring_order(n_dp)
    ahead = [(order[i], order[(i + 1) % n_dp]) for i in range(n_dp)]
    back = [(b, a) for a, b in ahead]

    def ring_step(right, left):
        return lax.ppermute(right, "dp", ahead), lax.ppermute(left, "dp", back)

    def ring_end(right, left):
        cut = right.shape[0] // 2
        top = lax.ppermute(right[:cut], "dp", ahead)
        bottom = lax.ppermute(left[cut:], "dp", back)
        return [top, bottom]

    ring1 = [(sent1, sent1)]
    for _ in range(1, half):
        ring1.append(ring_step(*ring1[-1]))
    end1 = ring_end(*ring1[-1])
    state = plane_step(*plane0, [sent1])
    line0 = line_steps(state, [ring1[1][0]])
    sent0, main0, side0 = update_step(0, *line0, slices0, [ring1[2][0]])
    ring0 = [(sent0, sent0)]
    for _ in range(1, half):
        ring0.append(ring_step(*ring0[-1]))
    end0 = ring_end(*ring0[-1])

    def blocks_of(sent, ring, end):
        return [sent] + [v for pair in ring[1:] for v in pair] + end

    adam_outs = [
        (channel_params.shape, f32),
        (bias_up.shape, f32),
        (channel_params.shape, f32),
        (channel_params.shape, f32),
        (momentum_up.shape, f32),
        (momentum_up.shape, f32),
        (bias_up.shape, f32),
        (bias_up.shape, f32),
        (turned[0].shape, f32),
        (turned[0].shape, f32),
    ]
    adam = call(adam_kernel, adam_outs, [VMEM] * 14, [], 1 << 20, 4 << 20, "adam", 16)
    (
        params_channel, params_bias, first_channel, second_channel,
        first_up, second_up, first_bias, second_bias, first_down, second_down,
    ) = adam(
        main0, main1, side0, side1,
        channel_params, bias_up, momentum_channel, variance_channel, momentum_up, variance_up,
        momentum_bias, variance_bias, *turned,
    )
    first_down, second_down = jnp.swapaxes(first_down, 1, 2), jnp.swapaxes(second_down, 1, 2)

    spread = call(
        functools.partial(spread_kernel, n_dp, layers, parts),
        [(weight_up.shape, f32), (weight_down.shape, f32)],
        [VMEM] * ((n_dp + 1) * layers),
        [pltpu.VMEM((width, quarter), f32)],
        1 << 20,
        5 << 20,
        "spread",
    )
    params_up, params_down = spread(*blocks_of(sent0, ring0, end0), *blocks_of(sent1, ring1, end1))

    give_near, give_far = after(give_near, line0[0]), after(give_far, line0[0])
    got_near, got_far = core_swap(give_near), core_swap(give_far)
    collect = call(
        collect_kernel, [((tokens, part), bf16)] * 2, [VMEM] * 4, [], 0, 1 << 20, "collect", 8
    )
    layer_output, input_grad = [
        v.reshape(rows, frames, part)
        for v in collect(keep_near, got_near, x_swap(keep_far), x_swap(got_far))
    ]
    return (
        layer_output,
        input_grad,
        params_channel,
        params_up,
        params_bias,
        params_down,
        first_channel,
        second_channel,
        first_up,
        second_up,
        first_bias,
        second_bias,
        first_down,
        second_down,
    )


def solution(mesh):
    return jax.shard_map(
        functools.partial(on_device, mesh.shape["dp"]),
        mesh=mesh,
        in_specs=(
            P("dp", None, "chan"),
            P("dp", None),
            P("dp", None, "chan"),
            P(None, None, "chan"),
            P(None, None, "chan"),
            P(None, "chan"),
            P(None, "chan", None),
            P(None, None, "chan"),
            P(None, None, "chan"),
            P(None, "dp", "chan"),
            P(None, "dp", "chan"),
            P(None, "chan"),
            P(None, "chan"),
            P(None, "chan", "dp"),
            P(None, "chan", "dp"),
        ),
        out_specs=(
            P("dp", None, "chan"),
            P("dp", None, "chan"),
            P(None, None, "chan"),
            P(None, None, "chan"),
            P(None, "chan"),
            P(None, "chan", None),
            P(None, None, "chan"),
            P(None, None, "chan"),
            P(None, "dp", "chan"),
            P(None, "dp", "chan"),
            P(None, "chan"),
            P(None, "chan"),
            P(None, "chan", "dp"),
            P(None, "chan", "dp"),
        ),
        check_vma=False,
    )
```

```python
import functools

import jax
import jax.numpy as jnp
from jax import lax
from jax.experimental import pallas as pl
from jax.experimental.pallas import tpu as pltpu
from jax.sharding import PartitionSpec as P

kernel_taps = 7
reach = kernel_taps // 2
norm_eps = 1e-06
beta_first = 0.8
beta_second = 0.9
adam_eps = 1e-08
decay_rate = 0.01
adam_step = 10.0

HALO = 16
PAD = 8
LANES = 128
PARAM_ROWS = 32
f32 = jnp.float32
bf16 = jnp.bfloat16


def xor_perm(size, bit):
    return [(i, i ^ bit) for i in range(size)]


def hi_lo(value):
    hi = lax.reduce_precision(value, 8, 7)
    return hi.astype(bf16), (value - hi).astype(bf16)


def place():
    me = lax.axis_index("chan")
    return me // 2, me % 2, lax.axis_index("dp")


def lanes_of(x, c, r):
    return pl.ds(pl.multiple_of(((x ^ (r // 2)) * 2 + (c ^ (r % 2))) * LANES, LANES), LANES)


def row_tiles(ext):
    own = ext - 2 * HALO
    tiles = [(0, HALO, False)]
    tiles += [(HALO + at, 32, True) for at in range(0, own, 32)]
    return tiles + [(HALO + own, HALO, False)]


def lane(j):
    return slice(j * LANES, (j + 1) * LANES)


def fold(value):
    return value.reshape(value.shape[0] // 8, 8, value.shape[1]).sum(axis=0)


def plus(total, value):
    return value if total is None else total + value


def column_sum(value):
    return jnp.sum(value, axis=0, keepdims=True)


def gelu_parts(h):
    tail = jnp.exp(-0.5 * h * h)
    d = 1.0 + (0.3275911 * 0.7071067811865476) * jnp.abs(h)
    t = pl.reciprocal(d, approx=True)
    t = t * (2.0 - d * t)
    poly = t * (
        0.127414796
        + t * (-0.142248368 + t * (0.7107068705 + t * (-0.7265760135 + t * 0.5307027145)))
    )
    low = poly * tail
    phi = jnp.where(h < 0.0, low, 1.0 - low)
    return h * phi, phi + h * tail * 0.3989422804014327


def load_frames(x, c, packets, ext, source):
    for r, ref in enumerate(packets):
        source[PAD : PAD + ext, lanes_of(x, c, r)] = ref[0:ext, :].astype(f32)
    clear_pads(source, ext)


def load_params(x, c, packets, ext, params):
    for r, ref in enumerate(packets):
        hi = ref[ext : ext + PARAM_ROWS, :].astype(f32)
        lo = ref[ext + PARAM_ROWS : ext + 2 * PARAM_ROWS, :].astype(f32)
        params[:, lanes_of(x, c, r)] = hi + lo


def clear_pads(ref, ext):
    zeros = jnp.zeros((PAD, ref.shape[1]), ref.dtype)
    ref[0:PAD, :] = zeros
    ref[PAD + ext : PAD + ext + PAD, :] = zeros


def load_bias(x, c, layer, chip, params, bias):
    width = bias.shape[1] // 2
    for r in range(2):
        rows = params[:, lanes_of(x, c, 2 * chip + r)]
        for j in range(width // LANES):
            k = 24 + layer * (width // LANES) + j
            bias[0:1, r * width + j * LANES : r * width + (j + 1) * LANES] = rows[k : k + 1]


def start_copies(pairs, sems):
    started = []
    for i, (src, dst) in enumerate(pairs):
        copy = pltpu.make_async_copy(src, dst, sems.at[i])
        copy.start()
        started.append(copy)
    return started


def local_weights(own, core, held):
    width = own.shape[-1]
    return [
        (ref.at[m], held.at[m, :, r * width : (r + 1) * width])
        for r, ref in ((0, own), (1, core))
        for m in range(2)
    ]


def far_weights(y, near, near_core, far, far_core, held):
    width = near.shape[-1]
    pairs = []
    for r, first, second in ((0, near, far), (1, near_core, far_core)):
        columns = slice(r * width, (r + 1) * width)
        pairs.append((first, held.at[y, :, columns]))
        pairs.append((second, held.at[1 - y, :, columns]))
    return pairs


def masks_at(ids, start, rows):
    here = ids[PAD + start : PAD + start + rows, :]
    masks = []
    for k in range(kernel_taps):
        at = PAD + start + k - reach
        masks.append(ids[at : at + rows, :] == here)
    return masks


def forward_norm(layer, source, ids, params, centred, rstd, normed, ext):
    width = source.shape[1]
    tiles = width // LANES
    base = layer * 12
    for start, rows, _ in row_tiles(ext):
        masks = masks_at(ids, start, rows)
        convs = []
        total = square = None
        for j in range(tiles):
            acc = params[base + 7 : base + 8, lane(j)]
            for k in range(kernel_taps):
                at = PAD + start + k - reach
                piece = source[at : at + rows, lane(j)]
                tap = params[base + k : base + k + 1, lane(j)]
                acc = acc + tap * (piece if k == reach else jnp.where(masks[k], piece, 0.0))
            convs.append(acc)
            total = plus(total, acc)
            square = plus(square, acc * acc)
        mean = jnp.sum(total, axis=1, keepdims=True) * (1.0 / width)
        var = jnp.sum(square, axis=1, keepdims=True) * (1.0 / width) - mean * mean
        scale = lax.rsqrt(var + norm_eps)
        rstd[start : start + rows, :] = jnp.broadcast_to(scale, (rows, LANES))
        for j in range(tiles):
            value = (convs[j] - mean) * scale
            centred[start : start + rows, lane(j)] = value
            gain = params[base + 8 : base + 9, lane(j)]
            shift = params[base + 9 : base + 10, lane(j)]
            normed[start : start + rows, lane(j)] = (value * gain + shift).astype(bf16)


def forward_half(bias, held, normed, active, slope, ext):
    quarter = held.shape[2] // 2
    half = ext // 2
    for r in range(2):
        cols = slice(r * quarter, (r + 1) * quarter)
        for at in (0, half):
            rows = slice(at, at + half)
            h = (
                jnp.dot(normed[rows, :], held[0, :, cols], preferred_element_type=f32)
                + bias[0:1, cols]
            )
            value, grad = gelu_parts(h)
            active[rows, cols] = value.astype(bf16)
            slope[rows, cols] = grad


def down_half(held, active, rows):
    return lax.dot_general(
        active[rows, :], held[1], (((1,), (1,)), ((), ())), preferred_element_type=f32
    )


def finish_branch(layer, source, params, held, active, partial, branch, ext, put):
    half = ext // 2
    base = layer * 12
    for at in (0, half):
        rows = slice(at, at + half)
        value = partial[rows, :] + down_half(held, active, rows) + params[base + 10 : base + 11, :]
        branch[rows, :] = value
        put(at, half, source[PAD + at : PAD + at + half, :] + params[base + 11 : base + 12, :] * value)


def branch_grad(layer, dy, params, low, ext):
    base = layer * 12
    for j in range(dy.shape[1] // LANES):
        scale = params[base + 11 : base + 12, lane(j)]
        for start, rows, _ in row_tiles(ext):
            low[start : start + rows, lane(j)] = (scale * dy[start : start + rows, lane(j)]).astype(bf16)


def put_grad(dp, out, parts, value):
    blocks, size, _ = out.shape
    rows = size // parts
    value = value.astype(out.dtype)
    for d in range(blocks):
        for j in range(parts):
            out[d ^ dp, j * rows : (j + 1) * rows] = value[d * rows : (d + 1) * rows, lane(j)]


def backward_half(dp, held, low, low_t, normed_t, active, slope, hidden_low, give, keep, bias_sums, ext):
    quarter = held.shape[2] // 2
    half = ext // 2
    inner = slice(HALO, ext - HALO)
    parts = quarter // LANES
    for r, out in ((0, keep), (1, give)):
        cols = slice(r * quarter, (r + 1) * quarter)
        sums = None
        for at in (0, half):
            rows = slice(at, at + half)
            grad = (
                jnp.dot(low[rows, :], held[1, :, cols], preferred_element_type=f32)
                * slope[rows, cols]
            )
            hidden_low[rows, cols] = grad.astype(bf16)
            sums = plus(sums, fold(grad[HALO:] if at == 0 else grad[: half - HALO]))
        bias_sums[0:1, cols] = column_sum(sums)
        put_grad(dp, out[1], parts, jnp.dot(low_t[...], active[inner, cols], preferred_element_type=f32))
        put_grad(
            dp, out[0], parts, jnp.dot(normed_t[...], hidden_low[inner, cols], preferred_element_type=f32)
        )


def back_half(held, hidden_low, rows):
    return lax.dot_general(
        hidden_low[rows, :], held[0], (((1,), (1,)), ((), ())), preferred_element_type=f32
    )


def backward_norm(
    layer, x, c, dy, source, ids, params, centred, rstd, branch, dnormed, dconv, small_c,
    bias_near, bias_far, side_give, side_keep, put, ext,
):
    width = source.shape[1]
    tiles = width // LANES
    quarter = bias_near.shape[1] // 2
    base = layer * 12
    small_c[...] = jnp.zeros_like(small_c)
    for j in range(tiles):
        scale = params[base + 11 : base + 12, lane(j)]
        sum_gamma = sum_bias = None
        for start, rows, inner in row_tiles(ext):
            if inner:
                grad = dy[start : start + rows, lane(j)]
                sum_gamma = plus(sum_gamma, fold(grad * branch[start : start + rows, lane(j)]))
                sum_bias = plus(sum_bias, fold(scale * grad))
        small_c[10:11, lane(j)] = column_sum(sum_bias)
        small_c[11:12, lane(j)] = column_sum(sum_gamma)

    clear_pads(dconv, ext)
    sums = [[None] * 3 for _ in range(tiles)]
    for start, rows, inner in row_tiles(ext):
        scale = rstd[start : start + rows, :]
        weighted, norms = [], []
        first = second = None
        for j in range(tiles):
            grad = dnormed[start : start + rows, lane(j)]
            norm = centred[start : start + rows, lane(j)]
            w = grad * params[base + 8 : base + 9, lane(j)]
            first = plus(first, w)
            second = plus(second, w * norm)
            weighted.append(w)
            norms.append(norm)
            if inner:
                sums[j][0] = plus(sums[j][0], fold(grad * norm))
                sums[j][1] = plus(sums[j][1], fold(grad))
        first = jnp.sum(first, axis=1, keepdims=True) * (1.0 / width)
        second = jnp.sum(second, axis=1, keepdims=True) * (1.0 / width)
        for j in range(tiles):
            value = scale * (weighted[j] - first - norms[j] * second)
            dconv[PAD + start : PAD + start + rows, lane(j)] = value
            if inner:
                sums[j][2] = plus(sums[j][2], fold(value))
    for j in range(tiles):
        small_c[8:9, lane(j)] = column_sum(sums[j][0])
        small_c[9:10, lane(j)] = column_sum(sums[j][1])
        small_c[7:8, lane(j)] = column_sum(sums[j][2])

    for j in range(tiles):
        taps = [params[base + k : base + k + 1, lane(j)] for k in range(kernel_taps)]
        sums = [None] * kernel_taps
        for start, rows, inner in row_tiles(ext):
            masks = masks_at(ids, start, rows)
            here = dconv[PAD + start : PAD + start + rows, lane(j)]
            total = dy[start : start + rows, lane(j)]
            for k in range(kernel_taps):
                mirror = kernel_taps - 1 - k
                at = PAD + start + mirror - reach
                piece = dconv[at : at + rows, lane(j)]
                total = total + taps[k] * (
                    piece if k == reach else jnp.where(masks[mirror], piece, 0.0)
                )
                if inner:
                    at = PAD + start + k - reach
                    piece = source[at : at + rows, lane(j)]
                    if k != reach:
                        piece = jnp.where(masks[k], piece, 0.0)
                    sums[k] = plus(sums[k], fold(piece * here))
            put(start, rows, inner, j, total)
        for k in range(kernel_taps):
            small_c[k : k + 1, lane(j)] = column_sum(sums[k])

    for r in range(4):
        sums = (bias_near if r < 2 else bias_far)[0:1, (r % 2) * quarter : (r % 2 + 1) * quarter]
        rows = [small_c[0:12, lanes_of(x, c, r)]]
        rows += [sums[:, lane(j)] for j in range(quarter // LANES)]
        rows += [jnp.zeros((16 - 12 - quarter // LANES, LANES), f32)]
        value = jnp.concatenate(rows, axis=0)
        if r % 2 == 0:
            side_keep[r // 2] = value
        else:
            hi = value.astype(bf16)
            side_give[r // 2, 0] = hi
            side_give[r // 2, 1] = (value - hi.astype(f32)).astype(bf16)


def start_rows(frames, flat, sems):
    rows, count, _ = frames.shape
    zeros = jnp.zeros((HALO, LANES), bf16)
    flat[0:HALO, :] = zeros
    flat[HALO + rows * count :, :] = zeros
    pairs = [(frames.at[r], flat.at[HALO + r * count : HALO + (r + 1) * count]) for r in range(rows)]
    return start_copies(pairs, sems)


def token_chunks(flat, own, outs):
    x, c, _ = place()
    ext = own + 2 * HALO
    for out, dx, dc in zip(outs, (1, 1, 0, 0), (0, 1, 0, 1)):
        at = pl.multiple_of(((x ^ dx) * 2 + (c ^ dc)) * own, HALO)
        out[0:ext, :] = flat[pl.ds(at, ext), :]


def pieces(source, target, count):
    rows = source.shape[0] // count
    cuts = [pl.ds(i * rows, rows) for i in range(count)]
    return [(source.at[cut], target.at[cut]) for cut in cuts]


def prepare_kernel(
    frames, chan_in, bias_in, up, down,
    give, here, beside, flat, chan, bias, up_held, down_held, sems, matrix_sems,
):
    x, c, dp = place()

    @pl.when(dp % 2 == 0)
    def start_up():
        start_copies(pieces(up.at[0], up_held, 4), matrix_sems)

    @pl.when(dp % 2 == 1)
    def start_down():
        start_copies(pieces(down.at[0], down_held, 4), matrix_sems)

    copies = start_rows(frames, flat, sems)
    smalls = start_copies([(chan_in, chan), (bias_in, bias)], sems.at[pl.ds(4, 2)])
    own = frames.shape[0] * frames.shape[1] // 4
    ext = own + 2 * HALO
    layers, parts = bias.shape[0], bias.shape[1] // LANES
    for copy in smalls:
        copy.wait()
    rows = [chan[:, l, :] for l in range(layers)]
    rows += [bias[l : l + 1, lane(j)] for l in range(layers) for j in range(parts)]
    rows += [jnp.zeros((PARAM_ROWS - (12 + parts) * layers, LANES), f32)]
    value = jnp.concatenate(rows, axis=0)
    hi = value.astype(bf16)
    lo = (value - hi.astype(f32)).astype(bf16)
    size = ext + 2 * PARAM_ROWS
    depth = give.shape[0] - 2 * size
    outs = (give.at[depth : depth + size], give.at[depth + size :], here, beside)
    for out in outs:
        out[ext : ext + PARAM_ROWS, :] = hi
        out[ext + PARAM_ROWS :, :] = lo
    for copy in copies:
        copy.wait()
    token_chunks(flat, own, outs)

    def put_matrix(value):
        for j in range(value.shape[1] // LANES):
            give[j * value.shape[0] : (j + 1) * value.shape[0], :] = value[:, lane(j)]

    @pl.when(dp % 2 == 0)
    def take_up():
        for i, (src, dst) in enumerate(pieces(up.at[0], up_held, 4)):
            pltpu.make_async_copy(src, dst, matrix_sems.at[i]).wait()
        put_matrix(up_held[...].astype(bf16))

    @pl.when(dp % 2 == 1)
    def take_down():
        for i, (src, dst) in enumerate(pieces(down.at[0], down_held, 4)):
            pltpu.make_async_copy(src, dst, matrix_sems.at[i]).wait()
        put_matrix(down_held[...].T.astype(bf16))


def split_kernel(got, matrix, near, far):
    rows, width = matrix.shape
    for j in range(width // LANES):
        matrix[:, lane(j)] = got[j * rows : (j + 1) * rows, :]
    at = rows * (width // LANES)
    size = near.shape[0]
    near[...] = got[at : at + size, :]
    far[...] = got[at + size :, :]


def rest_kernel(
    up, down, frames, segments, _,
    chosen, both0, both1, give0, give1, here, beside, ids, up0, down0, up1, down1,
    flat, columns, up_held, down_held, turned, sems, matrix_sems,
):
    x, c, dp = place()
    layers = up.shape[0]
    matrices = []
    for l in reversed(range(layers)):
        pairs = pieces(up.at[l], up_held.at[l], 4) + pieces(down.at[l], down_held.at[l], 4)
        matrices.append(start_copies(pairs, matrix_sems.at[pl.ds(8 * l, 8)]))
    copies = start_rows(frames, flat, sems)
    shard = up0.shape[0]
    mine = pl.ds(pl.multiple_of(dp * shard, shard), shard)
    for l, started, both, up_slice, down_slice in (
        (1, matrices[0], both1, up1, down1),
        (0, matrices[1], both0, up0, down0),
    ):
        for copy in started:
            copy.wait()
        both[0] = up_held[l].astype(bf16)
        up_slice[...] = up_held[l, mine, :]
        turned[...] = down_held[l].T
        both[1] = turned[...].astype(bf16)
        down_slice[...] = turned[mine, :]
    chosen[...] = both1[dp % 2]
    for copy in copies:
        copy.wait()
    token_chunks(flat, frames.shape[0] * frames.shape[1] // 4, (give0, give1, here, beside))

    rows, count = segments.shape
    tokens = rows * count
    edge = HALO + PAD
    none = jnp.full((edge, LANES), -1, jnp.int32)
    columns[0:edge, :] = none
    columns[edge + tokens :, :] = none
    for r in range(rows):
        row = jnp.broadcast_to(segments[r : r + 1, :] + 8 * r, (LANES, count))
        at = edge + r * count
        columns[at : at + count, :] = row.T
    at = pl.multiple_of((x * 2 + c) * (tokens // 4), HALO)
    ids[...] = columns[pl.ds(at, ids.shape[0]), :]


def first_kernel(
    ids, here, beside, near, far, own, core, _,
    centred, rstd, normed, active, slope, partial, source, params, bias, held, sems,
):
    ext = ids.shape[0] - 2 * PAD
    x, c, _d = place()
    packets = (here, beside, near, far)
    copies = start_copies(local_weights(own, core, held), sems)
    load_frames(x, c, packets, ext, source)
    load_params(x, c, packets, ext, params)
    load_bias(x, c, 0, 0, params, bias)
    forward_norm(0, source, ids, params, centred, rstd, normed, ext)
    for copy in copies:
        copy.wait()
    forward_half(bias, held, normed, active, slope, ext)
    for at in (0, ext // 2):
        rows = slice(at, at + ext // 2)
        partial[rows, :] = down_half(held, active, rows)


def second_kernel(
    source, params, normed, partial, w_near, w_near_core, w_far, w_far_core, _,
    next_source, active, slope, branch, bias, held, sems,
):
    ext = normed.shape[0]
    x, c, dp = place()
    copies = start_copies(far_weights(dp % 2, w_near, w_near_core, w_far, w_far_core, held), sems)
    load_bias(x, c, 0, 1, params, bias)
    clear_pads(next_source, ext)
    for copy in copies:
        copy.wait()
    forward_half(bias, held, normed, active, slope, ext)

    def put(at, rows, value):
        next_source[PAD + at : PAD + at + rows, :] = value

    finish_branch(0, source, params, held, active, partial, branch, ext, put)


def third_kernel(
    ids, source, params, own, core, _,
    centred, rstd, normed, active, slope, partial, bias, held, sems,
):
    ext = ids.shape[0] - 2 * PAD
    x, c, _d = place()
    copies = start_copies(local_weights(own, core, held), sems)
    load_bias(x, c, 1, 0, params, bias)
    forward_norm(1, source, ids, params, centred, rstd, normed, ext)
    for copy in copies:
        copy.wait()
    forward_half(bias, held, normed, active, slope, ext)
    for at in (0, ext // 2):
        rows = slice(at, at + ext // 2)
        partial[rows, :] = down_half(held, active, rows)


def fourth_kernel(
    cot_here, cot_beside, cot_near, cot_far, params, normed, active, slope, own, core,
    dy, low, low_t, normed_t, give0, give1, keep0, keep1, dnormed, bias_sums, hidden_low, held, sems,
):
    ext = dy.shape[0]
    x, c, dp = place()
    copies = start_copies(local_weights(own, core, held), sems)
    for r, ref in enumerate((cot_here, cot_beside, cot_near, cot_far)):
        dy[:, lanes_of(x, c, r)] = ref[...].astype(f32)
    branch_grad(1, dy, params, low, ext)
    low_t[...] = low[HALO : ext - HALO, :].T
    normed_t[...] = normed[HALO : ext - HALO, :].T
    for copy in copies:
        copy.wait()
    backward_half(
        dp, held, low, low_t, normed_t, active, slope, hidden_low, (give0, give1), (keep0, keep1), bias_sums, ext
    )
    for at in (0, ext // 2):
        rows = slice(at, at + ext // 2)
        dnormed[rows, :] = back_half(held, hidden_low, rows)


def fifth_kernel(
    source, params, normed, partial, low, low_t, normed_t, dnormed_near,
    w_near, w_near_core, w_far, w_far_core, _x, _y,
    branch, out, give0, give1, keep0, keep1, dnormed, bias_sums, bias, active, slope, hidden_low, held, sems,
):
    ext = normed.shape[0]
    x, c, dp = place()
    copies = start_copies(far_weights(dp % 2, w_near, w_near_core, w_far, w_far_core, held), sems)
    load_bias(x, c, 1, 1, params, bias)
    for copy in copies:
        copy.wait()
    forward_half(bias, held, normed, active, slope, ext)
    backward_half(
        dp, held, low, low_t, normed_t, active, slope, hidden_low, (give0, give1), (keep0, keep1), bias_sums, ext
    )

    def put(at, rows, value):
        if at == 0:
            out[0 : rows - HALO, :] = value[HALO:].astype(bf16)
        else:
            out[at - HALO :, :] = value[: rows - HALO].astype(bf16)

    finish_branch(1, source, params, held, active, partial, branch, ext, put)
    for at in (0, ext // 2):
        rows = slice(at, at + ext // 2)
        dnormed[rows, :] = dnormed_near[rows, :] + back_half(held, hidden_low, rows)


def sixth_kernel(
    ids, source, params, centred, rstd, branch, dy, dnormed, bias_near, bias_far, _,
    grad_source, side_give, side_keep, dconv, small_c,
):
    ext = dy.shape[0]
    x, c, _d = place()

    def put(start, rows, inner, j, value):
        grad_source[start : start + rows, lane(j)] = value

    backward_norm(
        1, x, c, dy, source, ids, params, centred, rstd, branch, dnormed, dconv, small_c,
        bias_near, bias_far, side_give, side_keep, put, ext,
    )


def seventh_kernel(
    dy, params, normed, active_near, slope_near, active_far, slope_far,
    own, core, w_near, w_near_core, w_far, w_far_core,
    hidden_near, hidden_far, give_near0, give_near1, give_far0, give_far1,
    keep_near0, keep_near1, keep_far0, keep_far1, bias_near, bias_far,
    low, low_t, normed_t, held_near, held_far, sems,
):
    ext = dy.shape[0]
    _x, _c, dp = place()
    pairs = local_weights(own, core, held_near)
    pairs += far_weights(dp % 2, w_near, w_near_core, w_far, w_far_core, held_far)
    copies = start_copies(pairs, sems)
    branch_grad(0, dy, params, low, ext)
    low_t[...] = low[HALO : ext - HALO, :].T
    normed_t[...] = normed[HALO : ext - HALO, :].T
    for copy in copies:
        copy.wait()
    backward_half(
        dp, held_near, low, low_t, normed_t, active_near, slope_near, hidden_near,
        (give_near0, give_near1), (keep_near0, keep_near1), bias_near, ext,
    )
    backward_half(
        dp, held_far, low, low_t, normed_t, active_far, slope_far, hidden_far,
        (give_far0, give_far1), (keep_far0, keep_far1), bias_far, ext,
    )


def eighth_kernel(
    ids, source, params, centred, rstd, branch, dy, hidden_near, hidden_far, bias_near, bias_far, first_out,
    own, core, w_near, w_near_core, w_far, w_far_core, _,
    out_give0, out_give1, out_keep0, out_keep1, side_give, side_keep,
    dnormed, dconv, small_c, out, held_near, held_far, sems,
):
    ext = dy.shape[0]
    x, c, dp = place()
    pairs = local_weights(own, core, held_near)
    pairs += far_weights(dp % 2, w_near, w_near_core, w_far, w_far_core, held_far)
    for copy in start_copies(pairs, sems):
        copy.wait()
    for at in (0, ext // 2):
        rows = slice(at, at + ext // 2)
        dnormed[rows, :] = back_half(held_near, hidden_near, rows) + back_half(held_far, hidden_far, rows)

    def put(start, rows, inner, j, value):
        if inner:
            out[start - HALO : start - HALO + rows, lane(j)] = value.astype(bf16)

    backward_norm(
        0, x, c, dy, source, ids, params, centred, rstd, branch, dnormed, dconv, small_c,
        bias_near, bias_far, side_give, side_keep, put, ext,
    )
    for i, ref in enumerate((first_out, out)):
        for r, piece in enumerate((out_keep0, out_give0, out_keep1, out_give1)):
            piece[i] = ref[:, lanes_of(x, c, r)]


def adamw(param, first, second, grad):
    first = beta_first * first + (1.0 - beta_first) * grad
    second = beta_second * second + (1.0 - beta_second) * grad * grad
    first_hat = first * (1.0 / (1.0 - beta_first**adam_step))
    second_hat = second * (1.0 / (1.0 - beta_second**adam_step))
    update = first_hat / (jnp.sqrt(second_hat) + adam_eps) + decay_rate * param
    return update, first, second


def to_packet(packet, at, value):
    packet[at : at + value.shape[0], :] = value.astype(bf16)


def side_to_packet(packet, value):
    rows = value.shape[0]
    at = packet.shape[0] - 2 * rows
    hi = value.astype(bf16)
    lo = (value - hi.astype(f32)).astype(bf16)
    packet[at : at + rows, :] = hi
    packet[at + rows :, :] = lo
    return hi.astype(f32) + lo.astype(f32)


def side_of(packet):
    at = packet.shape[0] - 64
    return packet[at : at + 32, :].astype(f32) + packet[at + 32 :, :].astype(f32)


def core_sum_kernel(got_near0, got_near1, got_far0, got_far1, keep_near0, keep_near1, keep_far0, keep_far1, *refs):
    to_x, to_y, up, down = refs[-4:]
    blocks, size, _ = got_near0.shape
    for d in range(blocks):
        up[d] = keep_near0[d] + got_near0[d].astype(f32)
        to_packet(to_x, d * size, keep_far0[d] + got_far0[d].astype(f32))
        for i, (got, keep) in enumerate(((got_near1, keep_near1), (got_far1, keep_far1))):
            value = keep[d] + got[d].astype(f32)
            if d % 2:
                to_packet(to_y, (i * (blocks // 2) + d // 2) * size, value)
            else:
                down[i, d // 2] = value


def cross_sum_kernel(from_x, from_y, up, down, got_side, keep_side, *refs):
    to_y, to_x, up_out, down_out, side_out = refs[-5:]
    blocks, size, _ = up.shape
    for d in range(blocks):
        value = up[d] + from_x[d * size : (d + 1) * size, :].astype(f32)
        if d % 2:
            to_packet(to_y, (d // 2) * size, value)
        else:
            up_out[d // 2] = value
    for d in range(blocks // 2):
        for i in range(2):
            at = (i * (blocks // 2) + d) * size
            value = down[i, d] + from_y[at : at + size, :].astype(f32)
            if i:
                to_packet(to_x, d * size, value)
            else:
                down_out[d] = value
    side = [keep_side[i] + (got_side[i, 0].astype(f32) + got_side[i, 1].astype(f32)) for i in range(2)]
    side_out[...] = side_to_packet(to_y, jnp.concatenate(side, axis=0))


def plane_sum_kernel(from_y, from_x, up, down, side, *refs):
    packet, main, side_out = refs[-3:]
    blocks, size, _ = up.shape
    for m, (got, held) in enumerate(((from_y, up), (from_x, down))):
        for d in range(blocks):
            value = held[d] + got[d * size : (d + 1) * size, :].astype(f32)
            if d % 2:
                to_packet(packet, (m * (blocks // 2) + d // 2) * size, value)
            else:
                main[m, d // 2] = value
    side_out[...] = side_to_packet(packet, side[...] + side_of(from_y))


def line_sum_kernel(got, held, side, *refs):
    packet, main, side_out = refs[-3:]
    _, blocks, size, _ = held.shape
    for m in range(2):
        for d in range(blocks):
            at = (m * blocks + d) * size
            value = held[m, d] + got[at : at + size, :].astype(f32)
            if d % 2:
                to_packet(packet, (m * (blocks // 2) + d // 2) * size, value)
            else:
                main[m, d // 2] = value
    side_out[...] = side_to_packet(packet, side[...] + side_of(got))


def update_kernel(layer, got, held, side, up, down, m_up, v_up, m_down, v_down, *refs):
    sent, main, side_near, side_far = refs[-4:]
    size = held.shape[2]
    if sent.shape[0] > 2 * size:
        sent[2 * size :, :] = refs[0][...]
    rows = up.shape[0]
    for m in range(2):
        main[m] = held[m, 0] + got[m * size : (m + 1) * size, :].astype(f32)
    total = side[...] + side_of(got)
    side_near[...] = total[0:16]
    side_far[...] = total[16:32]
    for m, (p, first, second) in enumerate(((up, m_up, v_up), (down, m_down, v_down))):
        for j in range(size // rows):
            cols, at = lane(j), j * rows
            u, _, _ = adamw(
                p[:, cols], first[layer, :, cols], second[layer, :, cols], main[m, at : at + rows]
            )
            sent[m * size + at : m * size + at + rows, :] = u.astype(bf16)


def adam_kernel(
    main0, main1, side0, side1, got0, got1, chan, bias,
    m_chan, v_chan, m_up, v_up, m_bias, v_bias, m_down, v_down,
    u_chan, u_bias, f_chan, s_chan, f_up, s_up, f_bias, s_bias, f_down, s_down,
):
    rows = m_up.shape[1]
    for l, (main, side, got) in enumerate(((main0, side0, got0), (main1, side1, got1))):
        g = side[...] + got[...]
        u_chan[:, l, :], f_chan[:, l, :], s_chan[:, l, :] = adamw(
            chan[:, l, :], m_chan[:, l, :], v_chan[:, l, :], g[0:12]
        )
        for j in range(main.shape[1] // rows):
            cols, at = lane(j), j * rows
            row = slice(l, l + 1)
            u_bias[row, cols], f_bias[row, cols], s_bias[row, cols] = adamw(
                bias[row, cols], m_bias[row, cols], v_bias[row, cols], g[12 + j : 13 + j]
            )
            _, f_up[l, :, cols], s_up[l, :, cols] = adamw(
                0.0, m_up[l, :, cols], v_up[l, :, cols], main[0, at : at + rows]
            )
            _, f_down[l, :, cols], s_down[l, :, cols] = adamw(
                0.0, m_down[l, :, cols], v_down[l, :, cols], main[1, at : at + rows]
            )


def ring_order(n_dp):
    return list(range(0, n_dp, 2)) + list(range(n_dp - 1, 0, -2))


def spread_kernel(layers, n_dp, parts, *refs):
    blocks = refs[: n_dp + 1]
    up_out, down_out, up, held, down, sems = refs[-6:]
    dp = lax.axis_index("dp")
    half = n_dp // 2
    spot = jnp.where(dp % 2 == 0, dp // 2, n_dp - 1 - dp // 2)

    def owner(distance):
        at = lax.rem(spot + distance + n_dp, n_dp)
        return jnp.where(at < half, 2 * at, 2 * (n_dp - 1 - at) + 1)

    distances = [0]
    for step in range(1, half):
        distances += [-step, step]
    rows = up.shape[1] // n_dp
    size = parts * rows
    copies = []
    for l in range(layers):
        start = 2 * size * l
        halves = [(d, ref, start, ref, start + size) for d, ref in zip(distances, blocks)]
        far = blocks[-2] if l == 0 else blocks[-1]
        halves.append((half, far, 0, far, size))
        for distance, first, first_at, second, second_at in halves:
            at = pl.ds(pl.multiple_of(owner(distance) * rows, rows), rows)
            for j in range(parts):
                start = first_at + j * rows
                up[l, at, lane(j)] = first[start : start + rows, :].astype(f32)
                start = second_at + j * rows
                held[at, lane(j)] = second[start : start + rows, :].astype(f32)
        copy = pltpu.make_async_copy(up.at[l], up_out.at[l], sems.at[2 * l])
        copy.start()
        copies.append(copy)
        for j in range(parts):
            down[l, lane(j), :] = held[:, lane(j)].T
        copy = pltpu.make_async_copy(down.at[l], down_out.at[l], sems.at[2 * l + 1])
        copy.start()
        copies.append(copy)
    for copy in copies:
        copy.wait()


def collect_kernel(own, core, near, far, out, grad):
    x, c, _ = place()
    rows = own.shape[1]
    for r, ref in enumerate((own, core, near, far)):
        at = pl.multiple_of(((x ^ (r // 2)) * 2 + (c ^ (r % 2))) * rows, HALO)
        out[pl.ds(at, rows), :] = ref[0]
        grad[pl.ds(at, rows), :] = ref[1]


VMEM = pl.BlockSpec(memory_space=pltpu.VMEM)
ANY = pl.BlockSpec(memory_space=pl.ANY)
HBM = pl.BlockSpec(memory_space=pltpu.HBM)


def call(kernel, outs, in_specs, scratch, name, limit=16, out_specs=None, aliases=None):
    return pl.pallas_call(
        kernel,
        out_shape=[jax.ShapeDtypeStruct(s, t) for s, t in outs],
        in_specs=in_specs,
        out_specs=out_specs or [VMEM] * len(outs),
        scratch_shapes=scratch,
        input_output_aliases=aliases or {},
        compiler_params=pltpu.CompilerParams(vmem_limit_bytes=limit * 1024 * 1024),
        cost_estimate=pl.CostEstimate(flops=0, bytes_accessed=0, transcendentals=0),
        name=name,
    )


def on_device(
    n_dp, frames_in, segments, cotangent, channel_params, weight_up, bias_up, weight_down,
    momentum_channel, variance_channel, momentum_up, variance_up, momentum_bias, variance_bias,
    momentum_down, variance_down,
):
    rows, frames, part = frames_in.shape
    layers, width, quarter = weight_up.shape
    chip_hidden = 2 * quarter
    tokens = rows * frames
    own = tokens // 4
    ext = own + 2 * HALO
    shard = width // n_dp
    parts = quarter // LANES

    def core_swap(v):
        return lax.ppermute(v, "chan", xor_perm(4, 1))

    def x_swap(v):
        return lax.ppermute(v, "chan", xor_perm(4, 2))

    def dp_swap(v, bit):
        return lax.ppermute(v, "dp", xor_perm(n_dp, bit))

    def after(value, *others):
        return lax.optimization_barrier((value, *others))[0]

    sems = pltpu.SemaphoreType.DMA((8,))
    width_sems = pltpu.SemaphoreType.DMA((16,))
    chan, m_chan, v_chan = [
        jnp.swapaxes(v, 0, 1) for v in (channel_params, momentum_channel, variance_channel)
    ]
    up_held = pltpu.VMEM((width, quarter), f32)
    down_held = pltpu.VMEM((quarter, width), f32)
    matrix = ((width, quarter), bf16)

    def in_hbm(*arrays):
        return [pltpu.with_memory_space_constraint(v, pltpu.HBM) for v in arrays]

    packet = ((ext + 2 * PARAM_ROWS, LANES), bf16)
    flat = pltpu.VMEM((tokens + 2 * HALO, LANES), bf16)
    depth = width * parts
    both_packets = ((depth + 2 * packet[0][0], LANES), bf16)
    give, here, beside = call(
        prepare_kernel, [both_packets, packet, packet], [HBM] * 5,
        [flat, pltpu.VMEM(chan.shape, f32), pltpu.VMEM(bias_up.shape, f32), up_held, down_held, sems, sems],
        "prepare",
    )(*in_hbm(frames_in, chan, bias_up, weight_up, weight_down))
    got_beside = core_swap(beside)
    near0, got_near, got_far = call(split_kernel, [matrix, packet, packet], [VMEM], [], "split")(x_swap(give))
    packets = [here, got_beside, got_near, core_swap(got_far)]
    cot_packet = ((ext, LANES), bf16)
    slice_shape = ((shard, quarter), f32)
    pair = ((2, width, quarter), bf16)
    chosen1, both0, both1, give0, give1, here, beside, ids, *slices = call(
        rest_kernel,
        [matrix, pair, pair] + [cot_packet] * 4 + [((ext + 2 * PAD, LANES), jnp.int32)] + [slice_shape] * 4,
        [HBM] * 3 + [VMEM, ANY],
        [flat, pltpu.VMEM((tokens + 2 * HALO + 2 * PAD, LANES), jnp.int32)]
        + [pltpu.VMEM(weight_up.shape, f32), pltpu.VMEM(weight_down.shape, f32), up_held, sems, width_sems],
        "rest", 24,
    )(*in_hbm(weight_up, weight_down, cotangent), segments, got_beside)
    near1 = x_swap(chosen1)
    slices0, slices1 = slices[:2], slices[2:]
    local0, local1 = [both0, core_swap(both0)], [both1, core_swap(both1)]
    cots = [here, core_swap(beside)]
    cots += [x_swap(after(give0, near0)), core_swap(x_swap(after(give1, near0)))]

    wide = (ext, width)
    padded = (ext + 2 * PAD, width)
    deep = (ext, chip_hidden)
    held = pltpu.VMEM((2, width, chip_hidden), bf16)
    bias = pltpu.VMEM((1, chip_hidden), f32)
    sums = ((1, chip_hidden), f32)
    params_shape = ((PARAM_ROWS, width), f32)
    turned = ((width, own), bf16)
    norm_shapes = [(wide, f32), ((ext, LANES), f32), (wide, bf16)]
    half_shapes = [(deep, bf16), (deep, f32), (wide, f32)]
    size = parts * shard
    grads = [((n_dp, size, LANES), bf16)] * 2 + [((n_dp, size, LANES), f32)] * 2
    side_shapes = [((2, 2, 16, LANES), bf16), ((2, 16, LANES), f32)]
    norm_scratch = [pltpu.VMEM(padded, f32), pltpu.VMEM((16, width), f32)]

    def buffers(shapes):
        return [pltpu.VMEM(s, t) for s, t in shapes]

    first = call(
        first_kernel, norm_shapes + half_shapes + [(padded, f32), params_shape],
        [VMEM] * 5 + [ANY] * 3, [bias, held, sems], "layer0_near", 24,
    )
    centred0, rstd0, normed0, active00, slope00, partial0, source0, params = first(
        ids, *packets, *local0, ids
    )
    far0 = dp_swap(near0, 1)
    far1 = dp_swap(near1, 1)
    away0 = [near0, core_swap(near0), far0, core_swap(far0)]
    second = call(
        second_kernel, [(padded, f32)] + half_shapes, [VMEM] * 4 + [ANY] * 5,
        [bias, held, sems], "layer0_far", 24,
    )
    source1, active01, slope01, branch0 = second(source0, params, normed0, partial0, *away0, near1)
    third = call(
        third_kernel, norm_shapes + half_shapes, [VMEM] * 3 + [ANY] * 3,
        [bias, held, sems], "layer1_near", 24,
    )
    centred1, rstd1, normed1, active10, slope10, partial1 = third(ids, source1, params, *local1, cots[2])
    fourth = call(
        fourth_kernel, [(wide, f32), (wide, bf16), turned, turned] + grads + [(wide, f32), sums],
        [VMEM] * 8 + [ANY] * 2, [pltpu.VMEM(deep, bf16), held, sems], "layer1_near_back", 24,
    )
    dy1, low1, low_t1, normed_t1, give_up, give_down, *keep10, dnormed1, bias10 = fourth(
        *cots, params, normed1, active10, slope10, *local1
    )
    got10 = [core_swap(give_up), core_swap(give_down)]
    away1 = [near1, core_swap(near1), far1, core_swap(after(far1, dnormed1))]
    fifth = call(
        fifth_kernel, [(wide, f32), ((own, width), bf16)] + grads + [(wide, f32), sums],
        [VMEM] * 8 + [ANY] * 6,
        [bias] + buffers(half_shapes[:2]) + [pltpu.VMEM(deep, bf16), held, sems], "layer1_far", 28,
    )
    branch1, first_out, give_up, give_down, *keep11, dnormed1, bias11 = fifth(
        source1, params, normed1, partial1, low1, low_t1, normed_t1, dnormed1, *away1, *got10
    )
    got11 = [core_swap(give_up), core_swap(give_down)]

    half = n_dp // 2
    piece = (size, LANES)
    side_shape = ((32, LANES), f32)

    def packet_of(blocks, side):
        return ((blocks * size + (64 if side else 0), LANES), bf16)

    def combine(kernel, outs, args, before, name):
        specs = [VMEM] * len(args) + [ANY] * len(before)
        return call(kernel, outs, specs, [], name)(*args, *before)

    def core_step(got_near, got_far, keep_near, keep_far):
        outs = [packet_of(n_dp, False), packet_of(n_dp, False), ((n_dp,) + piece, f32)]
        outs += [((2, half) + piece, f32)]
        return combine(core_sum_kernel, outs, [*got_near, *got_far, *keep_near, *keep_far], [], "core_sum")

    def cross_step(to_x, to_y, up, down, side_give, side_keep, before):
        outs = [packet_of(half, True), packet_of(half, False)]
        outs += [((half,) + piece, f32), ((half,) + piece, f32), side_shape]
        args = [x_swap(to_x), dp_swap(to_y, 1), up, down, core_swap(side_give), side_keep]
        return combine(cross_sum_kernel, outs, args, before, "cross_sum")

    def plane_step(to_y, to_x, up, down, side, before):
        outs = [packet_of(half, True), ((2, half // 2) + piece, f32), side_shape]
        args = [dp_swap(to_y, 1), x_swap(to_x), up, down, side]
        return combine(plane_sum_kernel, outs, args, before, "plane_sum")

    def line_step(packet, main, side, bit, before):
        left = main.shape[1] // 2
        outs = [packet_of(2 * left, True), ((2, left) + piece, f32), side_shape]
        return combine(line_sum_kernel, outs, [dp_swap(packet, bit), main, side], before, "line_sum")

    def line_steps(state, before):
        bit = 2
        while bit < half:
            state = line_step(*state, bit, before)
            bit *= 2
        return state

    down_moments = [jnp.swapaxes(v, 1, 2) for v in (momentum_down, variance_down)]

    def update_step(layer, packet, main, side, slices, others, before):
        outs = [packet_of(2 + 2 * len(others), False), ((2,) + piece, f32), ((16, LANES), f32), ((16, LANES), f32)]
        args = [dp_swap(packet, half), main, side, *slices, momentum_up, variance_up, *down_moments]
        args += others
        return combine(functools.partial(update_kernel, layer), outs, args, before, "update")

    order = ring_order(n_dp)
    ahead = [(order[i], order[(i + 1) % n_dp]) for i in range(n_dp)]
    back = [(b, a) for a, b in ahead]

    def ring_step(right, left):
        return lax.ppermute(right, "dp", ahead), lax.ppermute(left, "dp", back)

    def ring_end(right, left):
        cut = right.shape[0] // 2
        return lax.ppermute(right[:cut], "dp", ahead), lax.ppermute(left[cut:], "dp", back)

    def blocks_of(ring):
        return [ring[0][0]] + [v for pair in ring[1:] for v in pair]

    crossing1 = core_step(got10, got11, keep10, keep11)
    sixth = call(
        sixth_kernel, [(wide, f32)] + side_shapes, [VMEM] * 10 + [ANY], norm_scratch, "layer1_norm_back", 24
    )
    grad1, *sides1 = sixth(
        ids, source1, params, centred1, rstd1, branch1, dy1, dnormed1, bias10, bias11, crossing1[0]
    )
    seventh = call(
        seventh_kernel, [(deep, bf16)] * 2 + [grads[0]] * 4 + [grads[2]] * 4 + [sums] * 2,
        [VMEM] * 7 + [ANY] * 6, buffers([(wide, bf16), turned, turned]) + [held, held, sems],
        "layer0_back", 28,
    )
    hidden0, hidden1, *matrices0, bias00, bias01 = seventh(
        grad1, params, normed0, active00, slope00, active01, slope01, *local0, *away0
    )
    plane1 = cross_step(*crossing1, *sides1, [])
    eighth = call(
        eighth_kernel, [((2, own, LANES), bf16)] * 4 + side_shapes, [VMEM] * 12 + [ANY] * 7,
        buffers([(wide, f32)]) + norm_scratch + buffers([((own, width), bf16)]) + [held, held, sems],
        "layer0_norm_back", 28,
    )
    give_near, give_far, keep_near, keep_far, *sides0 = eighth(
        ids, source0, params, centred0, rstd0, branch0, grad1, hidden0, hidden1, bias00, bias01, first_out,
        *local0, *away0, bias01,
    )

    got0 = [core_swap(after(v, plane1[0], sides0[1])) for v in matrices0[:4]]
    crossing0 = core_step(got0[:2], got0[2:], matrices0[4:6], matrices0[6:])

    line1 = line_steps(plane_step(*plane1, []), [])
    plane0 = cross_step(*crossing0, *sides0, [line1[0]])
    sent1, main1, side1, side_far1 = update_step(1, *line1, slices1, [], [])
    line0 = line_steps(plane_step(*plane0, []), [])
    sent, main0, side0, side_far0 = update_step(0, *line0, slices0, [sent1], [])
    ring = [(sent, sent)]
    ring.append(ring_step(sent, sent))

    got1, got0 = x_swap(after(side_far1, sent)), x_swap(side_far0)
    got_near, got_far = core_swap(give_near), core_swap(give_far)
    tokens_near, tokens_far = x_swap(after(keep_far, sent)), x_swap(after(got_far, sent))
    layer_output, input_grad = call(
        collect_kernel, [((tokens, part), bf16)] * 2, [VMEM] * 4, [], "collect"
    )(keep_near, got_near, tokens_near, tokens_far)

    adam_outs = [
        (chan.shape, f32),
        (bias_up.shape, f32),
        (chan.shape, f32),
        (chan.shape, f32),
        (momentum_up.shape, f32),
        (momentum_up.shape, f32),
        (bias_up.shape, f32),
        (bias_up.shape, f32),
        (down_moments[0].shape, f32),
        (down_moments[0].shape, f32),
    ]
    (
        params_channel, params_bias, first_channel, second_channel,
        first_up, second_up, first_bias, second_bias, first_down, second_down,
    ) = call(adam_kernel, adam_outs, [VMEM] * 16, [], "adam")(
        main0, main1, side0, side1, got0, got1, chan, bias_up, m_chan, v_chan, momentum_up, variance_up,
        momentum_bias, variance_bias, *down_moments,
    )
    right, left = after(ring[1][0], got0, got1), after(ring[1][1], got0, got1)
    for step in range(2, half):
        if step == half - 1:
            right, left = after(right, first_up, tokens_far), after(left, first_up, tokens_far)
        right, left = ring_step(right, left)
        ring.append((right, left))
    right, left = after(right, layer_output), after(left, layer_output)
    ring.append(ring_end(right, left))
    whole = [(weight_up.shape, f32), (weight_down.shape, f32)]
    spread = call(
        functools.partial(spread_kernel, layers, n_dp, parts), whole, [VMEM] * (n_dp + 1),
        [pltpu.VMEM(weight_up.shape, f32), up_held, pltpu.VMEM(weight_down.shape, f32), sems],
        "spread", 16, [HBM, HBM],
    )
    params_up, params_down = spread(*blocks_of(ring))

    params_channel, first_channel, second_channel = [
        jnp.swapaxes(v, 0, 1) for v in (params_channel, first_channel, second_channel)
    ]
    first_down, second_down = jnp.swapaxes(first_down, 1, 2), jnp.swapaxes(second_down, 1, 2)

    layer_output, input_grad = [v.reshape(rows, frames, part) for v in (layer_output, input_grad)]
    return (
        layer_output,
        input_grad,
        params_channel,
        params_up,
        params_bias,
        params_down,
        first_channel,
        second_channel,
        first_up,
        second_up,
        first_bias,
        second_bias,
        first_down,
        second_down,
    )


def solution(mesh):
    return jax.shard_map(
        functools.partial(on_device, mesh.shape["dp"]),
        mesh=mesh,
        in_specs=(
            P("dp", None, "chan"),
            P("dp", None),
            P("dp", None, "chan"),
            P(None, None, "chan"),
            P(None, None, "chan"),
            P(None, "chan"),
            P(None, "chan", None),
            P(None, None, "chan"),
            P(None, None, "chan"),
            P(None, "dp", "chan"),
            P(None, "dp", "chan"),
            P(None, "chan"),
            P(None, "chan"),
            P(None, "chan", "dp"),
            P(None, "chan", "dp"),
        ),
        out_specs=(
            P("dp", None, "chan"),
            P("dp", None, "chan"),
            P(None, None, "chan"),
            P(None, None, "chan"),
            P(None, "chan"),
            P(None, "chan", None),
            P(None, None, "chan"),
            P(None, None, "chan"),
            P(None, "dp", "chan"),
            P(None, "dp", "chan"),
            P(None, "chan"),
            P(None, "chan"),
            P(None, "chan", "dp"),
            P(None, "chan", "dp"),
        ),
        check_vma=False,
    )
```

```python
import functools

import jax
import jax.numpy as jnp
from jax import lax
from jax.experimental import pallas as pl
from jax.experimental.pallas import tpu as pltpu
from jax.sharding import PartitionSpec as P

kernel_taps = 7
reach = kernel_taps // 2
norm_eps = 1e-06
beta_first = 0.8
beta_second = 0.9
adam_eps = 1e-08
decay_rate = 0.01
adam_step = 10.0

HALO = 16
PAD = 8
LANES = 128
PARAM_ROWS = 32
AXES = (("xyz", "yxz"), ("xzy", "yzx"))
LONG = 20_000_000_000
f32 = jnp.float32
bf16 = jnp.bfloat16


def xor_perm(size, bit):
    return [(i, i ^ bit) for i in range(size)]


def hi_lo(value):
    hi = lax.reduce_precision(value, 8, 7)
    return hi.astype(bf16), (value - hi).astype(bf16)


def place():
    me = lax.axis_index("chan")
    return me // 2, me % 2, lax.axis_index("dp")


def lanes_of(x, c, r):
    return pl.ds(pl.multiple_of(((x ^ (r // 2)) * 2 + (c ^ (r % 2))) * LANES, LANES), LANES)


def row_tiles(ext):
    own = ext - 2 * HALO
    tiles = [(0, HALO, False)]
    tiles += [(HALO + at, 32, True) for at in range(0, own, 32)]
    return tiles + [(HALO + own, HALO, False)]


def lane(j):
    return slice(j * LANES, (j + 1) * LANES)


def fold(value):
    return value.reshape(value.shape[0] // 8, 8, value.shape[1]).sum(axis=0)


def plus(total, value):
    return value if total is None else total + value


def column_sum(value):
    return jnp.sum(value, axis=0, keepdims=True)


def gelu_parts(h):
    tail = jnp.exp(-0.5 * h * h)
    d = 1.0 + (0.3275911 * 0.7071067811865476) * jnp.abs(h)
    t = pl.reciprocal(d, approx=True)
    t = t * (2.0 - d * t)
    poly = t * (
        0.127414796
        + t * (-0.142248368 + t * (0.7107068705 + t * (-0.7265760135 + t * 0.5307027145)))
    )
    low = poly * tail
    phi = jnp.where(h < 0.0, low, 1.0 - low)
    return h * phi, phi + h * tail * 0.3989422804014327


def load_frames(x, c, packets, ext, source):
    for r, ref in enumerate(packets):
        source[PAD : PAD + ext, lanes_of(x, c, r)] = ref[0:ext, :].astype(f32)
    clear_pads(source, ext)


def load_params(x, c, packets, ext, params):
    for r, ref in enumerate(packets):
        hi = ref[ext : ext + PARAM_ROWS, :].astype(f32)
        lo = ref[ext + PARAM_ROWS : ext + 2 * PARAM_ROWS, :].astype(f32)
        params[:, lanes_of(x, c, r)] = hi + lo


def clear_pads(ref, ext):
    zeros = jnp.zeros((PAD, ref.shape[1]), ref.dtype)
    ref[0:PAD, :] = zeros
    ref[PAD + ext : PAD + ext + PAD, :] = zeros


def load_bias(x, c, layer, chip, params, bias):
    width = bias.shape[1] // 2
    for r in range(2):
        rows = params[:, lanes_of(x, c, 2 * chip + r)]
        for j in range(width // LANES):
            k = 24 + layer * (width // LANES) + j
            bias[0:1, r * width + j * LANES : r * width + (j + 1) * LANES] = rows[k : k + 1]


def start_copies(pairs, sems):
    started = []
    for i, (src, dst) in enumerate(pairs):
        copy = pltpu.make_async_copy(src, dst, sems.at[i])
        copy.start()
        started.append(copy)
    return started


def hold_local(refs, held):
    width = refs[0].shape[-1]
    for i, ref in enumerate(refs):
        r, m = i // 2, i % 2
        held[m, :, r * width : (r + 1) * width] = ref[...]


def hold_far(y, near, near_core, far, far_core, held):
    width = near.shape[-1]
    for r, first, second in ((0, near, far), (1, near_core, far_core)):
        columns = slice(r * width, (r + 1) * width)
        held[y, :, columns] = first[...]
        held[1 - y, :, columns] = second[...]


def masks_at(ids, start, rows):
    here = ids[PAD + start : PAD + start + rows, :]
    masks = []
    for k in range(kernel_taps):
        at = PAD + start + k - reach
        masks.append(ids[at : at + rows, :] == here)
    return masks


def forward_norm(layer, source, ids, params, centred, rstd, normed, ext):
    width = source.shape[1]
    tiles = width // LANES
    base = layer * 12
    for start, rows, _ in row_tiles(ext):
        masks = masks_at(ids, start, rows)
        convs = []
        total = square = None
        for j in range(tiles):
            acc = params[base + 7 : base + 8, lane(j)]
            for k in range(kernel_taps):
                at = PAD + start + k - reach
                piece = source[at : at + rows, lane(j)]
                tap = params[base + k : base + k + 1, lane(j)]
                acc = acc + tap * (piece if k == reach else jnp.where(masks[k], piece, 0.0))
            convs.append(acc)
            total = plus(total, acc)
            square = plus(square, acc * acc)
        mean = jnp.sum(total, axis=1, keepdims=True) * (1.0 / width)
        var = jnp.sum(square, axis=1, keepdims=True) * (1.0 / width) - mean * mean
        scale = lax.rsqrt(var + norm_eps)
        rstd[start : start + rows, :] = jnp.broadcast_to(scale, (rows, LANES))
        for j in range(tiles):
            value = (convs[j] - mean) * scale
            centred[start : start + rows, lane(j)] = value
            gain = params[base + 8 : base + 9, lane(j)]
            shift = params[base + 9 : base + 10, lane(j)]
            normed[start : start + rows, lane(j)] = (value * gain + shift).astype(bf16)


def forward_half(bias, held, normed, active, slope, ext):
    quarter = held.shape[2] // 2
    half = ext // 2
    for r in range(2):
        cols = slice(r * quarter, (r + 1) * quarter)
        for at in (0, half):
            rows = slice(at, at + half)
            h = (
                jnp.dot(normed[rows, :], held[0, :, cols], preferred_element_type=f32)
                + bias[0:1, cols]
            )
            value, grad = gelu_parts(h)
            active[rows, cols] = value.astype(bf16)
            slope[rows, cols] = grad


def down_half(held, active, rows):
    return lax.dot_general(
        active[rows, :], held[1], (((1,), (1,)), ((), ())), preferred_element_type=f32
    )


def finish_branch(layer, source, params, held, active, partial, branch, ext, put):
    half = ext // 2
    base = layer * 12
    for at in (0, half):
        rows = slice(at, at + half)
        value = partial[rows, :] + down_half(held, active, rows) + params[base + 10 : base + 11, :]
        branch[rows, :] = value
        put(at, half, source[PAD + at : PAD + at + half, :] + params[base + 11 : base + 12, :] * value)


def branch_grad(layer, dy, params, low, ext):
    base = layer * 12
    for j in range(dy.shape[1] // LANES):
        scale = params[base + 11 : base + 12, lane(j)]
        for start, rows, _ in row_tiles(ext):
            low[start : start + rows, lane(j)] = (scale * dy[start : start + rows, lane(j)]).astype(bf16)


def put_grad(dp, out, parts, value):
    blocks, size, _ = out.shape
    rows = size // parts
    value = value.astype(out.dtype)
    for d in range(blocks):
        for j in range(parts):
            out[d ^ dp, j * rows : (j + 1) * rows] = value[d * rows : (d + 1) * rows, lane(j)]


def backward_half(dp, held, low, low_t, normed_t, active, slope, hidden_low, give, keep, bias_sums, ext):
    quarter = held.shape[2] // 2
    half = ext // 2
    inner = slice(HALO, ext - HALO)
    parts = quarter // LANES
    for r, out in ((0, keep), (1, give)):
        cols = slice(r * quarter, (r + 1) * quarter)
        sums = None
        for at in (0, half):
            rows = slice(at, at + half)
            grad = (
                jnp.dot(low[rows, :], held[1, :, cols], preferred_element_type=f32)
                * slope[rows, cols]
            )
            hidden_low[rows, cols] = grad.astype(bf16)
            sums = plus(sums, fold(grad[HALO:] if at == 0 else grad[: half - HALO]))
        bias_sums[0:1, cols] = column_sum(sums)
        put_grad(dp, out[1], parts, jnp.dot(low_t[...], active[inner, cols], preferred_element_type=f32))
        put_grad(
            dp, out[0], parts, jnp.dot(normed_t[...], hidden_low[inner, cols], preferred_element_type=f32)
        )


def back_half(held, hidden_low, rows):
    return lax.dot_general(
        hidden_low[rows, :], held[0], (((1,), (1,)), ((), ())), preferred_element_type=f32
    )


def backward_norm(
    layer, x, c, dy, source, ids, params, centred, rstd, branch, dnormed, dconv, small_c,
    bias_near, bias_far, side_give, side_keep, put, ext,
):
    width = source.shape[1]
    tiles = width // LANES
    quarter = bias_near.shape[1] // 2
    base = layer * 12
    small_c[...] = jnp.zeros_like(small_c)
    for j in range(tiles):
        scale = params[base + 11 : base + 12, lane(j)]
        sum_gamma = sum_bias = None
        for start, rows, inner in row_tiles(ext):
            if inner:
                grad = dy[start : start + rows, lane(j)]
                sum_gamma = plus(sum_gamma, fold(grad * branch[start : start + rows, lane(j)]))
                sum_bias = plus(sum_bias, fold(scale * grad))
        small_c[10:11, lane(j)] = column_sum(sum_bias)
        small_c[11:12, lane(j)] = column_sum(sum_gamma)

    clear_pads(dconv, ext)
    sums = [[None] * 3 for _ in range(tiles)]
    for start, rows, inner in row_tiles(ext):
        scale = rstd[start : start + rows, :]
        weighted, norms = [], []
        first = second = None
        for j in range(tiles):
            grad = dnormed[start : start + rows, lane(j)]
            norm = centred[start : start + rows, lane(j)]
            w = grad * params[base + 8 : base + 9, lane(j)]
            first = plus(first, w)
            second = plus(second, w * norm)
            weighted.append(w)
            norms.append(norm)
            if inner:
                sums[j][0] = plus(sums[j][0], fold(grad * norm))
                sums[j][1] = plus(sums[j][1], fold(grad))
        first = jnp.sum(first, axis=1, keepdims=True) * (1.0 / width)
        second = jnp.sum(second, axis=1, keepdims=True) * (1.0 / width)
        for j in range(tiles):
            value = scale * (weighted[j] - first - norms[j] * second)
            dconv[PAD + start : PAD + start + rows, lane(j)] = value
            if inner:
                sums[j][2] = plus(sums[j][2], fold(value))
    for j in range(tiles):
        small_c[8:9, lane(j)] = column_sum(sums[j][0])
        small_c[9:10, lane(j)] = column_sum(sums[j][1])
        small_c[7:8, lane(j)] = column_sum(sums[j][2])

    for j in range(tiles):
        taps = [params[base + k : base + k + 1, lane(j)] for k in range(kernel_taps)]
        sums = [None] * kernel_taps
        for start, rows, inner in row_tiles(ext):
            masks = masks_at(ids, start, rows)
            here = dconv[PAD + start : PAD + start + rows, lane(j)]
            total = dy[start : start + rows, lane(j)]
            for k in range(kernel_taps):
                mirror = kernel_taps - 1 - k
                at = PAD + start + mirror - reach
                piece = dconv[at : at + rows, lane(j)]
                total = total + taps[k] * (
                    piece if k == reach else jnp.where(masks[mirror], piece, 0.0)
                )
                if inner:
                    at = PAD + start + k - reach
                    piece = source[at : at + rows, lane(j)]
                    if k != reach:
                        piece = jnp.where(masks[k], piece, 0.0)
                    sums[k] = plus(sums[k], fold(piece * here))
            put(start, rows, inner, j, total)
        for k in range(kernel_taps):
            small_c[k : k + 1, lane(j)] = column_sum(sums[k])

    for r in range(4):
        sums = (bias_near if r < 2 else bias_far)[0:1, (r % 2) * quarter : (r % 2 + 1) * quarter]
        rows = [small_c[0:12, lanes_of(x, c, r)]]
        rows += [sums[:, lane(j)] for j in range(quarter // LANES)]
        rows += [jnp.zeros((16 - 12 - quarter // LANES, LANES), f32)]
        value = jnp.concatenate(rows, axis=0)
        if r % 2 == 0:
            side_keep[r // 2] = value
        else:
            hi = value.astype(bf16)
            side_give[r // 2, 0] = hi
            side_give[r // 2, 1] = (value - hi.astype(f32)).astype(bf16)


def start_rows(frames, flat, sems):
    rows, count, _ = frames.shape
    zeros = jnp.zeros((HALO, LANES), bf16)
    flat[0:HALO, :] = zeros
    flat[HALO + rows * count :, :] = zeros
    pairs = [(frames.at[r], flat.at[HALO + r * count : HALO + (r + 1) * count]) for r in range(rows)]
    return start_copies(pairs, sems)


def token_chunks(flat, own, outs):
    x, c, _ = place()
    ext = own + 2 * HALO
    for out, dx, dc in zip(outs, (1, 1, 0, 0), (0, 1, 0, 1)):
        at = pl.multiple_of(((x ^ dx) * 2 + (c ^ dc)) * own, HALO)
        out[0:ext, :] = flat[pl.ds(at, ext), :]


def pieces(source, target, count):
    rows = source.shape[0] // count
    cuts = [pl.ds(i * rows, rows) for i in range(count)]
    return [(source.at[cut], target.at[cut]) for cut in cuts]


def prepare_kernel(
    frames, chan_in, bias_in, up, down,
    give, here, beside, chosen, flat, chan, bias, up_held, down_held, sems, matrix_sems,
):
    x, c, dp = place()

    @pl.when(dp % 2 == 0)
    def start_up():
        start_copies(pieces(up.at[0], up_held, 4), matrix_sems)

    @pl.when(dp % 2 == 1)
    def start_down():
        start_copies(pieces(down.at[0], down_held, 4), matrix_sems)

    copies = start_rows(frames, flat, sems)
    smalls = start_copies([(chan_in, chan), (bias_in, bias)], sems.at[pl.ds(4, 2)])
    own = frames.shape[0] * frames.shape[1] // 4
    ext = own + 2 * HALO
    layers, parts = bias.shape[0], bias.shape[1] // LANES
    for copy in smalls:
        copy.wait()
    rows = [chan[:, l, :] for l in range(layers)]
    rows += [bias[l : l + 1, lane(j)] for l in range(layers) for j in range(parts)]
    rows += [jnp.zeros((PARAM_ROWS - (12 + parts) * layers, LANES), f32)]
    value = jnp.concatenate(rows, axis=0)
    hi = value.astype(bf16)
    lo = (value - hi.astype(f32)).astype(bf16)
    size = ext + 2 * PARAM_ROWS
    outs = (give.at[0:size], give.at[size:], here, beside)
    for out in outs:
        out[ext : ext + PARAM_ROWS, :] = hi
        out[ext + PARAM_ROWS :, :] = lo
    for copy in copies:
        copy.wait()
    token_chunks(flat, own, outs)

    @pl.when(dp % 2 == 0)
    def take_up():
        for i, (src, dst) in enumerate(pieces(up.at[0], up_held, 4)):
            pltpu.make_async_copy(src, dst, matrix_sems.at[i]).wait()
        chosen[...] = up_held[...].astype(bf16)

    @pl.when(dp % 2 == 1)
    def take_down():
        for i, (src, dst) in enumerate(pieces(down.at[0], down_held, 4)):
            pltpu.make_async_copy(src, dst, matrix_sems.at[i]).wait()
        chosen[...] = down_held[...].T.astype(bf16)


def rest_kernel(
    up, down, frames, segments, _,
    chosen, w00, w01, w10, w11, give, here, beside, ids, up0, down0, up1, down1,
    flat, columns, up_held, down_held, turned, sems, matrix_sems,
):
    x, c, dp = place()
    layers = up.shape[0]
    matrices = []
    for l in reversed(range(layers)):
        pairs = pieces(up.at[l], up_held.at[l], 4) + pieces(down.at[l], down_held.at[l], 4)
        matrices.append(start_copies(pairs, matrix_sems.at[pl.ds(8 * l, 8)]))
    copies = start_rows(frames, flat, sems)
    shard = up0.shape[0]
    mine = pl.ds(pl.multiple_of(dp * shard, shard), shard)
    for l, started, both, up_slice, down_slice in (
        (1, matrices[0], (w10, w11), up1, down1),
        (0, matrices[1], (w00, w01), up0, down0),
    ):
        for copy in started:
            copy.wait()
        both[0][...] = up_held[l].astype(bf16)
        up_slice[...] = up_held[l, mine, :]
        turned[...] = down_held[l].T
        both[1][...] = turned[...].astype(bf16)
        down_slice[...] = turned[mine, :]

    @pl.when(dp % 2 == 0)
    def choose_up():
        chosen[...] = w10[...]

    @pl.when(dp % 2 == 1)
    def choose_down():
        chosen[...] = w11[...]

    for copy in copies:
        copy.wait()
    ext = here.shape[0]
    token_chunks(flat, ext - 2 * HALO, (give.at[0:ext], give.at[ext:], here, beside))

    rows, count = segments.shape
    tokens = rows * count
    edge = HALO + PAD
    none = jnp.full((edge, LANES), -1, jnp.int32)
    columns[0:edge, :] = none
    columns[edge + tokens :, :] = none
    for r in range(rows):
        row = jnp.broadcast_to(segments[r : r + 1, :] + 8 * r, (LANES, count))
        at = edge + r * count
        columns[at : at + count, :] = row.T
    at = pl.multiple_of((x * 2 + c) * (tokens // 4), HALO)
    ids[...] = columns[pl.ds(at, ids.shape[0]), :]


def first_kernel(
    ids, here, beside, near, far, own_up, own_down, core_up, core_down, _,
    centred, rstd, normed, active, slope, partial, source, params, bias, held,
):
    ext = ids.shape[0] - 2 * PAD
    x, c, _d = place()
    packets = (here, beside, near.at[0 : here.shape[0]], far.at[here.shape[0] :])
    load_frames(x, c, packets, ext, source)
    load_params(x, c, packets, ext, params)
    load_bias(x, c, 0, 0, params, bias)
    forward_norm(0, source, ids, params, centred, rstd, normed, ext)
    hold_local((own_up, own_down, core_up, core_down), held)
    forward_half(bias, held, normed, active, slope, ext)
    for at in (0, ext // 2):
        rows = slice(at, at + ext // 2)
        partial[rows, :] = down_half(held, active, rows)


def second_kernel(
    source, params, normed, partial, w_near, w_near_core, w_far, w_far_core, _,
    next_source, active, slope, branch, bias, held,
):
    ext = normed.shape[0]
    x, c, dp = place()
    load_bias(x, c, 0, 1, params, bias)
    clear_pads(next_source, ext)
    hold_far(dp % 2, w_near, w_near_core, w_far, w_far_core, held)
    forward_half(bias, held, normed, active, slope, ext)

    def put(at, rows, value):
        next_source[PAD + at : PAD + at + rows, :] = value

    finish_branch(0, source, params, held, active, partial, branch, ext, put)


def third_kernel(
    ids, source, params, own_up, own_down, core_up, core_down, _,
    centred, rstd, normed, active, slope, partial, bias, held,
):
    ext = ids.shape[0] - 2 * PAD
    x, c, _d = place()
    load_bias(x, c, 1, 0, params, bias)
    forward_norm(1, source, ids, params, centred, rstd, normed, ext)
    hold_local((own_up, own_down, core_up, core_down), held)
    forward_half(bias, held, normed, active, slope, ext)
    for at in (0, ext // 2):
        rows = slice(at, at + ext // 2)
        partial[rows, :] = down_half(held, active, rows)


def fourth_kernel(
    cot_here, cot_beside, cot_near, cot_far, params, normed, active, slope, own_up, own_down, core_up, core_down,
    dy, low, low_t, normed_t, give, keep0, keep1, dnormed, bias_sums, hidden_low, held,
):
    ext = dy.shape[0]
    x, c, dp = place()
    refs = (cot_here, cot_beside, cot_near.at[0:ext], cot_far.at[ext:])
    for r, ref in enumerate(refs):
        dy[:, lanes_of(x, c, r)] = ref[...].astype(f32)
    branch_grad(1, dy, params, low, ext)
    low_t[...] = low[HALO : ext - HALO, :].T
    normed_t[...] = normed[HALO : ext - HALO, :].T
    hold_local((own_up, own_down, core_up, core_down), held)
    backward_half(
        dp, held, low, low_t, normed_t, active, slope, hidden_low, (give.at[0], give.at[1]), (keep0, keep1), bias_sums, ext
    )
    for at in (0, ext // 2):
        rows = slice(at, at + ext // 2)
        dnormed[rows, :] = back_half(held, hidden_low, rows)


def fifth_kernel(
    source, params, normed, partial, low, low_t, normed_t, dnormed_near,
    w_near, w_near_core, w_far, w_far_core,
    branch, out, give, keep0, keep1, dnormed, bias_sums, bias, active, slope, hidden_low, held,
):
    ext = normed.shape[0]
    x, c, dp = place()
    load_bias(x, c, 1, 1, params, bias)
    hold_far(dp % 2, w_near, w_near_core, w_far, w_far_core, held)
    forward_half(bias, held, normed, active, slope, ext)
    backward_half(
        dp, held, low, low_t, normed_t, active, slope, hidden_low, (give.at[0], give.at[1]), (keep0, keep1), bias_sums, ext
    )

    def put(at, rows, value):
        if at == 0:
            out[0 : rows - HALO, :] = value[HALO:].astype(bf16)
        else:
            out[at - HALO :, :] = value[: rows - HALO].astype(bf16)

    finish_branch(1, source, params, held, active, partial, branch, ext, put)
    for at in (0, ext // 2):
        rows = slice(at, at + ext // 2)
        dnormed[rows, :] = dnormed_near[rows, :] + back_half(held, hidden_low, rows)


def sixth_kernel(
    ids, source, params, centred, rstd, branch, dy, dnormed, bias_near, bias_far, _,
    grad_source, side_give, side_keep, dconv, small_c,
):
    ext = dy.shape[0]
    x, c, _d = place()

    def put(start, rows, inner, j, value):
        grad_source[start : start + rows, lane(j)] = value

    backward_norm(
        1, x, c, dy, source, ids, params, centred, rstd, branch, dnormed, dconv, small_c,
        bias_near, bias_far, side_give, side_keep, put, ext,
    )


def seventh_kernel(
    dy, params, normed, active_near, slope_near, active_far, slope_far,
    own_up, own_down, core_up, core_down, w_near, w_near_core, w_far, w_far_core,
    hidden_near, hidden_far, give,
    keep_near0, keep_near1, keep_far0, keep_far1, bias_near, bias_far,
    low, low_t, normed_t, held_near, held_far,
):
    ext = dy.shape[0]
    _x, _c, dp = place()
    branch_grad(0, dy, params, low, ext)
    low_t[...] = low[HALO : ext - HALO, :].T
    normed_t[...] = normed[HALO : ext - HALO, :].T
    hold_local((own_up, own_down, core_up, core_down), held_near)
    hold_far(dp % 2, w_near, w_near_core, w_far, w_far_core, held_far)
    backward_half(
        dp, held_near, low, low_t, normed_t, active_near, slope_near, hidden_near,
        (give.at[0], give.at[1]), (keep_near0, keep_near1), bias_near, ext,
    )
    backward_half(
        dp, held_far, low, low_t, normed_t, active_far, slope_far, hidden_far,
        (give.at[2], give.at[3]), (keep_far0, keep_far1), bias_far, ext,
    )


def eighth_kernel(
    ids, source, params, centred, rstd, branch, dy, hidden_near, hidden_far, bias_near, bias_far, first_out,
    own_up, own_down, core_up, core_down, w_near, w_near_core, w_far, w_far_core, _,
    out_give0, out_give1, out_keep0, out_keep1, side_give, side_keep,
    dnormed, dconv, small_c, out, held_near, held_far,
):
    ext = dy.shape[0]
    x, c, dp = place()
    hold_local((own_up, own_down, core_up, core_down), held_near)
    hold_far(dp % 2, w_near, w_near_core, w_far, w_far_core, held_far)
    for at in (0, ext // 2):
        rows = slice(at, at + ext // 2)
        dnormed[rows, :] = back_half(held_near, hidden_near, rows) + back_half(held_far, hidden_far, rows)

    def put(start, rows, inner, j, value):
        if inner:
            out[start - HALO : start - HALO + rows, lane(j)] = value.astype(bf16)

    backward_norm(
        0, x, c, dy, source, ids, params, centred, rstd, branch, dnormed, dconv, small_c,
        bias_near, bias_far, side_give, side_keep, put, ext,
    )
    for i, ref in enumerate((first_out, out)):
        for r, piece in enumerate((out_keep0, out_give0, out_keep1, out_give1)):
            piece[i] = ref[:, lanes_of(x, c, r)]


def adamw(param, first, second, grad):
    first = beta_first * first + (1.0 - beta_first) * grad
    second = beta_second * second + (1.0 - beta_second) * grad * grad
    first_hat = first * (1.0 / (1.0 - beta_first**adam_step))
    second_hat = second * (1.0 / (1.0 - beta_second**adam_step))
    update = first_hat / (jnp.sqrt(second_hat) + adam_eps) + decay_rate * param
    return update, first, second


def halving_plan(n_dp, axes):
    bits = {"x": lambda k: k[0], "y": lambda k: k[1] & 1, "z": lambda k: (k[1] >> 1) & 1}
    keys = [[(i, d) for i in range(2) for d in range(n_dp)] for _ in axes]
    plan = []
    for now in zip(*axes):
        give = [[k for k in keys[m] if bits[axis](k)] for m, axis in enumerate(now)]
        keep = [[k for k in keys[m] if not bits[axis](k)] for m, axis in enumerate(now)]
        groups = [(0, 1)] if now[0] == now[1] else [(0,), (1,)]
        plan.append((give, keep, groups))
        keys = keep
    return plan


def side_to_packet(packet, value):
    rows = value.shape[0]
    at = packet.shape[0] - 2 * rows
    hi = value.astype(bf16)
    lo = (value - hi.astype(f32)).astype(bf16)
    packet[at : at + rows, :] = hi
    packet[at + rows :, :] = lo
    return hi.astype(f32) + lo.astype(f32)


def side_of(packet):
    at = packet.shape[0] - 64
    return packet[at : at + 32, :].astype(f32) + packet[at + 32 :, :].astype(f32)


def put_blocks(step, packets, helds, value_of):
    give, keep, groups = step
    rows = helds[0].shape[1]
    for packet, group in zip(packets, groups):
        at = 0
        for m in group:
            for key in give[m]:
                packet[at : at + rows, :] = value_of(m, key).astype(bf16)
                at += rows
    for m, held in enumerate(helds):
        for at, key in enumerate(keep[m]):
            held[at] = value_of(m, key)


def got_blocks(step, gots, helds):
    _, keep, groups = step
    rows = helds[0].shape[1]
    places = {}
    for got, group in zip(gots, groups):
        at = 0
        for m in group:
            for spot, key in enumerate(keep[m]):
                places[m, key] = (got, at, spot)
                at += rows

    def value_of(m, key):
        got, at, spot = places[m, key]
        return helds[m][spot] + got[at : at + rows, :].astype(f32)

    return value_of


def marker_kernel(*refs):
    refs[-1][...] = jnp.zeros_like(refs[-1])


def core_sum_kernel(plan, count, *refs):
    got = [ref.at[i] for ref in refs[:count] for i in range(ref.shape[0])]
    keep = refs[count : count + 4]
    packets, helds = refs[-2 - len(plan[0][2]) : -2], refs[-2:]

    def value_of(m, key):
        i, d = key
        return keep[2 * i + m][d] + got[2 * i + m][d].astype(f32)

    put_blocks(plan[0], packets, helds, value_of)


def step_sum_kernel(plan, step, *refs):
    count, outs = len(plan[step - 1][2]), len(plan[step][2])
    gots, helds, rest = refs[:count], refs[count : count + 2], refs[count + 2 :]
    packets, helds_out, side_out = refs[-3 - outs : -3], refs[-3:-1], refs[-1]
    put_blocks(plan[step], packets, helds_out, got_blocks(plan[step - 1], gots, helds))
    if step == 1:
        got_side, keep_side = rest[:2]
        side = jnp.concatenate(
            [keep_side[i] + (got_side[i, 0].astype(f32) + got_side[i, 1].astype(f32)) for i in range(2)], axis=0
        )
    else:
        side = rest[0][...] + side_of(gots[0])
    side_out[...] = side_to_packet(packets[0], side)


def line_start_kernel(plan, *refs):
    count = len(plan[-1][2])
    gots, helds, side = refs[:count], refs[count : count + 2], refs[count + 2]
    packet, out, side_out = refs[-3:]
    value_of = got_blocks(plan[-1], gots, helds)
    rows = helds[0].shape[1]
    keep = plan[-1][1]
    half = len(keep[0]) // 2
    for m in range(2):
        for at, key in enumerate(keep[m]):
            value = value_of(m, key)
            if at % 2:
                start = (m * half + at // 2) * rows
                packet[start : start + rows, :] = value.astype(bf16)
            else:
                out[m * half + at // 2] = value
    side_out[...] = side_to_packet(packet, side[...] + side_of(gots[0]))


def line_sum_kernel(got, held, side, *refs):
    packet, out, side_out = refs[-3:]
    count, rows, _ = held.shape
    for at in range(count):
        value = held[at] + got[at * rows : (at + 1) * rows, :].astype(f32)
        if at % 2:
            packet[(at // 2) * rows : (at // 2 + 1) * rows, :] = value.astype(bf16)
        else:
            out[at // 2] = value
    side_out[...] = side_to_packet(packet, side[...] + side_of(got))


def update_kernel(layer, got, held, side, up, down, m_up, v_up, m_down, v_down, *refs):
    sent, main, side_near, side_far = refs[-4:]
    size = main.shape[1]
    if sent.shape[0] > 2 * size:
        sent[2 * size :, :] = refs[0][...]
    rows = up.shape[0]
    for m in range(2):
        main[m] = held[m] + got[m * size : (m + 1) * size, :].astype(f32)
    total = side[...] + side_of(got)
    side_near[...] = total[0:16]
    hi = total[16:32].astype(bf16)
    side_far[0:16, :] = hi
    side_far[16:32, :] = (total[16:32] - hi.astype(f32)).astype(bf16)
    for m, (p, first, second) in enumerate(((up, m_up, v_up), (down, m_down, v_down))):
        for j in range(size // rows):
            cols, at = lane(j), j * rows
            u, _, _ = adamw(
                p[:, cols], first[layer, :, cols], second[layer, :, cols], main[m, at : at + rows]
            )
            sent[m * size + at : m * size + at + rows, :] = u.astype(bf16)


def adam_kernel(
    main0, main1, side0, side1, far, chan, bias,
    m_chan, v_chan, m_up, v_up, m_bias, v_bias, m_down, v_down,
    u_chan, u_bias, f_chan, s_chan, f_up, s_up, f_bias, s_bias, f_down, s_down,
):
    rows = m_up.shape[1]
    base = far.shape[0] - 64
    for l, (main, side) in enumerate(((main0, side0), (main1, side1))):
        at = base + 32 * l
        g = side[...] + (far[at : at + 16, :].astype(f32) + far[at + 16 : at + 32, :].astype(f32))
        u_chan[:, l, :], f_chan[:, l, :], s_chan[:, l, :] = adamw(
            chan[:, l, :], m_chan[:, l, :], v_chan[:, l, :], g[0:12]
        )
        for j in range(main.shape[1] // rows):
            cols, at = lane(j), j * rows
            row = slice(l, l + 1)
            u_bias[row, cols], f_bias[row, cols], s_bias[row, cols] = adamw(
                bias[row, cols], m_bias[row, cols], v_bias[row, cols], g[12 + j : 13 + j]
            )
            _, f_up[l, :, cols], s_up[l, :, cols] = adamw(
                0.0, m_up[l, :, cols], v_up[l, :, cols], main[0, at : at + rows]
            )
            _, f_down[l, :, cols], s_down[l, :, cols] = adamw(
                0.0, m_down[l, :, cols], v_down[l, :, cols], main[1, at : at + rows]
            )


def ring_order(n_dp):
    return list(range(0, n_dp, 2)) + list(range(n_dp - 1, 0, -2))


def spread_kernel(layers, n_dp, parts, *refs):
    blocks = refs[: n_dp + 1]
    up_out, down_out, up, held, down, sems = refs[-6:]
    dp = lax.axis_index("dp")
    half = n_dp // 2
    spot = jnp.where(dp % 2 == 0, dp // 2, n_dp - 1 - dp // 2)

    def owner(distance):
        at = lax.rem(spot + distance + n_dp, n_dp)
        return jnp.where(at < half, 2 * at, 2 * (n_dp - 1 - at) + 1)

    distances = [0]
    for step in range(1, half):
        distances += [-step, step]
    rows = up.shape[1] // n_dp
    size = parts * rows
    copies = []
    for l in range(layers):
        start = 2 * size * l
        halves = [(d, ref, start, ref, start + size) for d, ref in zip(distances, blocks)]
        far = blocks[-2] if l == 0 else blocks[-1]
        halves.append((half, far, 0, far, size))
        for distance, first, first_at, second, second_at in halves:
            at = pl.ds(pl.multiple_of(owner(distance) * rows, rows), rows)
            for j in range(parts):
                start = first_at + j * rows
                up[l, at, lane(j)] = first[start : start + rows, :].astype(f32)
                start = second_at + j * rows
                held[at, lane(j)] = second[start : start + rows, :].astype(f32)
        copy = pltpu.make_async_copy(up.at[l], up_out.at[l], sems.at[2 * l])
        copy.start()
        copies.append(copy)
        for j in range(parts):
            down[l, lane(j), :] = held[:, lane(j)].T
        copy = pltpu.make_async_copy(down.at[l], down_out.at[l], sems.at[2 * l + 1])
        copy.start()
        copies.append(copy)
    for copy in copies:
        copy.wait()


def pack_kernel(keep, got, side0, side1, _, packet):
    rows = keep.shape[1]
    for i, ref in enumerate((keep, got)):
        for o in range(2):
            at = (2 * i + o) * rows
            packet[at : at + rows, :] = ref[o]
    packet[4 * rows : 4 * rows + 32, :] = side0[...]
    packet[4 * rows + 32 :, :] = side1[...]


def collect_kernel(own, core, far, out, grad):
    x, c, _ = place()
    rows = own.shape[1]
    for o, target in enumerate((out, grad)):
        for r in range(4):
            at = pl.multiple_of(((x ^ (r // 2)) * 2 + (c ^ (r % 2))) * rows, HALO)
            if r < 2:
                target[pl.ds(at, rows), :] = (own, core)[r][o]
            else:
                start = (2 * (r - 2) + o) * rows
                target[pl.ds(at, rows), :] = far[start : start + rows, :]


VMEM = pl.BlockSpec(memory_space=pltpu.VMEM)
ANY = pl.BlockSpec(memory_space=pl.ANY)
HBM = pl.BlockSpec(memory_space=pltpu.HBM)


def call(kernel, outs, in_specs, scratch, name, limit=16, out_specs=None, flops=0):
    return pl.pallas_call(
        kernel,
        out_shape=[jax.ShapeDtypeStruct(s, t) for s, t in outs],
        in_specs=in_specs,
        out_specs=out_specs or [VMEM] * len(outs),
        scratch_shapes=scratch,
        compiler_params=pltpu.CompilerParams(vmem_limit_bytes=limit * 1024 * 1024),
        cost_estimate=pl.CostEstimate(flops=flops, bytes_accessed=0, transcendentals=0),
        name=name,
    )


def on_device(
    n_dp, frames_in, segments, cotangent, channel_params, weight_up, bias_up, weight_down,
    momentum_channel, variance_channel, momentum_up, variance_up, momentum_bias, variance_bias,
    momentum_down, variance_down,
):
    rows, frames, part = frames_in.shape
    layers, width, quarter = weight_up.shape
    chip_hidden = 2 * quarter
    tokens = rows * frames
    own = tokens // 4
    ext = own + 2 * HALO
    shard = width // n_dp
    parts = quarter // LANES

    def core_swap(v):
        return lax.ppermute(v, "chan", xor_perm(4, 1))

    def x_swap(v):
        return lax.ppermute(v, "chan", xor_perm(4, 2))

    def dp_swap(v, bit):
        return lax.ppermute(v, "dp", xor_perm(n_dp, bit))

    def after(value, *others):
        return lax.optimization_barrier((value, *others))[0]

    sems = pltpu.SemaphoreType.DMA((8,))
    width_sems = pltpu.SemaphoreType.DMA((16,))
    chan, m_chan, v_chan = [
        jnp.swapaxes(v, 0, 1) for v in (channel_params, momentum_channel, variance_channel)
    ]
    up_held = pltpu.VMEM((width, quarter), f32)
    down_held = pltpu.VMEM((quarter, width), f32)
    matrix = ((width, quarter), bf16)

    def in_hbm(*arrays):
        return [pltpu.with_memory_space_constraint(v, pltpu.HBM) for v in arrays]

    packet = ((ext + 2 * PARAM_ROWS, LANES), bf16)
    flat = pltpu.VMEM((tokens + 2 * HALO, LANES), bf16)
    both_packets = ((2 * packet[0][0], LANES), bf16)
    give, here, beside, chosen0 = call(
        prepare_kernel, [both_packets, packet, packet, matrix], [HBM] * 5,
        [flat, pltpu.VMEM(chan.shape, f32), pltpu.VMEM(bias_up.shape, f32), up_held, down_held, sems, sems],
        "prepare",
    )(*in_hbm(frames_in, chan, bias_up, weight_up, weight_down))
    frames_far = x_swap(give)
    near0 = x_swap(chosen0)
    frames_core = core_swap(frames_far)
    packets = [here, core_swap(after(beside, frames_core)), frames_far, frames_core]
    cot_packet = ((ext, LANES), bf16)
    slice_shape = ((shard, quarter), f32)
    chosen1, *both, give, here, beside, ids, up0, down0, up1, down1 = call(
        rest_kernel,
        [matrix] * 5 + [((2 * ext, LANES), bf16)] + [cot_packet] * 2 + [((ext + 2 * PAD, LANES), jnp.int32)] + [slice_shape] * 4,
        [HBM] * 3 + [VMEM, ANY],
        [flat, pltpu.VMEM((tokens + 2 * HALO + 2 * PAD, LANES), jnp.int32)]
        + [pltpu.VMEM(weight_up.shape, f32), pltpu.VMEM(weight_down.shape, f32), up_held, sems, width_sems],
        "rest", 24, flops=LONG,
    )(*in_hbm(weight_up, weight_down, cotangent), segments, beside)
    near1 = x_swap(chosen1)
    slices0, slices1 = [up0, down0], [up1, down1]
    local0, local1 = [v + [core_swap(w) for w in v] for v in (both[:2], both[2:])]
    cots = [here, core_swap(beside)]

    wide = (ext, width)
    padded = (ext + 2 * PAD, width)
    deep = (ext, chip_hidden)
    held = pltpu.VMEM((2, width, chip_hidden), bf16)
    bias = pltpu.VMEM((1, chip_hidden), f32)
    sums = ((1, chip_hidden), f32)
    params_shape = ((PARAM_ROWS, width), f32)
    turned = ((width, own), bf16)
    norm_shapes = [(wide, f32), ((ext, LANES), f32), (wide, bf16)]
    half_shapes = [(deep, bf16), (deep, f32), (wide, f32)]
    size = parts * shard
    grads = [((2, n_dp, size, LANES), bf16)] + [((n_dp, size, LANES), f32)] * 2
    side_shapes = [((2, 2, 16, LANES), bf16), ((2, 16, LANES), f32)]
    norm_scratch = [pltpu.VMEM(padded, f32), pltpu.VMEM((16, width), f32)]

    def buffers(shapes):
        return [pltpu.VMEM(s, t) for s, t in shapes]

    first = call(
        first_kernel, norm_shapes + half_shapes + [(padded, f32), params_shape],
        [VMEM] * 9 + [ANY], [bias, held], "layer0_near", 24,
    )
    centred0, rstd0, normed0, active00, slope00, partial0, source0, params = first(
        ids, *packets, *local0, ids
    )
    cot_far = x_swap(after(give, near0))
    far0 = dp_swap(after(near0, partial0), 1)
    far1 = dp_swap(after(near1, partial0), 1)
    away0 = [near0, core_swap(near0), far0, core_swap(after(far0, near1, partial0))]
    second = call(
        second_kernel, [(padded, f32)] + half_shapes, [VMEM] * 8 + [ANY],
        [bias, held], "layer0_far", 24,
    )
    source1, active01, slope01, branch0 = second(source0, params, normed0, partial0, *away0, near1)
    third = call(
        third_kernel, norm_shapes + half_shapes, [VMEM] * 7 + [ANY],
        [bias, held], "layer1_near", 24,
    )
    centred1, rstd1, normed1, active10, slope10, partial1 = third(ids, source1, params, *local1, near1)
    cots += [cot_far, core_swap(after(cot_far, active10))]
    fourth = call(
        fourth_kernel, [(wide, f32), (wide, bf16), turned, turned] + grads + [(wide, f32), sums],
        [VMEM] * 12, [pltpu.VMEM(deep, bf16), held], "layer1_near_back", 24,
    )
    dy1, low1, low_t1, normed_t1, give10, *keep10, dnormed1, bias10 = fourth(
        *cots, params, normed1, active10, slope10, *local1
    )
    got10 = core_swap(give10)
    away1 = [near1, core_swap(near1), far1, core_swap(after(far1, dnormed1))]
    fifth = call(
        fifth_kernel, [(wide, f32), ((own, width), bf16)] + grads + [(wide, f32), sums],
        [VMEM] * 12,
        [bias] + buffers(half_shapes[:2]) + [pltpu.VMEM(deep, bf16), held], "layer1_far", 28, flops=LONG,
    )
    branch1, first_out, give11, *keep11, dnormed1, bias11 = fifth(
        source1, params, normed1, partial1, low1, low_t1, normed_t1, dnormed1, *away1
    )
    got11 = core_swap(give11)

    half = n_dp // 2
    plans = [halving_plan(n_dp, axes) for axes in AXES]
    side_shape = ((32, LANES), f32)

    def packet_of(blocks, side=False):
        return ((blocks * size + (64 if side else 0), LANES), bf16)

    def combine(kernel, outs, args, before, name, flops=0):
        specs = [VMEM] * len(args) + [ANY] * len(before)
        return call(kernel, outs, specs, [], name, flops=flops)(*args, *before)

    def step_outs(layer, step):
        give, keep, groups = plans[layer][step]
        outs = [packet_of(sum(len(give[m]) for m in g), step > 0 and n == 0) for n, g in enumerate(groups)]
        outs += [((len(k), size, LANES), f32) for k in keep]
        return outs + ([side_shape] if step else [])

    def exchange(layer, step, packets):
        swaps = {"x": x_swap, "y": lambda v: dp_swap(v, 1), "z": lambda v: dp_swap(v, 2)}
        groups = plans[layer][step][2]
        return [swaps[AXES[layer][g[0]][step]](v) for v, g in zip(packets, groups)]

    def core_step(layer, gots, keeps, before):
        kernel = functools.partial(core_sum_kernel, plans[layer], len(gots))
        outs = combine(kernel, step_outs(layer, 0), [*gots, *keeps], before, "core_sum")
        return outs[:-2], outs[-2:]

    def next_step(layer, step, got, helds, sides, before, flops=0):
        kernel = functools.partial(step_sum_kernel, plans[layer], step)
        outs = combine(kernel, step_outs(layer, step), [*got, *helds, *sides], before, "step_sum", flops)
        return outs[:-3], outs[-3:-1], outs[-1]

    def line_start(layer, got, helds, side, before):
        left = n_dp // 4
        outs = [packet_of(left, True), ((left, size, LANES), f32), side_shape]
        kernel = functools.partial(line_start_kernel, plans[layer])
        state = combine(kernel, outs, [*got, *helds, side], before, "line_start")
        bit = 4
        while bit < half:
            left //= 2
            outs = [packet_of(left, True), ((left, size, LANES), f32), side_shape]
            state = combine(line_sum_kernel, outs, [dp_swap(state[0], bit), *state[1:]], [], "line_sum")
            bit *= 2
        return state

    down_moments = [jnp.swapaxes(v, 1, 2) for v in (momentum_down, variance_down)]

    def update_step(layer, packet, main, side, slices, others, before):
        outs = [packet_of(2 + 2 * len(others)), ((2, size, LANES), f32)]
        outs += [((16, LANES), f32), ((32, LANES), bf16)]
        args = [dp_swap(packet, half), main, side, *slices, momentum_up, variance_up, *down_moments]
        args += others
        return combine(functools.partial(update_kernel, layer), outs, args, before, "update")

    order = ring_order(n_dp)
    ahead = [(order[i], order[(i + 1) % n_dp]) for i in range(n_dp)]
    back = [(b, a) for a, b in ahead]

    def ring_step(right, left):
        return lax.ppermute(right, "dp", ahead), lax.ppermute(left, "dp", back)

    def ring_end(right, left):
        cut = right.shape[0] // 2
        return lax.ppermute(right[:cut], "dp", ahead), lax.ppermute(left[cut:], "dp", back)

    def blocks_of(ring):
        return [ring[0][0]] + [v for pair in ring[1:] for v in pair]

    packets1, helds1 = core_step(1, [got10, got11], [*keep10, *keep11], [])
    sixth = call(
        sixth_kernel, [(wide, f32)] + side_shapes, [VMEM] * 10 + [ANY], norm_scratch, "layer1_norm_back", 24
    )
    grad1, *sides1 = sixth(
        ids, source1, params, centred1, rstd1, branch1, dy1, dnormed1, bias10, bias11, packets1[0]
    )
    seventh = call(
        seventh_kernel, [(deep, bf16)] * 2 + [((4, n_dp, size, LANES), bf16)] + [grads[1]] * 4 + [sums] * 2,
        [VMEM] * 15, buffers([(wide, bf16), turned, turned]) + [held, held],
        "layer0_back", 28,
    )
    hidden0, hidden1, *matrices0, bias00, bias01 = seventh(
        grad1, params, normed0, active00, slope00, active01, slope01, *local0, *away0
    )
    crossed1 = exchange(1, 0, packets1)
    marker = call(marker_kernel, [((8, LANES), f32)], [ANY] * 2, [], "marker", flops=LONG)(*crossed1)
    eighth = call(
        eighth_kernel, [((2, own, LANES), bf16)] * 4 + side_shapes, [VMEM] * 20 + [ANY],
        buffers([(wide, f32)]) + norm_scratch + buffers([((own, width), bf16)]) + [held, held],
        "layer0_norm_back", 28, flops=LONG,
    )
    give_near, give_far, keep_near, keep_far, *sides0 = eighth(
        ids, source0, params, centred0, rstd0, branch0, grad1, hidden0, hidden1, bias00, bias01, first_out,
        *local0, *away0, bias01,
    )

    packets0, helds0 = core_step(0, [core_swap(matrices0[0])], matrices0[1:], marker)
    crossed0 = exchange(0, 0, packets0)
    sides = [core_swap(sides1[0]), sides1[1]]
    packets1, helds1, side1 = next_step(1, 1, crossed1, helds1, sides, [packets0[0]])
    sides = [core_swap(sides0[0]), sides0[1]]
    packets0, helds0, side0 = next_step(0, 1, crossed0, helds0, sides, [], LONG)
    got = exchange(1, 1, packets1)
    packets1, helds1, side1 = next_step(1, 2, got, helds1, [side1], [packets0[0]], LONG)
    line1 = line_start(1, exchange(1, 2, packets1), helds1, side1, [])
    sent1, main1, side1, side_far1 = update_step(1, *line1, slices1, [], [])
    packets0, helds0, side0 = next_step(
        0, 2, exchange(0, 1, packets0), helds0, [side0], [packets1[0]]
    )
    line0 = line_start(0, exchange(0, 2, packets0), helds0, side0, [line1[0]])
    sent, main0, side0, side_far0 = update_step(0, *line0, slices0, [sent1], [])
    ring = [(sent, sent)]
    ring.append(ring_step(sent, sent))

    got_near, got_far = core_swap(give_near), core_swap(give_far)
    far_packet = ((4 * own + 64, LANES), bf16)
    from_far = x_swap(
        call(pack_kernel, [far_packet], [VMEM] * 4 + [ANY], [], "pack")(
            keep_far, got_far, side_far0, side_far1, sent
        )[0]
    )
    layer_output, input_grad = call(
        collect_kernel, [((tokens, part), bf16)] * 2, [VMEM] * 3, [], "collect"
    )(keep_near, got_near, from_far)

    adam_outs = [
        (chan.shape, f32),
        (bias_up.shape, f32),
        (chan.shape, f32),
        (chan.shape, f32),
        (momentum_up.shape, f32),
        (momentum_up.shape, f32),
        (bias_up.shape, f32),
        (bias_up.shape, f32),
        (down_moments[0].shape, f32),
        (down_moments[0].shape, f32),
    ]
    (
        params_channel, params_bias, first_channel, second_channel,
        first_up, second_up, first_bias, second_bias, first_down, second_down,
    ) = call(adam_kernel, adam_outs, [VMEM] * 15, [], "adam")(
        main0, main1, side0, side1, from_far, chan, bias_up, m_chan, v_chan, momentum_up, variance_up,
        momentum_bias, variance_bias, *down_moments,
    )
    right, left = ring[1]
    for step in range(2, half):
        right, left = ring_step(right, left)
        ring.append((right, left))
    ring.append(ring_end(right, left))
    whole = [(weight_up.shape, f32), (weight_down.shape, f32)]
    spread = call(
        functools.partial(spread_kernel, layers, n_dp, parts), whole, [VMEM] * (n_dp + 1) + [ANY] * 2,
        [pltpu.VMEM(weight_up.shape, f32), up_held, pltpu.VMEM(weight_down.shape, f32), sems],
        "spread", 16, [HBM, HBM],
    )
    params_up, params_down = spread(*blocks_of(ring), layer_output, first_up)

    params_channel, first_channel, second_channel = [
        jnp.swapaxes(v, 0, 1) for v in (params_channel, first_channel, second_channel)
    ]
    first_down, second_down = jnp.swapaxes(first_down, 1, 2), jnp.swapaxes(second_down, 1, 2)

    layer_output, input_grad = [v.reshape(rows, frames, part) for v in (layer_output, input_grad)]
    return (
        layer_output,
        input_grad,
        params_channel,
        params_up,
        params_bias,
        params_down,
        first_channel,
        second_channel,
        first_up,
        second_up,
        first_bias,
        second_bias,
        first_down,
        second_down,
    )


def solution(mesh):
    return jax.shard_map(
        functools.partial(on_device, mesh.shape["dp"]),
        mesh=mesh,
        in_specs=(
            P("dp", None, "chan"),
            P("dp", None),
            P("dp", None, "chan"),
            P(None, None, "chan"),
            P(None, None, "chan"),
            P(None, "chan"),
            P(None, "chan", None),
            P(None, None, "chan"),
            P(None, None, "chan"),
            P(None, "dp", "chan"),
            P(None, "dp", "chan"),
            P(None, "chan"),
            P(None, "chan"),
            P(None, "chan", "dp"),
            P(None, "chan", "dp"),
        ),
        out_specs=(
            P("dp", None, "chan"),
            P("dp", None, "chan"),
            P(None, None, "chan"),
            P(None, None, "chan"),
            P(None, "chan"),
            P(None, "chan", None),
            P(None, None, "chan"),
            P(None, None, "chan"),
            P(None, "dp", "chan"),
            P(None, "dp", "chan"),
            P(None, "chan"),
            P(None, "chan"),
            P(None, "chan", "dp"),
            P(None, "chan", "dp"),
        ),
        check_vma=False,
    )
```

```python
import functools

import jax
import jax.numpy as jnp
from jax import lax
from jax.experimental import pallas as pl
from jax.experimental.pallas import tpu as pltpu
from jax.sharding import PartitionSpec as P

kernel_taps = 7
reach = kernel_taps // 2
norm_eps = 1e-06
beta_first = 0.8
beta_second = 0.9
adam_eps = 1e-08
decay_rate = 0.01
adam_step = 10.0

HALO = 16
PAD = 8
LANES = 128
PARAM_ROWS = 32
AXES = (("xyz", "yxz"), ("xzy", "yzx"))
LONG = 20_000_000_000
f32 = jnp.float32
bf16 = jnp.bfloat16


def xor_perm(size, bit):
    return [(i, i ^ bit) for i in range(size)]


def hi_lo(value):
    hi = lax.reduce_precision(value, 8, 7)
    return hi.astype(bf16), (value - hi).astype(bf16)


def place():
    me = lax.axis_index("chan")
    return me // 2, me % 2, lax.axis_index("dp")


def lanes_of(x, c, r):
    return pl.ds(pl.multiple_of(((x ^ (r // 2)) * 2 + (c ^ (r % 2))) * LANES, LANES), LANES)


def row_tiles(ext):
    own = ext - 2 * HALO
    tiles = [(0, HALO, False)]
    tiles += [(HALO + at, 32, True) for at in range(0, own, 32)]
    return tiles + [(HALO + own, HALO, False)]


def lane(j):
    return slice(j * LANES, (j + 1) * LANES)


def fold(value):
    return value.reshape(value.shape[0] // 8, 8, value.shape[1]).sum(axis=0)


def plus(total, value):
    return value if total is None else total + value


def column_sum(value):
    return jnp.sum(value, axis=0, keepdims=True)


def gelu_parts(h):
    tail = jnp.exp(-0.5 * h * h)
    d = 1.0 + (0.3275911 * 0.7071067811865476) * jnp.abs(h)
    t = pl.reciprocal(d, approx=True)
    t = t * (2.0 - d * t)
    poly = t * (
        0.127414796
        + t * (-0.142248368 + t * (0.7107068705 + t * (-0.7265760135 + t * 0.5307027145)))
    )
    low = poly * tail
    phi = jnp.where(h < 0.0, low, 1.0 - low)
    return h * phi, phi + h * tail * 0.3989422804014327


def load_frames(x, c, packets, ext, source):
    for r, ref in enumerate(packets):
        source[PAD : PAD + ext, lanes_of(x, c, r)] = ref[0:ext, :].astype(f32)
    clear_pads(source, ext)


def load_params(x, c, packets, ext, params):
    for r, ref in enumerate(packets):
        hi = ref[ext : ext + PARAM_ROWS, :].astype(f32)
        lo = ref[ext + PARAM_ROWS : ext + 2 * PARAM_ROWS, :].astype(f32)
        params[:, lanes_of(x, c, r)] = hi + lo


def clear_pads(ref, ext):
    zeros = jnp.zeros((PAD, ref.shape[1]), ref.dtype)
    ref[0:PAD, :] = zeros
    ref[PAD + ext : PAD + ext + PAD, :] = zeros


def load_bias(x, c, layer, chip, params, bias):
    width = bias.shape[1] // 2
    for r in range(2):
        rows = params[:, lanes_of(x, c, 2 * chip + r)]
        for j in range(width // LANES):
            k = 24 + layer * (width // LANES) + j
            bias[0:1, r * width + j * LANES : r * width + (j + 1) * LANES] = rows[k : k + 1]


def start_copies(pairs, sems):
    started = []
    for i, (src, dst) in enumerate(pairs):
        copy = pltpu.make_async_copy(src, dst, sems.at[i])
        copy.start()
        started.append(copy)
    return started


def hold_local(refs, held):
    width = refs[0].shape[-1]
    for i, ref in enumerate(refs):
        r, m = i // 2, i % 2
        held[m, :, r * width : (r + 1) * width] = ref[...]


def hold_far(y, refs, held):
    near, near_core, far, *far_core = refs
    width = near.shape[-1]
    held[y, :, 0:width] = near[...]
    held[1 - y, :, 0:width] = far[...]
    held[y, :, width:] = near_core[...]
    at = 0
    for ref in far_core:
        held[1 - y, at : at + ref.shape[0], width:] = ref[...]
        at += ref.shape[0]


def masks_at(ids, start, rows):
    here = ids[PAD + start : PAD + start + rows, :]
    masks = []
    for k in range(kernel_taps):
        at = PAD + start + k - reach
        masks.append(ids[at : at + rows, :] == here)
    return masks


def forward_norm(layer, source, ids, params, centred, rstd, normed, ext):
    width = source.shape[1]
    tiles = width // LANES
    base = layer * 12
    for start, rows, _ in row_tiles(ext):
        masks = masks_at(ids, start, rows)
        convs = []
        total = square = None
        for j in range(tiles):
            acc = params[base + 7 : base + 8, lane(j)]
            for k in range(kernel_taps):
                at = PAD + start + k - reach
                piece = source[at : at + rows, lane(j)]
                tap = params[base + k : base + k + 1, lane(j)]
                acc = acc + tap * (piece if k == reach else jnp.where(masks[k], piece, 0.0))
            convs.append(acc)
            total = plus(total, acc)
            square = plus(square, acc * acc)
        mean = jnp.sum(total, axis=1, keepdims=True) * (1.0 / width)
        var = jnp.sum(square, axis=1, keepdims=True) * (1.0 / width) - mean * mean
        scale = lax.rsqrt(var + norm_eps)
        rstd[start : start + rows, :] = jnp.broadcast_to(scale, (rows, LANES))
        for j in range(tiles):
            value = (convs[j] - mean) * scale
            centred[start : start + rows, lane(j)] = value
            gain = params[base + 8 : base + 9, lane(j)]
            shift = params[base + 9 : base + 10, lane(j)]
            normed[start : start + rows, lane(j)] = (value * gain + shift).astype(bf16)


def forward_half(bias, held, normed, active, slope, ext):
    quarter = held.shape[2] // 2
    half = ext // 2
    for r in range(2):
        cols = slice(r * quarter, (r + 1) * quarter)
        for at in (0, half):
            rows = slice(at, at + half)
            h = (
                jnp.dot(normed[rows, :], held[0, :, cols], preferred_element_type=f32)
                + bias[0:1, cols]
            )
            value, grad = gelu_parts(h)
            active[rows, cols] = value.astype(bf16)
            slope[rows, cols] = grad


def down_half(held, active, rows):
    return lax.dot_general(
        active[rows, :], held[1], (((1,), (1,)), ((), ())), preferred_element_type=f32
    )


def finish_branch(layer, source, params, held, active, partial, branch, ext, put):
    half = ext // 2
    base = layer * 12
    for at in (0, half):
        rows = slice(at, at + half)
        value = partial[rows, :] + down_half(held, active, rows) + params[base + 10 : base + 11, :]
        branch[rows, :] = value
        put(at, half, source[PAD + at : PAD + at + half, :] + params[base + 11 : base + 12, :] * value)


def branch_grad(layer, dy, params, low, ext):
    base = layer * 12
    for j in range(dy.shape[1] // LANES):
        scale = params[base + 11 : base + 12, lane(j)]
        for start, rows, _ in row_tiles(ext):
            low[start : start + rows, lane(j)] = (scale * dy[start : start + rows, lane(j)]).astype(bf16)


def put_grad(dp, out, parts, value):
    blocks, size, _ = out.shape
    rows = size // parts
    value = value.astype(out.dtype)
    for d in range(blocks):
        for j in range(parts):
            out[d ^ dp, j * rows : (j + 1) * rows] = value[d * rows : (d + 1) * rows, lane(j)]


def backward_half(dp, held, low, low_t, normed_t, active, slope, hidden_low, give, keep, bias_sums, ext):
    quarter = held.shape[2] // 2
    half = ext // 2
    inner = slice(HALO, ext - HALO)
    parts = quarter // LANES
    for r, out in ((0, keep), (1, give)):
        cols = slice(r * quarter, (r + 1) * quarter)
        sums = None
        for at in (0, half):
            rows = slice(at, at + half)
            grad = (
                jnp.dot(low[rows, :], held[1, :, cols], preferred_element_type=f32)
                * slope[rows, cols]
            )
            hidden_low[rows, cols] = grad.astype(bf16)
            sums = plus(sums, fold(grad[HALO:] if at == 0 else grad[: half - HALO]))
        bias_sums[0:1, cols] = column_sum(sums)
        put_grad(dp, out[1], parts, jnp.dot(low_t[...], active[inner, cols], preferred_element_type=f32))
        put_grad(
            dp, out[0], parts, jnp.dot(normed_t[...], hidden_low[inner, cols], preferred_element_type=f32)
        )


def back_half(held, hidden_low, rows):
    return lax.dot_general(
        hidden_low[rows, :], held[0], (((1,), (1,)), ((), ())), preferred_element_type=f32
    )


def backward_norm(
    layer, x, c, dy, source, ids, params, centred, rstd, branch, dnormed, dconv, small_c,
    bias_near, bias_far, side_give, side_keep, put, ext,
):
    width = source.shape[1]
    tiles = width // LANES
    quarter = bias_near.shape[1] // 2
    base = layer * 12
    small_c[...] = jnp.zeros_like(small_c)
    for j in range(tiles):
        scale = params[base + 11 : base + 12, lane(j)]
        sum_gamma = sum_bias = None
        for start, rows, inner in row_tiles(ext):
            if inner:
                grad = dy[start : start + rows, lane(j)]
                sum_gamma = plus(sum_gamma, fold(grad * branch[start : start + rows, lane(j)]))
                sum_bias = plus(sum_bias, fold(scale * grad))
        small_c[10:11, lane(j)] = column_sum(sum_bias)
        small_c[11:12, lane(j)] = column_sum(sum_gamma)

    clear_pads(dconv, ext)
    sums = [[None] * 3 for _ in range(tiles)]
    for start, rows, inner in row_tiles(ext):
        scale = rstd[start : start + rows, :]
        weighted, norms = [], []
        first = second = None
        for j in range(tiles):
            grad = dnormed[start : start + rows, lane(j)]
            norm = centred[start : start + rows, lane(j)]
            w = grad * params[base + 8 : base + 9, lane(j)]
            first = plus(first, w)
            second = plus(second, w * norm)
            weighted.append(w)
            norms.append(norm)
            if inner:
                sums[j][0] = plus(sums[j][0], fold(grad * norm))
                sums[j][1] = plus(sums[j][1], fold(grad))
        first = jnp.sum(first, axis=1, keepdims=True) * (1.0 / width)
        second = jnp.sum(second, axis=1, keepdims=True) * (1.0 / width)
        for j in range(tiles):
            value = scale * (weighted[j] - first - norms[j] * second)
            dconv[PAD + start : PAD + start + rows, lane(j)] = value
            if inner:
                sums[j][2] = plus(sums[j][2], fold(value))
    for j in range(tiles):
        small_c[8:9, lane(j)] = column_sum(sums[j][0])
        small_c[9:10, lane(j)] = column_sum(sums[j][1])
        small_c[7:8, lane(j)] = column_sum(sums[j][2])

    for j in range(tiles):
        taps = [params[base + k : base + k + 1, lane(j)] for k in range(kernel_taps)]
        sums = [None] * kernel_taps
        for start, rows, inner in row_tiles(ext):
            masks = masks_at(ids, start, rows)
            here = dconv[PAD + start : PAD + start + rows, lane(j)]
            total = dy[start : start + rows, lane(j)]
            for k in range(kernel_taps):
                mirror = kernel_taps - 1 - k
                at = PAD + start + mirror - reach
                piece = dconv[at : at + rows, lane(j)]
                total = total + taps[k] * (
                    piece if k == reach else jnp.where(masks[mirror], piece, 0.0)
                )
                if inner:
                    at = PAD + start + k - reach
                    piece = source[at : at + rows, lane(j)]
                    if k != reach:
                        piece = jnp.where(masks[k], piece, 0.0)
                    sums[k] = plus(sums[k], fold(piece * here))
            put(start, rows, inner, j, total)
        for k in range(kernel_taps):
            small_c[k : k + 1, lane(j)] = column_sum(sums[k])

    for r in range(4):
        sums = (bias_near if r < 2 else bias_far)[0:1, (r % 2) * quarter : (r % 2 + 1) * quarter]
        rows = [small_c[0:12, lanes_of(x, c, r)]]
        rows += [sums[:, lane(j)] for j in range(quarter // LANES)]
        rows += [jnp.zeros((16 - 12 - quarter // LANES, LANES), f32)]
        value = jnp.concatenate(rows, axis=0)
        if r % 2 == 0:
            side_keep[r // 2] = value
        else:
            hi = value.astype(bf16)
            side_give[r // 2, 0] = hi
            side_give[r // 2, 1] = (value - hi.astype(f32)).astype(bf16)


def start_rows(frames, flat, sems):
    rows, count, _ = frames.shape
    zeros = jnp.zeros((HALO, LANES), bf16)
    flat[0:HALO, :] = zeros
    flat[HALO + rows * count :, :] = zeros
    pairs = [(frames.at[r], flat.at[HALO + r * count : HALO + (r + 1) * count]) for r in range(rows)]
    return start_copies(pairs, sems)


def token_chunks(flat, own, outs):
    x, c, _ = place()
    ext = own + 2 * HALO
    for out, dx, dc in zip(outs, (1, 1, 0, 0), (0, 1, 0, 1)):
        at = pl.multiple_of(((x ^ dx) * 2 + (c ^ dc)) * own, HALO)
        out[0:ext, :] = flat[pl.ds(at, ext), :]


def pieces(source, target, count):
    rows = source.shape[0] // count
    cuts = [pl.ds(i * rows, rows) for i in range(count)]
    return [(source.at[cut], target.at[cut]) for cut in cuts]


def prepare_kernel(
    frames, chan_in, bias_in, up, down,
    give, here, beside, chosen, flat, chan, bias, up_held, down_held, sems, matrix_sems,
):
    x, c, dp = place()

    @pl.when(dp % 2 == 0)
    def start_up():
        start_copies(pieces(up.at[0], up_held, 4), matrix_sems)

    @pl.when(dp % 2 == 1)
    def start_down():
        start_copies(pieces(down.at[0], down_held, 4), matrix_sems)

    copies = start_rows(frames, flat, sems)
    smalls = start_copies([(chan_in, chan), (bias_in, bias)], sems.at[pl.ds(4, 2)])
    own = frames.shape[0] * frames.shape[1] // 4
    ext = own + 2 * HALO
    layers, parts = bias.shape[0], bias.shape[1] // LANES
    for copy in smalls:
        copy.wait()
    rows = [chan[:, l, :] for l in range(layers)]
    rows += [bias[l : l + 1, lane(j)] for l in range(layers) for j in range(parts)]
    rows += [jnp.zeros((PARAM_ROWS - (12 + parts) * layers, LANES), f32)]
    value = jnp.concatenate(rows, axis=0)
    hi = value.astype(bf16)
    lo = (value - hi.astype(f32)).astype(bf16)
    size = ext + 2 * PARAM_ROWS
    outs = (give.at[0:size], give.at[size:], here, beside)
    for out in outs:
        out[ext : ext + PARAM_ROWS, :] = hi
        out[ext + PARAM_ROWS :, :] = lo
    for copy in copies:
        copy.wait()
    token_chunks(flat, own, outs)

    @pl.when(dp % 2 == 0)
    def take_up():
        for i, (src, dst) in enumerate(pieces(up.at[0], up_held, 4)):
            pltpu.make_async_copy(src, dst, matrix_sems.at[i]).wait()
        chosen[...] = up_held[...].astype(bf16)

    @pl.when(dp % 2 == 1)
    def take_down():
        for i, (src, dst) in enumerate(pieces(down.at[0], down_held, 4)):
            pltpu.make_async_copy(src, dst, matrix_sems.at[i]).wait()
        chosen[...] = down_held[...].T.astype(bf16)


def split_kernel(whole, *refs):
    first, second = refs[-2:]
    first[...] = whole[0 : first.shape[0], :]
    second[...] = whole[first.shape[0] :, :]


def rest_kernel(
    up, down, frames, segments, _,
    chosen, w00, w01, w10, w11, give, here, beside, ids, up0, down0, up1, down1,
    flat, columns, up_held, down_held, turned, sems, matrix_sems,
):
    x, c, dp = place()
    layers = up.shape[0]
    matrices = []
    for l in reversed(range(layers)):
        pairs = pieces(up.at[l], up_held.at[l], 4) + pieces(down.at[l], down_held.at[l], 4)
        matrices.append(start_copies(pairs, matrix_sems.at[pl.ds(8 * l, 8)]))
    copies = start_rows(frames, flat, sems)
    shard = up0.shape[0]
    mine = pl.ds(pl.multiple_of(dp * shard, shard), shard)
    for l, started, both, up_slice, down_slice in (
        (1, matrices[0], (w10, w11), up1, down1),
        (0, matrices[1], (w00, w01), up0, down0),
    ):
        for copy in started:
            copy.wait()
        both[0][...] = up_held[l].astype(bf16)
        up_slice[...] = up_held[l, mine, :]
        turned[...] = down_held[l].T
        both[1][...] = turned[...].astype(bf16)
        down_slice[...] = turned[mine, :]

    @pl.when(dp % 2 == 0)
    def choose_up():
        chosen[...] = w10[...]

    @pl.when(dp % 2 == 1)
    def choose_down():
        chosen[...] = w11[...]

    for copy in copies:
        copy.wait()
    ext = here.shape[0]
    token_chunks(flat, ext - 2 * HALO, (give.at[0:ext], give.at[ext:], here, beside))

    rows, count = segments.shape
    tokens = rows * count
    edge = HALO + PAD
    none = jnp.full((edge, LANES), -1, jnp.int32)
    columns[0:edge, :] = none
    columns[edge + tokens :, :] = none
    for r in range(rows):
        row = jnp.broadcast_to(segments[r : r + 1, :] + 8 * r, (LANES, count))
        at = edge + r * count
        columns[at : at + count, :] = row.T
    at = pl.multiple_of((x * 2 + c) * (tokens // 4), HALO)
    ids[...] = columns[pl.ds(at, ids.shape[0]), :]


def first_kernel(
    ids, here, beside, near, far, own_up, own_down, core_up, core_down, _,
    centred, rstd, normed, active, slope, partial, source, params, bias, held,
):
    ext = ids.shape[0] - 2 * PAD
    x, c, _d = place()
    packets = (here, beside, near.at[0 : here.shape[0]], far.at[here.shape[0] :])
    load_frames(x, c, packets, ext, source)
    load_params(x, c, packets, ext, params)
    load_bias(x, c, 0, 0, params, bias)
    forward_norm(0, source, ids, params, centred, rstd, normed, ext)
    hold_local((own_up, own_down, core_up, core_down), held)
    forward_half(bias, held, normed, active, slope, ext)
    for at in (0, ext // 2):
        rows = slice(at, at + ext // 2)
        partial[rows, :] = down_half(held, active, rows)


def second_kernel(
    source, params, normed, partial, w_near, w_near_core, w_far, w_far_core0, w_far_core1, _,
    next_source, active, slope, branch, bias, held,
):
    ext = normed.shape[0]
    x, c, dp = place()
    load_bias(x, c, 0, 1, params, bias)
    clear_pads(next_source, ext)
    hold_far(dp % 2, (w_near, w_near_core, w_far, w_far_core0, w_far_core1), held)
    forward_half(bias, held, normed, active, slope, ext)

    def put(at, rows, value):
        next_source[PAD + at : PAD + at + rows, :] = value

    finish_branch(0, source, params, held, active, partial, branch, ext, put)


def third_kernel(
    ids, source, params, own_up, own_down, core_up, core_down, _,
    centred, rstd, normed, active, slope, partial, bias, held,
):
    ext = ids.shape[0] - 2 * PAD
    x, c, _d = place()
    load_bias(x, c, 1, 0, params, bias)
    forward_norm(1, source, ids, params, centred, rstd, normed, ext)
    hold_local((own_up, own_down, core_up, core_down), held)
    forward_half(bias, held, normed, active, slope, ext)
    for at in (0, ext // 2):
        rows = slice(at, at + ext // 2)
        partial[rows, :] = down_half(held, active, rows)


def fourth_kernel(
    cot_here, cot_beside, cot_near, cot_far, params, normed, active, slope, own_up, own_down, core_up, core_down,
    dy, low, low_t, normed_t, give, keep0, keep1, dnormed, bias_sums, hidden_low, held,
):
    ext = dy.shape[0]
    x, c, dp = place()
    refs = (cot_here, cot_beside, cot_near.at[0:ext], cot_far.at[ext:])
    for r, ref in enumerate(refs):
        dy[:, lanes_of(x, c, r)] = ref[...].astype(f32)
    branch_grad(1, dy, params, low, ext)
    low_t[...] = low[HALO : ext - HALO, :].T
    normed_t[...] = normed[HALO : ext - HALO, :].T
    hold_local((own_up, own_down, core_up, core_down), held)
    backward_half(
        dp, held, low, low_t, normed_t, active, slope, hidden_low, (give.at[0], give.at[1]), (keep0, keep1), bias_sums, ext
    )
    for at in (0, ext // 2):
        rows = slice(at, at + ext // 2)
        dnormed[rows, :] = back_half(held, hidden_low, rows)


def fifth_kernel(
    source, params, normed, partial, low, low_t, normed_t, dnormed_near,
    w_near, w_near_core, w_far, w_far_core,
    branch, out, give, keep0, keep1, dnormed, bias_sums, bias, active, slope, hidden_low, held,
):
    ext = normed.shape[0]
    x, c, dp = place()
    load_bias(x, c, 1, 1, params, bias)
    hold_far(dp % 2, (w_near, w_near_core, w_far, w_far_core), held)
    forward_half(bias, held, normed, active, slope, ext)
    backward_half(
        dp, held, low, low_t, normed_t, active, slope, hidden_low, (give.at[0], give.at[1]), (keep0, keep1), bias_sums, ext
    )

    def put(at, rows, value):
        if at == 0:
            out[0 : rows - HALO, :] = value[HALO:].astype(bf16)
        else:
            out[at - HALO :, :] = value[: rows - HALO].astype(bf16)

    finish_branch(1, source, params, held, active, partial, branch, ext, put)
    for at in (0, ext // 2):
        rows = slice(at, at + ext // 2)
        dnormed[rows, :] = dnormed_near[rows, :] + back_half(held, hidden_low, rows)


def sixth_kernel(
    ids, source, params, centred, rstd, branch, dy, dnormed, bias_near, bias_far, _,
    grad_source, side_give, side_keep, dconv, small_c,
):
    ext = dy.shape[0]
    x, c, _d = place()

    def put(start, rows, inner, j, value):
        grad_source[start : start + rows, lane(j)] = value

    backward_norm(
        1, x, c, dy, source, ids, params, centred, rstd, branch, dnormed, dconv, small_c,
        bias_near, bias_far, side_give, side_keep, put, ext,
    )


def seventh_kernel(
    dy, params, normed, active_near, slope_near, active_far, slope_far,
    own_up, own_down, core_up, core_down, w_near, w_near_core, w_far, w_far_core0, w_far_core1,
    hidden_near, hidden_far, give,
    keep_near0, keep_near1, keep_far0, keep_far1, bias_near, bias_far,
    low, low_t, normed_t, held_near, held_far,
):
    ext = dy.shape[0]
    _x, _c, dp = place()
    branch_grad(0, dy, params, low, ext)
    low_t[...] = low[HALO : ext - HALO, :].T
    normed_t[...] = normed[HALO : ext - HALO, :].T
    hold_local((own_up, own_down, core_up, core_down), held_near)
    hold_far(dp % 2, (w_near, w_near_core, w_far, w_far_core0, w_far_core1), held_far)
    backward_half(
        dp, held_near, low, low_t, normed_t, active_near, slope_near, hidden_near,
        (give.at[0], give.at[1]), (keep_near0, keep_near1), bias_near, ext,
    )
    backward_half(
        dp, held_far, low, low_t, normed_t, active_far, slope_far, hidden_far,
        (give.at[2], give.at[3]), (keep_far0, keep_far1), bias_far, ext,
    )


def eighth_kernel(
    ids, source, params, centred, rstd, branch, dy, hidden_near, hidden_far, bias_near, bias_far, first_out,
    own_up, own_down, core_up, core_down, w_near, w_near_core, w_far, w_far_core0, w_far_core1, _,
    out_give0, out_give1, out_keep0, out_keep1, side_give, side_keep,
    dnormed, dconv, small_c, out, held_near, held_far,
):
    ext = dy.shape[0]
    x, c, dp = place()
    hold_local((own_up, own_down, core_up, core_down), held_near)
    hold_far(dp % 2, (w_near, w_near_core, w_far, w_far_core0, w_far_core1), held_far)
    for at in (0, ext // 2):
        rows = slice(at, at + ext // 2)
        dnormed[rows, :] = back_half(held_near, hidden_near, rows) + back_half(held_far, hidden_far, rows)

    def put(start, rows, inner, j, value):
        if inner:
            out[start - HALO : start - HALO + rows, lane(j)] = value.astype(bf16)

    backward_norm(
        0, x, c, dy, source, ids, params, centred, rstd, branch, dnormed, dconv, small_c,
        bias_near, bias_far, side_give, side_keep, put, ext,
    )
    for i, ref in enumerate((first_out, out)):
        for r, piece in enumerate((out_keep0, out_give0, out_keep1, out_give1)):
            piece[i] = ref[:, lanes_of(x, c, r)]


def adamw(param, first, second, grad):
    first = beta_first * first + (1.0 - beta_first) * grad
    second = beta_second * second + (1.0 - beta_second) * grad * grad
    first_hat = first * (1.0 / (1.0 - beta_first**adam_step))
    second_hat = second * (1.0 / (1.0 - beta_second**adam_step))
    update = first_hat / (jnp.sqrt(second_hat) + adam_eps) + decay_rate * param
    return update, first, second


def halving_plan(n_dp, axes):
    bits = {"x": lambda k: k[0], "y": lambda k: k[1] & 1, "z": lambda k: (k[1] >> 1) & 1}
    keys = [[(i, d) for i in range(2) for d in range(n_dp)] for _ in axes]
    plan = []
    for now in zip(*axes):
        give = [[k for k in keys[m] if bits[axis](k)] for m, axis in enumerate(now)]
        keep = [[k for k in keys[m] if not bits[axis](k)] for m, axis in enumerate(now)]
        groups = [(0, 1)] if now[0] == now[1] else [(0,), (1,)]
        plan.append((give, keep, groups))
        keys = keep
    return plan


def side_to_packet(packet, value):
    rows = value.shape[0]
    at = packet.shape[0] - 2 * rows
    hi = value.astype(bf16)
    lo = (value - hi.astype(f32)).astype(bf16)
    packet[at : at + rows, :] = hi
    packet[at + rows :, :] = lo
    return hi.astype(f32) + lo.astype(f32)


def side_of(packet):
    at = packet.shape[0] - 64
    return packet[at : at + 32, :].astype(f32) + packet[at + 32 :, :].astype(f32)


def put_blocks(step, packets, helds, value_of):
    give, keep, groups = step
    rows = helds[0].shape[1]
    for packet, group in zip(packets, groups):
        at = 0
        for m in group:
            for key in give[m]:
                packet[at : at + rows, :] = value_of(m, key).astype(bf16)
                at += rows
    for m, held in enumerate(helds):
        for at, key in enumerate(keep[m]):
            held[at] = value_of(m, key)


def got_blocks(step, gots, helds):
    _, keep, groups = step
    rows = helds[0].shape[1]
    places = {}
    for got, group in zip(gots, groups):
        at = 0
        for m in group:
            for spot, key in enumerate(keep[m]):
                places[m, key] = (got, at, spot)
                at += rows

    def value_of(m, key):
        got, at, spot = places[m, key]
        return helds[m][spot] + got[at : at + rows, :].astype(f32)

    return value_of


def core_sum_kernel(plan, count, *refs):
    got = [ref.at[i] for ref in refs[:count] for i in range(ref.shape[0])]
    keep = refs[count : count + 4]
    packets, helds = refs[-2 - len(plan[0][2]) : -2], refs[-2:]

    def value_of(m, key):
        i, d = key
        return keep[2 * i + m][d] + got[2 * i + m][d].astype(f32)

    put_blocks(plan[0], packets, helds, value_of)


def step_sum_kernel(plan, step, *refs):
    count, outs = len(plan[step - 1][2]), len(plan[step][2])
    gots, helds, rest = refs[:count], refs[count : count + 2], refs[count + 2 :]
    packets, helds_out, side_out = refs[-3 - outs : -3], refs[-3:-1], refs[-1]
    put_blocks(plan[step], packets, helds_out, got_blocks(plan[step - 1], gots, helds))
    if step == 1:
        got_side, keep_side = rest[:2]
        side = jnp.concatenate(
            [keep_side[i] + (got_side[i, 0].astype(f32) + got_side[i, 1].astype(f32)) for i in range(2)], axis=0
        )
    else:
        side = rest[0][...] + side_of(gots[0])
    side_out[...] = side_to_packet(packets[0], side)


def line_start_kernel(plan, *refs):
    count = len(plan[-1][2])
    gots, helds, side = refs[:count], refs[count : count + 2], refs[count + 2]
    packet, out, side_out = refs[-3:]
    value_of = got_blocks(plan[-1], gots, helds)
    rows = helds[0].shape[1]
    keep = plan[-1][1]
    half = len(keep[0]) // 2
    for m in range(2):
        for at, key in enumerate(keep[m]):
            value = value_of(m, key)
            if at % 2:
                start = (m * half + at // 2) * rows
                packet[start : start + rows, :] = value.astype(bf16)
            else:
                out[m * half + at // 2] = value
    side_out[...] = side_to_packet(packet, side[...] + side_of(gots[0]))


def line_sum_kernel(got, held, side, *refs):
    packet, out, side_out = refs[-3:]
    count, rows, _ = held.shape
    for at in range(count):
        value = held[at] + got[at * rows : (at + 1) * rows, :].astype(f32)
        if at % 2:
            packet[(at // 2) * rows : (at // 2 + 1) * rows, :] = value.astype(bf16)
        else:
            out[at // 2] = value
    side_out[...] = side_to_packet(packet, side[...] + side_of(got))


def update_kernel(layer, got, held, side, up, down, m_up, v_up, m_down, v_down, *refs):
    sent, main, side_near, side_far = refs[-4:]
    size = main.shape[1]
    if sent.shape[0] > 2 * size:
        sent[2 * size :, :] = refs[0][...]
    rows = up.shape[0]
    for m in range(2):
        main[m] = held[m] + got[m * size : (m + 1) * size, :].astype(f32)
    total = side[...] + side_of(got)
    side_near[...] = total[0:16]
    hi = total[16:32].astype(bf16)
    side_far[0:16, :] = hi
    side_far[16:32, :] = (total[16:32] - hi.astype(f32)).astype(bf16)
    for m, (p, first, second) in enumerate(((up, m_up, v_up), (down, m_down, v_down))):
        for j in range(size // rows):
            cols, at = lane(j), j * rows
            u, _, _ = adamw(
                p[:, cols], first[layer, :, cols], second[layer, :, cols], main[m, at : at + rows]
            )
            sent[m * size + at : m * size + at + rows, :] = u.astype(bf16)


def adam_kernel(
    main0, main1, side0, side1, far, chan, bias,
    m_chan, v_chan, m_up, v_up, m_bias, v_bias, m_down, v_down,
    u_chan, u_bias, f_chan, s_chan, f_up, s_up, f_bias, s_bias, f_down, s_down, token,
):
    token[...] = jnp.zeros_like(token)
    rows = m_up.shape[1]
    base = far.shape[0] - 64
    for l, (main, side) in enumerate(((main0, side0), (main1, side1))):
        at = base + 32 * l
        g = side[...] + (far[at : at + 16, :].astype(f32) + far[at + 16 : at + 32, :].astype(f32))
        u_chan[:, l, :], f_chan[:, l, :], s_chan[:, l, :] = adamw(
            chan[:, l, :], m_chan[:, l, :], v_chan[:, l, :], g[0:12]
        )
        for j in range(main.shape[1] // rows):
            cols, at = lane(j), j * rows
            row = slice(l, l + 1)
            u_bias[row, cols], f_bias[row, cols], s_bias[row, cols] = adamw(
                bias[row, cols], m_bias[row, cols], v_bias[row, cols], g[12 + j : 13 + j]
            )
            _, f_up[l, :, cols], s_up[l, :, cols] = adamw(
                0.0, m_up[l, :, cols], v_up[l, :, cols], main[0, at : at + rows]
            )
            _, f_down[l, :, cols], s_down[l, :, cols] = adamw(
                0.0, m_down[l, :, cols], v_down[l, :, cols], main[1, at : at + rows]
            )


def ring_order(n_dp):
    return list(range(0, n_dp, 2)) + list(range(n_dp - 1, 0, -2))


def spread_kernel(layers, n_dp, parts, *refs):
    blocks = refs[: n_dp + 1]
    up_out, down_out, up, held, down, sems = refs[-6:]
    dp = lax.axis_index("dp")
    half = n_dp // 2
    spot = jnp.where(dp % 2 == 0, dp // 2, n_dp - 1 - dp // 2)

    def owner(distance):
        at = lax.rem(spot + distance + n_dp, n_dp)
        return jnp.where(at < half, 2 * at, 2 * (n_dp - 1 - at) + 1)

    distances = [0]
    for step in range(1, half):
        distances += [-step, step]
    rows = up.shape[1] // n_dp
    size = parts * rows
    copies = []
    for l in range(layers):
        start = 2 * size * l
        halves = [(d, ref, start, ref, start + size) for d, ref in zip(distances, blocks)]
        far = blocks[-2] if l == 0 else blocks[-1]
        halves.append((half, far, 0, far, size))
        for distance, first, first_at, second, second_at in halves:
            at = pl.ds(pl.multiple_of(owner(distance) * rows, rows), rows)
            for j in range(parts):
                start = first_at + j * rows
                up[l, at, lane(j)] = first[start : start + rows, :].astype(f32)
                start = second_at + j * rows
                held[at, lane(j)] = second[start : start + rows, :].astype(f32)
        copies += start_copies(pieces(up.at[l], up_out.at[l], 4), sems.at[pl.ds(8 * l, 4)])
        for j in range(parts):
            down[l, lane(j), :] = held[:, lane(j)].T
            pair = (down.at[l, lane(j)], down_out.at[l, lane(j)])
            copies += start_copies([pair], sems.at[pl.ds(8 * l + 4 + j, 1)])
    for copy in copies:
        copy.wait()


def pack_kernel(keep, got, side0, side1, _, packet):
    rows = keep.shape[1]
    for i, ref in enumerate((keep, got)):
        for o in range(2):
            at = (2 * i + o) * rows
            packet[at : at + rows, :] = ref[o]
    packet[4 * rows : 4 * rows + 32, :] = side0[...]
    packet[4 * rows + 32 :, :] = side1[...]


def collect_kernel(own, core, far, out, grad, token):
    token[...] = jnp.zeros_like(token)
    x, c, _ = place()
    rows = own.shape[1]
    for o, target in enumerate((out, grad)):
        for r in range(4):
            at = pl.multiple_of(((x ^ (r // 2)) * 2 + (c ^ (r % 2))) * rows, HALO)
            if r < 2:
                target[pl.ds(at, rows), :] = (own, core)[r][o]
            else:
                start = (2 * (r - 2) + o) * rows
                target[pl.ds(at, rows), :] = far[start : start + rows, :]


VMEM = pl.BlockSpec(memory_space=pltpu.VMEM)
ANY = pl.BlockSpec(memory_space=pl.ANY)
HBM = pl.BlockSpec(memory_space=pltpu.HBM)


def call(kernel, outs, in_specs, scratch, name, limit=16, out_specs=None, flops=0):
    return pl.pallas_call(
        kernel,
        out_shape=[jax.ShapeDtypeStruct(s, t) for s, t in outs],
        in_specs=in_specs,
        out_specs=out_specs or [VMEM] * len(outs),
        scratch_shapes=scratch,
        compiler_params=pltpu.CompilerParams(vmem_limit_bytes=limit * 1024 * 1024),
        cost_estimate=pl.CostEstimate(flops=flops, bytes_accessed=0, transcendentals=0),
        name=name,
    )


def on_device(
    n_dp, frames_in, segments, cotangent, channel_params, weight_up, bias_up, weight_down,
    momentum_channel, variance_channel, momentum_up, variance_up, momentum_bias, variance_bias,
    momentum_down, variance_down,
):
    rows, frames, part = frames_in.shape
    layers, width, quarter = weight_up.shape
    chip_hidden = 2 * quarter
    tokens = rows * frames
    own = tokens // 4
    ext = own + 2 * HALO
    shard = width // n_dp
    parts = quarter // LANES

    def core_swap(v):
        return lax.ppermute(v, "chan", xor_perm(4, 1))

    def x_swap(v):
        return lax.ppermute(v, "chan", xor_perm(4, 2))

    def dp_swap(v, bit):
        return lax.ppermute(v, "dp", xor_perm(n_dp, bit))

    def after(value, *others):
        return lax.optimization_barrier((value, *others))[0]

    sems = pltpu.SemaphoreType.DMA((8,))
    width_sems = pltpu.SemaphoreType.DMA((16,))
    chan, m_chan, v_chan = [
        jnp.swapaxes(v, 0, 1) for v in (channel_params, momentum_channel, variance_channel)
    ]
    up_held = pltpu.VMEM((width, quarter), f32)
    down_held = pltpu.VMEM((quarter, width), f32)
    matrix = ((width, quarter), bf16)

    def in_hbm(*arrays):
        return [pltpu.with_memory_space_constraint(v, pltpu.HBM) for v in arrays]

    packet = ((ext + 2 * PARAM_ROWS, LANES), bf16)
    flat = pltpu.VMEM((tokens + 2 * HALO, LANES), bf16)
    both_packets = ((2 * packet[0][0], LANES), bf16)
    give, here, beside, chosen0 = call(
        prepare_kernel, [both_packets, packet, packet, matrix], [HBM] * 5,
        [flat, pltpu.VMEM(chan.shape, f32), pltpu.VMEM(bias_up.shape, f32), up_held, down_held, sems, sems],
        "prepare",
    )(*in_hbm(frames_in, chan, bias_up, weight_up, weight_down))
    frames_far = x_swap(give)
    near0 = x_swap(chosen0)
    frames_core = core_swap(frames_far)
    packets = [here, core_swap(beside), frames_far, frames_core]
    cot_packet = ((ext, LANES), bf16)
    slice_shape = ((shard, quarter), f32)
    chosen1, *both, give, here, beside, ids, up0, down0, up1, down1 = call(
        rest_kernel,
        [matrix] * 5 + [((2 * ext, LANES), bf16)] + [cot_packet] * 2 + [((ext + 2 * PAD, LANES), jnp.int32)] + [slice_shape] * 4,
        [HBM] * 3 + [VMEM, ANY],
        [flat, pltpu.VMEM((tokens + 2 * HALO + 2 * PAD, LANES), jnp.int32)]
        + [pltpu.VMEM(weight_up.shape, f32), pltpu.VMEM(weight_down.shape, f32), up_held, sems, width_sems],
        "rest", 24, flops=LONG,
    )(*in_hbm(weight_up, weight_down, cotangent), segments, beside)
    near1 = x_swap(chosen1)
    slices0, slices1 = [up0, down0], [up1, down1]
    local0, local1 = [v + [core_swap(w) for w in v] for v in (both[:2], both[2:])]
    cots = [here, core_swap(beside)]

    wide = (ext, width)
    padded = (ext + 2 * PAD, width)
    deep = (ext, chip_hidden)
    held = pltpu.VMEM((2, width, chip_hidden), bf16)
    bias = pltpu.VMEM((1, chip_hidden), f32)
    sums = ((1, chip_hidden), f32)
    params_shape = ((PARAM_ROWS, width), f32)
    turned = ((width, own), bf16)
    norm_shapes = [(wide, f32), ((ext, LANES), f32), (wide, bf16)]
    half_shapes = [(deep, bf16), (deep, f32), (wide, f32)]
    size = parts * shard
    grads = [((2, n_dp, size, LANES), bf16)] + [((n_dp, size, LANES), f32)] * 2
    side_shapes = [((2, 2, 16, LANES), bf16), ((2, 16, LANES), f32)]
    norm_scratch = [pltpu.VMEM(padded, f32), pltpu.VMEM((16, width), f32)]

    def buffers(shapes):
        return [pltpu.VMEM(s, t) for s, t in shapes]

    first = call(
        first_kernel, norm_shapes + half_shapes + [(padded, f32), params_shape],
        [VMEM] * 9 + [ANY], [bias, held], "layer0_near", 24,
    )
    centred0, rstd0, normed0, active00, slope00, partial0, source0, params = first(
        ids, *packets, *local0, ids
    )
    cot_far = x_swap(after(give, near0))
    far0 = dp_swap(after(near0, chosen1), 1)
    far1 = dp_swap(after(near1, partial0), 1)
    pieces0 = call(split_kernel, [((width // 2, quarter), bf16)] * 2, [VMEM] + [ANY] * 2, [], "split")(
        far0, partial0, partial0
    )
    away0 = [near0, core_swap(near0), far0] + [core_swap(v) for v in pieces0]
    second = call(
        second_kernel, [(padded, f32)] + half_shapes, [VMEM] * 9 + [ANY],
        [bias, held], "layer0_far", 24,
    )
    source1, active01, slope01, branch0 = second(source0, params, normed0, partial0, *away0, partial0)
    third = call(
        third_kernel, norm_shapes + half_shapes, [VMEM] * 7 + [ANY],
        [bias, held], "layer1_near", 24,
    )
    centred1, rstd1, normed1, active10, slope10, partial1 = third(ids, source1, params, *local1, cots[1])
    cots += [cot_far, core_swap(cot_far)]
    fourth = call(
        fourth_kernel, [(wide, f32), (wide, bf16), turned, turned] + grads + [(wide, f32), sums],
        [VMEM] * 12, [pltpu.VMEM(deep, bf16), held], "layer1_near_back", 24,
    )
    dy1, low1, low_t1, normed_t1, give10, *keep10, dnormed1, bias10 = fourth(
        *cots, params, normed1, active10, slope10, *local1
    )
    got10 = core_swap(give10)
    away1 = [near1, core_swap(near1), far1, core_swap(after(far1, active10))]
    fifth = call(
        fifth_kernel, [(wide, f32), ((own, width), bf16)] + grads + [(wide, f32), sums],
        [VMEM] * 12,
        [bias] + buffers(half_shapes[:2]) + [pltpu.VMEM(deep, bf16), held], "layer1_far", 28, flops=LONG,
    )
    branch1, first_out, give11, *keep11, dnormed1, bias11 = fifth(
        source1, params, normed1, partial1, low1, low_t1, normed_t1, dnormed1, *away1
    )
    got11 = core_swap(give11)

    half = n_dp // 2
    plans = [halving_plan(n_dp, axes) for axes in AXES]
    side_shape = ((32, LANES), f32)

    def packet_of(blocks, side=False):
        return ((blocks * size + (64 if side else 0), LANES), bf16)

    def combine(kernel, outs, args, before, name, flops=0):
        specs = [VMEM] * len(args) + [ANY] * len(before)
        return call(kernel, outs, specs, [], name, flops=flops)(*args, *before)

    def step_outs(layer, step):
        give, keep, groups = plans[layer][step]
        outs = [packet_of(sum(len(give[m]) for m in g), step > 0 and n == 0) for n, g in enumerate(groups)]
        outs += [((len(k), size, LANES), f32) for k in keep]
        return outs + ([side_shape] if step else [])

    def exchange(layer, step, packets):
        swaps = {"x": x_swap, "y": lambda v: dp_swap(v, 1), "z": lambda v: dp_swap(v, 2)}
        groups = plans[layer][step][2]
        return [swaps[AXES[layer][g[0]][step]](v) for v, g in zip(packets, groups)]

    def core_step(layer, gots, keeps, before):
        kernel = functools.partial(core_sum_kernel, plans[layer], len(gots))
        outs = combine(kernel, step_outs(layer, 0), [*gots, *keeps], before, "core_sum")
        return outs[:-2], outs[-2:]

    def next_step(layer, step, got, helds, sides, before, flops=0):
        kernel = functools.partial(step_sum_kernel, plans[layer], step)
        outs = combine(kernel, step_outs(layer, step), [*got, *helds, *sides], before, "step_sum", flops)
        return outs[:-3], outs[-3:-1], outs[-1]

    def line_start(layer, got, helds, side, before):
        left = n_dp // 4
        outs = [packet_of(left, True), ((left, size, LANES), f32), side_shape]
        kernel = functools.partial(line_start_kernel, plans[layer])
        state = combine(kernel, outs, [*got, *helds, side], before, "line_start")
        bit = 4
        while bit < half:
            left //= 2
            outs = [packet_of(left, True), ((left, size, LANES), f32), side_shape]
            state = combine(line_sum_kernel, outs, [dp_swap(state[0], bit), *state[1:]], [], "line_sum")
            bit *= 2
        return state

    down_moments = [jnp.swapaxes(v, 1, 2) for v in (momentum_down, variance_down)]

    def update_step(layer, packet, main, side, slices, others, before):
        outs = [packet_of(2 + 2 * len(others)), ((2, size, LANES), f32)]
        outs += [((16, LANES), f32), ((32, LANES), bf16)]
        args = [dp_swap(packet, half), main, side, *slices, momentum_up, variance_up, *down_moments]
        args += others
        return combine(functools.partial(update_kernel, layer), outs, args, before, "update")

    order = ring_order(n_dp)
    ahead = [(order[i], order[(i + 1) % n_dp]) for i in range(n_dp)]
    back = [(b, a) for a, b in ahead]

    def ring_step(right, left):
        return lax.ppermute(right, "dp", ahead), lax.ppermute(left, "dp", back)

    def ring_end(right, left):
        cut = right.shape[0] // 2
        return lax.ppermute(right[:cut], "dp", ahead), lax.ppermute(left[cut:], "dp", back)

    def blocks_of(ring):
        return [ring[0][0]] + [v for pair in ring[1:] for v in pair]

    packets1, helds1 = core_step(1, [got10, got11], [*keep10, *keep11], [])
    sixth = call(
        sixth_kernel, [(wide, f32)] + side_shapes, [VMEM] * 10 + [ANY], norm_scratch, "layer1_norm_back", 24
    )
    grad1, *sides1 = sixth(
        ids, source1, params, centred1, rstd1, branch1, dy1, dnormed1, bias10, bias11, packets1[0]
    )
    seventh = call(
        seventh_kernel, [(deep, bf16)] * 2 + [((4, n_dp, size, LANES), bf16)] + [grads[1]] * 4 + [sums] * 2,
        [VMEM] * 16, buffers([(wide, bf16), turned, turned]) + [held, held],
        "layer0_back", 28,
    )
    hidden0, hidden1, *matrices0, bias00, bias01 = seventh(
        grad1, params, normed0, active00, slope00, active01, slope01, *local0, *away0
    )
    eighth = call(
        eighth_kernel, [((2, own, LANES), bf16)] * 4 + side_shapes, [VMEM] * 21 + [ANY],
        buffers([(wide, f32)]) + norm_scratch + buffers([((own, width), bf16)]) + [held, held],
        "layer0_norm_back", 28, flops=LONG,
    )
    give_near, give_far, keep_near, keep_far, *sides0 = eighth(
        ids, source0, params, centred0, rstd0, branch0, grad1, hidden0, hidden1, bias00, bias01, first_out,
        *local0, *away0, bias01,
    )

    sides = [core_swap(sides1[0]), sides1[1]]
    packets1, helds1, side1 = next_step(1, 1, exchange(1, 0, packets1), helds1, sides, [], LONG)
    packets0, helds0 = core_step(0, [core_swap(matrices0[0])], matrices0[1:], [packets1[0]])
    crossed0 = exchange(0, 0, packets0)
    sides = [core_swap(sides0[0]), sides0[1]]
    got = exchange(1, 1, packets1)
    packets1, helds1, side1 = next_step(1, 2, got, helds1, [side1], [])
    packets0, helds0, side0 = next_step(0, 1, crossed0, helds0, sides, [packets1[0]], LONG)
    got0 = exchange(0, 1, packets0)
    line1 = line_start(1, exchange(1, 2, packets1), helds1, side1, [])
    packets0, helds0, side0 = next_step(0, 2, got0, helds0, [side0], [line1[0]])
    sent1, main1, side1, side_far1 = update_step(1, *line1, slices1, [], [])
    line0 = line_start(0, exchange(0, 2, packets0), helds0, side0, [])
    sent, main0, side0, side_far0 = update_step(0, *line0, slices0, [sent1], [])
    ring = [(sent, sent)]
    ring.append(ring_step(sent, sent))

    got_near, got_far = core_swap(give_near), core_swap(give_far)
    far_packet = ((4 * own + 64, LANES), bf16)
    from_far = x_swap(
        call(pack_kernel, [far_packet], [VMEM] * 4 + [ANY], [], "pack")(
            keep_far, got_far, side_far0, side_far1, sent
        )[0]
    )
    token = ((8, LANES), f32)
    layer_output, input_grad, tokens_token = call(
        collect_kernel, [((tokens, part), bf16)] * 2 + [token], [VMEM] * 3, [], "collect"
    )(keep_near, got_near, from_far)

    adam_outs = [
        (chan.shape, f32),
        (bias_up.shape, f32),
        (chan.shape, f32),
        (chan.shape, f32),
        (momentum_up.shape, f32),
        (momentum_up.shape, f32),
        (bias_up.shape, f32),
        (bias_up.shape, f32),
        (down_moments[0].shape, f32),
        (down_moments[0].shape, f32),
        token,
    ]
    (
        params_channel, params_bias, first_channel, second_channel,
        first_up, second_up, first_bias, second_bias, first_down, second_down, adam_token,
    ) = call(adam_kernel, adam_outs, [VMEM] * 15, [], "adam")(
        main0, main1, side0, side1, from_far, chan, bias_up, m_chan, v_chan, momentum_up, variance_up,
        momentum_bias, variance_bias, *down_moments,
    )
    right, left = ring[1]
    for step in range(2, half):
        right, left = ring_step(right, left)
        ring.append((right, left))
    ring.append(ring_end(right, left))
    whole = [(weight_up.shape, f32), (weight_down.shape, f32)]
    spread = call(
        functools.partial(spread_kernel, layers, n_dp, parts), whole, [VMEM] * (n_dp + 1) + [ANY] * 2,
        [pltpu.VMEM(weight_up.shape, f32), up_held, pltpu.VMEM(weight_down.shape, f32), width_sems],
        "spread", 16, [HBM, HBM],
    )
    params_up, params_down = spread(*blocks_of(ring), tokens_token, adam_token)

    params_channel, first_channel, second_channel = [
        jnp.swapaxes(v, 0, 1) for v in (params_channel, first_channel, second_channel)
    ]
    first_down, second_down = jnp.swapaxes(first_down, 1, 2), jnp.swapaxes(second_down, 1, 2)

    layer_output, input_grad = [v.reshape(rows, frames, part) for v in (layer_output, input_grad)]
    return (
        layer_output,
        input_grad,
        params_channel,
        params_up,
        params_bias,
        params_down,
        first_channel,
        second_channel,
        first_up,
        second_up,
        first_bias,
        second_bias,
        first_down,
        second_down,
    )


def solution(mesh):
    return jax.shard_map(
        functools.partial(on_device, mesh.shape["dp"]),
        mesh=mesh,
        in_specs=(
            P("dp", None, "chan"),
            P("dp", None),
            P("dp", None, "chan"),
            P(None, None, "chan"),
            P(None, None, "chan"),
            P(None, "chan"),
            P(None, "chan", None),
            P(None, None, "chan"),
            P(None, None, "chan"),
            P(None, "dp", "chan"),
            P(None, "dp", "chan"),
            P(None, "chan"),
            P(None, "chan"),
            P(None, "chan", "dp"),
            P(None, "chan", "dp"),
        ),
        out_specs=(
            P("dp", None, "chan"),
            P("dp", None, "chan"),
            P(None, None, "chan"),
            P(None, None, "chan"),
            P(None, "chan"),
            P(None, "chan", None),
            P(None, None, "chan"),
            P(None, None, "chan"),
            P(None, "dp", "chan"),
            P(None, "dp", "chan"),
            P(None, "chan"),
            P(None, "chan"),
            P(None, "chan", "dp"),
            P(None, "chan", "dp"),
        ),
        check_vma=False,
    )
```

```python
import functools

import jax
import jax.numpy as jnp
from jax import lax
from jax.experimental import pallas as pl
from jax.experimental.pallas import tpu as pltpu
from jax.sharding import PartitionSpec as P

kernel_taps = 7
reach = kernel_taps // 2
norm_eps = 1e-06
beta_first = 0.8
beta_second = 0.9
adam_eps = 1e-08
decay_rate = 0.01
adam_step = 10.0

HALO = 16
PAD = 8
LANES = 128
PARAM_ROWS = 32
AXES = (("xyz", "yxz"), ("xzy", "yzx"))
LONG = 20_000_000_000
f32 = jnp.float32
bf16 = jnp.bfloat16


def xor_perm(size, bit):
    return [(i, i ^ bit) for i in range(size)]


def hi_lo(value):
    hi = lax.reduce_precision(value, 8, 7)
    return hi.astype(bf16), (value - hi).astype(bf16)


def place():
    me = lax.axis_index("chan")
    return me // 2, me % 2, lax.axis_index("dp")


def lanes_of(x, c, r):
    return pl.ds(pl.multiple_of(((x ^ (r // 2)) * 2 + (c ^ (r % 2))) * LANES, LANES), LANES)


def row_tiles(ext):
    own = ext - 2 * HALO
    tiles = [(0, HALO, False)]
    tiles += [(HALO + at, 32, True) for at in range(0, own, 32)]
    return tiles + [(HALO + own, HALO, False)]


def lane(j):
    return slice(j * LANES, (j + 1) * LANES)


def fold(value):
    return value.reshape(value.shape[0] // 8, 8, value.shape[1]).sum(axis=0)


def plus(total, value):
    return value if total is None else total + value


def column_sum(value):
    return jnp.sum(value, axis=0, keepdims=True)


def gelu_parts(h):
    tail = jnp.exp(-0.5 * h * h)
    d = 1.0 + (0.3275911 * 0.7071067811865476) * jnp.abs(h)
    t = pl.reciprocal(d, approx=True)
    t = t * (2.0 - d * t)
    poly = t * (
        0.127414796
        + t * (-0.142248368 + t * (0.7107068705 + t * (-0.7265760135 + t * 0.5307027145)))
    )
    low = poly * tail
    phi = jnp.where(h < 0.0, low, 1.0 - low)
    return h * phi, phi + h * tail * 0.3989422804014327


def load_frames(x, c, packets, ext, source):
    for r, ref in enumerate(packets):
        source[PAD : PAD + ext, lanes_of(x, c, r)] = ref[0:ext, :].astype(f32)
    clear_pads(source, ext)


def load_params(x, c, packets, ext, params):
    for r, ref in enumerate(packets):
        hi = ref[ext : ext + PARAM_ROWS, :].astype(f32)
        lo = ref[ext + PARAM_ROWS : ext + 2 * PARAM_ROWS, :].astype(f32)
        params[:, lanes_of(x, c, r)] = hi + lo


def clear_pads(ref, ext):
    zeros = jnp.zeros((PAD, ref.shape[1]), ref.dtype)
    ref[0:PAD, :] = zeros
    ref[PAD + ext : PAD + ext + PAD, :] = zeros


def load_bias(x, c, layer, chip, params, bias):
    width = bias.shape[1] // 2
    for r in range(2):
        rows = params[:, lanes_of(x, c, 2 * chip + r)]
        for j in range(width // LANES):
            k = 24 + layer * (width // LANES) + j
            bias[0:1, r * width + j * LANES : r * width + (j + 1) * LANES] = rows[k : k + 1]


def start_copies(pairs, sems):
    started = []
    for i, (src, dst) in enumerate(pairs):
        copy = pltpu.make_async_copy(src, dst, sems.at[i])
        copy.start()
        started.append(copy)
    return started


def hold_local(refs, held):
    width = refs[0].shape[-1]
    for i, ref in enumerate(refs):
        r, m = i // 2, i % 2
        held[m, :, r * width : (r + 1) * width] = ref[...]


def hold_far(y, refs, held):
    near, near_core, far, *far_core = refs
    width = near.shape[-1]
    held[y, :, 0:width] = near[...]
    held[1 - y, :, 0:width] = far[...]
    held[y, :, width:] = near_core[...]
    at = 0
    for ref in far_core:
        held[1 - y, at : at + ref.shape[0], width:] = ref[...]
        at += ref.shape[0]


def masks_at(ids, start, rows):
    here = ids[PAD + start : PAD + start + rows, :]
    masks = []
    for k in range(kernel_taps):
        at = PAD + start + k - reach
        masks.append(ids[at : at + rows, :] == here)
    return masks


def forward_norm(layer, source, ids, params, centred, rstd, normed, ext):
    width = source.shape[1]
    tiles = width // LANES
    base = layer * 12
    for start, rows, _ in row_tiles(ext):
        masks = masks_at(ids, start, rows)
        convs = []
        total = square = None
        for j in range(tiles):
            acc = params[base + 7 : base + 8, lane(j)]
            for k in range(kernel_taps):
                at = PAD + start + k - reach
                piece = source[at : at + rows, lane(j)]
                tap = params[base + k : base + k + 1, lane(j)]
                acc = acc + tap * (piece if k == reach else jnp.where(masks[k], piece, 0.0))
            convs.append(acc)
            total = plus(total, acc)
            square = plus(square, acc * acc)
        mean = jnp.sum(total, axis=1, keepdims=True) * (1.0 / width)
        var = jnp.sum(square, axis=1, keepdims=True) * (1.0 / width) - mean * mean
        scale = lax.rsqrt(var + norm_eps)
        rstd[start : start + rows, :] = jnp.broadcast_to(scale, (rows, LANES))
        for j in range(tiles):
            value = (convs[j] - mean) * scale
            centred[start : start + rows, lane(j)] = value
            gain = params[base + 8 : base + 9, lane(j)]
            shift = params[base + 9 : base + 10, lane(j)]
            normed[start : start + rows, lane(j)] = (value * gain + shift).astype(bf16)


def forward_half(bias, held, normed, active, slope, ext):
    quarter = held.shape[2] // 2
    half = ext // 2
    for r in range(2):
        cols = slice(r * quarter, (r + 1) * quarter)
        for at in (0, half):
            rows = slice(at, at + half)
            h = (
                jnp.dot(normed[rows, :], held[0, :, cols], preferred_element_type=f32)
                + bias[0:1, cols]
            )
            value, grad = gelu_parts(h)
            active[rows, cols] = value.astype(bf16)
            slope[rows, cols] = grad


def down_half(held, active, rows):
    return lax.dot_general(
        active[rows, :], held[1], (((1,), (1,)), ((), ())), preferred_element_type=f32
    )


def finish_branch(layer, source, params, held, active, partial, branch, ext, put):
    half = ext // 2
    base = layer * 12
    for at in (0, half):
        rows = slice(at, at + half)
        value = partial[rows, :] + down_half(held, active, rows) + params[base + 10 : base + 11, :]
        branch[rows, :] = value
        put(at, half, source[PAD + at : PAD + at + half, :] + params[base + 11 : base + 12, :] * value)


def branch_grad(layer, dy, params, low, ext):
    base = layer * 12
    for j in range(dy.shape[1] // LANES):
        scale = params[base + 11 : base + 12, lane(j)]
        for start, rows, _ in row_tiles(ext):
            low[start : start + rows, lane(j)] = (scale * dy[start : start + rows, lane(j)]).astype(bf16)


def put_grad(dp, out, parts, value):
    blocks, size, _ = out.shape
    rows = size // parts
    value = value.astype(out.dtype)
    for d in range(blocks):
        for j in range(parts):
            out[d ^ dp, j * rows : (j + 1) * rows] = value[d * rows : (d + 1) * rows, lane(j)]


def backward_half(dp, held, low, low_t, normed_t, active, slope, hidden_low, give, keep, bias_sums, ext):
    quarter = held.shape[2] // 2
    half = ext // 2
    inner = slice(HALO, ext - HALO)
    parts = quarter // LANES
    for r, out in ((0, keep), (1, give)):
        cols = slice(r * quarter, (r + 1) * quarter)
        sums = None
        for at in (0, half):
            rows = slice(at, at + half)
            grad = (
                jnp.dot(low[rows, :], held[1, :, cols], preferred_element_type=f32)
                * slope[rows, cols]
            )
            hidden_low[rows, cols] = grad.astype(bf16)
            sums = plus(sums, fold(grad[HALO:] if at == 0 else grad[: half - HALO]))
        bias_sums[0:1, cols] = column_sum(sums)
        put_grad(dp, out[1], parts, jnp.dot(low_t[...], active[inner, cols], preferred_element_type=f32))
        put_grad(
            dp, out[0], parts, jnp.dot(normed_t[...], hidden_low[inner, cols], preferred_element_type=f32)
        )


def back_half(held, hidden_low, rows):
    return lax.dot_general(
        hidden_low[rows, :], held[0], (((1,), (1,)), ((), ())), preferred_element_type=f32
    )


def backward_norm(
    layer, x, c, dy, source, ids, params, centred, rstd, branch, dnormed, dconv, small_c,
    bias_near, bias_far, side_give, side_keep, put, ext,
):
    width = source.shape[1]
    tiles = width // LANES
    quarter = bias_near.shape[1] // 2
    base = layer * 12
    small_c[...] = jnp.zeros_like(small_c)
    for j in range(tiles):
        scale = params[base + 11 : base + 12, lane(j)]
        sum_gamma = sum_bias = None
        for start, rows, inner in row_tiles(ext):
            if inner:
                grad = dy[start : start + rows, lane(j)]
                sum_gamma = plus(sum_gamma, fold(grad * branch[start : start + rows, lane(j)]))
                sum_bias = plus(sum_bias, fold(scale * grad))
        small_c[10:11, lane(j)] = column_sum(sum_bias)
        small_c[11:12, lane(j)] = column_sum(sum_gamma)

    clear_pads(dconv, ext)
    sums = [[None] * 3 for _ in range(tiles)]
    for start, rows, inner in row_tiles(ext):
        scale = rstd[start : start + rows, :]
        weighted, norms = [], []
        first = second = None
        for j in range(tiles):
            grad = dnormed[start : start + rows, lane(j)]
            norm = centred[start : start + rows, lane(j)]
            w = grad * params[base + 8 : base + 9, lane(j)]
            first = plus(first, w)
            second = plus(second, w * norm)
            weighted.append(w)
            norms.append(norm)
            if inner:
                sums[j][0] = plus(sums[j][0], fold(grad * norm))
                sums[j][1] = plus(sums[j][1], fold(grad))
        first = jnp.sum(first, axis=1, keepdims=True) * (1.0 / width)
        second = jnp.sum(second, axis=1, keepdims=True) * (1.0 / width)
        for j in range(tiles):
            value = scale * (weighted[j] - first - norms[j] * second)
            dconv[PAD + start : PAD + start + rows, lane(j)] = value
            if inner:
                sums[j][2] = plus(sums[j][2], fold(value))
    for j in range(tiles):
        small_c[8:9, lane(j)] = column_sum(sums[j][0])
        small_c[9:10, lane(j)] = column_sum(sums[j][1])
        small_c[7:8, lane(j)] = column_sum(sums[j][2])

    for j in range(tiles):
        taps = [params[base + k : base + k + 1, lane(j)] for k in range(kernel_taps)]
        sums = [None] * kernel_taps
        for start, rows, inner in row_tiles(ext):
            masks = masks_at(ids, start, rows)
            here = dconv[PAD + start : PAD + start + rows, lane(j)]
            total = dy[start : start + rows, lane(j)]
            for k in range(kernel_taps):
                mirror = kernel_taps - 1 - k
                at = PAD + start + mirror - reach
                piece = dconv[at : at + rows, lane(j)]
                total = total + taps[k] * (
                    piece if k == reach else jnp.where(masks[mirror], piece, 0.0)
                )
                if inner:
                    at = PAD + start + k - reach
                    piece = source[at : at + rows, lane(j)]
                    if k != reach:
                        piece = jnp.where(masks[k], piece, 0.0)
                    sums[k] = plus(sums[k], fold(piece * here))
            put(start, rows, inner, j, total)
        for k in range(kernel_taps):
            small_c[k : k + 1, lane(j)] = column_sum(sums[k])

    for r in range(4):
        sums = (bias_near if r < 2 else bias_far)[0:1, (r % 2) * quarter : (r % 2 + 1) * quarter]
        rows = [small_c[0:12, lanes_of(x, c, r)]]
        rows += [sums[:, lane(j)] for j in range(quarter // LANES)]
        rows += [jnp.zeros((16 - 12 - quarter // LANES, LANES), f32)]
        value = jnp.concatenate(rows, axis=0)
        if r % 2 == 0:
            side_keep[r // 2] = value
        else:
            hi = value.astype(bf16)
            side_give[r // 2, 0] = hi
            side_give[r // 2, 1] = (value - hi.astype(f32)).astype(bf16)


def start_rows(frames, flat, sems):
    rows, count, _ = frames.shape
    zeros = jnp.zeros((HALO, LANES), bf16)
    flat[0:HALO, :] = zeros
    flat[HALO + rows * count :, :] = zeros
    pairs = [(frames.at[r], flat.at[HALO + r * count : HALO + (r + 1) * count]) for r in range(rows)]
    return start_copies(pairs, sems)


def token_chunks(flat, own, outs):
    x, c, _ = place()
    ext = own + 2 * HALO
    for out, dx, dc in zip(outs, (1, 1, 0, 0), (0, 1, 0, 1)):
        at = pl.multiple_of(((x ^ dx) * 2 + (c ^ dc)) * own, HALO)
        out[0:ext, :] = flat[pl.ds(at, ext), :]


def pieces(source, target, count):
    rows = source.shape[0] // count
    cuts = [pl.ds(i * rows, rows) for i in range(count)]
    return [(source.at[cut], target.at[cut]) for cut in cuts]


def prepare_kernel(
    frames, chan_in, bias_in, up, down,
    give, here, beside, chosen, flat, chan, bias, up_held, down_held, sems, matrix_sems,
):
    x, c, dp = place()

    @pl.when(dp % 2 == 0)
    def start_up():
        start_copies(pieces(up.at[0], up_held, 4), matrix_sems)

    @pl.when(dp % 2 == 1)
    def start_down():
        start_copies(pieces(down.at[0], down_held, 4), matrix_sems)

    copies = start_rows(frames, flat, sems)
    smalls = start_copies([(chan_in, chan), (bias_in, bias)], sems.at[pl.ds(4, 2)])
    own = frames.shape[0] * frames.shape[1] // 4
    ext = own + 2 * HALO
    layers, parts = bias.shape[0], bias.shape[1] // LANES
    for copy in smalls:
        copy.wait()
    rows = [chan[:, l, :] for l in range(layers)]
    rows += [bias[l : l + 1, lane(j)] for l in range(layers) for j in range(parts)]
    rows += [jnp.zeros((PARAM_ROWS - (12 + parts) * layers, LANES), f32)]
    value = jnp.concatenate(rows, axis=0)
    hi = value.astype(bf16)
    lo = (value - hi.astype(f32)).astype(bf16)
    size = ext + 2 * PARAM_ROWS
    outs = (give.at[0:size], give.at[size:], here, beside)
    for out in outs:
        out[ext : ext + PARAM_ROWS, :] = hi
        out[ext + PARAM_ROWS :, :] = lo
    for copy in copies:
        copy.wait()
    token_chunks(flat, own, outs)

    @pl.when(dp % 2 == 0)
    def take_up():
        for i, (src, dst) in enumerate(pieces(up.at[0], up_held, 4)):
            pltpu.make_async_copy(src, dst, matrix_sems.at[i]).wait()
        chosen[...] = up_held[...].astype(bf16)

    @pl.when(dp % 2 == 1)
    def take_down():
        for i, (src, dst) in enumerate(pieces(down.at[0], down_held, 4)):
            pltpu.make_async_copy(src, dst, matrix_sems.at[i]).wait()
        chosen[...] = down_held[...].T.astype(bf16)


def split_kernel(whole, *refs):
    first, second = refs[-2:]
    first[...] = whole[0 : first.shape[0], :]
    second[...] = whole[first.shape[0] :, :]


def rest_kernel(
    up, down, frames, segments, _,
    chosen, w00, w01, w10, w11, give, here, beside, ids, up0, down0, up1, down1,
    flat, columns, up_held, down_held, turned, sems, matrix_sems,
):
    x, c, dp = place()
    layers = up.shape[0]
    matrices = []
    for l in reversed(range(layers)):
        pairs = pieces(up.at[l], up_held.at[l], 4) + pieces(down.at[l], down_held.at[l], 4)
        matrices.append(start_copies(pairs, matrix_sems.at[pl.ds(8 * l, 8)]))
    copies = start_rows(frames, flat, sems)
    shard = up0.shape[0]
    mine = pl.ds(pl.multiple_of(dp * shard, shard), shard)
    for l, started, both, up_slice, down_slice in (
        (1, matrices[0], (w10, w11), up1, down1),
        (0, matrices[1], (w00, w01), up0, down0),
    ):
        for copy in started:
            copy.wait()
        both[0][...] = up_held[l].astype(bf16)
        up_slice[...] = up_held[l, mine, :]
        turned[...] = down_held[l].T
        both[1][...] = turned[...].astype(bf16)
        down_slice[...] = turned[mine, :]

    @pl.when(dp % 2 == 0)
    def choose_up():
        chosen[...] = w10[...]

    @pl.when(dp % 2 == 1)
    def choose_down():
        chosen[...] = w11[...]

    for copy in copies:
        copy.wait()
    ext = here.shape[0]
    token_chunks(flat, ext - 2 * HALO, (give.at[0:ext], give.at[ext:], here, beside))

    rows, count = segments.shape
    tokens = rows * count
    edge = HALO + PAD
    none = jnp.full((edge, LANES), -1, jnp.int32)
    columns[0:edge, :] = none
    columns[edge + tokens :, :] = none
    for r in range(rows):
        row = jnp.broadcast_to(segments[r : r + 1, :] + 8 * r, (LANES, count))
        at = edge + r * count
        columns[at : at + count, :] = row.T
    at = pl.multiple_of((x * 2 + c) * (tokens // 4), HALO)
    ids[...] = columns[pl.ds(at, ids.shape[0]), :]


def first_kernel(
    ids, here, beside, near, far, own_up, own_down, core_up, core_down, _,
    centred, rstd, normed, active, slope, partial, source, params, bias, held,
):
    ext = ids.shape[0] - 2 * PAD
    x, c, _d = place()
    packets = (here, beside, near.at[0 : here.shape[0]], far.at[here.shape[0] :])
    load_frames(x, c, packets, ext, source)
    load_params(x, c, packets, ext, params)
    load_bias(x, c, 0, 0, params, bias)
    forward_norm(0, source, ids, params, centred, rstd, normed, ext)
    hold_local((own_up, own_down, core_up, core_down), held)
    forward_half(bias, held, normed, active, slope, ext)
    for at in (0, ext // 2):
        rows = slice(at, at + ext // 2)
        partial[rows, :] = down_half(held, active, rows)


def second_kernel(
    source, params, normed, partial, w_near, w_near_core, w_far, w_far_core0, w_far_core1, _,
    next_source, active, slope, branch, bias, held,
):
    ext = normed.shape[0]
    x, c, dp = place()
    load_bias(x, c, 0, 1, params, bias)
    clear_pads(next_source, ext)
    hold_far(dp % 2, (w_near, w_near_core, w_far, w_far_core0, w_far_core1), held)
    forward_half(bias, held, normed, active, slope, ext)

    def put(at, rows, value):
        next_source[PAD + at : PAD + at + rows, :] = value

    finish_branch(0, source, params, held, active, partial, branch, ext, put)


def third_kernel(
    ids, source, params, own_up, own_down, core_up, core_down, _,
    centred, rstd, normed, active, slope, partial, bias, held,
):
    ext = ids.shape[0] - 2 * PAD
    x, c, _d = place()
    load_bias(x, c, 1, 0, params, bias)
    forward_norm(1, source, ids, params, centred, rstd, normed, ext)
    hold_local((own_up, own_down, core_up, core_down), held)
    forward_half(bias, held, normed, active, slope, ext)
    for at in (0, ext // 2):
        rows = slice(at, at + ext // 2)
        partial[rows, :] = down_half(held, active, rows)


def fourth_kernel(
    cot_here, cot_beside, cot_near, cot_far, params, normed, active, slope, own_up, own_down, core_up, core_down,
    dy, low, low_t, normed_t, give, keep0, keep1, hidden_low, bias_sums, held,
):
    ext = dy.shape[0]
    x, c, dp = place()
    refs = (cot_here, cot_beside, cot_near.at[0:ext], cot_far.at[ext:])
    for r, ref in enumerate(refs):
        dy[:, lanes_of(x, c, r)] = ref[...].astype(f32)
    branch_grad(1, dy, params, low, ext)
    low_t[...] = low[HALO : ext - HALO, :].T
    normed_t[...] = normed[HALO : ext - HALO, :].T
    hold_local((own_up, own_down, core_up, core_down), held)
    backward_half(
        dp, held, low, low_t, normed_t, active, slope, hidden_low, (give.at[0], give.at[1]), (keep0, keep1), bias_sums, ext
    )


def fifth_kernel(
    params, normed, low, low_t, normed_t, w_near, w_near_core, w_far, w_far_core,
    give, keep0, keep1, bias_sums, active, hidden_low, held, bias, slope,
):
    ext = normed.shape[0]
    x, c, dp = place()
    load_bias(x, c, 1, 1, params, bias)
    hold_far(dp % 2, (w_near, w_near_core, w_far, w_far_core), held)
    forward_half(bias, held, normed, active, slope, ext)
    backward_half(
        dp, held, low, low_t, normed_t, active, slope, hidden_low, (give.at[0], give.at[1]), (keep0, keep1), bias_sums, ext
    )


def branch_kernel(
    source, params, partial, active, hidden_far, held_far, hidden_near, own_up, own_down, core_up, core_down, _,
    branch, out, dnormed, held_near,
):
    ext = partial.shape[0]
    hold_local((own_up, own_down, core_up, core_down), held_near)

    def put(at, rows, value):
        if at == 0:
            out[0 : rows - HALO, :] = value[HALO:].astype(bf16)
        else:
            out[at - HALO :, :] = value[: rows - HALO].astype(bf16)

    finish_branch(1, source, params, held_far, active, partial, branch, ext, put)
    for at in (0, ext // 2):
        rows = slice(at, at + ext // 2)
        dnormed[rows, :] = back_half(held_near, hidden_near, rows) + back_half(held_far, hidden_far, rows)


def sixth_kernel(
    ids, source, params, centred, rstd, branch, dy, dnormed, bias_near, bias_far, _,
    grad_source, side_give, side_keep, dconv, small_c,
):
    ext = dy.shape[0]
    x, c, _d = place()

    def put(start, rows, inner, j, value):
        grad_source[start : start + rows, lane(j)] = value

    backward_norm(
        1, x, c, dy, source, ids, params, centred, rstd, branch, dnormed, dconv, small_c,
        bias_near, bias_far, side_give, side_keep, put, ext,
    )


def seventh_kernel(
    dy, params, normed, active_near, slope_near, active_far, slope_far,
    own_up, own_down, core_up, core_down, w_near, w_near_core, w_far, w_far_core0, w_far_core1,
    hidden_near, hidden_far, give,
    keep_near0, keep_near1, keep_far0, keep_far1, bias_near, bias_far,
    low, low_t, normed_t, held_near, held_far,
):
    ext = dy.shape[0]
    _x, _c, dp = place()
    branch_grad(0, dy, params, low, ext)
    low_t[...] = low[HALO : ext - HALO, :].T
    normed_t[...] = normed[HALO : ext - HALO, :].T
    hold_local((own_up, own_down, core_up, core_down), held_near)
    hold_far(dp % 2, (w_near, w_near_core, w_far, w_far_core0, w_far_core1), held_far)
    backward_half(
        dp, held_near, low, low_t, normed_t, active_near, slope_near, hidden_near,
        (give.at[0], give.at[1]), (keep_near0, keep_near1), bias_near, ext,
    )
    backward_half(
        dp, held_far, low, low_t, normed_t, active_far, slope_far, hidden_far,
        (give.at[2], give.at[3]), (keep_far0, keep_far1), bias_far, ext,
    )


def eighth_kernel(
    ids, source, params, centred, rstd, branch, dy, hidden_near, hidden_far, bias_near, bias_far, first_out,
    own_up, own_down, core_up, core_down, w_near, w_near_core, w_far, w_far_core0, w_far_core1, _,
    out_give0, out_give1, out_keep0, out_keep1, side_give, side_keep,
    dnormed, dconv, small_c, out, held_near, held_far,
):
    ext = dy.shape[0]
    x, c, dp = place()
    hold_local((own_up, own_down, core_up, core_down), held_near)
    hold_far(dp % 2, (w_near, w_near_core, w_far, w_far_core0, w_far_core1), held_far)
    for at in (0, ext // 2):
        rows = slice(at, at + ext // 2)
        dnormed[rows, :] = back_half(held_near, hidden_near, rows) + back_half(held_far, hidden_far, rows)

    def put(start, rows, inner, j, value):
        if inner:
            out[start - HALO : start - HALO + rows, lane(j)] = value.astype(bf16)

    backward_norm(
        0, x, c, dy, source, ids, params, centred, rstd, branch, dnormed, dconv, small_c,
        bias_near, bias_far, side_give, side_keep, put, ext,
    )
    for i, ref in enumerate((first_out, out)):
        for r, piece in enumerate((out_keep0, out_give0, out_keep1, out_give1)):
            piece[i] = ref[:, lanes_of(x, c, r)]


def adamw(param, first, second, grad):
    first = beta_first * first + (1.0 - beta_first) * grad
    second = beta_second * second + (1.0 - beta_second) * grad * grad
    first_hat = first * (1.0 / (1.0 - beta_first**adam_step))
    second_hat = second * (1.0 / (1.0 - beta_second**adam_step))
    update = first_hat / (jnp.sqrt(second_hat) + adam_eps) + decay_rate * param
    return update, first, second


def halving_plan(n_dp, axes):
    bits = {"x": lambda k: k[0], "y": lambda k: k[1] & 1, "z": lambda k: (k[1] >> 1) & 1}
    keys = [[(i, d) for i in range(2) for d in range(n_dp)] for _ in axes]
    plan = []
    for now in zip(*axes):
        give = [[k for k in keys[m] if bits[axis](k)] for m, axis in enumerate(now)]
        keep = [[k for k in keys[m] if not bits[axis](k)] for m, axis in enumerate(now)]
        groups = [(0, 1)] if now[0] == now[1] else [(0,), (1,)]
        plan.append((give, keep, groups))
        keys = keep
    return plan


def side_to_packet(packet, value):
    rows = value.shape[0]
    at = packet.shape[0] - 2 * rows
    hi = value.astype(bf16)
    lo = (value - hi.astype(f32)).astype(bf16)
    packet[at : at + rows, :] = hi
    packet[at + rows :, :] = lo
    return hi.astype(f32) + lo.astype(f32)


def side_of(packet):
    at = packet.shape[0] - 64
    return packet[at : at + 32, :].astype(f32) + packet[at + 32 :, :].astype(f32)


def put_blocks(step, packets, helds, value_of):
    give, keep, groups = step
    rows = helds[0].shape[1]
    for packet, group in zip(packets, groups):
        at = 0
        for m in group:
            for key in give[m]:
                packet[at : at + rows, :] = value_of(m, key).astype(bf16)
                at += rows
    for m, held in enumerate(helds):
        for at, key in enumerate(keep[m]):
            held[at] = value_of(m, key)


def got_blocks(step, gots, helds):
    _, keep, groups = step
    rows = helds[0].shape[1]
    places = {}
    for got, group in zip(gots, groups):
        at = 0
        for m in group:
            for spot, key in enumerate(keep[m]):
                places[m, key] = (got, at, spot)
                at += rows

    def value_of(m, key):
        got, at, spot = places[m, key]
        return helds[m][spot] + got[at : at + rows, :].astype(f32)

    return value_of


def core_sum_kernel(plan, count, *refs):
    got = [ref.at[i] for ref in refs[:count] for i in range(ref.shape[0])]
    keep = refs[count : count + 4]
    packets, helds = refs[-2 - len(plan[0][2]) : -2], refs[-2:]

    def value_of(m, key):
        i, d = key
        return keep[2 * i + m][d] + got[2 * i + m][d].astype(f32)

    put_blocks(plan[0], packets, helds, value_of)


def step_sum_kernel(plan, step, *refs):
    count, outs = len(plan[step - 1][2]), len(plan[step][2])
    gots, helds, rest = refs[:count], refs[count : count + 2], refs[count + 2 :]
    packets, helds_out, side_out = refs[-3 - outs : -3], refs[-3:-1], refs[-1]
    put_blocks(plan[step], packets, helds_out, got_blocks(plan[step - 1], gots, helds))
    if step == 1:
        got_side, keep_side = rest[:2]
        side = jnp.concatenate(
            [keep_side[i] + (got_side[i, 0].astype(f32) + got_side[i, 1].astype(f32)) for i in range(2)], axis=0
        )
    else:
        side = rest[0][...] + side_of(gots[0])
    side_out[...] = side_to_packet(packets[0], side)


def line_start_kernel(plan, *refs):
    count = len(plan[-1][2])
    gots, helds, side = refs[:count], refs[count : count + 2], refs[count + 2]
    packet, out, side_out = refs[-3:]
    value_of = got_blocks(plan[-1], gots, helds)
    rows = helds[0].shape[1]
    keep = plan[-1][1]
    half = len(keep[0]) // 2
    for m in range(2):
        for at, key in enumerate(keep[m]):
            value = value_of(m, key)
            if at % 2:
                start = (m * half + at // 2) * rows
                packet[start : start + rows, :] = value.astype(bf16)
            else:
                out[m * half + at // 2] = value
    side_out[...] = side_to_packet(packet, side[...] + side_of(gots[0]))


def line_sum_kernel(got, held, side, *refs):
    packet, out, side_out = refs[-3:]
    count, rows, _ = held.shape
    for at in range(count):
        value = held[at] + got[at * rows : (at + 1) * rows, :].astype(f32)
        if at % 2:
            packet[(at // 2) * rows : (at // 2 + 1) * rows, :] = value.astype(bf16)
        else:
            out[at // 2] = value
    side_out[...] = side_to_packet(packet, side[...] + side_of(got))


def update_kernel(layer, got, held, side, up, down, m_up, v_up, m_down, v_down, *refs):
    sent, main, side_near, side_far = refs[-4:]
    size = main.shape[1]
    if sent.shape[0] > 2 * size:
        sent[2 * size :, :] = refs[0][...]
    rows = up.shape[0]
    for m in range(2):
        main[m] = held[m] + got[m * size : (m + 1) * size, :].astype(f32)
    total = side[...] + side_of(got)
    side_near[...] = total[0:16]
    hi = total[16:32].astype(bf16)
    side_far[0:16, :] = hi
    side_far[16:32, :] = (total[16:32] - hi.astype(f32)).astype(bf16)
    for m, (p, first, second) in enumerate(((up, m_up, v_up), (down, m_down, v_down))):
        for j in range(size // rows):
            cols, at = lane(j), j * rows
            u, _, _ = adamw(
                p[:, cols], first[layer, :, cols], second[layer, :, cols], main[m, at : at + rows]
            )
            sent[m * size + at : m * size + at + rows, :] = u.astype(bf16)


def adam_kernel(
    main0, main1, side0, side1, far, chan, bias,
    m_chan, v_chan, m_up, v_up, m_bias, v_bias, m_down, v_down,
    u_chan, u_bias, f_chan, s_chan, f_up, s_up, f_bias, s_bias, f_down, s_down, token,
):
    token[...] = jnp.zeros_like(token)
    rows = m_up.shape[1]
    base = far.shape[0] - 64
    for l, (main, side) in enumerate(((main0, side0), (main1, side1))):
        at = base + 32 * l
        g = side[...] + (far[at : at + 16, :].astype(f32) + far[at + 16 : at + 32, :].astype(f32))
        u_chan[:, l, :], f_chan[:, l, :], s_chan[:, l, :] = adamw(
            chan[:, l, :], m_chan[:, l, :], v_chan[:, l, :], g[0:12]
        )
        for j in range(main.shape[1] // rows):
            cols, at = lane(j), j * rows
            row = slice(l, l + 1)
            u_bias[row, cols], f_bias[row, cols], s_bias[row, cols] = adamw(
                bias[row, cols], m_bias[row, cols], v_bias[row, cols], g[12 + j : 13 + j]
            )
            _, f_up[l, :, cols], s_up[l, :, cols] = adamw(
                0.0, m_up[l, :, cols], v_up[l, :, cols], main[0, at : at + rows]
            )
            _, f_down[l, :, cols], s_down[l, :, cols] = adamw(
                0.0, m_down[l, :, cols], v_down[l, :, cols], main[1, at : at + rows]
            )


def ring_order(n_dp):
    return list(range(0, n_dp, 2)) + list(range(n_dp - 1, 0, -2))


def ring_owner(n_dp):
    dp = lax.axis_index("dp")
    half = n_dp // 2
    spot = jnp.where(dp % 2 == 0, dp // 2, n_dp - 1 - dp // 2)

    def owner(distance):
        at = lax.rem(spot + distance + n_dp, n_dp)
        return jnp.where(at < half, 2 * at, 2 * (n_dp - 1 - at) + 1)

    return owner


def far_group(n_dp, rows):
    first = ring_owner(n_dp)(n_dp // 2) * rows
    return first // LANES, pl.ds(pl.multiple_of(first % LANES, rows), rows)


def spread_kernel(layers, n_dp, parts, *refs):
    blocks = refs[: n_dp - 1]
    up_out, down_out, up_group, held_group, up, held, down, sems = refs[-8:]
    owner = ring_owner(n_dp)
    distances = [0]
    for step in range(1, n_dp // 2):
        distances += [-step, step]
    rows = up.shape[1] // n_dp
    size = parts * rows
    groups = up.shape[1] // LANES
    group, _ = far_group(n_dp, rows)

    def copies_of(l, k):
        part = pl.ds(k * LANES, LANES)
        pairs = ((up.at[l, part], up_out.at[l, part]), (down.at[l, :, part], down_out.at[l, :, part]))
        return [pltpu.make_async_copy(*pair, sems.at[2 * (l * groups + k) + i]) for i, pair in enumerate(pairs)]

    def each(l, k, act):
        def run():
            for copy in copies_of(l, k):
                act(copy)

        pl.when(group != k)(run)

    for l in range(layers):
        for distance, ref in zip(distances, blocks):
            at = pl.ds(pl.multiple_of(owner(distance) * rows, rows), rows)
            for j in range(parts):
                start = 2 * size * l + j * rows
                up[l, at, lane(j)] = ref[start : start + rows, :].astype(f32)
                start += size
                held[l, at, lane(j)] = ref[start : start + rows, :].astype(f32)
        for j in range(parts):
            down[l, lane(j), :] = held[l, :, lane(j)].T
        for k in range(groups):
            each(l, k, lambda copy: copy.start())
    whole = pl.ds(pl.multiple_of(group * LANES, LANES), LANES)
    for l in range(layers):
        up_group[l] = up[l, whole, :]
        held_group[l] = held[l, whole, :]
    for l in range(layers):
        for k in range(groups):
            each(l, k, lambda copy: copy.wait())


def last_spread_kernel(layers, n_dp, parts, top, bottom, up_group, held_group, *refs):
    up_out, down_out, up, held, down, sems = refs[-6:]
    rows = top.shape[0] // (2 * parts)
    size = parts * rows
    group, at = far_group(n_dp, rows)
    whole = pl.ds(pl.multiple_of(group * LANES, LANES), LANES)
    copies = []
    for l, far in enumerate((top, bottom)):
        up[l] = up_group[l]
        held[l] = held_group[l]
        for j in range(parts):
            up[l, at, lane(j)] = far[j * rows : (j + 1) * rows, :].astype(f32)
            held[l, at, lane(j)] = far[size + j * rows : size + (j + 1) * rows, :].astype(f32)
        for j in range(parts):
            down[l, lane(j), :] = held[l, :, lane(j)].T
        pairs = [(up.at[l], up_out.at[l, whole]), (down.at[l], down_out.at[l, :, whole])]
        copies += start_copies(pairs, sems.at[pl.ds(2 * l, 2)])
    for copy in copies:
        copy.wait()


def pack_kernel(keep, got, side0, side1, _, packet):
    rows = keep.shape[1]
    for i, ref in enumerate((keep, got)):
        for o in range(2):
            at = (2 * i + o) * rows
            packet[at : at + rows, :] = ref[o]
    packet[4 * rows : 4 * rows + 32, :] = side0[...]
    packet[4 * rows + 32 :, :] = side1[...]


def collect_kernel(own, core, far, out, grad, token):
    token[...] = jnp.zeros_like(token)
    x, c, _ = place()
    rows = own.shape[1]
    for o, target in enumerate((out, grad)):
        for r in range(4):
            at = pl.multiple_of(((x ^ (r // 2)) * 2 + (c ^ (r % 2))) * rows, HALO)
            if r < 2:
                target[pl.ds(at, rows), :] = (own, core)[r][o]
            else:
                start = (2 * (r - 2) + o) * rows
                target[pl.ds(at, rows), :] = far[start : start + rows, :]


VMEM = pl.BlockSpec(memory_space=pltpu.VMEM)
ANY = pl.BlockSpec(memory_space=pl.ANY)
HBM = pl.BlockSpec(memory_space=pltpu.HBM)


def call(kernel, outs, in_specs, scratch, name, limit=16, out_specs=None, flops=0, aliases=None):
    return pl.pallas_call(
        kernel,
        out_shape=[jax.ShapeDtypeStruct(s, t) for s, t in outs],
        in_specs=in_specs,
        out_specs=out_specs or [VMEM] * len(outs),
        scratch_shapes=scratch,
        input_output_aliases=aliases or {},
        compiler_params=pltpu.CompilerParams(vmem_limit_bytes=limit * 1024 * 1024),
        cost_estimate=pl.CostEstimate(flops=flops, bytes_accessed=0, transcendentals=0),
        name=name,
    )


def on_device(
    n_dp, frames_in, segments, cotangent, channel_params, weight_up, bias_up, weight_down,
    momentum_channel, variance_channel, momentum_up, variance_up, momentum_bias, variance_bias,
    momentum_down, variance_down,
):
    rows, frames, part = frames_in.shape
    layers, width, quarter = weight_up.shape
    chip_hidden = 2 * quarter
    tokens = rows * frames
    own = tokens // 4
    ext = own + 2 * HALO
    shard = width // n_dp
    parts = quarter // LANES

    def core_swap(v):
        return lax.ppermute(v, "chan", xor_perm(4, 1))

    def x_swap(v):
        return lax.ppermute(v, "chan", xor_perm(4, 2))

    def dp_swap(v, bit):
        return lax.ppermute(v, "dp", xor_perm(n_dp, bit))

    def after(value, *others):
        return lax.optimization_barrier((value, *others))[0]

    sems = pltpu.SemaphoreType.DMA((8,))
    width_sems = pltpu.SemaphoreType.DMA((16,))
    chan, m_chan, v_chan = [
        jnp.swapaxes(v, 0, 1) for v in (channel_params, momentum_channel, variance_channel)
    ]
    up_held = pltpu.VMEM((width, quarter), f32)
    down_held = pltpu.VMEM((quarter, width), f32)
    matrix = ((width, quarter), bf16)

    def in_hbm(*arrays):
        return [pltpu.with_memory_space_constraint(v, pltpu.HBM) for v in arrays]

    packet = ((ext + 2 * PARAM_ROWS, LANES), bf16)
    flat = pltpu.VMEM((tokens + 2 * HALO, LANES), bf16)
    both_packets = ((2 * packet[0][0], LANES), bf16)
    give, here, beside, chosen0 = call(
        prepare_kernel, [both_packets, packet, packet, matrix], [HBM] * 5,
        [flat, pltpu.VMEM(chan.shape, f32), pltpu.VMEM(bias_up.shape, f32), up_held, down_held, sems, sems],
        "prepare",
    )(*in_hbm(frames_in, chan, bias_up, weight_up, weight_down))
    frames_far = x_swap(give)
    near0 = x_swap(chosen0)
    frames_core = core_swap(frames_far)
    packets = [here, core_swap(beside), frames_far, frames_core]
    cot_packet = ((ext, LANES), bf16)
    slice_shape = ((shard, quarter), f32)
    chosen1, *both, give, here, beside, ids, up0, down0, up1, down1 = call(
        rest_kernel,
        [matrix] * 5 + [((2 * ext, LANES), bf16)] + [cot_packet] * 2 + [((ext + 2 * PAD, LANES), jnp.int32)] + [slice_shape] * 4,
        [HBM] * 3 + [VMEM, ANY],
        [flat, pltpu.VMEM((tokens + 2 * HALO + 2 * PAD, LANES), jnp.int32)]
        + [pltpu.VMEM(weight_up.shape, f32), pltpu.VMEM(weight_down.shape, f32), up_held, sems, width_sems],
        "rest", 24, flops=LONG,
    )(*in_hbm(weight_up, weight_down, cotangent), segments, beside)
    near1 = x_swap(chosen1)
    slices0, slices1 = [up0, down0], [up1, down1]
    local0, local1 = [v + [core_swap(w) for w in v] for v in (both[:2], both[2:])]
    cots = [here, core_swap(beside)]

    wide = (ext, width)
    padded = (ext + 2 * PAD, width)
    deep = (ext, chip_hidden)
    held = pltpu.VMEM((2, width, chip_hidden), bf16)
    bias = pltpu.VMEM((1, chip_hidden), f32)
    sums = ((1, chip_hidden), f32)
    params_shape = ((PARAM_ROWS, width), f32)
    turned = ((width, own), bf16)
    norm_shapes = [(wide, f32), ((ext, LANES), f32), (wide, bf16)]
    half_shapes = [(deep, bf16), (deep, f32), (wide, f32)]
    size = parts * shard
    grads = [((2, n_dp, size, LANES), bf16)] + [((n_dp, size, LANES), f32)] * 2
    side_shapes = [((2, 2, 16, LANES), bf16), ((2, 16, LANES), f32)]
    norm_scratch = [pltpu.VMEM(padded, f32), pltpu.VMEM((16, width), f32)]

    def buffers(shapes):
        return [pltpu.VMEM(s, t) for s, t in shapes]

    first = call(
        first_kernel, norm_shapes + half_shapes + [(padded, f32), params_shape],
        [VMEM] * 9 + [ANY], [bias, held], "layer0_near", 24,
    )
    centred0, rstd0, normed0, active00, slope00, partial0, source0, params = first(
        ids, *packets, *local0, ids
    )
    cot_far = x_swap(after(give, near0))
    far0 = dp_swap(after(near0, chosen1), 1)
    far1 = dp_swap(after(near1, partial0), 1)
    pieces0 = call(split_kernel, [((width // 2, quarter), bf16)] * 2, [VMEM] + [ANY] * 2, [], "split")(
        far0, partial0, partial0
    )
    away0 = [near0, core_swap(near0), far0] + [core_swap(v) for v in pieces0]
    second = call(
        second_kernel, [(padded, f32)] + half_shapes, [VMEM] * 9 + [ANY],
        [bias, held], "layer0_far", 24,
    )
    source1, active01, slope01, branch0 = second(source0, params, normed0, partial0, *away0, partial0)
    third = call(
        third_kernel, norm_shapes + half_shapes, [VMEM] * 7 + [ANY],
        [bias, held], "layer1_near", 24,
    )
    centred1, rstd1, normed1, active10, slope10, partial1 = third(ids, source1, params, *local1, cots[1])
    cots += [cot_far, core_swap(cot_far)]
    fourth = call(
        fourth_kernel, [(wide, f32), (wide, bf16), turned, turned] + grads + [(deep, bf16), sums],
        [VMEM] * 12, [held], "layer1_near_back", 24,
    )
    dy1, low1, low_t1, normed_t1, give10, *keep10, hidden10, bias10 = fourth(
        *cots, params, normed1, active10, slope10, *local1
    )
    got10 = core_swap(give10)
    away1 = [near1, core_swap(near1), far1, core_swap(after(far1, active10))]
    fifth = call(
        fifth_kernel, grads + [sums, (deep, bf16), (deep, bf16), ((2, width, chip_hidden), bf16)],
        [VMEM] * 9, [bias] + buffers([(deep, f32)]), "layer1_far", 28, flops=LONG,
    )
    give11, *keep11, bias11, active11, hidden11, held11 = fifth(
        params, normed1, low1, low_t1, normed_t1, *away1
    )
    got11 = core_swap(give11)
    branch1, first_out, dnormed1 = call(
        branch_kernel, [(wide, f32), ((own, width), bf16), (wide, f32)], [VMEM] * 11 + [ANY], [held],
        "layer1_branch", 24, flops=LONG,
    )(source1, params, partial1, active11, hidden11, held11, hidden10, *local1, bias11)

    half = n_dp // 2
    plans = [halving_plan(n_dp, axes) for axes in AXES]
    side_shape = ((32, LANES), f32)

    def packet_of(blocks, side=False):
        return ((blocks * size + (64 if side else 0), LANES), bf16)

    def combine(kernel, outs, args, before, name, flops=0):
        specs = [VMEM] * len(args) + [ANY] * len(before)
        return call(kernel, outs, specs, [], name, flops=flops)(*args, *before)

    def step_outs(layer, step):
        give, keep, groups = plans[layer][step]
        outs = [packet_of(sum(len(give[m]) for m in g), step > 0 and n == 0) for n, g in enumerate(groups)]
        outs += [((len(k), size, LANES), f32) for k in keep]
        return outs + ([side_shape] if step else [])

    def exchange(layer, step, packets):
        swaps = {"x": x_swap, "y": lambda v: dp_swap(v, 1), "z": lambda v: dp_swap(v, 2)}
        groups = plans[layer][step][2]
        return [swaps[AXES[layer][g[0]][step]](v) for v, g in zip(packets, groups)]

    def core_step(layer, gots, keeps, before):
        kernel = functools.partial(core_sum_kernel, plans[layer], len(gots))
        outs = combine(kernel, step_outs(layer, 0), [*gots, *keeps], before, "core_sum")
        return outs[:-2], outs[-2:]

    def next_step(layer, step, got, helds, sides, before, flops=0):
        kernel = functools.partial(step_sum_kernel, plans[layer], step)
        outs = combine(kernel, step_outs(layer, step), [*got, *helds, *sides], before, "step_sum", flops)
        return outs[:-3], outs[-3:-1], outs[-1]

    def line_start(layer, got, helds, side, before):
        left = n_dp // 4
        outs = [packet_of(left, True), ((left, size, LANES), f32), side_shape]
        kernel = functools.partial(line_start_kernel, plans[layer])
        state = combine(kernel, outs, [*got, *helds, side], before, "line_start")
        bit = 4
        while bit < half:
            left //= 2
            outs = [packet_of(left, True), ((left, size, LANES), f32), side_shape]
            state = combine(line_sum_kernel, outs, [dp_swap(state[0], bit), *state[1:]], [], "line_sum")
            bit *= 2
        return state

    down_moments = [jnp.swapaxes(v, 1, 2) for v in (momentum_down, variance_down)]

    def update_step(layer, packet, main, side, slices, others, before):
        outs = [packet_of(2 + 2 * len(others)), ((2, size, LANES), f32)]
        outs += [((16, LANES), f32), ((32, LANES), bf16)]
        args = [dp_swap(packet, half), main, side, *slices, momentum_up, variance_up, *down_moments]
        args += others
        return combine(functools.partial(update_kernel, layer), outs, args, before, "update")

    order = ring_order(n_dp)
    ahead = [(order[i], order[(i + 1) % n_dp]) for i in range(n_dp)]
    back = [(b, a) for a, b in ahead]

    def ring_step(right, left):
        return lax.ppermute(right, "dp", ahead), lax.ppermute(left, "dp", back)

    def ring_end(right, left):
        cut = right.shape[0] // 2
        return lax.ppermute(right[:cut], "dp", ahead), lax.ppermute(left[cut:], "dp", back)

    def blocks_of(ring):
        return [ring[0][0]] + [v for pair in ring[1:] for v in pair]

    packets1, helds1 = core_step(1, [got10, got11], [*keep10, *keep11], [branch1])
    sixth = call(
        sixth_kernel, [(wide, f32)] + side_shapes, [VMEM] * 10 + [ANY], norm_scratch, "layer1_norm_back", 24
    )
    grad1, *sides1 = sixth(
        ids, source1, params, centred1, rstd1, branch1, dy1, dnormed1, bias10, bias11, packets1[0]
    )
    seventh = call(
        seventh_kernel, [(deep, bf16)] * 2 + [((4, n_dp, size, LANES), bf16)] + [grads[1]] * 4 + [sums] * 2,
        [VMEM] * 16, buffers([(wide, bf16), turned, turned]) + [held, held],
        "layer0_back", 28,
    )
    hidden0, hidden1, *matrices0, bias00, bias01 = seventh(
        grad1, params, normed0, active00, slope00, active01, slope01, *local0, *away0
    )
    eighth = call(
        eighth_kernel, [((2, own, LANES), bf16)] * 4 + side_shapes, [VMEM] * 21 + [ANY],
        buffers([(wide, f32)]) + norm_scratch + buffers([((own, width), bf16)]) + [held, held],
        "layer0_norm_back", 28, flops=LONG,
    )
    give_near, give_far, keep_near, keep_far, *sides0 = eighth(
        ids, source0, params, centred0, rstd0, branch0, grad1, hidden0, hidden1, bias00, bias01, first_out,
        *local0, *away0, bias01,
    )

    sides = [core_swap(sides1[0]), sides1[1]]
    packets1, helds1, side1 = next_step(1, 1, exchange(1, 0, packets1), helds1, sides, [], LONG)
    packets0, helds0 = core_step(0, [core_swap(matrices0[0])], matrices0[1:], [packets1[0]])
    crossed0 = exchange(0, 0, packets0)
    sides = [core_swap(sides0[0]), sides0[1]]
    got = exchange(1, 1, packets1)
    packets1, helds1, side1 = next_step(1, 2, got, helds1, [side1], [])
    packets0, helds0, side0 = next_step(0, 1, crossed0, helds0, sides, [packets1[0]], LONG)
    got0 = exchange(0, 1, packets0)
    line1 = line_start(1, exchange(1, 2, packets1), helds1, side1, [])
    packets0, helds0, side0 = next_step(0, 2, got0, helds0, [side0], [line1[0]])
    sent1, main1, side1, side_far1 = update_step(1, *line1, slices1, [], [])
    line0 = line_start(0, exchange(0, 2, packets0), helds0, side0, [])
    sent, main0, side0, side_far0 = update_step(0, *line0, slices0, [sent1], [])
    ring = [(sent, sent)]
    ring.append(ring_step(sent, sent))

    got_near, got_far = core_swap(give_near), core_swap(give_far)
    far_packet = ((4 * own + 64, LANES), bf16)
    from_far = x_swap(
        call(pack_kernel, [far_packet], [VMEM] * 4 + [ANY], [], "pack")(
            keep_far, got_far, side_far0, side_far1, sent
        )[0]
    )
    token = ((8, LANES), f32)
    layer_output, input_grad, tokens_token = call(
        collect_kernel, [((tokens, part), bf16)] * 2 + [token], [VMEM] * 3, [], "collect"
    )(keep_near, got_near, from_far)

    adam_outs = [
        (chan.shape, f32),
        (bias_up.shape, f32),
        (chan.shape, f32),
        (chan.shape, f32),
        (momentum_up.shape, f32),
        (momentum_up.shape, f32),
        (bias_up.shape, f32),
        (bias_up.shape, f32),
        (down_moments[0].shape, f32),
        (down_moments[0].shape, f32),
        token,
    ]
    (
        params_channel, params_bias, first_channel, second_channel,
        first_up, second_up, first_bias, second_bias, first_down, second_down, adam_token,
    ) = call(adam_kernel, adam_outs, [VMEM] * 15, [], "adam")(
        main0, main1, side0, side1, from_far, chan, bias_up, m_chan, v_chan, momentum_up, variance_up,
        momentum_bias, variance_bias, *down_moments,
    )
    right, left = ring[1]
    for step in range(2, half):
        right, left = ring_step(right, left)
        ring.append((right, left))
    ring.append(ring_end(right, left))
    whole = [(weight_up.shape, f32), (weight_down.shape, f32)]
    group_shape = ((layers, LANES, quarter), f32)
    group_scratch = buffers([group_shape, group_shape, ((layers, quarter, LANES), f32)])
    spread = call(
        functools.partial(spread_kernel, layers, n_dp, parts), whole + [group_shape] * 2, [VMEM] * (n_dp - 1),
        buffers([(weight_up.shape, f32)] * 2 + [(weight_down.shape, f32)]) + [width_sems],
        "spread", 16, [HBM, HBM, VMEM, VMEM],
    )
    last_spread = call(
        functools.partial(last_spread_kernel, layers, n_dp, parts), whole, [VMEM] * 4 + [HBM] * 2 + [ANY] * 2,
        group_scratch + [sems], "last_spread", 16, [HBM, HBM], aliases={4: 0, 5: 1},
    )
    blocks = blocks_of(ring)
    params_up, params_down, *missing = spread(*blocks[:-2])
    params_up, params_down = last_spread(
        *blocks[-2:], *missing, params_up, params_down, tokens_token, adam_token
    )

    params_channel, first_channel, second_channel = [
        jnp.swapaxes(v, 0, 1) for v in (params_channel, first_channel, second_channel)
    ]
    first_down, second_down = jnp.swapaxes(first_down, 1, 2), jnp.swapaxes(second_down, 1, 2)

    layer_output, input_grad = [v.reshape(rows, frames, part) for v in (layer_output, input_grad)]
    return (
        layer_output,
        input_grad,
        params_channel,
        params_up,
        params_bias,
        params_down,
        first_channel,
        second_channel,
        first_up,
        second_up,
        first_bias,
        second_bias,
        first_down,
        second_down,
    )


def solution(mesh):
    return jax.shard_map(
        functools.partial(on_device, mesh.shape["dp"]),
        mesh=mesh,
        in_specs=(
            P("dp", None, "chan"),
            P("dp", None),
            P("dp", None, "chan"),
            P(None, None, "chan"),
            P(None, None, "chan"),
            P(None, "chan"),
            P(None, "chan", None),
            P(None, None, "chan"),
            P(None, None, "chan"),
            P(None, "dp", "chan"),
            P(None, "dp", "chan"),
            P(None, "chan"),
            P(None, "chan"),
            P(None, "chan", "dp"),
            P(None, "chan", "dp"),
        ),
        out_specs=(
            P("dp", None, "chan"),
            P("dp", None, "chan"),
            P(None, None, "chan"),
            P(None, None, "chan"),
            P(None, "chan"),
            P(None, "chan", None),
            P(None, None, "chan"),
            P(None, None, "chan"),
            P(None, "dp", "chan"),
            P(None, "dp", "chan"),
            P(None, "chan"),
            P(None, "chan"),
            P(None, "chan", "dp"),
            P(None, "chan", "dp"),
        ),
        check_vma=False,
    )
```

```python
import functools

import jax
import jax.numpy as jnp
from jax import lax
from jax.experimental import pallas as pl
from jax.experimental.pallas import tpu as pltpu
from jax.sharding import PartitionSpec as P

kernel_taps = 7
reach = kernel_taps // 2
norm_eps = 1e-06
beta_first = 0.8
beta_second = 0.9
adam_eps = 1e-08
decay_rate = 0.01
adam_step = 10.0

HALO = 16
PAD = 8
LANES = 128
PARAM_ROWS = 32
AXES = (("xyz", "yxz"), ("xzy", "yzx"))
LONG = 20_000_000_000
f32 = jnp.float32
bf16 = jnp.bfloat16


def xor_perm(size, bit):
    return [(i, i ^ bit) for i in range(size)]


def hi_lo(value):
    hi = lax.reduce_precision(value, 8, 7)
    return hi.astype(bf16), (value - hi).astype(bf16)


def place():
    me = lax.axis_index("chan")
    return me // 2, me % 2, lax.axis_index("dp")


def lanes_of(x, c, r):
    return pl.ds(pl.multiple_of(((x ^ (r // 2)) * 2 + (c ^ (r % 2))) * LANES, LANES), LANES)


def row_tiles(ext):
    own = ext - 2 * HALO
    tiles = [(0, HALO, False)]
    tiles += [(HALO + at, 32, True) for at in range(0, own, 32)]
    return tiles + [(HALO + own, HALO, False)]


def lane(j):
    return slice(j * LANES, (j + 1) * LANES)


def fold(value):
    return value.reshape(value.shape[0] // 8, 8, value.shape[1]).sum(axis=0)


def plus(total, value):
    return value if total is None else total + value


def column_sum(value):
    return jnp.sum(value, axis=0, keepdims=True)


def gelu_parts(h):
    tail = jnp.exp2(h * h * -0.7213475204444817)
    d = 1.0 + (0.3275911 * 0.7071067811865476) * jnp.abs(h)
    t = pl.reciprocal(d, approx=True)
    t = t * (2.0 - d * t)
    poly = t * (
        0.127414796
        + t * (-0.142248368 + t * (0.7107068705 + t * (-0.7265760135 + t * 0.5307027145)))
    )
    low = poly * tail
    phi = jnp.where(h < 0.0, low, 1.0 - low)
    return h * phi, phi + h * tail * 0.3989422804014327


def load_frames(x, c, packets, ext, source):
    for r, ref in enumerate(packets):
        source[PAD : PAD + ext, lanes_of(x, c, r)] = ref[0:ext, :].astype(f32)
    clear_pads(source, ext)


def load_params(x, c, packets, ext, params):
    for r, ref in enumerate(packets):
        hi = ref[ext : ext + PARAM_ROWS, :].astype(f32)
        lo = ref[ext + PARAM_ROWS : ext + 2 * PARAM_ROWS, :].astype(f32)
        params[:, lanes_of(x, c, r)] = hi + lo


def clear_pads(ref, ext):
    zeros = jnp.zeros((PAD, ref.shape[1]), ref.dtype)
    ref[0:PAD, :] = zeros
    ref[PAD + ext : PAD + ext + PAD, :] = zeros


def load_bias(x, c, layer, chip, params, bias):
    width = bias.shape[1] // 2
    for r in range(2):
        rows = params[:, lanes_of(x, c, 2 * chip + r)]
        for j in range(width // LANES):
            k = 24 + layer * (width // LANES) + j
            bias[0:1, r * width + j * LANES : r * width + (j + 1) * LANES] = rows[k : k + 1]


def start_copies(pairs, sems):
    started = []
    for i, (src, dst) in enumerate(pairs):
        copy = pltpu.make_async_copy(src, dst, sems.at[i])
        copy.start()
        started.append(copy)
    return started


def hold_local(refs, held):
    width = refs[0].shape[-1]
    for i, ref in enumerate(refs):
        r, m = i // 2, i % 2
        held[m, :, r * width : (r + 1) * width] = ref[...]


def hold_far(y, refs, held):
    near, near_core, far, *far_core = refs
    width = near.shape[-1]
    held[y, :, 0:width] = near[...]
    held[1 - y, :, 0:width] = far[...]
    held[y, :, width:] = near_core[...]
    at = 0
    for ref in far_core:
        held[1 - y, at : at + ref.shape[0], width:] = ref[...]
        at += ref.shape[0]


def masks_at(ids, start, rows):
    here = ids[PAD + start : PAD + start + rows, :]
    masks = []
    for k in range(kernel_taps):
        at = PAD + start + k - reach
        masks.append(ids[at : at + rows, :] == here)
    return masks


def forward_norm(layer, source, ids, params, centred, rstd, normed, ext):
    width = source.shape[1]
    tiles = width // LANES
    base = layer * 12
    for start, rows, _ in row_tiles(ext):
        masks = masks_at(ids, start, rows)
        convs = []
        total = square = None
        for j in range(tiles):
            acc = params[base + 7 : base + 8, lane(j)]
            for k in range(kernel_taps):
                at = PAD + start + k - reach
                piece = source[at : at + rows, lane(j)]
                tap = params[base + k : base + k + 1, lane(j)]
                acc = acc + tap * (piece if k == reach else jnp.where(masks[k], piece, 0.0))
            convs.append(acc)
            total = plus(total, acc)
            square = plus(square, acc * acc)
        mean = jnp.sum(total, axis=1, keepdims=True) * (1.0 / width)
        var = jnp.sum(square, axis=1, keepdims=True) * (1.0 / width) - mean * mean
        scale = lax.rsqrt(var + norm_eps)
        rstd[start : start + rows, :] = jnp.broadcast_to(scale, (rows, LANES))
        for j in range(tiles):
            value = (convs[j] - mean) * scale
            centred[start : start + rows, lane(j)] = value
            gain = params[base + 8 : base + 9, lane(j)]
            shift = params[base + 9 : base + 10, lane(j)]
            normed[start : start + rows, lane(j)] = (value * gain + shift).astype(bf16)


def forward_half(bias, held, normed, active, slope, ext):
    quarter = held.shape[2] // 2
    half = ext // 2
    for r in range(2):
        cols = slice(r * quarter, (r + 1) * quarter)
        for at in (0, half):
            rows = slice(at, at + half)
            h = (
                jnp.dot(normed[rows, :], held[0, :, cols], preferred_element_type=f32)
                + bias[0:1, cols]
            )
            value, grad = gelu_parts(h)
            active[rows, cols] = value.astype(bf16)
            slope[rows, cols] = grad


def down_half(held, active, rows):
    return lax.dot_general(
        active[rows, :], held[1], (((1,), (1,)), ((), ())), preferred_element_type=f32
    )


def finish_branch(layer, source, params, held, active, partial, branch, ext, put):
    half = ext // 2
    base = layer * 12
    for at in (0, half):
        rows = slice(at, at + half)
        value = partial[rows, :] + down_half(held, active, rows) + params[base + 10 : base + 11, :]
        branch[rows, :] = value
        put(at, half, source[PAD + at : PAD + at + half, :] + params[base + 11 : base + 12, :] * value)


def branch_grad(layer, dy, params, low, ext):
    base = layer * 12
    for j in range(dy.shape[1] // LANES):
        scale = params[base + 11 : base + 12, lane(j)]
        for start, rows, _ in row_tiles(ext):
            low[start : start + rows, lane(j)] = (scale * dy[start : start + rows, lane(j)]).astype(bf16)


def put_grad(dp, out, parts, value):
    blocks, size, _ = out.shape
    rows = size // parts
    value = value.astype(out.dtype)
    for d in range(blocks):
        for j in range(parts):
            out[d ^ dp, j * rows : (j + 1) * rows] = value[d * rows : (d + 1) * rows, lane(j)]


def backward_half(dp, held, low, low_t, normed_t, active, slope, hidden_low, give, keep, bias_sums, ext):
    quarter = held.shape[2] // 2
    half = ext // 2
    inner = slice(HALO, ext - HALO)
    parts = quarter // LANES
    for r, out in ((0, keep), (1, give)):
        cols = slice(r * quarter, (r + 1) * quarter)
        sums = None
        for at in (0, half):
            rows = slice(at, at + half)
            grad = (
                jnp.dot(low[rows, :], held[1, :, cols], preferred_element_type=f32)
                * slope[rows, cols]
            )
            hidden_low[rows, cols] = grad.astype(bf16)
            sums = plus(sums, fold(grad[HALO:] if at == 0 else grad[: half - HALO]))
        bias_sums[0:1, cols] = column_sum(sums)
        put_grad(dp, out[1], parts, jnp.dot(low_t[...], active[inner, cols], preferred_element_type=f32))
        put_grad(
            dp, out[0], parts, jnp.dot(normed_t[...], hidden_low[inner, cols], preferred_element_type=f32)
        )


def back_half(held, hidden_low, rows):
    return lax.dot_general(
        hidden_low[rows, :], held[0], (((1,), (1,)), ((), ())), preferred_element_type=f32
    )


def backward_norm(
    layer, x, c, dy, source, ids, params, centred, rstd, branch, dnormed, dconv, small_c,
    bias_near, bias_far, side_give, side_keep, put, ext,
):
    width = source.shape[1]
    tiles = width // LANES
    quarter = bias_near.shape[1] // 2
    base = layer * 12
    small_c[...] = jnp.zeros_like(small_c)
    for j in range(tiles):
        scale = params[base + 11 : base + 12, lane(j)]
        sum_gamma = sum_bias = None
        for start, rows, inner in row_tiles(ext):
            if inner:
                grad = dy[start : start + rows, lane(j)]
                sum_gamma = plus(sum_gamma, fold(grad * branch[start : start + rows, lane(j)]))
                sum_bias = plus(sum_bias, fold(scale * grad))
        small_c[10:11, lane(j)] = column_sum(sum_bias)
        small_c[11:12, lane(j)] = column_sum(sum_gamma)

    clear_pads(dconv, ext)
    sums = [[None] * 3 for _ in range(tiles)]
    for start, rows, inner in row_tiles(ext):
        scale = rstd[start : start + rows, :]
        weighted, norms = [], []
        first = second = None
        for j in range(tiles):
            grad = dnormed[start : start + rows, lane(j)]
            norm = centred[start : start + rows, lane(j)]
            w = grad * params[base + 8 : base + 9, lane(j)]
            first = plus(first, w)
            second = plus(second, w * norm)
            weighted.append(w)
            norms.append(norm)
            if inner:
                sums[j][0] = plus(sums[j][0], fold(grad * norm))
                sums[j][1] = plus(sums[j][1], fold(grad))
        first = jnp.sum(first, axis=1, keepdims=True) * (1.0 / width)
        second = jnp.sum(second, axis=1, keepdims=True) * (1.0 / width)
        for j in range(tiles):
            value = scale * (weighted[j] - first - norms[j] * second)
            dconv[PAD + start : PAD + start + rows, lane(j)] = value
            if inner:
                sums[j][2] = plus(sums[j][2], fold(value))
    for j in range(tiles):
        small_c[8:9, lane(j)] = column_sum(sums[j][0])
        small_c[9:10, lane(j)] = column_sum(sums[j][1])
        small_c[7:8, lane(j)] = column_sum(sums[j][2])

    for j in range(tiles):
        taps = [params[base + k : base + k + 1, lane(j)] for k in range(kernel_taps)]
        sums = [None] * kernel_taps
        for start, rows, inner in row_tiles(ext):
            masks = masks_at(ids, start, rows)
            here = dconv[PAD + start : PAD + start + rows, lane(j)]
            total = dy[start : start + rows, lane(j)]
            for k in range(kernel_taps):
                mirror = kernel_taps - 1 - k
                at = PAD + start + mirror - reach
                piece = dconv[at : at + rows, lane(j)]
                total = total + taps[k] * (
                    piece if k == reach else jnp.where(masks[mirror], piece, 0.0)
                )
                if inner:
                    at = PAD + start + k - reach
                    piece = source[at : at + rows, lane(j)]
                    if k != reach:
                        piece = jnp.where(masks[k], piece, 0.0)
                    sums[k] = plus(sums[k], fold(piece * here))
            put(start, rows, inner, j, total)
        for k in range(kernel_taps):
            small_c[k : k + 1, lane(j)] = column_sum(sums[k])

    for r in range(4):
        sums = (bias_near if r < 2 else bias_far)[0:1, (r % 2) * quarter : (r % 2 + 1) * quarter]
        rows = [small_c[0:12, lanes_of(x, c, r)]]
        rows += [sums[:, lane(j)] for j in range(quarter // LANES)]
        rows += [jnp.zeros((16 - 12 - quarter // LANES, LANES), f32)]
        value = jnp.concatenate(rows, axis=0)
        if r % 2 == 0:
            side_keep[r // 2] = value
        else:
            hi = value.astype(bf16)
            side_give[r // 2, 0] = hi
            side_give[r // 2, 1] = (value - hi.astype(f32)).astype(bf16)


def start_rows(frames, flat, sems):
    rows, count, _ = frames.shape
    zeros = jnp.zeros((HALO, LANES), bf16)
    flat[0:HALO, :] = zeros
    flat[HALO + rows * count :, :] = zeros
    pairs = [(frames.at[r], flat.at[HALO + r * count : HALO + (r + 1) * count]) for r in range(rows)]
    return start_copies(pairs, sems)


def token_chunks(flat, own, outs):
    x, c, _ = place()
    ext = own + 2 * HALO
    for out, dx, dc in zip(outs, (1, 1, 0, 0), (0, 1, 0, 1)):
        at = pl.multiple_of(((x ^ dx) * 2 + (c ^ dc)) * own, HALO)
        out[0:ext, :] = flat[pl.ds(at, ext), :]


def pieces(source, target, count):
    rows = source.shape[0] // count
    cuts = [pl.ds(i * rows, rows) for i in range(count)]
    return [(source.at[cut], target.at[cut]) for cut in cuts]


def prepare_kernel(
    frames, chan_in, bias_in, up, down,
    give, here, beside, chosen, flat, chan, bias, up_held, down_held, sems, matrix_sems,
):
    x, c, dp = place()

    @pl.when(dp % 2 == 0)
    def start_up():
        start_copies(pieces(up.at[0], up_held, 4), matrix_sems)

    @pl.when(dp % 2 == 1)
    def start_down():
        start_copies(pieces(down.at[0], down_held, 4), matrix_sems)

    copies = start_rows(frames, flat, sems)
    smalls = start_copies([(chan_in, chan), (bias_in, bias)], sems.at[pl.ds(4, 2)])
    own = frames.shape[0] * frames.shape[1] // 4
    ext = own + 2 * HALO
    layers, parts = bias.shape[0], bias.shape[1] // LANES
    for copy in smalls:
        copy.wait()
    rows = [chan[:, l, :] for l in range(layers)]
    rows += [bias[l : l + 1, lane(j)] for l in range(layers) for j in range(parts)]
    rows += [jnp.zeros((PARAM_ROWS - (12 + parts) * layers, LANES), f32)]
    value = jnp.concatenate(rows, axis=0)
    hi = value.astype(bf16)
    lo = (value - hi.astype(f32)).astype(bf16)
    size = ext + 2 * PARAM_ROWS
    outs = (give.at[0:size], give.at[size:], here, beside)
    for out in outs:
        out[ext : ext + PARAM_ROWS, :] = hi
        out[ext + PARAM_ROWS :, :] = lo
    for copy in copies:
        copy.wait()
    token_chunks(flat, own, outs)

    @pl.when(dp % 2 == 0)
    def take_up():
        for i, (src, dst) in enumerate(pieces(up.at[0], up_held, 4)):
            pltpu.make_async_copy(src, dst, matrix_sems.at[i]).wait()
        chosen[...] = up_held[...].astype(bf16)

    @pl.when(dp % 2 == 1)
    def take_down():
        for i, (src, dst) in enumerate(pieces(down.at[0], down_held, 4)):
            pltpu.make_async_copy(src, dst, matrix_sems.at[i]).wait()
        chosen[...] = down_held[...].T.astype(bf16)


def split_kernel(whole, *refs):
    first, second = refs[-2:]
    first[...] = whole[0 : first.shape[0], :]
    second[...] = whole[first.shape[0] :, :]


def rest_kernel(
    up, down, frames, segments, _,
    chosen, w00, w01, w10, w11, give, here, beside, ids, up0, down0, up1, down1,
    flat, columns, up_held, down_held, turned, sems, matrix_sems,
):
    x, c, dp = place()
    layers = up.shape[0]
    matrices = []
    for l in reversed(range(layers)):
        pairs = pieces(up.at[l], up_held.at[l], 4) + pieces(down.at[l], down_held.at[l], 4)
        matrices.append(start_copies(pairs, matrix_sems.at[pl.ds(8 * l, 8)]))
    copies = start_rows(frames, flat, sems)
    shard = up0.shape[0]
    mine = pl.ds(pl.multiple_of(dp * shard, shard), shard)
    for l, started, both, up_slice, down_slice in (
        (1, matrices[0], (w10, w11), up1, down1),
        (0, matrices[1], (w00, w01), up0, down0),
    ):
        for copy in started:
            copy.wait()
        both[0][...] = up_held[l].astype(bf16)
        up_slice[...] = up_held[l, mine, :]
        turned[...] = down_held[l].T
        both[1][...] = turned[...].astype(bf16)
        down_slice[...] = turned[mine, :]

    @pl.when(dp % 2 == 0)
    def choose_up():
        chosen[...] = w10[...]

    @pl.when(dp % 2 == 1)
    def choose_down():
        chosen[...] = w11[...]

    for copy in copies:
        copy.wait()
    ext = here.shape[0]
    token_chunks(flat, ext - 2 * HALO, (give.at[0:ext], give.at[ext:], here, beside))

    rows, count = segments.shape
    tokens = rows * count
    edge = HALO + PAD
    none = jnp.full((edge, LANES), -1, jnp.int32)
    columns[0:edge, :] = none
    columns[edge + tokens :, :] = none
    for r in range(rows):
        row = jnp.broadcast_to(segments[r : r + 1, :] + 8 * r, (LANES, count))
        at = edge + r * count
        columns[at : at + count, :] = row.T
    at = pl.multiple_of((x * 2 + c) * (tokens // 4), HALO)
    ids[...] = columns[pl.ds(at, ids.shape[0]), :]


def first_kernel(
    ids, here, beside, near, far, own_up, own_down, core_up, core_down, _,
    centred, rstd, normed, active, slope, partial, source, params, bias, held,
):
    ext = ids.shape[0] - 2 * PAD
    x, c, _d = place()
    packets = (here, beside, near.at[0 : here.shape[0]], far.at[here.shape[0] :])
    load_frames(x, c, packets, ext, source)
    load_params(x, c, packets, ext, params)
    load_bias(x, c, 0, 0, params, bias)
    forward_norm(0, source, ids, params, centred, rstd, normed, ext)
    hold_local((own_up, own_down, core_up, core_down), held)
    forward_half(bias, held, normed, active, slope, ext)
    for at in (0, ext // 2):
        rows = slice(at, at + ext // 2)
        partial[rows, :] = down_half(held, active, rows)


def second_kernel(
    source, params, normed, partial, w_near, w_near_core, w_far, w_far_core0, w_far_core1, _,
    next_source, active, slope, branch, bias, held,
):
    ext = normed.shape[0]
    x, c, dp = place()
    load_bias(x, c, 0, 1, params, bias)
    clear_pads(next_source, ext)
    hold_far(dp % 2, (w_near, w_near_core, w_far, w_far_core0, w_far_core1), held)
    forward_half(bias, held, normed, active, slope, ext)

    def put(at, rows, value):
        next_source[PAD + at : PAD + at + rows, :] = value

    finish_branch(0, source, params, held, active, partial, branch, ext, put)


def third_kernel(
    ids, source, params, own_up, own_down, core_up, core_down, _,
    centred, rstd, normed, active, slope, partial, bias, held,
):
    ext = ids.shape[0] - 2 * PAD
    x, c, _d = place()
    load_bias(x, c, 1, 0, params, bias)
    forward_norm(1, source, ids, params, centred, rstd, normed, ext)
    hold_local((own_up, own_down, core_up, core_down), held)
    forward_half(bias, held, normed, active, slope, ext)
    for at in (0, ext // 2):
        rows = slice(at, at + ext // 2)
        partial[rows, :] = down_half(held, active, rows)


def fourth_kernel(
    cot_here, cot_beside, cot_near, cot_far, params, normed, active, slope, own_up, own_down, core_up, core_down,
    dy, low, low_t, normed_t, give, keep0, keep1, hidden_low, bias_sums, held,
):
    ext = dy.shape[0]
    x, c, dp = place()
    refs = (cot_here, cot_beside, cot_near.at[0:ext], cot_far.at[ext:])
    for r, ref in enumerate(refs):
        dy[:, lanes_of(x, c, r)] = ref[...].astype(f32)
    branch_grad(1, dy, params, low, ext)
    low_t[...] = low[HALO : ext - HALO, :].T
    normed_t[...] = normed[HALO : ext - HALO, :].T
    hold_local((own_up, own_down, core_up, core_down), held)
    backward_half(
        dp, held, low, low_t, normed_t, active, slope, hidden_low, (give.at[0], give.at[1]), (keep0, keep1), bias_sums, ext
    )


def fifth_kernel(
    params, normed, low, low_t, normed_t, w_near, w_near_core, w_far, w_far_core,
    give, keep0, keep1, bias_sums, active, hidden_low, held, bias, slope,
):
    ext = normed.shape[0]
    x, c, dp = place()
    load_bias(x, c, 1, 1, params, bias)
    hold_far(dp % 2, (w_near, w_near_core, w_far, w_far_core), held)
    forward_half(bias, held, normed, active, slope, ext)
    backward_half(
        dp, held, low, low_t, normed_t, active, slope, hidden_low, (give.at[0], give.at[1]), (keep0, keep1), bias_sums, ext
    )


def branch_kernel(
    source, params, partial, active, hidden_far, held_far, hidden_near, own_up, own_down, core_up, core_down, _,
    branch, out, dnormed, held_near,
):
    ext = partial.shape[0]
    hold_local((own_up, own_down, core_up, core_down), held_near)

    def put(at, rows, value):
        if at == 0:
            out[0 : rows - HALO, :] = value[HALO:].astype(bf16)
        else:
            out[at - HALO :, :] = value[: rows - HALO].astype(bf16)

    finish_branch(1, source, params, held_far, active, partial, branch, ext, put)
    for at in (0, ext // 2):
        rows = slice(at, at + ext // 2)
        dnormed[rows, :] = back_half(held_near, hidden_near, rows) + back_half(held_far, hidden_far, rows)


def sixth_kernel(
    ids, source, params, centred, rstd, branch, dy, dnormed, bias_near, bias_far, _,
    grad_source, side_give, side_keep, dconv, small_c,
):
    ext = dy.shape[0]
    x, c, _d = place()

    def put(start, rows, inner, j, value):
        grad_source[start : start + rows, lane(j)] = value

    backward_norm(
        1, x, c, dy, source, ids, params, centred, rstd, branch, dnormed, dconv, small_c,
        bias_near, bias_far, side_give, side_keep, put, ext,
    )


def seventh_kernel(
    dy, params, normed, active_near, slope_near, active_far, slope_far,
    own_up, own_down, core_up, core_down, w_near, w_near_core, w_far, w_far_core0, w_far_core1,
    hidden_near, hidden_far, give,
    keep_near0, keep_near1, keep_far0, keep_far1, bias_near, bias_far,
    low, low_t, normed_t, held_near, held_far,
):
    ext = dy.shape[0]
    _x, _c, dp = place()
    branch_grad(0, dy, params, low, ext)
    low_t[...] = low[HALO : ext - HALO, :].T
    normed_t[...] = normed[HALO : ext - HALO, :].T
    hold_local((own_up, own_down, core_up, core_down), held_near)
    hold_far(dp % 2, (w_near, w_near_core, w_far, w_far_core0, w_far_core1), held_far)
    backward_half(
        dp, held_near, low, low_t, normed_t, active_near, slope_near, hidden_near,
        (give.at[0], give.at[1]), (keep_near0, keep_near1), bias_near, ext,
    )
    backward_half(
        dp, held_far, low, low_t, normed_t, active_far, slope_far, hidden_far,
        (give.at[2], give.at[3]), (keep_far0, keep_far1), bias_far, ext,
    )


def eighth_kernel(
    ids, source, params, centred, rstd, branch, dy, hidden_near, hidden_far, bias_near, bias_far, first_out,
    own_up, own_down, core_up, core_down, w_near, w_near_core, w_far, w_far_core0, w_far_core1, _,
    out_give0, out_give1, out_keep0, out_keep1, side_give, side_keep,
    dnormed, dconv, small_c, out, held_near, held_far,
):
    ext = dy.shape[0]
    x, c, dp = place()
    hold_local((own_up, own_down, core_up, core_down), held_near)
    hold_far(dp % 2, (w_near, w_near_core, w_far, w_far_core0, w_far_core1), held_far)
    for at in (0, ext // 2):
        rows = slice(at, at + ext // 2)
        dnormed[rows, :] = back_half(held_near, hidden_near, rows) + back_half(held_far, hidden_far, rows)

    def put(start, rows, inner, j, value):
        if inner:
            out[start - HALO : start - HALO + rows, lane(j)] = value.astype(bf16)

    backward_norm(
        0, x, c, dy, source, ids, params, centred, rstd, branch, dnormed, dconv, small_c,
        bias_near, bias_far, side_give, side_keep, put, ext,
    )
    for i, ref in enumerate((first_out, out)):
        for r, piece in enumerate((out_keep0, out_give0, out_keep1, out_give1)):
            piece[i] = ref[:, lanes_of(x, c, r)]


def adamw(param, first, second, grad):
    first = beta_first * first + (1.0 - beta_first) * grad
    second = beta_second * second + (1.0 - beta_second) * grad * grad
    first_hat = first * (1.0 / (1.0 - beta_first**adam_step))
    second_hat = second * (1.0 / (1.0 - beta_second**adam_step))
    update = first_hat / (jnp.sqrt(second_hat) + adam_eps) + decay_rate * param
    return update, first, second


def halving_plan(n_dp, axes):
    bits = {"x": lambda k: k[0], "y": lambda k: k[1] & 1, "z": lambda k: (k[1] >> 1) & 1}
    keys = [[(i, d) for i in range(2) for d in range(n_dp)] for _ in axes]
    plan = []
    for now in zip(*axes):
        give = [[k for k in keys[m] if bits[axis](k)] for m, axis in enumerate(now)]
        keep = [[k for k in keys[m] if not bits[axis](k)] for m, axis in enumerate(now)]
        groups = [(0, 1)] if now[0] == now[1] else [(0,), (1,)]
        plan.append((give, keep, groups))
        keys = keep
    return plan


def side_to_packet(packet, value):
    rows = value.shape[0]
    at = packet.shape[0] - 2 * rows
    hi = value.astype(bf16)
    lo = (value - hi.astype(f32)).astype(bf16)
    packet[at : at + rows, :] = hi
    packet[at + rows :, :] = lo
    return hi.astype(f32) + lo.astype(f32)


def side_of(packet):
    at = packet.shape[0] - 64
    return packet[at : at + 32, :].astype(f32) + packet[at + 32 :, :].astype(f32)


def put_blocks(step, packets, helds, value_of):
    give, keep, groups = step
    rows = helds[0].shape[1]
    for packet, group in zip(packets, groups):
        at = 0
        for m in group:
            for key in give[m]:
                packet[at : at + rows, :] = value_of(m, key).astype(bf16)
                at += rows
    for m, held in enumerate(helds):
        for at, key in enumerate(keep[m]):
            held[at] = value_of(m, key)


def got_blocks(step, gots, helds):
    _, keep, groups = step
    rows = helds[0].shape[1]
    places = {}
    for got, group in zip(gots, groups):
        at = 0
        for m in group:
            for spot, key in enumerate(keep[m]):
                places[m, key] = (got, at, spot)
                at += rows

    def value_of(m, key):
        got, at, spot = places[m, key]
        return helds[m][spot] + got[at : at + rows, :].astype(f32)

    return value_of


def core_sum_kernel(plan, count, *refs):
    got = [ref.at[i] for ref in refs[:count] for i in range(ref.shape[0])]
    keep = refs[count : count + 4]
    packets, helds = refs[-2 - len(plan[0][2]) : -2], refs[-2:]

    def value_of(m, key):
        i, d = key
        return keep[2 * i + m][d] + got[2 * i + m][d].astype(f32)

    put_blocks(plan[0], packets, helds, value_of)


def step_sum_kernel(plan, step, *refs):
    count, outs = len(plan[step - 1][2]), len(plan[step][2])
    gots, helds, rest = refs[:count], refs[count : count + 2], refs[count + 2 :]
    packets, helds_out, side_out = refs[-3 - outs : -3], refs[-3:-1], refs[-1]
    put_blocks(plan[step], packets, helds_out, got_blocks(plan[step - 1], gots, helds))
    if step == 1:
        got_side, keep_side = rest[:2]
        side = jnp.concatenate(
            [keep_side[i] + (got_side[i, 0].astype(f32) + got_side[i, 1].astype(f32)) for i in range(2)], axis=0
        )
    else:
        side = rest[0][...] + side_of(gots[0])
    side_out[...] = side_to_packet(packets[0], side)


def line_start_kernel(plan, *refs):
    count = len(plan[-1][2])
    gots, helds, side = refs[:count], refs[count : count + 2], refs[count + 2]
    packet, out, side_out = refs[-3:]
    value_of = got_blocks(plan[-1], gots, helds)
    rows = helds[0].shape[1]
    keep = plan[-1][1]
    half = len(keep[0]) // 2
    for m in range(2):
        for at, key in enumerate(keep[m]):
            value = value_of(m, key)
            if at % 2:
                start = (m * half + at // 2) * rows
                packet[start : start + rows, :] = value.astype(bf16)
            else:
                out[m * half + at // 2] = value
    side_out[...] = side_to_packet(packet, side[...] + side_of(gots[0]))


def line_sum_kernel(got, held, side, *refs):
    packet, out, side_out = refs[-3:]
    count, rows, _ = held.shape
    for at in range(count):
        value = held[at] + got[at * rows : (at + 1) * rows, :].astype(f32)
        if at % 2:
            packet[(at // 2) * rows : (at // 2 + 1) * rows, :] = value.astype(bf16)
        else:
            out[at // 2] = value
    side_out[...] = side_to_packet(packet, side[...] + side_of(got))


def update_kernel(layer, got, held, side, up, down, m_up, v_up, m_down, v_down, *refs):
    sent, main, side_near, side_far = refs[-4:]
    size = main.shape[1]
    if sent.shape[0] > 2 * size:
        sent[2 * size :, :] = refs[0][...]
    rows = up.shape[0]
    for m in range(2):
        main[m] = held[m] + got[m * size : (m + 1) * size, :].astype(f32)
    total = side[...] + side_of(got)
    side_near[...] = total[0:16]
    hi = total[16:32].astype(bf16)
    side_far[0:16, :] = hi
    side_far[16:32, :] = (total[16:32] - hi.astype(f32)).astype(bf16)
    for m, (p, first, second) in enumerate(((up, m_up, v_up), (down, m_down, v_down))):
        for j in range(size // rows):
            cols, at = lane(j), j * rows
            u, _, _ = adamw(
                p[:, cols], first[layer, :, cols], second[layer, :, cols], main[m, at : at + rows]
            )
            sent[m * size + at : m * size + at + rows, :] = u.astype(bf16)


def adam_kernel(main0, main1, m_up, v_up, m_down, v_down, f_up, s_up, f_down, s_down, token):
    token[...] = jnp.zeros_like(token)
    rows = m_up.shape[1]
    for l, main in enumerate((main0, main1)):
        for j in range(main.shape[1] // rows):
            cols, at = lane(j), j * rows
            for m, (first, second, first_out, second_out) in enumerate(
                ((m_up, v_up, f_up, s_up), (m_down, v_down, f_down, s_down))
            ):
                _, first_out[l, :, cols], second_out[l, :, cols] = adamw(
                    0.0, first[l, :, cols], second[l, :, cols], main[m, at : at + rows]
                )


def small_adam_kernel(
    side0, side1, far, chan, bias, m_chan, v_chan, m_bias, v_bias,
    u_chan, u_bias, f_chan, s_chan, f_bias, s_bias, token,
):
    token[...] = jnp.zeros_like(token)
    base = far.shape[0] - 64
    for l, side in enumerate((side0, side1)):
        at = base + 32 * l
        g = side[...] + (far[at : at + 16, :].astype(f32) + far[at + 16 : at + 32, :].astype(f32))
        u_chan[:, l, :], f_chan[:, l, :], s_chan[:, l, :] = adamw(
            chan[:, l, :], m_chan[:, l, :], v_chan[:, l, :], g[0:12]
        )
        for j in range(bias.shape[1] // LANES):
            row, cols = slice(l, l + 1), lane(j)
            u_bias[row, cols], f_bias[row, cols], s_bias[row, cols] = adamw(
                bias[row, cols], m_bias[row, cols], v_bias[row, cols], g[12 + j : 13 + j]
            )


def ring_order(n_dp):
    return list(range(0, n_dp, 2)) + list(range(n_dp - 1, 0, -2))


def ring_owner(n_dp):
    dp = lax.axis_index("dp")
    half = n_dp // 2
    spot = jnp.where(dp % 2 == 0, dp // 2, n_dp - 1 - dp // 2)

    def owner(distance):
        at = lax.rem(spot + distance + n_dp, n_dp)
        return jnp.where(at < half, 2 * at, 2 * (n_dp - 1 - at) + 1)

    return owner


def far_group(n_dp, rows):
    first = ring_owner(n_dp)(n_dp // 2) * rows
    return first // LANES, pl.ds(pl.multiple_of(first % LANES, rows), rows)


def spread_kernel(layers, n_dp, parts, *refs):
    blocks = refs[: n_dp - 1]
    up_out, down_out, up_group, held_group, up, held, down, sems = refs[-8:]
    owner = ring_owner(n_dp)
    distances = [0]
    for step in range(1, n_dp // 2):
        distances += [-step, step]
    rows = up.shape[1] // n_dp
    size = parts * rows
    groups = up.shape[1] // LANES
    group, _ = far_group(n_dp, rows)

    def copies_of(l, k):
        part = pl.ds(k * LANES, LANES)
        pairs = ((up.at[l, part], up_out.at[l, part]), (down.at[l, :, part], down_out.at[l, :, part]))
        return [pltpu.make_async_copy(*pair, sems.at[2 * (l * groups + k) + i]) for i, pair in enumerate(pairs)]

    def each(l, k, act):
        def run():
            for copy in copies_of(l, k):
                act(copy)

        pl.when(group != k)(run)

    for l in range(layers):
        for distance, ref in zip(distances, blocks):
            at = pl.ds(pl.multiple_of(owner(distance) * rows, rows), rows)
            for j in range(parts):
                start = 2 * size * l + j * rows
                up[l, at, lane(j)] = ref[start : start + rows, :].astype(f32)
                start += size
                held[l, at, lane(j)] = ref[start : start + rows, :].astype(f32)
        for j in range(parts):
            down[l, lane(j), :] = held[l, :, lane(j)].T
        for k in range(groups):
            each(l, k, lambda copy: copy.start())
    whole = pl.ds(pl.multiple_of(group * LANES, LANES), LANES)
    for l in range(layers):
        up_group[l] = up[l, whole, :]
        held_group[l] = held[l, whole, :]
    for l in range(layers):
        for k in range(groups):
            each(l, k, lambda copy: copy.wait())


def last_spread_kernel(layers, n_dp, parts, top, bottom, up_group, held_group, *refs):
    up_out, down_out, up, held, down, sems = refs[-6:]
    rows = top.shape[0] // (2 * parts)
    size = parts * rows
    group, at = far_group(n_dp, rows)
    whole = pl.ds(pl.multiple_of(group * LANES, LANES), LANES)
    copies = []
    for l, far in enumerate((top, bottom)):
        up[l] = up_group[l]
        held[l] = held_group[l]
        for j in range(parts):
            up[l, at, lane(j)] = far[j * rows : (j + 1) * rows, :].astype(f32)
            held[l, at, lane(j)] = far[size + j * rows : size + (j + 1) * rows, :].astype(f32)
        for j in range(parts):
            down[l, lane(j), :] = held[l, :, lane(j)].T
        pairs = [(up.at[l], up_out.at[l, whole]), (down.at[l], down_out.at[l, :, whole])]
        copies += start_copies(pairs, sems.at[pl.ds(2 * l, 2)])
    for copy in copies:
        copy.wait()


def pack_kernel(keep, got, side0, side1, _, packet):
    rows = keep.shape[1]
    for i, ref in enumerate((keep, got)):
        for o in range(2):
            at = (2 * i + o) * rows
            packet[at : at + rows, :] = ref[o]
    packet[4 * rows : 4 * rows + 32, :] = side0[...]
    packet[4 * rows + 32 :, :] = side1[...]


def collect_kernel(own, core, far, out, grad, token):
    token[...] = jnp.zeros_like(token)
    x, c, _ = place()
    rows = own.shape[1]
    for o, target in enumerate((out, grad)):
        for r in range(4):
            at = pl.multiple_of(((x ^ (r // 2)) * 2 + (c ^ (r % 2))) * rows, HALO)
            if r < 2:
                target[pl.ds(at, rows), :] = (own, core)[r][o]
            else:
                start = (2 * (r - 2) + o) * rows
                target[pl.ds(at, rows), :] = far[start : start + rows, :]


VMEM = pl.BlockSpec(memory_space=pltpu.VMEM)
ANY = pl.BlockSpec(memory_space=pl.ANY)
HBM = pl.BlockSpec(memory_space=pltpu.HBM)


def call(kernel, outs, in_specs, scratch, name, limit=16, out_specs=None, flops=0, aliases=None):
    return pl.pallas_call(
        kernel,
        out_shape=[jax.ShapeDtypeStruct(s, t) for s, t in outs],
        in_specs=in_specs,
        out_specs=out_specs or [VMEM] * len(outs),
        scratch_shapes=scratch,
        input_output_aliases=aliases or {},
        compiler_params=pltpu.CompilerParams(vmem_limit_bytes=limit * 1024 * 1024),
        cost_estimate=pl.CostEstimate(flops=flops, bytes_accessed=0, transcendentals=0),
        name=name,
    )


def on_device(
    n_dp, frames_in, segments, cotangent, channel_params, weight_up, bias_up, weight_down,
    momentum_channel, variance_channel, momentum_up, variance_up, momentum_bias, variance_bias,
    momentum_down, variance_down,
):
    rows, frames, part = frames_in.shape
    layers, width, quarter = weight_up.shape
    chip_hidden = 2 * quarter
    tokens = rows * frames
    own = tokens // 4
    ext = own + 2 * HALO
    shard = width // n_dp
    parts = quarter // LANES

    def core_swap(v):
        return lax.ppermute(v, "chan", xor_perm(4, 1))

    def x_swap(v):
        return lax.ppermute(v, "chan", xor_perm(4, 2))

    def dp_swap(v, bit):
        return lax.ppermute(v, "dp", xor_perm(n_dp, bit))

    def after(value, *others):
        return lax.optimization_barrier((value, *others))[0]

    sems = pltpu.SemaphoreType.DMA((8,))
    width_sems = pltpu.SemaphoreType.DMA((16,))
    chan, m_chan, v_chan = [
        jnp.swapaxes(v, 0, 1) for v in (channel_params, momentum_channel, variance_channel)
    ]
    up_held = pltpu.VMEM((width, quarter), f32)
    down_held = pltpu.VMEM((quarter, width), f32)
    matrix = ((width, quarter), bf16)

    def in_hbm(*arrays):
        return [pltpu.with_memory_space_constraint(v, pltpu.HBM) for v in arrays]

    packet = ((ext + 2 * PARAM_ROWS, LANES), bf16)
    flat = pltpu.VMEM((tokens + 2 * HALO, LANES), bf16)
    both_packets = ((2 * packet[0][0], LANES), bf16)
    give, here, beside, chosen0 = call(
        prepare_kernel, [both_packets, packet, packet, matrix], [HBM] * 5,
        [flat, pltpu.VMEM(chan.shape, f32), pltpu.VMEM(bias_up.shape, f32), up_held, down_held, sems, sems],
        "prepare",
    )(*in_hbm(frames_in, chan, bias_up, weight_up, weight_down))
    frames_far = x_swap(give)
    near0 = x_swap(chosen0)
    frames_core = core_swap(frames_far)
    packets = [here, core_swap(beside), frames_far, frames_core]
    cot_packet = ((ext, LANES), bf16)
    slice_shape = ((shard, quarter), f32)
    chosen1, *both, give, here, beside, ids, up0, down0, up1, down1 = call(
        rest_kernel,
        [matrix] * 5 + [((2 * ext, LANES), bf16)] + [cot_packet] * 2 + [((ext + 2 * PAD, LANES), jnp.int32)] + [slice_shape] * 4,
        [HBM] * 3 + [VMEM, ANY],
        [flat, pltpu.VMEM((tokens + 2 * HALO + 2 * PAD, LANES), jnp.int32)]
        + [pltpu.VMEM(weight_up.shape, f32), pltpu.VMEM(weight_down.shape, f32), up_held, sems, width_sems],
        "rest", 24, flops=LONG,
    )(*in_hbm(weight_up, weight_down, cotangent), segments, beside)
    near1 = x_swap(chosen1)
    slices0, slices1 = [up0, down0], [up1, down1]
    local0, local1 = [v + [core_swap(w) for w in v] for v in (both[:2], both[2:])]
    cots = [here, core_swap(beside)]

    wide = (ext, width)
    padded = (ext + 2 * PAD, width)
    deep = (ext, chip_hidden)
    held = pltpu.VMEM((2, width, chip_hidden), bf16)
    bias = pltpu.VMEM((1, chip_hidden), f32)
    sums = ((1, chip_hidden), f32)
    params_shape = ((PARAM_ROWS, width), f32)
    turned = ((width, own), bf16)
    norm_shapes = [(wide, f32), ((ext, LANES), f32), (wide, bf16)]
    half_shapes = [(deep, bf16), (deep, f32), (wide, f32)]
    size = parts * shard
    grads = [((2, n_dp, size, LANES), bf16)] + [((n_dp, size, LANES), f32)] * 2
    side_shapes = [((2, 2, 16, LANES), bf16), ((2, 16, LANES), f32)]
    norm_scratch = [pltpu.VMEM(padded, f32), pltpu.VMEM((16, width), f32)]

    def buffers(shapes):
        return [pltpu.VMEM(s, t) for s, t in shapes]

    first = call(
        first_kernel, norm_shapes + half_shapes + [(padded, f32), params_shape],
        [VMEM] * 9 + [ANY], [bias, held], "layer0_near", 24,
    )
    centred0, rstd0, normed0, active00, slope00, partial0, source0, params = first(
        ids, *packets, *local0, ids
    )
    cot_far = x_swap(after(give, near0))
    far0 = dp_swap(after(near0, chosen1), 1)
    far1 = dp_swap(after(near1, partial0), 1)
    pieces0 = call(split_kernel, [((width // 2, quarter), bf16)] * 2, [VMEM] + [ANY] * 2, [], "split")(
        far0, partial0, partial0
    )
    away0 = [near0, core_swap(near0), far0] + [core_swap(v) for v in pieces0]
    second = call(
        second_kernel, [(padded, f32)] + half_shapes, [VMEM] * 9 + [ANY],
        [bias, held], "layer0_far", 24,
    )
    source1, active01, slope01, branch0 = second(source0, params, normed0, partial0, *away0, partial0)
    third = call(
        third_kernel, norm_shapes + half_shapes, [VMEM] * 7 + [ANY],
        [bias, held], "layer1_near", 24,
    )
    centred1, rstd1, normed1, active10, slope10, partial1 = third(ids, source1, params, *local1, cots[1])
    cots += [cot_far, core_swap(cot_far)]
    fourth = call(
        fourth_kernel, [(wide, f32), (wide, bf16), turned, turned] + grads + [(deep, bf16), sums],
        [VMEM] * 12, [held], "layer1_near_back", 24,
    )
    dy1, low1, low_t1, normed_t1, give10, *keep10, hidden10, bias10 = fourth(
        *cots, params, normed1, active10, slope10, *local1
    )
    got10 = core_swap(give10)
    away1 = [near1, core_swap(near1), far1, core_swap(after(far1, active10))]
    fifth = call(
        fifth_kernel, grads + [sums, (deep, bf16), (deep, bf16), ((2, width, chip_hidden), bf16)],
        [VMEM] * 9, [bias] + buffers([(deep, f32)]), "layer1_far", 28, flops=LONG,
    )
    give11, *keep11, bias11, active11, hidden11, held11 = fifth(
        params, normed1, low1, low_t1, normed_t1, *away1
    )
    got11 = core_swap(give11)
    branch1, first_out, dnormed1 = call(
        branch_kernel, [(wide, f32), ((own, width), bf16), (wide, f32)], [VMEM] * 11 + [ANY], [held],
        "layer1_branch", 24, flops=LONG,
    )(source1, params, partial1, active11, hidden11, held11, hidden10, *local1, bias11)

    half = n_dp // 2
    plans = [halving_plan(n_dp, axes) for axes in AXES]
    side_shape = ((32, LANES), f32)

    def packet_of(blocks, side=False):
        return ((blocks * size + (64 if side else 0), LANES), bf16)

    def combine(kernel, outs, args, before, name, flops=0):
        specs = [VMEM] * len(args) + [ANY] * len(before)
        return call(kernel, outs, specs, [], name, flops=flops)(*args, *before)

    def step_outs(layer, step):
        give, keep, groups = plans[layer][step]
        outs = [packet_of(sum(len(give[m]) for m in g), step > 0 and n == 0) for n, g in enumerate(groups)]
        outs += [((len(k), size, LANES), f32) for k in keep]
        return outs + ([side_shape] if step else [])

    def exchange(layer, step, packets):
        swaps = {"x": x_swap, "y": lambda v: dp_swap(v, 1), "z": lambda v: dp_swap(v, 2)}
        groups = plans[layer][step][2]
        return [swaps[AXES[layer][g[0]][step]](v) for v, g in zip(packets, groups)]

    def core_step(layer, gots, keeps, before):
        kernel = functools.partial(core_sum_kernel, plans[layer], len(gots))
        outs = combine(kernel, step_outs(layer, 0), [*gots, *keeps], before, "core_sum")
        return outs[:-2], outs[-2:]

    def next_step(layer, step, got, helds, sides, before, flops=0):
        kernel = functools.partial(step_sum_kernel, plans[layer], step)
        outs = combine(kernel, step_outs(layer, step), [*got, *helds, *sides], before, "step_sum", flops)
        return outs[:-3], outs[-3:-1], outs[-1]

    def line_start(layer, got, helds, side, before):
        left = n_dp // 4
        outs = [packet_of(left, True), ((left, size, LANES), f32), side_shape]
        kernel = functools.partial(line_start_kernel, plans[layer])
        state = combine(kernel, outs, [*got, *helds, side], before, "line_start")
        bit = 4
        while bit < half:
            left //= 2
            outs = [packet_of(left, True), ((left, size, LANES), f32), side_shape]
            state = combine(line_sum_kernel, outs, [dp_swap(state[0], bit), *state[1:]], [], "line_sum")
            bit *= 2
        return state

    down_moments = [jnp.swapaxes(v, 1, 2) for v in (momentum_down, variance_down)]

    def update_step(layer, packet, main, side, slices, others, before):
        outs = [packet_of(2 + 2 * len(others)), ((2, size, LANES), f32)]
        outs += [((16, LANES), f32), ((32, LANES), bf16)]
        args = [dp_swap(packet, half), main, side, *slices, momentum_up, variance_up, *down_moments]
        args += others
        return combine(functools.partial(update_kernel, layer), outs, args, before, "update")

    order = ring_order(n_dp)
    ahead = [(order[i], order[(i + 1) % n_dp]) for i in range(n_dp)]
    back = [(b, a) for a, b in ahead]

    def ring_step(right, left):
        return lax.ppermute(right, "dp", ahead), lax.ppermute(left, "dp", back)

    def ring_end(right, left):
        cut = right.shape[0] // 2
        return lax.ppermute(right[:cut], "dp", ahead), lax.ppermute(left[cut:], "dp", back)

    def blocks_of(ring):
        return [ring[0][0]] + [v for pair in ring[1:] for v in pair]

    packets1, helds1 = core_step(1, [got10, got11], [*keep10, *keep11], [branch1])
    sixth = call(
        sixth_kernel, [(wide, f32)] + side_shapes, [VMEM] * 10 + [ANY], norm_scratch, "layer1_norm_back", 24
    )
    grad1, *sides1 = sixth(
        ids, source1, params, centred1, rstd1, branch1, dy1, dnormed1, bias10, bias11, packets1[0]
    )
    seventh = call(
        seventh_kernel, [(deep, bf16)] * 2 + [((4, n_dp, size, LANES), bf16)] + [grads[1]] * 4 + [sums] * 2,
        [VMEM] * 16, buffers([(wide, bf16), turned, turned]) + [held, held],
        "layer0_back", 28,
    )
    hidden0, hidden1, *matrices0, bias00, bias01 = seventh(
        grad1, params, normed0, active00, slope00, active01, slope01, *local0, *away0
    )
    eighth = call(
        eighth_kernel, [((2, own, LANES), bf16)] * 4 + side_shapes, [VMEM] * 21 + [ANY],
        buffers([(wide, f32)]) + norm_scratch + buffers([((own, width), bf16)]) + [held, held],
        "layer0_norm_back", 28, flops=LONG,
    )
    give_near, give_far, keep_near, keep_far, *sides0 = eighth(
        ids, source0, params, centred0, rstd0, branch0, grad1, hidden0, hidden1, bias00, bias01, first_out,
        *local0, *away0, bias01,
    )

    sides = [core_swap(sides1[0]), sides1[1]]
    packets1, helds1, side1 = next_step(1, 1, exchange(1, 0, packets1), helds1, sides, [], LONG)
    packets0, helds0 = core_step(0, [core_swap(matrices0[0])], matrices0[1:], [packets1[0]])
    crossed0 = exchange(0, 0, packets0)
    sides = [core_swap(sides0[0]), sides0[1]]
    got = exchange(1, 1, packets1)
    packets1, helds1, side1 = next_step(1, 2, got, helds1, [side1], [])
    packets0, helds0, side0 = next_step(0, 1, crossed0, helds0, sides, [packets1[0]], LONG)
    got0 = exchange(0, 1, packets0)
    line1 = line_start(1, exchange(1, 2, packets1), helds1, side1, [])
    packets0, helds0, side0 = next_step(0, 2, got0, helds0, [side0], [line1[0]])
    sent1, main1, side1, side_far1 = update_step(1, *line1, slices1, [], [])
    line0 = line_start(0, exchange(0, 2, packets0), helds0, side0, [])
    sent, main0, side0, side_far0 = update_step(0, *line0, slices0, [sent1], [])
    ring = [(sent, sent)]
    ring.append(ring_step(sent, sent))

    got_near, got_far = core_swap(give_near), core_swap(give_far)
    far_packet = ((4 * own + 64, LANES), bf16)
    from_far = x_swap(
        call(pack_kernel, [far_packet], [VMEM] * 4 + [ANY], [], "pack")(
            keep_far, got_far, side_far0, side_far1, sent
        )[0]
    )
    token = ((8, LANES), f32)
    layer_output, input_grad, tokens_token = call(
        collect_kernel, [((tokens, part), bf16)] * 2 + [token], [VMEM] * 3, [], "collect"
    )(keep_near, got_near, from_far)

    chan_shape, bias_shape = (chan.shape, f32), (bias_up.shape, f32)
    adam_outs = [(momentum_up.shape, f32)] * 2 + [(down_moments[0].shape, f32)] * 2 + [token]
    first_up, second_up, first_down, second_down, matrix_token = call(
        adam_kernel, adam_outs, [VMEM] * 6, [], "adam"
    )(main0, main1, momentum_up, variance_up, *down_moments)
    small_outs = [chan_shape, bias_shape, chan_shape, chan_shape, bias_shape, bias_shape, token]
    params_channel, params_bias, first_channel, second_channel, first_bias, second_bias, adam_token = call(
        small_adam_kernel, small_outs, [VMEM] * 9, [], "small_adam"
    )(side0, side1, from_far, chan, bias_up, m_chan, v_chan, momentum_bias, variance_bias)
    right, left = ring[1]
    for step in range(2, half):
        if step == 2:
            right, left = after(right, matrix_token), after(left, matrix_token)
        right, left = ring_step(right, left)
        ring.append((right, left))
    ring.append(ring_end(right, left))
    whole = [(weight_up.shape, f32), (weight_down.shape, f32)]
    group_shape = ((layers, LANES, quarter), f32)
    group_scratch = buffers([group_shape, group_shape, ((layers, quarter, LANES), f32)])
    spread = call(
        functools.partial(spread_kernel, layers, n_dp, parts), whole + [group_shape] * 2, [VMEM] * (n_dp - 1),
        buffers([(weight_up.shape, f32)] * 2 + [(weight_down.shape, f32)]) + [width_sems],
        "spread", 16, [HBM, HBM, VMEM, VMEM],
    )
    last_spread = call(
        functools.partial(last_spread_kernel, layers, n_dp, parts), whole, [VMEM] * 4 + [HBM] * 2 + [ANY] * 2,
        group_scratch + [sems], "last_spread", 16, [HBM, HBM], aliases={4: 0, 5: 1},
    )
    blocks = blocks_of(ring)
    params_up, params_down, *missing = spread(*blocks[:-2])
    params_up, params_down = last_spread(
        *blocks[-2:], *missing, params_up, params_down, tokens_token, adam_token
    )

    params_channel, first_channel, second_channel = [
        jnp.swapaxes(v, 0, 1) for v in (params_channel, first_channel, second_channel)
    ]
    first_down, second_down = jnp.swapaxes(first_down, 1, 2), jnp.swapaxes(second_down, 1, 2)

    layer_output, input_grad = [v.reshape(rows, frames, part) for v in (layer_output, input_grad)]
    return (
        layer_output,
        input_grad,
        params_channel,
        params_up,
        params_bias,
        params_down,
        first_channel,
        second_channel,
        first_up,
        second_up,
        first_bias,
        second_bias,
        first_down,
        second_down,
    )


def solution(mesh):
    return jax.shard_map(
        functools.partial(on_device, mesh.shape["dp"]),
        mesh=mesh,
        in_specs=(
            P("dp", None, "chan"),
            P("dp", None),
            P("dp", None, "chan"),
            P(None, None, "chan"),
            P(None, None, "chan"),
            P(None, "chan"),
            P(None, "chan", None),
            P(None, None, "chan"),
            P(None, None, "chan"),
            P(None, "dp", "chan"),
            P(None, "dp", "chan"),
            P(None, "chan"),
            P(None, "chan"),
            P(None, "chan", "dp"),
            P(None, "chan", "dp"),
        ),
        out_specs=(
            P("dp", None, "chan"),
            P("dp", None, "chan"),
            P(None, None, "chan"),
            P(None, None, "chan"),
            P(None, "chan"),
            P(None, "chan", None),
            P(None, None, "chan"),
            P(None, None, "chan"),
            P(None, "dp", "chan"),
            P(None, "dp", "chan"),
            P(None, "chan"),
            P(None, "chan"),
            P(None, "chan", "dp"),
            P(None, "chan", "dp"),
        ),
        check_vma=False,
    )
```

```python
import functools

import jax
import jax.numpy as jnp
from jax import lax
from jax.experimental import pallas as pl
from jax.experimental.pallas import tpu as pltpu
from jax.sharding import PartitionSpec as P

kernel_taps = 7
reach = kernel_taps // 2
norm_eps = 1e-06
beta_first = 0.8
beta_second = 0.9
adam_eps = 1e-08
decay_rate = 0.01
adam_step = 10.0

HALO = 16
PAD = 8
LANES = 128
PARAM_ROWS = 32
AXES = (("xyz", "yxz"), ("xzy", "yzx"))
LONG = 20_000_000_000
f32 = jnp.float32
bf16 = jnp.bfloat16


def xor_perm(size, bit):
    return [(i, i ^ bit) for i in range(size)]


def hi_lo(value):
    hi = lax.reduce_precision(value, 8, 7)
    return hi.astype(bf16), (value - hi).astype(bf16)


def place():
    me = lax.axis_index("chan")
    return me // 2, me % 2, lax.axis_index("dp")


def lanes_of(x, c, r):
    return pl.ds(pl.multiple_of(((x ^ (r // 2)) * 2 + (c ^ (r % 2))) * LANES, LANES), LANES)


def row_tiles(ext):
    own = ext - 2 * HALO
    tiles = [(0, HALO, False)]
    tiles += [(HALO + at, 32, True) for at in range(0, own, 32)]
    return tiles + [(HALO + own, HALO, False)]


def lane(j):
    return slice(j * LANES, (j + 1) * LANES)


def fold(value):
    return value.reshape(value.shape[0] // 8, 8, value.shape[1]).sum(axis=0)


def plus(total, value):
    return value if total is None else total + value


def column_sum(value):
    return jnp.sum(value, axis=0, keepdims=True)


def gelu_parts(h):
    tail = jnp.exp2(h * h * -0.7213475204444817)
    d = 1.0 + (0.3275911 * 0.7071067811865476) * jnp.abs(h)
    t = pl.reciprocal(d, approx=True)
    t = t * (2.0 - d * t)
    poly = t * (
        0.127414796
        + t * (-0.142248368 + t * (0.7107068705 + t * (-0.7265760135 + t * 0.5307027145)))
    )
    low = poly * tail
    phi = jnp.where(h < 0.0, low, 1.0 - low)
    return h * phi, phi + h * tail * 0.3989422804014327


def load_frames(x, c, packets, ext, source):
    for r, ref in enumerate(packets):
        source[PAD : PAD + ext, lanes_of(x, c, r)] = ref[0:ext, :].astype(f32)
    clear_pads(source, ext)


def load_params(x, c, packets, ext, params):
    for r, ref in enumerate(packets):
        hi = ref[ext : ext + PARAM_ROWS, :].astype(f32)
        lo = ref[ext + PARAM_ROWS : ext + 2 * PARAM_ROWS, :].astype(f32)
        params[:, lanes_of(x, c, r)] = hi + lo


def clear_pads(ref, ext):
    zeros = jnp.zeros((PAD, ref.shape[1]), ref.dtype)
    ref[0:PAD, :] = zeros
    ref[PAD + ext : PAD + ext + PAD, :] = zeros


def load_bias(x, c, layer, chip, params, bias):
    width = bias.shape[1] // 2
    for r in range(2):
        rows = params[:, lanes_of(x, c, 2 * chip + r)]
        for j in range(width // LANES):
            k = 24 + layer * (width // LANES) + j
            bias[0:1, r * width + j * LANES : r * width + (j + 1) * LANES] = rows[k : k + 1]


def start_copies(pairs, sems):
    started = []
    for i, (src, dst) in enumerate(pairs):
        copy = pltpu.make_async_copy(src, dst, sems.at[i])
        copy.start()
        started.append(copy)
    return started


def hold_local(refs, held):
    width = refs[0].shape[-1]
    for i, ref in enumerate(refs):
        r, m = i // 2, i % 2
        held[m, :, r * width : (r + 1) * width] = ref[...]


def hold_far(y, refs, held):
    near, near_core, far, *far_core = refs
    width = near.shape[-1]
    held[y, :, 0:width] = near[...]
    held[1 - y, :, 0:width] = far[...]
    held[y, :, width:] = near_core[...]
    at = 0
    for ref in far_core:
        held[1 - y, at : at + ref.shape[0], width:] = ref[...]
        at += ref.shape[0]


def masks_at(ids, start, rows):
    here = ids[PAD + start : PAD + start + rows, :]
    masks = []
    for k in range(kernel_taps):
        at = PAD + start + k - reach
        masks.append(ids[at : at + rows, :] == here)
    return masks


def forward_norm(layer, source, ids, params, centred, rstd, normed, ext):
    width = source.shape[1]
    tiles = width // LANES
    base = layer * 12
    for start, rows, _ in row_tiles(ext):
        masks = masks_at(ids, start, rows)
        convs = []
        total = square = None
        for j in range(tiles):
            acc = params[base + 7 : base + 8, lane(j)]
            for k in range(kernel_taps):
                at = PAD + start + k - reach
                piece = source[at : at + rows, lane(j)]
                tap = params[base + k : base + k + 1, lane(j)]
                acc = acc + tap * (piece if k == reach else jnp.where(masks[k], piece, 0.0))
            convs.append(acc)
            total = plus(total, acc)
            square = plus(square, acc * acc)
        mean = jnp.sum(total, axis=1, keepdims=True) * (1.0 / width)
        var = jnp.sum(square, axis=1, keepdims=True) * (1.0 / width) - mean * mean
        scale = lax.rsqrt(var + norm_eps)
        rstd[start : start + rows, :] = jnp.broadcast_to(scale, (rows, LANES))
        for j in range(tiles):
            value = (convs[j] - mean) * scale
            centred[start : start + rows, lane(j)] = value
            gain = params[base + 8 : base + 9, lane(j)]
            shift = params[base + 9 : base + 10, lane(j)]
            normed[start : start + rows, lane(j)] = (value * gain + shift).astype(bf16)


def forward_half(bias, held, normed, active, slope, ext):
    quarter = held.shape[2] // 2
    half = ext // 2
    for r in range(2):
        cols = slice(r * quarter, (r + 1) * quarter)
        for at in (0, half):
            rows = slice(at, at + half)
            h = (
                jnp.dot(normed[rows, :], held[0, :, cols], preferred_element_type=f32)
                + bias[0:1, cols]
            )
            value, grad = gelu_parts(h)
            active[rows, cols] = value.astype(bf16)
            slope[rows, cols] = grad


def down_half(held, active, rows):
    return lax.dot_general(
        active[rows, :], held[1], (((1,), (1,)), ((), ())), preferred_element_type=f32
    )


def finish_branch(layer, source, params, held, active, partial, branch, ext, put):
    half = ext // 2
    base = layer * 12
    for at in (0, half):
        rows = slice(at, at + half)
        value = partial[rows, :] + down_half(held, active, rows) + params[base + 10 : base + 11, :]
        branch[rows, :] = value
        put(at, half, source[PAD + at : PAD + at + half, :] + params[base + 11 : base + 12, :] * value)


def branch_grad(layer, dy, params, low, ext):
    base = layer * 12
    for j in range(dy.shape[1] // LANES):
        scale = params[base + 11 : base + 12, lane(j)]
        for start, rows, _ in row_tiles(ext):
            low[start : start + rows, lane(j)] = (scale * dy[start : start + rows, lane(j)]).astype(bf16)


def put_grad(dp, out, parts, value):
    blocks, size, _ = out.shape
    rows = size // parts
    value = value.astype(out.dtype)
    for d in range(blocks):
        for j in range(parts):
            out[d ^ dp, j * rows : (j + 1) * rows] = value[d * rows : (d + 1) * rows, lane(j)]


def backward_half(dp, held, low, low_t, normed_t, active, slope, hidden_low, give, keep, bias_sums, ext):
    quarter = held.shape[2] // 2
    half = ext // 2
    inner = slice(HALO, ext - HALO)
    parts = quarter // LANES
    for r, out in ((0, keep), (1, give)):
        cols = slice(r * quarter, (r + 1) * quarter)
        sums = None
        for at in (0, half):
            rows = slice(at, at + half)
            grad = (
                jnp.dot(low[rows, :], held[1, :, cols], preferred_element_type=f32)
                * slope[rows, cols]
            )
            hidden_low[rows, cols] = grad.astype(bf16)
            sums = plus(sums, fold(grad[HALO:] if at == 0 else grad[: half - HALO]))
        bias_sums[0:1, cols] = column_sum(sums)
        put_grad(dp, out[1], parts, jnp.dot(low_t[...], active[inner, cols], preferred_element_type=f32))
        put_grad(
            dp, out[0], parts, jnp.dot(normed_t[...], hidden_low[inner, cols], preferred_element_type=f32)
        )


def back_half(held, hidden_low, rows):
    return lax.dot_general(
        hidden_low[rows, :], held[0], (((1,), (1,)), ((), ())), preferred_element_type=f32
    )


def backward_norm(
    layer, x, c, dy, source, ids, params, centred, rstd, branch, dnormed, dconv, small_c,
    bias_near, bias_far, side_give, side_keep, put, ext,
):
    width = source.shape[1]
    tiles = width // LANES
    quarter = bias_near.shape[1] // 2
    base = layer * 12
    small_c[...] = jnp.zeros_like(small_c)
    for j in range(tiles):
        scale = params[base + 11 : base + 12, lane(j)]
        sum_gamma = sum_bias = None
        for start, rows, inner in row_tiles(ext):
            if inner:
                grad = dy[start : start + rows, lane(j)]
                sum_gamma = plus(sum_gamma, fold(grad * branch[start : start + rows, lane(j)]))
                sum_bias = plus(sum_bias, fold(scale * grad))
        small_c[10:11, lane(j)] = column_sum(sum_bias)
        small_c[11:12, lane(j)] = column_sum(sum_gamma)

    clear_pads(dconv, ext)
    sums = [[None] * 3 for _ in range(tiles)]
    for start, rows, inner in row_tiles(ext):
        scale = rstd[start : start + rows, :]
        weighted, norms = [], []
        first = second = None
        for j in range(tiles):
            grad = dnormed[start : start + rows, lane(j)]
            norm = centred[start : start + rows, lane(j)]
            w = grad * params[base + 8 : base + 9, lane(j)]
            first = plus(first, w)
            second = plus(second, w * norm)
            weighted.append(w)
            norms.append(norm)
            if inner:
                sums[j][0] = plus(sums[j][0], fold(grad * norm))
                sums[j][1] = plus(sums[j][1], fold(grad))
        first = jnp.sum(first, axis=1, keepdims=True) * (1.0 / width)
        second = jnp.sum(second, axis=1, keepdims=True) * (1.0 / width)
        for j in range(tiles):
            value = scale * (weighted[j] - first - norms[j] * second)
            dconv[PAD + start : PAD + start + rows, lane(j)] = value
            if inner:
                sums[j][2] = plus(sums[j][2], fold(value))
    for j in range(tiles):
        small_c[8:9, lane(j)] = column_sum(sums[j][0])
        small_c[9:10, lane(j)] = column_sum(sums[j][1])
        small_c[7:8, lane(j)] = column_sum(sums[j][2])

    for j in range(tiles):
        taps = [params[base + k : base + k + 1, lane(j)] for k in range(kernel_taps)]
        sums = [None] * kernel_taps
        for start, rows, inner in row_tiles(ext):
            masks = masks_at(ids, start, rows)
            here = dconv[PAD + start : PAD + start + rows, lane(j)]
            total = dy[start : start + rows, lane(j)]
            for k in range(kernel_taps):
                mirror = kernel_taps - 1 - k
                at = PAD + start + mirror - reach
                piece = dconv[at : at + rows, lane(j)]
                total = total + taps[k] * (
                    piece if k == reach else jnp.where(masks[mirror], piece, 0.0)
                )
                if inner:
                    at = PAD + start + k - reach
                    piece = source[at : at + rows, lane(j)]
                    if k != reach:
                        piece = jnp.where(masks[k], piece, 0.0)
                    sums[k] = plus(sums[k], fold(piece * here))
            put(start, rows, inner, j, total)
        for k in range(kernel_taps):
            small_c[k : k + 1, lane(j)] = column_sum(sums[k])

    for r in range(4):
        sums = (bias_near if r < 2 else bias_far)[0:1, (r % 2) * quarter : (r % 2 + 1) * quarter]
        rows = [small_c[0:12, lanes_of(x, c, r)]]
        rows += [sums[:, lane(j)] for j in range(quarter // LANES)]
        rows += [jnp.zeros((16 - 12 - quarter // LANES, LANES), f32)]
        value = jnp.concatenate(rows, axis=0)
        if r % 2 == 0:
            side_keep[r // 2] = value
        else:
            hi = value.astype(bf16)
            side_give[r // 2, 0] = hi
            side_give[r // 2, 1] = (value - hi.astype(f32)).astype(bf16)


def start_rows(frames, flat, sems):
    rows, count, _ = frames.shape
    zeros = jnp.zeros((HALO, LANES), bf16)
    flat[0:HALO, :] = zeros
    flat[HALO + rows * count :, :] = zeros
    pairs = [(frames.at[r], flat.at[HALO + r * count : HALO + (r + 1) * count]) for r in range(rows)]
    return start_copies(pairs, sems)


def token_chunks(flat, own, outs):
    x, c, _ = place()
    ext = own + 2 * HALO
    for out, dx, dc in zip(outs, (1, 1, 0, 0), (0, 1, 0, 1)):
        at = pl.multiple_of(((x ^ dx) * 2 + (c ^ dc)) * own, HALO)
        out[0:ext, :] = flat[pl.ds(at, ext), :]


def pieces(source, target, count):
    rows = source.shape[0] // count
    cuts = [pl.ds(i * rows, rows) for i in range(count)]
    return [(source.at[cut], target.at[cut]) for cut in cuts]


def prepare_kernel(
    frames, chan_in, bias_in, up, down,
    give, here, beside, chosen, flat, chan, bias, up_held, down_held, sems, matrix_sems,
):
    x, c, dp = place()

    @pl.when(dp % 2 == 0)
    def start_up():
        start_copies(pieces(up.at[0], up_held, 4), matrix_sems)

    @pl.when(dp % 2 == 1)
    def start_down():
        start_copies(pieces(down.at[0], down_held, 4), matrix_sems)

    copies = start_rows(frames, flat, sems)
    smalls = start_copies([(chan_in, chan), (bias_in, bias)], sems.at[pl.ds(4, 2)])
    own = frames.shape[0] * frames.shape[1] // 4
    ext = own + 2 * HALO
    layers, parts = bias.shape[0], bias.shape[1] // LANES
    for copy in smalls:
        copy.wait()
    rows = [chan[:, l, :] for l in range(layers)]
    rows += [bias[l : l + 1, lane(j)] for l in range(layers) for j in range(parts)]
    rows += [jnp.zeros((PARAM_ROWS - (12 + parts) * layers, LANES), f32)]
    value = jnp.concatenate(rows, axis=0)
    hi = value.astype(bf16)
    lo = (value - hi.astype(f32)).astype(bf16)
    size = ext + 2 * PARAM_ROWS
    outs = (give.at[0:size], give.at[size:], here, beside)
    for out in outs:
        out[ext : ext + PARAM_ROWS, :] = hi
        out[ext + PARAM_ROWS :, :] = lo
    for copy in copies:
        copy.wait()
    token_chunks(flat, own, outs)

    @pl.when(dp % 2 == 0)
    def take_up():
        for i, (src, dst) in enumerate(pieces(up.at[0], up_held, 4)):
            pltpu.make_async_copy(src, dst, matrix_sems.at[i]).wait()
        chosen[...] = up_held[...].astype(bf16)

    @pl.when(dp % 2 == 1)
    def take_down():
        for i, (src, dst) in enumerate(pieces(down.at[0], down_held, 4)):
            pltpu.make_async_copy(src, dst, matrix_sems.at[i]).wait()
        chosen[...] = down_held[...].T.astype(bf16)


def split_kernel(whole, *refs):
    first, second = refs[-2:]
    first[...] = whole[0 : first.shape[0], :]
    second[...] = whole[first.shape[0] :, :]


def rest_kernel(
    up, down, frames, segments, _,
    chosen, w00, w01, w10, w11, give, here, beside, ids, up0, down0, up1, down1,
    flat, columns, up_held, down_held, turned, sems, matrix_sems,
):
    x, c, dp = place()
    layers = up.shape[0]
    matrices = []
    for l in reversed(range(layers)):
        pairs = pieces(up.at[l], up_held.at[l], 4) + pieces(down.at[l], down_held.at[l], 4)
        matrices.append(start_copies(pairs, matrix_sems.at[pl.ds(8 * l, 8)]))
    copies = start_rows(frames, flat, sems)
    shard = up0.shape[0]
    mine = pl.ds(pl.multiple_of(dp * shard, shard), shard)
    for l, started, both, up_slice, down_slice in (
        (1, matrices[0], (w10, w11), up1, down1),
        (0, matrices[1], (w00, w01), up0, down0),
    ):
        for copy in started:
            copy.wait()
        both[0][...] = up_held[l].astype(bf16)
        up_slice[...] = up_held[l, mine, :]
        turned[...] = down_held[l].T
        both[1][...] = turned[...].astype(bf16)
        down_slice[...] = turned[mine, :]

    @pl.when(dp % 2 == 0)
    def choose_up():
        chosen[...] = w10[...]

    @pl.when(dp % 2 == 1)
    def choose_down():
        chosen[...] = w11[...]

    for copy in copies:
        copy.wait()
    ext = here.shape[0]
    token_chunks(flat, ext - 2 * HALO, (give.at[0:ext], give.at[ext:], here, beside))

    rows, count = segments.shape
    tokens = rows * count
    edge = HALO + PAD
    none = jnp.full((edge, LANES), -1, jnp.int32)
    columns[0:edge, :] = none
    columns[edge + tokens :, :] = none
    for r in range(rows):
        row = jnp.broadcast_to(segments[r : r + 1, :] + 8 * r, (LANES, count))
        at = edge + r * count
        columns[at : at + count, :] = row.T
    at = pl.multiple_of((x * 2 + c) * (tokens // 4), HALO)
    ids[...] = columns[pl.ds(at, ids.shape[0]), :]


def first_kernel(
    ids, here, beside, near, far, own_up, own_down, core_up, core_down, _,
    centred, rstd, normed, active, slope, partial, source, params, bias, held,
):
    ext = ids.shape[0] - 2 * PAD
    x, c, _d = place()
    packets = (here, beside, near.at[0 : here.shape[0]], far.at[here.shape[0] :])
    load_frames(x, c, packets, ext, source)
    load_params(x, c, packets, ext, params)
    load_bias(x, c, 0, 0, params, bias)
    forward_norm(0, source, ids, params, centred, rstd, normed, ext)
    hold_local((own_up, own_down, core_up, core_down), held)
    forward_half(bias, held, normed, active, slope, ext)
    for at in (0, ext // 2):
        rows = slice(at, at + ext // 2)
        partial[rows, :] = down_half(held, active, rows)


def second_kernel(
    source, params, normed, partial, w_near, w_near_core, w_far, w_far_core0, w_far_core1, _,
    next_source, active, slope, branch, bias, held,
):
    ext = normed.shape[0]
    x, c, dp = place()
    load_bias(x, c, 0, 1, params, bias)
    clear_pads(next_source, ext)
    hold_far(dp % 2, (w_near, w_near_core, w_far, w_far_core0, w_far_core1), held)
    forward_half(bias, held, normed, active, slope, ext)

    def put(at, rows, value):
        next_source[PAD + at : PAD + at + rows, :] = value

    finish_branch(0, source, params, held, active, partial, branch, ext, put)


def third_kernel(
    ids, source, params, own_up, own_down, core_up, core_down, _,
    centred, rstd, normed, active, slope, partial, bias, held,
):
    ext = ids.shape[0] - 2 * PAD
    x, c, _d = place()
    load_bias(x, c, 1, 0, params, bias)
    forward_norm(1, source, ids, params, centred, rstd, normed, ext)
    hold_local((own_up, own_down, core_up, core_down), held)
    forward_half(bias, held, normed, active, slope, ext)
    for at in (0, ext // 2):
        rows = slice(at, at + ext // 2)
        partial[rows, :] = down_half(held, active, rows)


def fourth_kernel(
    cot_here, cot_beside, cot_near, cot_far, params, normed, active, slope, own_up, own_down, core_up, core_down,
    dy, low, low_t, normed_t, give, keep0, keep1, hidden_low, bias_sums, held,
):
    ext = dy.shape[0]
    x, c, dp = place()
    refs = (cot_here, cot_beside, cot_near.at[0:ext], cot_far.at[ext:])
    for r, ref in enumerate(refs):
        dy[:, lanes_of(x, c, r)] = ref[...].astype(f32)
    branch_grad(1, dy, params, low, ext)
    low_t[...] = low[HALO : ext - HALO, :].T
    normed_t[...] = normed[HALO : ext - HALO, :].T
    hold_local((own_up, own_down, core_up, core_down), held)
    backward_half(
        dp, held, low, low_t, normed_t, active, slope, hidden_low, (give.at[0], give.at[1]), (keep0, keep1), bias_sums, ext
    )


def fifth_kernel(
    params, normed, low, low_t, normed_t, w_near, w_near_core, w_far, w_far_core,
    give, keep0, keep1, bias_sums, active, hidden_low, held, bias, slope,
):
    ext = normed.shape[0]
    x, c, dp = place()
    load_bias(x, c, 1, 1, params, bias)
    hold_far(dp % 2, (w_near, w_near_core, w_far, w_far_core), held)
    forward_half(bias, held, normed, active, slope, ext)
    backward_half(
        dp, held, low, low_t, normed_t, active, slope, hidden_low, (give.at[0], give.at[1]), (keep0, keep1), bias_sums, ext
    )


def branch_kernel(
    source, params, partial, active, hidden_far, held_far, hidden_near, own_up, own_down, core_up, core_down, _,
    branch, out, dnormed, held_near,
):
    ext = partial.shape[0]
    hold_local((own_up, own_down, core_up, core_down), held_near)

    def put(at, rows, value):
        if at == 0:
            out[0 : rows - HALO, :] = value[HALO:].astype(bf16)
        else:
            out[at - HALO :, :] = value[: rows - HALO].astype(bf16)

    finish_branch(1, source, params, held_far, active, partial, branch, ext, put)
    for at in (0, ext // 2):
        rows = slice(at, at + ext // 2)
        dnormed[rows, :] = back_half(held_near, hidden_near, rows) + back_half(held_far, hidden_far, rows)


def sixth_kernel(
    ids, source, params, centred, rstd, branch, dy, dnormed, bias_near, bias_far, _,
    grad_source, side_give, side_keep, dconv, small_c,
):
    ext = dy.shape[0]
    x, c, _d = place()

    def put(start, rows, inner, j, value):
        grad_source[start : start + rows, lane(j)] = value

    backward_norm(
        1, x, c, dy, source, ids, params, centred, rstd, branch, dnormed, dconv, small_c,
        bias_near, bias_far, side_give, side_keep, put, ext,
    )


def seventh_kernel(
    dy, params, normed, active_near, slope_near, active_far, slope_far,
    own_up, own_down, core_up, core_down, w_near, w_near_core, w_far, w_far_core0, w_far_core1,
    hidden_near, hidden_far, give,
    keep_near0, keep_near1, keep_far0, keep_far1, bias_near, bias_far,
    low, low_t, normed_t, held_near, held_far,
):
    ext = dy.shape[0]
    _x, _c, dp = place()
    branch_grad(0, dy, params, low, ext)
    low_t[...] = low[HALO : ext - HALO, :].T
    normed_t[...] = normed[HALO : ext - HALO, :].T
    hold_local((own_up, own_down, core_up, core_down), held_near)
    hold_far(dp % 2, (w_near, w_near_core, w_far, w_far_core0, w_far_core1), held_far)
    backward_half(
        dp, held_near, low, low_t, normed_t, active_near, slope_near, hidden_near,
        (give.at[0], give.at[1]), (keep_near0, keep_near1), bias_near, ext,
    )
    backward_half(
        dp, held_far, low, low_t, normed_t, active_far, slope_far, hidden_far,
        (give.at[2], give.at[3]), (keep_far0, keep_far1), bias_far, ext,
    )


def eighth_kernel(
    ids, source, params, centred, rstd, branch, dy, hidden_near, hidden_far, bias_near, bias_far, first_out,
    own_up, own_down, core_up, core_down, w_near, w_near_core, w_far, w_far_core0, w_far_core1, _,
    out_give0, out_give1, out_keep0, out_keep1, side_give, side_keep,
    dnormed, dconv, small_c, out, held_near, held_far,
):
    ext = dy.shape[0]
    x, c, dp = place()
    hold_local((own_up, own_down, core_up, core_down), held_near)
    hold_far(dp % 2, (w_near, w_near_core, w_far, w_far_core0, w_far_core1), held_far)
    for at in (0, ext // 2):
        rows = slice(at, at + ext // 2)
        dnormed[rows, :] = back_half(held_near, hidden_near, rows) + back_half(held_far, hidden_far, rows)

    def put(start, rows, inner, j, value):
        if inner:
            out[start - HALO : start - HALO + rows, lane(j)] = value.astype(bf16)

    backward_norm(
        0, x, c, dy, source, ids, params, centred, rstd, branch, dnormed, dconv, small_c,
        bias_near, bias_far, side_give, side_keep, put, ext,
    )
    for i, ref in enumerate((first_out, out)):
        for r, piece in enumerate((out_keep0, out_give0, out_keep1, out_give1)):
            piece[i] = ref[:, lanes_of(x, c, r)]


def adamw(param, first, second, grad):
    first = beta_first * first + (1.0 - beta_first) * grad
    second = beta_second * second + (1.0 - beta_second) * grad * grad
    first_hat = first * (1.0 / (1.0 - beta_first**adam_step))
    second_hat = second * (1.0 / (1.0 - beta_second**adam_step))
    update = first_hat / (jnp.sqrt(second_hat) + adam_eps) + decay_rate * param
    return update, first, second


def halving_plan(n_dp, axes):
    bits = {"x": lambda k: k[0], "y": lambda k: k[1] & 1, "z": lambda k: (k[1] >> 1) & 1}
    keys = [[(i, d) for i in range(2) for d in range(n_dp)] for _ in axes]
    plan = []
    for now in zip(*axes):
        give = [[k for k in keys[m] if bits[axis](k)] for m, axis in enumerate(now)]
        keep = [[k for k in keys[m] if not bits[axis](k)] for m, axis in enumerate(now)]
        groups = [(0, 1)] if now[0] == now[1] else [(0,), (1,)]
        plan.append((give, keep, groups))
        keys = keep
    return plan


def side_to_packet(packet, value):
    rows = value.shape[0]
    at = packet.shape[0] - 2 * rows
    hi = value.astype(bf16)
    lo = (value - hi.astype(f32)).astype(bf16)
    packet[at : at + rows, :] = hi
    packet[at + rows :, :] = lo
    return hi.astype(f32) + lo.astype(f32)


def side_of(packet):
    at = packet.shape[0] - 64
    return packet[at : at + 32, :].astype(f32) + packet[at + 32 :, :].astype(f32)


def put_blocks(step, packets, helds, value_of):
    give, keep, groups = step
    rows = helds[0].shape[1]
    for packet, group in zip(packets, groups):
        at = 0
        for m in group:
            for key in give[m]:
                packet[at : at + rows, :] = value_of(m, key).astype(bf16)
                at += rows
    for m, held in enumerate(helds):
        for at, key in enumerate(keep[m]):
            held[at] = value_of(m, key)


def got_blocks(step, gots, helds):
    _, keep, groups = step
    rows = helds[0].shape[1]
    places = {}
    for got, group in zip(gots, groups):
        at = 0
        for m in group:
            for spot, key in enumerate(keep[m]):
                places[m, key] = (got, at, spot)
                at += rows

    def value_of(m, key):
        got, at, spot = places[m, key]
        return helds[m][spot] + got[at : at + rows, :].astype(f32)

    return value_of


def core_sum_kernel(plan, count, *refs):
    got = [ref.at[i] for ref in refs[:count] for i in range(ref.shape[0])]
    keep = refs[count : count + 4]
    packets, helds = refs[-2 - len(plan[0][2]) : -2], refs[-2:]

    def value_of(m, key):
        i, d = key
        return keep[2 * i + m][d] + got[2 * i + m][d].astype(f32)

    put_blocks(plan[0], packets, helds, value_of)


def step_sum_kernel(plan, step, *refs):
    count, outs = len(plan[step - 1][2]), len(plan[step][2])
    gots, helds, rest = refs[:count], refs[count : count + 2], refs[count + 2 :]
    packets, helds_out, side_out = refs[-3 - outs : -3], refs[-3:-1], refs[-1]
    put_blocks(plan[step], packets, helds_out, got_blocks(plan[step - 1], gots, helds))
    if step == 1:
        got_side, keep_side = rest[:2]
        side = jnp.concatenate(
            [keep_side[i] + (got_side[i, 0].astype(f32) + got_side[i, 1].astype(f32)) for i in range(2)], axis=0
        )
    else:
        side = rest[0][...] + side_of(gots[0])
    side_out[...] = side_to_packet(packets[0], side)


def line_start_kernel(plan, *refs):
    count = len(plan[-1][2])
    gots, helds, side = refs[:count], refs[count : count + 2], refs[count + 2]
    packet, out, side_out = refs[-3:]
    value_of = got_blocks(plan[-1], gots, helds)
    rows = helds[0].shape[1]
    keep = plan[-1][1]
    half = len(keep[0]) // 2
    for m in range(2):
        for at, key in enumerate(keep[m]):
            value = value_of(m, key)
            if at % 2:
                start = (m * half + at // 2) * rows
                packet[start : start + rows, :] = value.astype(bf16)
            else:
                out[m * half + at // 2] = value
    side_out[...] = side_to_packet(packet, side[...] + side_of(gots[0]))


def line_sum_kernel(got, held, side, *refs):
    packet, out, side_out = refs[-3:]
    count, rows, _ = held.shape
    for at in range(count):
        value = held[at] + got[at * rows : (at + 1) * rows, :].astype(f32)
        if at % 2:
            packet[(at // 2) * rows : (at // 2 + 1) * rows, :] = value.astype(bf16)
        else:
            out[at // 2] = value
    side_out[...] = side_to_packet(packet, side[...] + side_of(got))


def update_kernel(layer, got, held, side, up, down, m_up, v_up, m_down, v_down, *refs):
    sent, main, side_near, side_far = refs[-4:]
    size = main.shape[1]
    if sent.shape[0] > 2 * size:
        sent[2 * size :, :] = refs[0][...]
    rows = up.shape[0]
    for m in range(2):
        main[m] = held[m] + got[m * size : (m + 1) * size, :].astype(f32)
    total = side[...] + side_of(got)
    side_near[...] = total[0:16]
    hi = total[16:32].astype(bf16)
    side_far[0:16, :] = hi
    side_far[16:32, :] = (total[16:32] - hi.astype(f32)).astype(bf16)
    for m, (p, first, second) in enumerate(((up, m_up, v_up), (down, m_down, v_down))):
        for j in range(size // rows):
            cols, at = lane(j), j * rows
            u, _, _ = adamw(
                p[:, cols], first[layer, :, cols], second[layer, :, cols], main[m, at : at + rows]
            )
            sent[m * size + at : m * size + at + rows, :] = u.astype(bf16)


def adam_kernel(main0, main1, m_up, v_up, m_down, v_down, f_up, s_up, f_down, s_down, token):
    token[...] = jnp.zeros_like(token)
    rows = m_up.shape[1]
    for l, main in enumerate((main0, main1)):
        for j in range(main.shape[1] // rows):
            cols, at = lane(j), j * rows
            for m, (first, second, first_out, second_out) in enumerate(
                ((m_up, v_up, f_up, s_up), (m_down, v_down, f_down, s_down))
            ):
                _, first_out[l, :, cols], second_out[l, :, cols] = adamw(
                    0.0, first[l, :, cols], second[l, :, cols], main[m, at : at + rows]
                )


def small_adam_kernel(
    side0, side1, far, chan, bias, m_chan, v_chan, m_bias, v_bias,
    u_chan, u_bias, f_chan, s_chan, f_bias, s_bias, token,
):
    token[...] = jnp.zeros_like(token)
    base = far.shape[0] - 64
    for l, side in enumerate((side0, side1)):
        at = base + 32 * l
        g = side[...] + (far[at : at + 16, :].astype(f32) + far[at + 16 : at + 32, :].astype(f32))
        u_chan[:, l, :], f_chan[:, l, :], s_chan[:, l, :] = adamw(
            chan[:, l, :], m_chan[:, l, :], v_chan[:, l, :], g[0:12]
        )
        for j in range(bias.shape[1] // LANES):
            row, cols = slice(l, l + 1), lane(j)
            u_bias[row, cols], f_bias[row, cols], s_bias[row, cols] = adamw(
                bias[row, cols], m_bias[row, cols], v_bias[row, cols], g[12 + j : 13 + j]
            )


def ring_order(n_dp):
    return list(range(0, n_dp, 2)) + list(range(n_dp - 1, 0, -2))


def ring_owner(n_dp):
    dp = lax.axis_index("dp")
    half = n_dp // 2
    spot = jnp.where(dp % 2 == 0, dp // 2, n_dp - 1 - dp // 2)

    def owner(distance):
        at = lax.rem(spot + distance + n_dp, n_dp)
        return jnp.where(at < half, 2 * at, 2 * (n_dp - 1 - at) + 1)

    return owner


def far_group(n_dp, rows):
    first = ring_owner(n_dp)(n_dp // 2) * rows
    return first // LANES, pl.ds(pl.multiple_of(first % LANES, rows), rows)


def spread_kernel(layers, n_dp, parts, *refs):
    blocks = refs[: n_dp - 1]
    up_out, down_out, up_group, held_group, up, held, down, sems = refs[-8:]
    owner = ring_owner(n_dp)
    distances = [0]
    for step in range(1, n_dp // 2):
        distances += [-step, step]
    rows = up.shape[1] // n_dp
    size = parts * rows
    groups = up.shape[1] // LANES
    group, _ = far_group(n_dp, rows)

    def copies_of(l, k):
        part = pl.ds(k * LANES, LANES)
        pairs = ((up.at[l, part], up_out.at[l, part]), (down.at[l, :, part], down_out.at[l, :, part]))
        return [pltpu.make_async_copy(*pair, sems.at[2 * (l * groups + k) + i]) for i, pair in enumerate(pairs)]

    def each(l, k, act):
        def run():
            for copy in copies_of(l, k):
                act(copy)

        pl.when(group != k)(run)

    for l in range(layers):
        for distance, ref in zip(distances, blocks):
            at = pl.ds(pl.multiple_of(owner(distance) * rows, rows), rows)
            for j in range(parts):
                start = 2 * size * l + j * rows
                up[l, at, lane(j)] = ref[start : start + rows, :].astype(f32)
                start += size
                held[l, at, lane(j)] = ref[start : start + rows, :].astype(f32)
        for j in range(parts):
            down[l, lane(j), :] = held[l, :, lane(j)].T
        for k in range(groups):
            each(l, k, lambda copy: copy.start())
    whole = pl.ds(pl.multiple_of(group * LANES, LANES), LANES)
    for l in range(layers):
        up_group[l] = up[l, whole, :]
        held_group[l] = held[l, whole, :]
    for l in range(layers):
        for k in range(groups):
            each(l, k, lambda copy: copy.wait())


def last_spread_kernel(layers, n_dp, parts, top, bottom, up_group, held_group, *refs):
    up_out, down_out, up, held, down, sems = refs[-6:]
    rows = top.shape[0] // (2 * parts)
    size = parts * rows
    group, at = far_group(n_dp, rows)
    whole = pl.ds(pl.multiple_of(group * LANES, LANES), LANES)
    copies = []
    for l, far in enumerate((top, bottom)):
        up[l] = up_group[l]
        held[l] = held_group[l]
        for j in range(parts):
            up[l, at, lane(j)] = far[j * rows : (j + 1) * rows, :].astype(f32)
            held[l, at, lane(j)] = far[size + j * rows : size + (j + 1) * rows, :].astype(f32)
        for j in range(parts):
            down[l, lane(j), :] = held[l, :, lane(j)].T
        pairs = [(up.at[l], up_out.at[l, whole]), (down.at[l], down_out.at[l, :, whole])]
        copies += start_copies(pairs, sems.at[pl.ds(2 * l, 2)])
    for copy in copies:
        copy.wait()


def pack_kernel(keep, got, side0, side1, _, packet):
    rows = keep.shape[1]
    for i, ref in enumerate((keep, got)):
        for o in range(2):
            at = (2 * i + o) * rows
            packet[at : at + rows, :] = ref[o]
    packet[4 * rows : 4 * rows + 32, :] = side0[...]
    packet[4 * rows + 32 :, :] = side1[...]


def collect_kernel(own, core, far, out, grad, token):
    token[...] = jnp.zeros_like(token)
    x, c, _ = place()
    rows = own.shape[1]
    for o, target in enumerate((out, grad)):
        for r in range(4):
            at = pl.multiple_of(((x ^ (r // 2)) * 2 + (c ^ (r % 2))) * rows, HALO)
            if r < 2:
                target[pl.ds(at, rows), :] = (own, core)[r][o]
            else:
                start = (2 * (r - 2) + o) * rows
                target[pl.ds(at, rows), :] = far[start : start + rows, :]


def finish_kernel(own, core, far, *refs):
    collect_kernel(own, core, far, refs[8], refs[9], refs[-1])
    small_adam_kernel(refs[0], refs[1], far, *refs[2:8], *refs[10:])


VMEM = pl.BlockSpec(memory_space=pltpu.VMEM)
ANY = pl.BlockSpec(memory_space=pl.ANY)
HBM = pl.BlockSpec(memory_space=pltpu.HBM)


def call(kernel, outs, in_specs, scratch, name, limit=16, out_specs=None, flops=0, aliases=None):
    return pl.pallas_call(
        kernel,
        out_shape=[jax.ShapeDtypeStruct(s, t) for s, t in outs],
        in_specs=in_specs,
        out_specs=out_specs or [VMEM] * len(outs),
        scratch_shapes=scratch,
        input_output_aliases=aliases or {},
        compiler_params=pltpu.CompilerParams(vmem_limit_bytes=limit * 1024 * 1024),
        cost_estimate=pl.CostEstimate(flops=flops, bytes_accessed=0, transcendentals=0),
        name=name,
    )


def on_device(
    n_dp, frames_in, segments, cotangent, channel_params, weight_up, bias_up, weight_down,
    momentum_channel, variance_channel, momentum_up, variance_up, momentum_bias, variance_bias,
    momentum_down, variance_down,
):
    rows, frames, part = frames_in.shape
    layers, width, quarter = weight_up.shape
    chip_hidden = 2 * quarter
    tokens = rows * frames
    own = tokens // 4
    ext = own + 2 * HALO
    shard = width // n_dp
    parts = quarter // LANES

    def core_swap(v):
        return lax.ppermute(v, "chan", xor_perm(4, 1))

    def x_swap(v):
        return lax.ppermute(v, "chan", xor_perm(4, 2))

    def dp_swap(v, bit):
        return lax.ppermute(v, "dp", xor_perm(n_dp, bit))

    def after(value, *others):
        return lax.optimization_barrier((value, *others))[0]

    sems = pltpu.SemaphoreType.DMA((8,))
    width_sems = pltpu.SemaphoreType.DMA((16,))
    chan, m_chan, v_chan = [
        jnp.swapaxes(v, 0, 1) for v in (channel_params, momentum_channel, variance_channel)
    ]
    up_held = pltpu.VMEM((width, quarter), f32)
    down_held = pltpu.VMEM((quarter, width), f32)
    matrix = ((width, quarter), bf16)

    def in_hbm(*arrays):
        return [pltpu.with_memory_space_constraint(v, pltpu.HBM) for v in arrays]

    packet = ((ext + 2 * PARAM_ROWS, LANES), bf16)
    flat = pltpu.VMEM((tokens + 2 * HALO, LANES), bf16)
    both_packets = ((2 * packet[0][0], LANES), bf16)
    give, here, beside, chosen0 = call(
        prepare_kernel, [both_packets, packet, packet, matrix], [HBM] * 5,
        [flat, pltpu.VMEM(chan.shape, f32), pltpu.VMEM(bias_up.shape, f32), up_held, down_held, sems, sems],
        "prepare",
    )(*in_hbm(frames_in, chan, bias_up, weight_up, weight_down))
    frames_far = x_swap(give)
    near0 = x_swap(chosen0)
    frames_core = core_swap(frames_far)
    packets = [here, core_swap(beside), frames_far, frames_core]
    cot_packet = ((ext, LANES), bf16)
    slice_shape = ((shard, quarter), f32)
    chosen1, *both, give, here, beside, ids, up0, down0, up1, down1 = call(
        rest_kernel,
        [matrix] * 5 + [((2 * ext, LANES), bf16)] + [cot_packet] * 2 + [((ext + 2 * PAD, LANES), jnp.int32)] + [slice_shape] * 4,
        [HBM] * 3 + [VMEM, ANY],
        [flat, pltpu.VMEM((tokens + 2 * HALO + 2 * PAD, LANES), jnp.int32)]
        + [pltpu.VMEM(weight_up.shape, f32), pltpu.VMEM(weight_down.shape, f32), up_held, sems, width_sems],
        "rest", 24, flops=LONG,
    )(*in_hbm(weight_up, weight_down, cotangent), segments, beside)
    near1 = x_swap(chosen1)
    slices0, slices1 = [up0, down0], [up1, down1]
    local0, local1 = [v + [core_swap(w) for w in v] for v in (both[:2], both[2:])]
    cots = [here, core_swap(beside)]

    wide = (ext, width)
    padded = (ext + 2 * PAD, width)
    deep = (ext, chip_hidden)
    held = pltpu.VMEM((2, width, chip_hidden), bf16)
    bias = pltpu.VMEM((1, chip_hidden), f32)
    sums = ((1, chip_hidden), f32)
    params_shape = ((PARAM_ROWS, width), f32)
    turned = ((width, own), bf16)
    norm_shapes = [(wide, f32), ((ext, LANES), f32), (wide, bf16)]
    half_shapes = [(deep, bf16), (deep, f32), (wide, f32)]
    size = parts * shard
    grads = [((2, n_dp, size, LANES), bf16)] + [((n_dp, size, LANES), f32)] * 2
    side_shapes = [((2, 2, 16, LANES), bf16), ((2, 16, LANES), f32)]
    norm_scratch = [pltpu.VMEM(padded, f32), pltpu.VMEM((16, width), f32)]

    def buffers(shapes):
        return [pltpu.VMEM(s, t) for s, t in shapes]

    first = call(
        first_kernel, norm_shapes + half_shapes + [(padded, f32), params_shape],
        [VMEM] * 9 + [ANY], [bias, held], "layer0_near", 24,
    )
    centred0, rstd0, normed0, active00, slope00, partial0, source0, params = first(
        ids, *packets, *local0, ids
    )
    cot_far = x_swap(after(give, near0))
    far0 = dp_swap(after(near0, chosen1), 1)
    far1 = dp_swap(after(near1, partial0), 1)
    pieces0 = call(split_kernel, [((width // 2, quarter), bf16)] * 2, [VMEM] + [ANY] * 2, [], "split")(
        far0, partial0, partial0
    )
    away0 = [near0, core_swap(near0), far0] + [core_swap(v) for v in pieces0]
    second = call(
        second_kernel, [(padded, f32)] + half_shapes, [VMEM] * 9 + [ANY],
        [bias, held], "layer0_far", 24,
    )
    source1, active01, slope01, branch0 = second(source0, params, normed0, partial0, *away0, partial0)
    third = call(
        third_kernel, norm_shapes + half_shapes, [VMEM] * 7 + [ANY],
        [bias, held], "layer1_near", 24,
    )
    centred1, rstd1, normed1, active10, slope10, partial1 = third(ids, source1, params, *local1, cots[1])
    cots += [cot_far, core_swap(cot_far)]
    fourth = call(
        fourth_kernel, [(wide, f32), (wide, bf16), turned, turned] + grads + [(deep, bf16), sums],
        [VMEM] * 12, [held], "layer1_near_back", 24,
    )
    dy1, low1, low_t1, normed_t1, give10, *keep10, hidden10, bias10 = fourth(
        *cots, params, normed1, active10, slope10, *local1
    )
    got10 = core_swap(give10)
    away1 = [near1, core_swap(near1), far1, core_swap(after(far1, active10))]
    fifth = call(
        fifth_kernel, grads + [sums, (deep, bf16), (deep, bf16), ((2, width, chip_hidden), bf16)],
        [VMEM] * 9, [bias] + buffers([(deep, f32)]), "layer1_far", 28, flops=LONG,
    )
    give11, *keep11, bias11, active11, hidden11, held11 = fifth(
        params, normed1, low1, low_t1, normed_t1, *away1
    )
    got11 = core_swap(give11)
    branch1, first_out, dnormed1 = call(
        branch_kernel, [(wide, f32), ((own, width), bf16), (wide, f32)], [VMEM] * 11 + [ANY], [held],
        "layer1_branch", 24, flops=LONG,
    )(source1, params, partial1, active11, hidden11, held11, hidden10, *local1, bias11)

    half = n_dp // 2
    plans = [halving_plan(n_dp, axes) for axes in AXES]
    side_shape = ((32, LANES), f32)

    def packet_of(blocks, side=False):
        return ((blocks * size + (64 if side else 0), LANES), bf16)

    def combine(kernel, outs, args, before, name, flops=0):
        specs = [VMEM] * len(args) + [ANY] * len(before)
        return call(kernel, outs, specs, [], name, flops=flops)(*args, *before)

    def step_outs(layer, step):
        give, keep, groups = plans[layer][step]
        outs = [packet_of(sum(len(give[m]) for m in g), step > 0 and n == 0) for n, g in enumerate(groups)]
        outs += [((len(k), size, LANES), f32) for k in keep]
        return outs + ([side_shape] if step else [])

    def exchange(layer, step, packets):
        swaps = {"x": x_swap, "y": lambda v: dp_swap(v, 1), "z": lambda v: dp_swap(v, 2)}
        groups = plans[layer][step][2]
        return [swaps[AXES[layer][g[0]][step]](v) for v, g in zip(packets, groups)]

    def core_step(layer, gots, keeps, before):
        kernel = functools.partial(core_sum_kernel, plans[layer], len(gots))
        outs = combine(kernel, step_outs(layer, 0), [*gots, *keeps], before, "core_sum")
        return outs[:-2], outs[-2:]

    def next_step(layer, step, got, helds, sides, before, flops=0):
        kernel = functools.partial(step_sum_kernel, plans[layer], step)
        outs = combine(kernel, step_outs(layer, step), [*got, *helds, *sides], before, "step_sum", flops)
        return outs[:-3], outs[-3:-1], outs[-1]

    def line_start(layer, got, helds, side, before):
        left = n_dp // 4
        outs = [packet_of(left, True), ((left, size, LANES), f32), side_shape]
        kernel = functools.partial(line_start_kernel, plans[layer])
        state = combine(kernel, outs, [*got, *helds, side], before, "line_start")
        bit = 4
        while bit < half:
            left //= 2
            outs = [packet_of(left, True), ((left, size, LANES), f32), side_shape]
            state = combine(line_sum_kernel, outs, [dp_swap(state[0], bit), *state[1:]], [], "line_sum")
            bit *= 2
        return state

    down_moments = [jnp.swapaxes(v, 1, 2) for v in (momentum_down, variance_down)]

    def update_step(layer, packet, main, side, slices, others, before):
        outs = [packet_of(2 + 2 * len(others)), ((2, size, LANES), f32)]
        outs += [((16, LANES), f32), ((32, LANES), bf16)]
        args = [dp_swap(packet, half), main, side, *slices, momentum_up, variance_up, *down_moments]
        args += others
        return combine(functools.partial(update_kernel, layer), outs, args, before, "update")

    order = ring_order(n_dp)
    ahead = [(order[i], order[(i + 1) % n_dp]) for i in range(n_dp)]
    back = [(b, a) for a, b in ahead]

    def ring_step(right, left):
        return lax.ppermute(right, "dp", ahead), lax.ppermute(left, "dp", back)

    def ring_end(right, left):
        cut = right.shape[0] // 2
        return lax.ppermute(right[:cut], "dp", ahead), lax.ppermute(left[cut:], "dp", back)

    def blocks_of(ring):
        return [ring[0][0]] + [v for pair in ring[1:] for v in pair]

    packets1, helds1 = core_step(1, [got10, got11], [*keep10, *keep11], [branch1])
    sixth = call(
        sixth_kernel, [(wide, f32)] + side_shapes, [VMEM] * 10 + [ANY], norm_scratch, "layer1_norm_back", 24
    )
    grad1, *sides1 = sixth(
        ids, source1, params, centred1, rstd1, branch1, dy1, dnormed1, bias10, bias11, packets1[0]
    )
    seventh = call(
        seventh_kernel, [(deep, bf16)] * 2 + [((4, n_dp, size, LANES), bf16)] + [grads[1]] * 4 + [sums] * 2,
        [VMEM] * 16, buffers([(wide, bf16), turned, turned]) + [held, held],
        "layer0_back", 28,
    )
    hidden0, hidden1, *matrices0, bias00, bias01 = seventh(
        grad1, params, normed0, active00, slope00, active01, slope01, *local0, *away0
    )
    eighth = call(
        eighth_kernel, [((2, own, LANES), bf16)] * 4 + side_shapes, [VMEM] * 21 + [ANY],
        buffers([(wide, f32)]) + norm_scratch + buffers([((own, width), bf16)]) + [held, held],
        "layer0_norm_back", 28, flops=LONG,
    )
    give_near, give_far, keep_near, keep_far, *sides0 = eighth(
        ids, source0, params, centred0, rstd0, branch0, grad1, hidden0, hidden1, bias00, bias01, first_out,
        *local0, *away0, bias01,
    )

    sides = [core_swap(sides1[0]), sides1[1]]
    packets1, helds1, side1 = next_step(1, 1, exchange(1, 0, packets1), helds1, sides, [], LONG)
    packets0, helds0 = core_step(0, [core_swap(matrices0[0])], matrices0[1:], [packets1[0]])
    crossed0 = exchange(0, 0, packets0)
    sides = [core_swap(sides0[0]), sides0[1]]
    got = exchange(1, 1, packets1)
    packets1, helds1, side1 = next_step(1, 2, got, helds1, [side1], [])
    packets0, helds0, side0 = next_step(0, 1, crossed0, helds0, sides, [packets1[0]], LONG)
    got0 = exchange(0, 1, packets0)
    line1 = line_start(1, exchange(1, 2, packets1), helds1, side1, [])
    packets0, helds0, side0 = next_step(0, 2, got0, helds0, [side0], [line1[0]])
    sent1, main1, side1, side_far1 = update_step(1, *line1, slices1, [], [])
    line0 = line_start(0, exchange(0, 2, packets0), helds0, side0, [])
    sent, main0, side0, side_far0 = update_step(0, *line0, slices0, [sent1], [])
    ring = [(sent, sent)]
    ring.append(ring_step(sent, sent))

    got_near, got_far = core_swap(give_near), core_swap(give_far)
    far_packet = ((4 * own + 64, LANES), bf16)
    from_far = x_swap(
        call(pack_kernel, [far_packet], [VMEM] * 4 + [ANY], [], "pack")(
            keep_far, got_far, side_far0, side_far1, sent
        )[0]
    )
    token = ((8, LANES), f32)
    chan_shape, bias_shape = (chan.shape, f32), (bias_up.shape, f32)
    adam_outs = [(momentum_up.shape, f32)] * 2 + [(down_moments[0].shape, f32)] * 2 + [token]
    first_up, second_up, first_down, second_down, matrix_token = call(
        adam_kernel, adam_outs, [VMEM] * 6, [], "adam"
    )(main0, main1, momentum_up, variance_up, *down_moments)
    small_outs = [chan_shape, bias_shape, chan_shape, chan_shape, bias_shape, bias_shape, token]
    (
        layer_output, input_grad,
        params_channel, params_bias, first_channel, second_channel, first_bias, second_bias, finish_token,
    ) = call(finish_kernel, [((tokens, part), bf16)] * 2 + small_outs, [VMEM] * 11, [], "finish")(
        keep_near, got_near, from_far,
        side0, side1, chan, bias_up, m_chan, v_chan, momentum_bias, variance_bias,
    )
    right, left = ring[1]
    for step in range(2, half):
        if step == 2:
            right, left = after(right, matrix_token), after(left, matrix_token)
        right, left = ring_step(right, left)
        ring.append((right, left))
    ring.append(ring_end(right, left))
    whole = [(weight_up.shape, f32), (weight_down.shape, f32)]
    group_shape = ((layers, LANES, quarter), f32)
    group_scratch = buffers([group_shape, group_shape, ((layers, quarter, LANES), f32)])
    spread = call(
        functools.partial(spread_kernel, layers, n_dp, parts), whole + [group_shape] * 2, [VMEM] * (n_dp - 1),
        buffers([(weight_up.shape, f32)] * 2 + [(weight_down.shape, f32)]) + [width_sems],
        "spread", 16, [HBM, HBM, VMEM, VMEM],
    )
    last_spread = call(
        functools.partial(last_spread_kernel, layers, n_dp, parts), whole, [VMEM] * 4 + [HBM] * 2 + [ANY],
        group_scratch + [sems], "last_spread", 16, [HBM, HBM], aliases={4: 0, 5: 1},
    )
    blocks = blocks_of(ring)
    params_up, params_down, *missing = spread(*blocks[:-2])
    params_up, params_down = last_spread(
        *blocks[-2:], *missing, params_up, params_down, finish_token
    )

    params_channel, first_channel, second_channel = [
        jnp.swapaxes(v, 0, 1) for v in (params_channel, first_channel, second_channel)
    ]
    first_down, second_down = jnp.swapaxes(first_down, 1, 2), jnp.swapaxes(second_down, 1, 2)

    layer_output, input_grad = [v.reshape(rows, frames, part) for v in (layer_output, input_grad)]
    return (
        layer_output,
        input_grad,
        params_channel,
        params_up,
        params_bias,
        params_down,
        first_channel,
        second_channel,
        first_up,
        second_up,
        first_bias,
        second_bias,
        first_down,
        second_down,
    )


def solution(mesh):
    return jax.shard_map(
        functools.partial(on_device, mesh.shape["dp"]),
        mesh=mesh,
        in_specs=(
            P("dp", None, "chan"),
            P("dp", None),
            P("dp", None, "chan"),
            P(None, None, "chan"),
            P(None, None, "chan"),
            P(None, "chan"),
            P(None, "chan", None),
            P(None, None, "chan"),
            P(None, None, "chan"),
            P(None, "dp", "chan"),
            P(None, "dp", "chan"),
            P(None, "chan"),
            P(None, "chan"),
            P(None, "chan", "dp"),
            P(None, "chan", "dp"),
        ),
        out_specs=(
            P("dp", None, "chan"),
            P("dp", None, "chan"),
            P(None, None, "chan"),
            P(None, None, "chan"),
            P(None, "chan"),
            P(None, "chan", None),
            P(None, None, "chan"),
            P(None, None, "chan"),
            P(None, "dp", "chan"),
            P(None, "dp", "chan"),
            P(None, "chan"),
            P(None, "chan"),
            P(None, "chan", "dp"),
            P(None, "chan", "dp"),
        ),
        check_vma=False,
    )
```
